32 devices in a mesh: groups: 2 (over y), adapter: 4 (over z), segment: 2 (over x), replica: 2 (over core).
Axes of the slice: x: 2, y: 2, z: 4, core: 2. Of those that a mesh axis runs over, the one named last changes fastest.
Arguments:
- saved_layer_input: bfloat16 [2, 2816, 4096], P('segment', ('groups', 'adapter', 'replica')), parts along dimension 1, may hold values from -6 to 6
- value_output_gradient: bfloat16 [2, 2816, 1024], P('segment', ('groups', 'adapter', 'replica')), parts along dimension 1, may hold values from -6 to 6
- token_adapter_index: int32 [2, 2816, 1], P('segment', ('groups', 'adapter', 'replica')), parts along dimension 1, may hold values from 0 to 7; in each aligned block of 176 rows (0 to 175, 176 to 351, ..., all dimensions but the last counted through in order) at most 33 rows name the same one
- adapter_slot_index: int32 [16], P('groups'), parts along dimension 0, may hold values from 0 to 7, each once
- frozen_value_weight: bfloat16 [2, 4096, 1024], P('segment', 'adapter'), may hold values from -0.1875 to 0.1875
- adapter_down_weight: bfloat16 [2, 8, 16, 4096], P('segment', 'adapter'), may hold values from -0.09375 to 0.09375
- adapter_up_weight: bfloat16 [2, 8, 16, 1024], P('segment', 'adapter'), may hold values from -0.1875 to 0.1875
Outputs:
- passed_grads: bfloat16 [2, 2816, 4096], P('segment', ('groups', 'adapter', 'replica')), parts along dimension 1
- grad_down: bfloat16 [4, 8, 16, 4096], P(('groups', 'segment'), 'adapter'), parts along dimension 0
- grad_up: bfloat16 [4, 8, 16, 1024], P(('groups', 'segment'), 'adapter'), parts along dimension 0
The draws below stay inside these ranges and needn't reach their ends.
There are 2 independent parts, one for each index of `groups`. The reference program is written for one: setup_inputs(seed, part) draws one part's arguments, and reference() takes and returns one part's arrays. A program takes and returns all parts, laid end to end along the dimension named above; an argument that names none is the same for every part. Nothing has to cross between parts.
Inputs may be any that keep to these rules, and one draw needn't show every extreme that they name: `token_adapter_index`: within the 176 tokens of one device no adapter is named by more than 33 tokens. `adapter_slot_index`: each slot is taken by exactly one adapter.
All inputs are finite; a program needn't handle non-finite values.
Results may differ from the reference program's by a relative error of at most 0.0085.
Values may be sent and summed in bfloat16 or wider, within the bound.
No kernel may reach another device: no remote copies, remote signals or barrier semaphores. Data moves between devices by JAX's collectives and lax.ppermute only.
A program may use at most 64 MiB of HBM per device.

```python
import math
import jax
import jax.numpy as jnp
import numpy as np

MODEL_WIDTH = 4096
VALUE_WIDTH = 1024
ADAPTER_RANK = 16
TOK_DEV = 176
ADAPTER_TOTAL = 8
CAP = 33
ROWS = 1408
N_SEGMENT = 2


def block_levels(rng, extent, split, smallest, largest):
    level, own = 1.0, jax.random.fold_in(rng, 6)
    for axis_at, blocks in split:
        heights = jnp.exp(jax.random.uniform(jax.random.fold_in(own, axis_at), (blocks,), jnp.float32, smallest / len(split), largest / len(split)))
        level = level * jnp.repeat(heights, extent[axis_at] // blocks).reshape([-1 if axis == axis_at else 1 for axis in range(len(extent))])
    return level


def assign_block(rng, own, number, rows, number_of, top, reach, skew):
    sequence = jax.random.permutation(rng, number_of)
    crowded, common = portions_of(number_of, rows * top, reach, skew, True), portions_of(number_of, rows * top, reach, skew, False)
    places = jnp.arange(number_of)

    def named(tallies, offset_by):
        used = int((tallies > 0).sum())
        fixed = max(1, used // 4)
        moved = fixed + (places - fixed + offset_by * (used - fixed)) % max(1, number_of - fixed)
        return jnp.zeros((number_of,), jnp.int32).at[sequence[jnp.where(places < fixed, places, moved)]].set(jnp.asarray(tallies, jnp.int32))

    tallies = jnp.where(number % 4 == 0, named(crowded, number // 4), named(common, number - number // 4 - 1))
    mixed = jax.random.permutation(jax.random.fold_in(own, 3), number_of)
    donor, taker = mixed[0:number_of // 2 * 2:2], mixed[1:number_of // 2 * 2:2]
    slack = jnp.minimum(tallies[donor] - 1, reach - tallies[taker]) // 2
    slack = jnp.where((donor == sequence[0]) | (taker == sequence[0]) | (tallies[taker] == 0), 0, jnp.maximum(slack, 0))
    moved = jax.random.randint(jax.random.fold_in(own, 4), (number_of // 2,), 0, 1 << 20) % (slack + 1)
    tallies = tallies.at[donor].add(-moved).at[taker].add(moved)
    labels = jnp.searchsorted(jnp.cumsum(tallies), jnp.arange(rows * top), side="right").astype(jnp.int32)
    table = labels.reshape(top, rows).T
    table = table[jax.random.permutation(jax.random.fold_in(own, 1), rows)]
    offset_by = jax.random.randint(jax.random.fold_in(own, 2), (rows, 1), 0, top)
    return jnp.take_along_axis(table, (jnp.arange(top)[None, :] + offset_by) % top, axis=1)


def portions_of(count, total, bound, skew, full):
    loads = [(1 << 20) // math.isqrt(standing ** skew) + 1 for standing in range(1, count + 1)]
    largest = bound if full else min(bound, max(-(-total // count), total * loads[0] // sum(loads)))
    least = 1 if total - largest >= count - 1 else 0
    given, spare = [largest] + [least] * (count - 1), total - largest - least * (count - 1)
    while spare > 0:
        free = [i for i in range(1, count) if given[i] < largest] or [i for i in range(1, count) if given[i] < bound]
        mass, budget = sum([loads[i] for i in free]), spare
        for i in free:
            more = min(bound - given[i], max(1, budget * loads[i] // mass), spare)
            given[i] = given[i] + more
            spare = spare - more
    return np.array(given)


def scatter_about(key, dims, scale, bound, cuts=(), held_as=jnp.bfloat16):
    drawn = scale * jax.random.normal(key, dims, jnp.float32)
    if cuts:
        drawn = drawn * block_levels(key, dims, cuts, -0.22, 0.18)
    return jnp.clip(drawn, -bound, bound).astype(held_as)


def setup_inputs(seed: int = 0, part: int = 0) -> dict:
    keys = jax.random.split(jax.random.key(seed), 8)
    part_splits = jax.random.split(jax.random.fold_in(keys[7], part), 8)
    saved_layer_input = scatter_about(part_splits[0], (N_SEGMENT, ROWS, MODEL_WIDTH), 1.0, 6.0, ((0, 2), (1, 8)))
    value_output_gradient = scatter_about(part_splits[1], (N_SEGMENT, ROWS, VALUE_WIDTH), 1.0, 6.0, ((0, 2), (1, 8)))
    token_adapter_index_keys = jax.random.split(jax.random.fold_in(part_splits[2], 1), N_SEGMENT * ROWS // TOK_DEV)
    token_adapter_index_turns = jax.random.permutation(jax.random.fold_in(part_splits[2], 3), N_SEGMENT * ROWS // TOK_DEV)
    token_adapter_index = jax.vmap(lambda own, number: assign_block(jax.random.fold_in(part_splits[2], 2), own, number, TOK_DEV, ADAPTER_TOTAL, 1, CAP, 2))(token_adapter_index_keys, token_adapter_index_turns).reshape((N_SEGMENT, ROWS, 1))
    adapter_slot_index = jax.random.permutation(part_splits[3], ADAPTER_TOTAL).astype(jnp.int32)
    frozen_value_weight = scatter_about(keys[4], (N_SEGMENT, MODEL_WIDTH, VALUE_WIDTH), VALUE_WIDTH ** -0.5, 0.1875, ((0, 2), (1, 4)))
    adapter_down_weight = scatter_about(keys[5], (N_SEGMENT, ADAPTER_TOTAL, ADAPTER_RANK, MODEL_WIDTH), MODEL_WIDTH ** -0.5, 0.09375, ((0, 2), (1, 4)))
    adapter_up_weight = scatter_about(keys[6], (N_SEGMENT, ADAPTER_TOTAL, ADAPTER_RANK, VALUE_WIDTH), VALUE_WIDTH ** -0.5, 0.1875, ((0, 2), (1, 4)))
    return {"saved_layer_input": saved_layer_input, "value_output_gradient": value_output_gradient, "token_adapter_index": token_adapter_index, "adapter_slot_index": adapter_slot_index, "frozen_value_weight": frozen_value_weight, "adapter_down_weight": adapter_down_weight, "adapter_up_weight": adapter_up_weight}


ADAPTER_SCALE = 2.0


def reference(saved_layer_input, value_output_gradient, token_adapter_index, adapter_slot_index, frozen_value_weight, adapter_down_weight, adapter_up_weight):
    count_adapters = adapter_slot_index.shape[0]
    hidden_width = saved_layer_input.shape[2]
    value_proj_width = value_output_gradient.shape[2]
    slot_range = jnp.arange(count_adapters, dtype=jnp.int32)
    total_list = []
    down_list = []
    up_list = []
    for section_number in range(N_SEGMENT):
        inputs = saved_layer_input[section_number]
        grad_rows = value_output_gradient[section_number]
        row_ids = token_adapter_index[section_number, :, 0].astype(jnp.int32)
        onehot = row_ids[:, None] == slot_range[None, :]
        slot_row = jnp.sum(jnp.where(onehot, adapter_slot_index[None, :], 0), axis=1).astype(jnp.int32)
        slot_mask = slot_row[:, None] == slot_range[None, :]
        keep_mask = jnp.repeat(slot_mask, ADAPTER_RANK, axis=1)
        gathered_down_maps = adapter_down_weight[section_number].reshape(count_adapters * ADAPTER_RANK, hidden_width)
        gathered_up_maps = adapter_up_weight[section_number].reshape(count_adapters * ADAPTER_RANK, value_proj_width)
        frozen_matrix = jnp.dot(grad_rows, frozen_value_weight[section_number].T, preferred_element_type=jnp.float32).astype(jnp.bfloat16)
        proj_in = jnp.dot(inputs, gathered_down_maps.T, preferred_element_type=jnp.float32).astype(jnp.bfloat16)
        proj_grad = jnp.dot(grad_rows, gathered_up_maps.T, preferred_element_type=jnp.float32).astype(jnp.bfloat16)
        zero_fill = jnp.zeros_like(proj_in)
        in_sel = jnp.where(keep_mask, proj_in, zero_fill)
        selected_gradient = jnp.where(keep_mask, proj_grad, zero_fill)
        adapter_portion = (ADAPTER_SCALE * jnp.dot(selected_gradient, gathered_down_maps, preferred_element_type=jnp.float32)).astype(jnp.bfloat16)
        gradient_total = (frozen_matrix.astype(jnp.float32) + adapter_portion.astype(jnp.float32)).astype(jnp.bfloat16)
        total_list.append(gradient_total)
        down_grad = ADAPTER_SCALE * jnp.dot(selected_gradient.T, inputs, preferred_element_type=jnp.float32)
        up_grad = ADAPTER_SCALE * jnp.dot(in_sel.T, grad_rows, preferred_element_type=jnp.float32)
        down_list.append(down_grad.reshape(count_adapters, ADAPTER_RANK, hidden_width).astype(jnp.bfloat16))
        up_list.append(up_grad.reshape(count_adapters, ADAPTER_RANK, value_proj_width).astype(jnp.bfloat16))
    stacked = jnp.stack(total_list, axis=0)
    passed_grads = jnp.concatenate([stacked[1:], stacked[:1]], axis=0)
    return passed_grads, jnp.stack(down_list, axis=0), jnp.stack(up_list, axis=0)
```

```python
import jax
import jax.numpy as jnp
from jax import lax
from jax.sharding import PartitionSpec as P

ADAPTER_SCALE = 2.0
COPIES = ("groups", "replica")
LINE = ("adapter", "groups", "replica")


def passed_along(x, axis, by):
    size = lax.axis_size(axis)
    return lax.ppermute(x, axis, [(i, (i + by) % size) for i in range(size)])


def my_piece(x, parts):
    rows = x.shape[0] // parts
    piece = lax.axis_index("groups") * lax.axis_size("replica") + lax.axis_index("replica")
    return lax.dynamic_slice_in_dim(x, piece * rows, rows, axis=0)


def on_device(
    saved_layer_input,
    value_output_gradient,
    token_adapter_index,
    adapter_slot_index,
    frozen_value_weight,
    adapter_down_weight,
    adapter_up_weight,
):
    inputs = saved_layer_input[0]
    grad_rows = value_output_gradient[0]
    row_ids = token_adapter_index[0, :, 0]
    width = inputs.shape[1]
    value_width = grad_rows.shape[1]
    adapters = adapter_slot_index.shape[0]
    holders = lax.axis_size("adapter")
    copies = lax.axis_size("groups") * lax.axis_size("replica")
    slots, rank = adapter_down_weight.shape[1:3]
    frozen = frozen_value_weight[0]
    shard = frozen.shape[0]
    chunks = max(1, shard // 256)
    step = shard // chunks

    both = jnp.concatenate(
        [
            adapter_down_weight[0].reshape(slots * rank, width),
            adapter_up_weight[0].reshape(slots * rank, value_width),
        ],
        axis=1,
    )
    both = lax.all_gather(my_piece(both, copies), LINE, axis=0, tiled=True)
    down, up = both[:, :width], both[:, width:]

    weights = [
        lax.all_gather(
            my_piece(frozen[c * step : (c + 1) * step], copies), LINE, axis=0, tiled=True
        )
        for c in range(chunks)
    ]

    slot_range = jnp.arange(adapters, dtype=jnp.int32)
    slot_row = jnp.sum(
        jnp.where(row_ids[:, None] == slot_range[None, :], adapter_slot_index[None, :], 0), axis=1
    )
    owner = jnp.arange(adapters * rank, dtype=jnp.int32) // rank
    keep = slot_row[:, None] == owner[None, :]

    proj_in = jnp.einsum("td,rd->tr", inputs, down, preferred_element_type=jnp.float32)
    proj_grad = jnp.einsum("tk,rk->tr", grad_rows, up, preferred_element_type=jnp.float32)
    in_sel = jnp.where(keep, proj_in, 0.0).astype(jnp.bfloat16)
    grad_sel = jnp.where(keep, proj_grad, 0.0).astype(jnp.bfloat16)
    part = jnp.concatenate(
        [
            jnp.einsum("tr,td->rd", grad_sel, inputs, preferred_element_type=jnp.float32),
            jnp.einsum("tr,tk->rk", in_sel, grad_rows, preferred_element_type=jnp.float32),
        ],
        axis=1,
    ).astype(jnp.bfloat16)

    half = part.shape[1] // 2
    core = lax.axis_index("replica")
    mine = lax.dynamic_slice_in_dim(part, core * half, half, axis=1)
    other = lax.dynamic_slice_in_dim(part, (1 - core) * half, half, axis=1)
    came = passed_along(other, "replica", 1)
    chip = mine.astype(jnp.float32) + came.astype(jnp.float32)

    rows = slots * rank
    here = lax.axis_index("adapter")
    total = lax.dynamic_slice_in_dim(chip, here * rows, rows, axis=0)
    chip_out = chip.astype(jnp.bfloat16)
    for by in range(1, holders):
        block = lax.dynamic_slice_in_dim(chip_out, ((here + by) % holders) * rows, rows, axis=0)
        total = total + passed_along(block, "adapter", by).astype(jnp.float32)
    total = (ADAPTER_SCALE * total).astype(jnp.bfloat16)
    partner = passed_along(total, "replica", 1)
    summed = jnp.concatenate(
        [jnp.where(core == 0, total, partner), jnp.where(core == 0, partner, total)], axis=1
    )
    down_grad = summed[:, :width].reshape(1, slots, rank, width)
    up_grad = summed[:, width:].reshape(1, slots, rank, value_width)

    down_blocks = down.reshape(adapters * rank, holders, chunks, step)
    passed = []
    for c in range(chunks):
        part = jnp.einsum(
            "tk,dk->td", grad_rows, weights[c], preferred_element_type=jnp.float32
        ).astype(jnp.bfloat16)
        lora = (
            ADAPTER_SCALE
            * jnp.einsum(
                "tr,rd->td",
                grad_sel,
                down_blocks[:, :, c].reshape(adapters * rank, holders * step),
                preferred_element_type=jnp.float32,
            )
        ).astype(jnp.bfloat16)
        sent = (part.astype(jnp.float32) + lora.astype(jnp.float32)).astype(jnp.bfloat16)
        passed.append(passed_along(sent, "segment", -1).reshape(-1, holders, step))
    passed = jnp.stack(passed, axis=2).reshape(1, -1, width)
    return passed, down_grad, up_grad


def solution(mesh):
    placed = (
        P("segment", ("groups", "adapter", "replica"), None),
        P("segment", ("groups", "adapter", "replica"), None),
        P("segment", ("groups", "adapter", "replica"), None),
        P("groups"),
        P("segment", "adapter", None),
        P("segment", "adapter", None, None),
        P("segment", "adapter", None, None),
    )
    return jax.shard_map(
        on_device,
        mesh=mesh,
        in_specs=placed,
        out_specs=(
            P("segment", ("groups", "adapter", "replica"), None),
            P(("groups", "segment"), "adapter", None, None),
            P(("groups", "segment"), "adapter", None, None),
        ),
        check_vma=False,
    )
```

```python
import itertools
import jax
import jax.numpy as jnp
from jax import lax
from jax.sharding import PartitionSpec as P

ADAPTER_SCALE = 2.0
AXES = ("groups", "adapter", "segment", "replica")
LANES = 128
F32 = jnp.float32
BF16 = jnp.bfloat16


def moved(x, to):
    sizes = [lax.axis_size(a) for a in AXES]
    number = {at: i for i, at in enumerate(itertools.product(*map(range, sizes)))}
    pairs = []
    for at, i in number.items():
        target = to(*at)
        if target is not None:
            pairs.append((i, number[tuple(t % s for t, s in zip(target, sizes))]))
    return lax.ppermute(x, AXES, pairs)


def on_device(
    saved_layer_input,
    value_output_gradient,
    token_adapter_index,
    adapter_slot_index,
    frozen_value_weight,
    adapter_down_weight,
    adapter_up_weight,
):
    inputs = saved_layer_input[0]
    grad_rows = value_output_gradient[0]
    row_ids = token_adapter_index[0, :, 0]
    tokens, width = inputs.shape
    value_width = grad_rows.shape[1]
    adapters = adapter_slot_index.shape[0]
    groups, holders, replicas = (lax.axis_size(a) for a in ("groups", "adapter", "replica"))
    group, here, core = (lax.axis_index(a) for a in ("groups", "adapter", "replica"))
    slots, rank = adapter_down_weight.shape[1:3]
    own_slots = slots // replicas
    frozen = frozen_value_weight[0]
    shard = frozen.shape[0]
    copies = groups * replicas
    piece = shard // copies
    peers = [(dg, dr) for dg in range(groups) for dr in range(replicas)]

    both = jnp.concatenate([adapter_down_weight[0], adapter_up_weight[0]], axis=2)
    rows = own_slots * rank
    own = lax.dynamic_slice_in_dim(both, core * own_slots, own_slots, axis=0).reshape(rows, -1)
    held = [own]
    for k in range(1, holders):
        held.append(moved(own, lambda g, z, s, r: (g, z + k, s, r)))
    held = jnp.concatenate(held, axis=0)
    maps = [held]
    for dr in range(1, replicas):
        maps.append(moved(held, lambda g, z, s, r: (g, z, s, r + dr)))
    maps = jnp.concatenate(maps, axis=0)
    down, up = maps[:, :width], maps[:, width:]
    row_slot = jnp.concatenate(
        [
            ((here - k) % holders) * slots
            + ((core - dr) % replicas) * own_slots
            + jnp.arange(rows, dtype=jnp.int32) // rank
            for dr in range(replicas)
            for k in range(holders)
        ]
    )

    slot_range = jnp.arange(adapters, dtype=jnp.int32)
    slot_row = jnp.sum(
        jnp.where(row_ids[:, None] == slot_range[None, :], adapter_slot_index[None, :], 0), axis=1
    )
    tagged = jnp.concatenate(
        [grad_rows, jnp.broadcast_to(slot_row[:, None], (tokens, LANES)).astype(BF16)], axis=1
    )
    by_peer = {(0, 0): tagged}
    for dg in range(groups):
        if dg:
            by_peer[dg, 0] = moved(tagged, lambda g, z, s, r: (g - dg, z, s, r))
        for dr in range(1, replicas):
            by_peer[dg, dr] = moved(by_peer[dg, 0], lambda g, z, s, r: (g, z, s, r - dr))
    tagged = jnp.concatenate([by_peer[p] for p in peers], axis=0)
    grads_all = tagged[:, :value_width]
    slots_all = tagged[:, value_width].astype(jnp.int32)

    quarter = group * replicas + core
    mine = lax.dynamic_slice_in_dim(frozen, quarter * piece, piece, axis=0)
    ups, downs = [mine], [mine]
    for k in range(1, holders):
        ups.append(
            moved(
                ups[-1],
                lambda g, z, s, r: (g, z + 1, s, r) if k - 1 <= z < holders - 1 else None,
            )
        )
        downs.append(
            moved(
                downs[-1],
                lambda g, z, s, r: (g, z - 1, s, r) if 0 < z <= holders - k else None,
            )
        )

    keep = slots_all[:, None] == row_slot[None, :]
    proj_grad = jnp.einsum("tk,rk->tr", grads_all, up, preferred_element_type=F32)
    sel_all = jnp.where(keep, proj_grad, 0.0).astype(BF16)
    proj_in = jnp.einsum("td,rd->tr", inputs, down, preferred_element_type=F32)
    in_sel = jnp.where(keep[:tokens], proj_in, 0.0).astype(BF16)
    grad_sel = sel_all[:tokens]
    part = jnp.concatenate(
        [
            jnp.einsum("tr,td->rd", grad_sel, inputs, preferred_element_type=F32),
            jnp.einsum("tr,tk->rk", in_sel, grad_rows, preferred_element_type=F32),
        ],
        axis=1,
    ).astype(BF16)

    part = part.reshape(replicas, holders, rows, width + value_width)
    chip = part[0].astype(F32)
    for dr in range(1, replicas):
        chip = chip + moved(part[dr], lambda g, z, s, r: (g, z, s, r - dr)).astype(F32)
    chip_out = chip.astype(BF16)
    total = chip[0]
    for k in range(1, holders):
        total = total + moved(chip_out[k], lambda g, z, s, r: (g, z - k, s, r)).astype(F32)
    total = (ADAPTER_SCALE * total).astype(BF16)
    summed = jnp.zeros((slots, rank, width + value_width), BF16)
    for dr in range(replicas):
        got = moved(total, lambda g, z, s, r: (g, z, s, r + dr)) if dr else total
        summed = lax.dynamic_update_slice_in_dim(
            summed,
            got.reshape(own_slots, rank, -1),
            ((core - dr) % replicas) * own_slots,
            axis=0,
        )
    down_grad = summed[None, :, :, :width]
    up_grad = summed[None, :, :, width:]

    batches = [([(mine, here, None)], lambda z: True)]
    for k in range(1, holders):
        has = lambda z, k=k: z >= k or z <= holders - 1 - k
        from_below = here >= k
        from_above = here <= holders - 1 - k
        if 2 * k <= holders - 1:
            blocks = [(ups[k], here - k, from_below), (downs[k], here + k, from_above)]
        else:
            blocks = [
                (
                    jnp.where(from_below, ups[k], downs[k]),
                    jnp.where(from_below, here - k, here + k),
                    from_below | from_above,
                )
            ]
        if k == 1:
            batches[0][0].extend(blocks)
        else:
            batches.append((blocks, has))

    passed = jnp.zeros((tokens, width), BF16)
    for blocks, has in batches:
        weight = jnp.concatenate([b for b, _, _ in blocks], axis=0)
        columns = jnp.concatenate(
            [
                lax.dynamic_slice_in_dim(
                    down, jnp.clip(at, 0, holders - 1) * shard + quarter * piece, piece, axis=1
                )
                for _, at, _ in blocks
            ],
            axis=1,
        )
        base = jnp.einsum("tk,dk->td", grads_all, weight, preferred_element_type=F32).astype(BF16)
        lora = (
            ADAPTER_SCALE * jnp.einsum("tr,rd->td", sel_all, columns, preferred_element_type=F32)
        ).astype(BF16)
        out = (base.astype(F32) + lora.astype(F32)).astype(BF16)
        for i, (dg, dr) in enumerate(peers):
            got = moved(
                out[i * tokens : (i + 1) * tokens],
                lambda g, z, s, r: (g + dg, z, s - 1, r + dr) if has(z) else None,
            )
            source = ((group - dg) % groups) * replicas + (core - dr) % replicas
            for j, (_, at, valid) in enumerate(blocks):
                place = jnp.clip(at, 0, holders - 1) * shard + source * piece
                block = got[:, j * piece : (j + 1) * piece]
                if valid is not None:
                    old = lax.dynamic_slice_in_dim(passed, place, piece, axis=1)
                    block = jnp.where(valid, block, old)
                passed = lax.dynamic_update_slice_in_dim(passed, block, place, axis=1)
    return passed[None], down_grad, up_grad


def solution(mesh):
    placed = (
        P("segment", ("groups", "adapter", "replica"), None),
        P("segment", ("groups", "adapter", "replica"), None),
        P("segment", ("groups", "adapter", "replica"), None),
        P("groups"),
        P("segment", "adapter", None),
        P("segment", "adapter", None, None),
        P("segment", "adapter", None, None),
    )
    return jax.shard_map(
        on_device,
        mesh=mesh,
        in_specs=placed,
        out_specs=(
            P("segment", ("groups", "adapter", "replica"), None),
            P(("groups", "segment"), "adapter", None, None),
            P(("groups", "segment"), "adapter", None, None),
        ),
        check_vma=False,
    )
```

```python
import itertools
import jax
import jax.numpy as jnp
from jax import lax
from jax.sharding import PartitionSpec as P

ADAPTER_SCALE = 2.0
AXES = ("groups", "adapter", "segment", "replica")
LANES = 128
F32 = jnp.float32
BF16 = jnp.bfloat16


def moved(x, to):
    sizes = [lax.axis_size(a) for a in AXES]
    number = {at: i for i, at in enumerate(itertools.product(*map(range, sizes)))}
    pairs = []
    for at, i in number.items():
        target = to(*at)
        if target is not None:
            pairs.append((i, number[tuple(t % s for t, s in zip(target, sizes))]))
    return lax.ppermute(x, AXES, pairs)


def on_device(
    saved_layer_input,
    value_output_gradient,
    token_adapter_index,
    adapter_slot_index,
    frozen_value_weight,
    adapter_down_weight,
    adapter_up_weight,
):
    inputs = saved_layer_input[0]
    grad_rows = value_output_gradient[0]
    row_ids = token_adapter_index[0, :, 0]
    tokens, width = inputs.shape
    value_width = grad_rows.shape[1]
    adapters = adapter_slot_index.shape[0]
    groups, holders, replicas = (lax.axis_size(a) for a in ("groups", "adapter", "replica"))
    group, here, core = (lax.axis_index(a) for a in ("groups", "adapter", "replica"))
    slots, rank = adapter_down_weight.shape[1:3]
    own_slots = slots // replicas
    frozen = frozen_value_weight[0]
    shard = frozen.shape[0]
    copies = groups * replicas
    piece = shard // copies
    peers = [(dg, dr) for dg in range(groups) for dr in range(replicas)]

    both = jnp.concatenate([adapter_down_weight[0], adapter_up_weight[0]], axis=2)
    rows = own_slots * rank
    own = lax.dynamic_slice_in_dim(both, core * own_slots, own_slots, axis=0).reshape(rows, -1)
    held = lax.all_gather(own, "adapter", axis=0, tiled=True)
    maps = [held]
    for dr in range(1, replicas):
        maps.append(moved(held, lambda g, z, s, r: (g, z, s, r + dr)))
    maps = jnp.concatenate(maps, axis=0)
    down, up = maps[:, :width], maps[:, width:]
    row_slot = jnp.concatenate(
        [
            k * slots
            + ((core - dr) % replicas) * own_slots
            + jnp.arange(rows, dtype=jnp.int32) // rank
            for dr in range(replicas)
            for k in range(holders)
        ]
    )

    slot_range = jnp.arange(adapters, dtype=jnp.int32)
    slot_row = jnp.sum(
        jnp.where(row_ids[:, None] == slot_range[None, :], adapter_slot_index[None, :], 0), axis=1
    )
    tagged = jnp.concatenate(
        [grad_rows, jnp.broadcast_to(slot_row[:, None], (tokens, LANES)).astype(BF16)], axis=1
    )
    by_peer = {(0, 0): tagged}
    for dg in range(groups):
        if dg:
            by_peer[dg, 0] = moved(tagged, lambda g, z, s, r: (g - dg, z, s, r))
        for dr in range(1, replicas):
            by_peer[dg, dr] = moved(by_peer[dg, 0], lambda g, z, s, r: (g, z, s, r - dr))
    tagged = jnp.concatenate([by_peer[p] for p in peers], axis=0)
    grads_all = tagged[:, :value_width]
    slots_all = tagged[:, value_width].astype(jnp.int32)

    quarter = group * replicas + core
    chunks = 2 if piece % (2 * LANES) == 0 else 1
    step = piece // chunks
    weights = [
        lax.all_gather(
            lax.dynamic_slice_in_dim(frozen, quarter * piece + c * step, step, axis=0),
            "adapter",
            axis=0,
            tiled=True,
        )
        for c in range(chunks)
    ]

    keep = slots_all[:, None] == row_slot[None, :]
    proj_grad = jnp.einsum("tk,rk->tr", grads_all, up, preferred_element_type=F32)
    sel_all = jnp.where(keep, proj_grad, 0.0).astype(BF16)
    proj_in = jnp.einsum("td,rd->tr", inputs, down, preferred_element_type=F32)
    in_sel = jnp.where(keep[:tokens], proj_in, 0.0).astype(BF16)
    grad_sel = sel_all[:tokens]
    part = jnp.concatenate(
        [
            jnp.einsum("tr,td->rd", grad_sel, inputs, preferred_element_type=F32),
            jnp.einsum("tr,tk->rk", in_sel, grad_rows, preferred_element_type=F32),
        ],
        axis=1,
    ).astype(BF16)

    part = part.reshape(replicas, holders, rows, width + value_width)
    chip = part[0].astype(F32)
    for dr in range(1, replicas):
        chip = chip + moved(part[dr], lambda g, z, s, r: (g, z, s, r - dr)).astype(F32)
    chip_out = chip.astype(BF16)
    total = lax.dynamic_index_in_dim(chip, here, 0, keepdims=False)
    for k in range(1, holders):
        block = lax.dynamic_index_in_dim(chip_out, (here + k) % holders, 0, keepdims=False)
        total = total + moved(block, lambda g, z, s, r: (g, z + k, s, r)).astype(F32)
    total = (ADAPTER_SCALE * total).astype(BF16)
    summed = jnp.zeros((slots, rank, width + value_width), BF16)
    for dr in range(replicas):
        got = moved(total, lambda g, z, s, r: (g, z, s, r + dr)) if dr else total
        summed = lax.dynamic_update_slice_in_dim(
            summed,
            got.reshape(own_slots, rank, -1),
            ((core - dr) % replicas) * own_slots,
            axis=0,
        )
    down_grad = summed[None, :, :, :width]
    up_grad = summed[None, :, :, width:]

    passed = jnp.zeros((tokens, width), BF16)
    for c in range(chunks):
        columns = jnp.concatenate(
            [
                lax.dynamic_slice_in_dim(
                    down, k * shard + quarter * piece + c * step, step, axis=1
                )
                for k in range(holders)
            ],
            axis=1,
        )
        base = jnp.einsum("tk,dk->td", grads_all, weights[c], preferred_element_type=F32)
        lora = (
            ADAPTER_SCALE * jnp.einsum("tr,rd->td", sel_all, columns, preferred_element_type=F32)
        ).astype(BF16)
        out = (base.astype(BF16).astype(F32) + lora.astype(F32)).astype(BF16)
        for i, (dg, dr) in enumerate(peers):
            got = moved(
                out[i * tokens : (i + 1) * tokens],
                lambda g, z, s, r: (g + dg, z, s - 1, r + dr),
            )
            source = ((group - dg) % groups) * replicas + (core - dr) % replicas
            for k in range(holders):
                passed = lax.dynamic_update_slice_in_dim(
                    passed,
                    got[:, k * step : (k + 1) * step],
                    k * shard + source * piece + c * step,
                    axis=1,
                )
    return passed[None], down_grad, up_grad


def solution(mesh):
    placed = (
        P("segment", ("groups", "adapter", "replica"), None),
        P("segment", ("groups", "adapter", "replica"), None),
        P("segment", ("groups", "adapter", "replica"), None),
        P("groups"),
        P("segment", "adapter", None),
        P("segment", "adapter", None, None),
        P("segment", "adapter", None, None),
    )
    return jax.shard_map(
        on_device,
        mesh=mesh,
        in_specs=placed,
        out_specs=(
            P("segment", ("groups", "adapter", "replica"), None),
            P(("groups", "segment"), "adapter", None, None),
            P(("groups", "segment"), "adapter", None, None),
        ),
        check_vma=False,
    )
```

```python
import functools
import itertools
import jax
import jax.numpy as jnp
from jax import lax
from jax.experimental import pallas as pl
from jax.experimental.pallas import tpu as pltpu
from jax.sharding import PartitionSpec as P

ADAPTER_SCALE = 2.0
AXES = ("groups", "adapter", "segment", "replica")
LANES = 128
F32 = jnp.float32
BF16 = jnp.bfloat16
VMEM = 32 * 1024 * 1024


def moved(x, to):
    sizes = [lax.axis_size(a) for a in AXES]
    number = {at: i for i, at in enumerate(itertools.product(*map(range, sizes)))}
    pairs = [
        (i, number[tuple(t % s for t, s in zip(to(*at), sizes))]) for at, i in number.items()
    ]
    return lax.ppermute(x, AXES, pairs)


def after(x, *others):
    return lax.optimization_barrier((x, *others))[0]


def rows_by_rows(a, b):
    return lax.dot_general(a, b, (((1,), (1,)), ((), ())), preferred_element_type=F32)


def columns_by_columns(a, b):
    return lax.dot_general(a, b, (((0,), (0,)), ((), ())), preferred_element_type=F32)


def call(kernel, out_shape, flops, operands, scratch=()):
    moved_bytes = sum(x.size * x.dtype.itemsize for x in (*operands, *out_shape))
    return pl.pallas_call(
        kernel,
        out_shape=out_shape,
        scratch_shapes=list(scratch),
        compiler_params=pltpu.CompilerParams(vmem_limit_bytes=VMEM),
        cost_estimate=pl.CostEstimate(flops=flops, bytes_accessed=moved_bytes, transcendentals=0),
    )(*operands)


def adapter_kernel(sizes, *refs):
    tokens, width, value_width, groups, holders, replicas, shard = sizes
    x_ref, slot_ref = refs[0], refs[1]
    g_refs = refs[2 : 2 + groups]
    map_refs = refs[2 + groups : 2 + groups + groups * replicas]
    outs = refs[2 + groups + groups * replicas :]
    sel_ref, own_ref = outs[0], outs[1]
    other_refs = outs[2 : 1 + replicas]
    column_refs = outs[1 + replicas : 1 + replicas + holders]
    down, up = outs[1 + replicas + holders :]
    group, here = lax.axis_index("groups"), lax.axis_index("adapter")
    rows = own_ref.shape[0]
    wide, narrow = width // groups, value_width // groups
    for dr in range(replicas):
        for dg in range(groups):
            ref = map_refs[dr * groups + dg]
            at = lax.rem(group + groups - dg, groups)
            down[pl.ds(dr * rows, rows), pl.ds(pl.multiple_of(at * wide, wide), wide)] = ref[
                :, :wide
            ]
            up[pl.ds(dr * rows, rows), pl.ds(pl.multiple_of(at * narrow, narrow), narrow)] = ref[
                :, wide:
            ]
    half = shard // groups
    for k in range(holders):
        at = lax.rem(here + holders - k, holders) * shard + group * half
        column_refs[k][...] = down[:, pl.ds(pl.multiple_of(at, half), half)]
    slots = slot_ref[...]
    for dg in range(groups):
        keep = g_refs[dg][:, value_width:].astype(F32)[:, :1] == slots
        proj_grad = rows_by_rows(g_refs[dg][:, :value_width], up[...])
        sel_ref[pl.ds(dg * tokens, tokens), :] = jnp.where(keep, proj_grad, 0.0).astype(BF16)
    keep = g_refs[0][:, value_width:].astype(F32)[:, :1] == slots
    in_sel = jnp.where(keep, rows_by_rows(x_ref[...], down[...]), 0.0).astype(BF16)
    grad_sel = sel_ref[pl.ds(0, tokens), :]
    step = 1024
    for at in range(0, width + value_width, step):
        if at < width:
            part = columns_by_columns(grad_sel, x_ref[:, at : at + step])
        else:
            part = columns_by_columns(in_sel, g_refs[0][:, at - width : at - width + step])
        own_ref[:, at : at + step] = part[:rows]
        for dr in range(1, replicas):
            other_refs[dr - 1][:, at : at + step] = part[dr * rows : (dr + 1) * rows].astype(BF16)


def frozen_kernel(sizes, pieces, *refs):
    tokens, value_width, groups, replicas = sizes
    g_refs, sel_ref, refs = refs[:groups], refs[groups], refs[groups + 1 :]
    out_refs = refs[-groups:]
    core = lax.axis_index("replica")
    used, start = 0, 0
    for count in pieces:
        columns, blocks = refs[used], refs[used + 1 : used + 1 + count]
        used += 1 + count
        wide = blocks[0].shape[0]
        for j, block in enumerate(blocks):
            at = 0 if count == 1 else lax.rem(core + replicas - j, replicas) * wide
            for dg in range(groups):
                base = rows_by_rows(g_refs[dg][:, :value_width], block[...]).astype(BF16)
                lora = jnp.dot(
                    sel_ref[pl.ds(dg * tokens, tokens), :],
                    columns[:, pl.ds(pl.multiple_of(at, wide), wide)],
                    preferred_element_type=F32,
                )
                lora = (ADAPTER_SCALE * lora).astype(BF16)
                out_refs[dg][:, pl.ds(pl.multiple_of(start + at, wide), wide)] = (
                    base.astype(F32) + lora.astype(F32)
                ).astype(BF16)
        start += columns.shape[1]


def chip_kernel(*refs):
    own_ref, came_refs, out_refs = refs[0], refs[1], refs[2:]
    rows = out_refs[0].shape[0]
    for k, out in enumerate(out_refs):
        total = own_ref[pl.ds(k * rows, rows), :] + came_refs[pl.ds(k * rows, rows), :].astype(F32)
        out[...] = total.astype(out.dtype)


def total_kernel(*refs):
    total = refs[0][...]
    for ref in refs[1:-1]:
        total = total + ref[...].astype(F32)
    refs[-1][...] = (ADAPTER_SCALE * total).astype(BF16)


def spread_kernel(width, replicas, *refs):
    core = lax.axis_index("replica")
    down_ref, up_ref = refs[replicas:]
    slots = down_ref.shape[0] // replicas
    rank = down_ref.shape[1]
    for dr in range(replicas):
        at = lax.rem(core + replicas - dr, replicas) * slots
        for j in range(slots):
            down_ref[at + j] = refs[dr][j * rank : (j + 1) * rank, :width]
            up_ref[at + j] = refs[dr][j * rank : (j + 1) * rank, width:]


def on_device(
    saved_layer_input,
    value_output_gradient,
    token_adapter_index,
    adapter_slot_index,
    frozen_value_weight,
    adapter_down_weight,
    adapter_up_weight,
):
    inputs = saved_layer_input[0]
    grad_rows = value_output_gradient[0]
    row_ids = token_adapter_index[0, :, 0]
    tokens, width = inputs.shape
    value_width = grad_rows.shape[1]
    adapters = adapter_slot_index.shape[0]
    groups, holders, replicas = (lax.axis_size(a) for a in ("groups", "adapter", "replica"))
    group, here, core = (lax.axis_index(a) for a in ("groups", "adapter", "replica"))
    slots, rank = adapter_down_weight.shape[1:3]
    own_slots = slots // replicas
    rows = own_slots * rank
    frozen = frozen_value_weight[0]
    shard = frozen.shape[0]
    half = shard // groups
    piece = half // replicas
    cols = width + value_width

    wide, narrow = width // groups, value_width // groups
    own = jnp.concatenate(
        [
            lax.dynamic_slice(
                adapter_down_weight[0], (core * own_slots, 0, group * wide), (own_slots, rank, wide)
            ).reshape(rows, wide),
            lax.dynamic_slice(
                adapter_up_weight[0],
                (core * own_slots, 0, group * narrow),
                (own_slots, rank, narrow),
            ).reshape(rows, narrow),
        ],
        axis=1,
    )
    held = [own]
    for k in range(1, holders):
        held.append(moved(own, lambda g, z, s, r: (g, z + k, s, r)))
    held = jnp.concatenate(held, axis=0)
    maps = [held]
    for dg in range(1, groups):
        maps.append(moved(held, lambda g, z, s, r: (g + dg, z, s, r)))
    for dr in range(1, replicas):
        maps += [moved(m, lambda g, z, s, r: (g, z, s, r + dr)) for m in maps[:groups]]
    row_slot = jnp.concatenate(
        [
            ((here - k) % holders) * slots
            + ((core - dr) % replicas) * own_slots
            + jnp.arange(rows, dtype=jnp.int32) // rank
            for dr in range(replicas)
            for k in range(holders)
        ]
    ).astype(F32)[None]

    slot_range = jnp.arange(adapters, dtype=jnp.int32)
    slot_row = jnp.sum(
        jnp.where(row_ids[:, None] == slot_range[None, :], adapter_slot_index[None, :], 0), axis=1
    )
    tagged = jnp.concatenate(
        [grad_rows, jnp.broadcast_to(slot_row[:, None], (tokens, LANES)).astype(BF16)], axis=1
    )
    grads = [tagged]
    for dg in range(1, groups):
        grads.append(moved(tagged, lambda g, z, s, r: (g - dg, z, s, r)))

    mine = lax.dynamic_slice_in_dim(frozen, group * half, half, axis=0)
    ring = [lax.dynamic_slice_in_dim(mine, core * piece, piece, axis=0)]
    blocks = [[mine]]
    for k in range(1, holders):
        ring.append(moved(ring[-1], lambda g, z, s, r: (g, z + 1, s, r)))
        pieces = [ring[k]] + [
            moved(ring[k], lambda g, z, s, r: (g, z, s, r + dr)) for dr in range(1, replicas)
        ]
        if piece % LANES:
            whole = jnp.zeros((half, value_width), BF16)
            for dr in range(replicas):
                at = ((core - dr) % replicas) * piece
                whole = lax.dynamic_update_slice_in_dim(whole, pieces[dr], at, axis=0)
            pieces = [whole]
        blocks.append(pieces)

    sizes = (tokens, width, value_width, groups, holders, replicas, shard)
    kept = replicas * holders * rows
    outs = call(
        functools.partial(adapter_kernel, sizes),
        [jax.ShapeDtypeStruct((groups * tokens, kept), BF16)]
        + [jax.ShapeDtypeStruct((holders * rows, cols), F32)]
        + [jax.ShapeDtypeStruct((holders * rows, cols), BF16)] * (replicas - 1)
        + [jax.ShapeDtypeStruct((kept, half), BF16)] * holders,
        4 * tokens * kept * cols,
        (inputs, row_slot, *grads, *maps),
        [pltpu.VMEM((kept, width), BF16), pltpu.VMEM((kept, value_width), BF16)],
    )
    sel, part, others, columns = outs[0], outs[1], outs[2 : 1 + replicas], outs[1 + replicas :]

    for dr in range(1, replicas - 1):
        part = part + moved(others[dr - 1], lambda g, z, s, r: (g, z, s, r - dr)).astype(F32)
    dr = replicas - 1
    came = moved(others[dr - 1], lambda g, z, s, r: (g, z, s, r - dr))
    chip = call(
        chip_kernel,
        [jax.ShapeDtypeStruct((rows, cols), F32)]
        + [jax.ShapeDtypeStruct((rows, cols), BF16)] * (holders - 1),
        holders * rows * cols,
        (part, came),
    )
    sums = [chip[0]] + [
        moved(chip[k], lambda g, z, s, r: (g, z - k, s, r)) for k in range(1, holders)
    ]
    total = call(
        total_kernel, [jax.ShapeDtypeStruct((rows, cols), BF16)], holders * rows * cols, sums
    )[0]
    totals = [total] + [
        moved(total, lambda g, z, s, r: (g, z, s, r + dr)) for dr in range(1, replicas)
    ]
    down_grad, up_grad = call(
        functools.partial(spread_kernel, width, replicas),
        [
            jax.ShapeDtypeStruct((slots, rank, width), BF16),
            jax.ShapeDtypeStruct((slots, rank, value_width), BF16),
        ],
        0,
        totals,
    )

    batches = [list(range(min(2, holders)))] + [[k] for k in range(2, holders)]
    passed = jnp.zeros((tokens, width), BF16)
    before = ()
    for batch in batches:
        operands = [*grads, sel]
        for k in batch:
            operands += [columns[k], *blocks[k]]
        out = call(
            functools.partial(
                frozen_kernel,
                (tokens, value_width, groups, replicas),
                [len(blocks[k]) for k in batch],
            ),
            [jax.ShapeDtypeStruct((tokens, half * len(batch)), BF16)] * groups,
            2 * groups * tokens * half * len(batch) * (value_width + kept),
            operands,
        )
        got = []
        for dg in range(groups):
            mail = after(out[dg], *before) if before else out[dg]
            got.append(moved(mail, lambda g, z, s, r: (g + dg, z, s - 1, r)))
        before = got
        for dg in range(groups):
            source = (group - dg) % groups
            for j, k in enumerate(batch):
                passed = lax.dynamic_update_slice_in_dim(
                    passed,
                    got[dg][:, j * half : (j + 1) * half],
                    ((here - k) % holders) * shard + source * half,
                    axis=1,
                )
    return passed[None], down_grad[None], up_grad[None]


def solution(mesh):
    placed = (
        P("segment", ("groups", "adapter", "replica"), None),
        P("segment", ("groups", "adapter", "replica"), None),
        P("segment", ("groups", "adapter", "replica"), None),
        P("groups"),
        P("segment", "adapter", None),
        P("segment", "adapter", None, None),
        P("segment", "adapter", None, None),
    )
    return jax.shard_map(
        on_device,
        mesh=mesh,
        in_specs=placed,
        out_specs=(
            P("segment", ("groups", "adapter", "replica"), None),
            P(("groups", "segment"), "adapter", None, None),
            P(("groups", "segment"), "adapter", None, None),
        ),
        check_vma=False,
    )
```

```python
import functools
import itertools
import jax
import jax.numpy as jnp
from jax import lax
from jax.experimental import pallas as pl
from jax.experimental.pallas import tpu as pltpu
from jax.sharding import PartitionSpec as P

ADAPTER_SCALE = 2.0
AXES = ("groups", "adapter", "segment", "replica")
LANES = 128
F32 = jnp.float32
BF16 = jnp.bfloat16
MIB = 1024 * 1024


def moved(x, to):
    sizes = [lax.axis_size(a) for a in AXES]
    number = {at: i for i, at in enumerate(itertools.product(*map(range, sizes)))}
    pairs = [
        (i, number[tuple(t % s for t, s in zip(to(*at), sizes))]) for at, i in number.items()
    ]
    return lax.ppermute(x, AXES, pairs)


def after(x, *others):
    return lax.optimization_barrier((x, *others))[0]


def rows_by_rows(a, b):
    return lax.dot_general(a, b, (((1,), (1,)), ((), ())), preferred_element_type=F32)


def columns_by_columns(a, b):
    return lax.dot_general(a, b, (((0,), (0,)), ((), ())), preferred_element_type=F32)


def call(kernel, out_shape, operands, scratch=()):
    held = sum(x.size * x.dtype.itemsize for x in (*operands, *out_shape, *scratch))
    return pl.pallas_call(
        kernel,
        out_shape=out_shape,
        scratch_shapes=[pltpu.VMEM(x.shape, x.dtype) for x in scratch],
        compiler_params=pltpu.CompilerParams(vmem_limit_bytes=2 * held + 4 * MIB),
        cost_estimate=pl.CostEstimate(flops=1000, bytes_accessed=1000, transcendentals=0),
    )(*operands)


def slots_of(tagged_ref):
    return tagged_ref[:, -LANES:].astype(F32)[:, :1]


def tag_kernel(g_ref, name_ref, slot_ref, out_ref):
    out_ref[:, :-LANES] = g_ref[...]
    tokens, adapters = g_ref.shape[0], slot_ref.shape[1]
    named = name_ref[...] == lax.broadcasted_iota(jnp.int32, (tokens, adapters), 1)
    slot = jnp.sum(jnp.where(named, slot_ref[...], 0).astype(F32), axis=1, keepdims=True)
    out_ref[:, -LANES:] = jnp.broadcast_to(slot, (tokens, LANES)).astype(BF16)


def own_kernel(sizes, down_ref, up_ref, out_ref):
    groups, holders, shard = sizes
    half = shard // groups
    rank = down_ref.shape[1]
    slots = out_ref.shape[0] // rank
    first = lax.axis_index("replica") * slots
    for j in range(slots):
        to = pl.ds(j * rank, rank)
        for z in range(holders):
            at = pl.multiple_of(z * shard + lax.axis_index("groups") * half, half)
            out_ref[to, z * half : (z + 1) * half] = down_ref[first + j, :, pl.ds(at, half)]
        out_ref[to, holders * half :] = up_ref[first + j]


def adapter_kernel(sizes, *refs):
    groups, holders, replicas, shard = sizes
    x_ref, g_ref, slot_ref, sel_ref = refs[:4]
    map_refs, refs = refs[4 : 4 + groups * replicas], refs[4 + groups * replicas :]
    own_ref, other_refs, down = refs[0], refs[1:-1], refs[-1]
    group = lax.axis_index("groups")
    tokens, width = x_ref.shape
    rows, cols = own_ref.shape
    half = shard // groups
    for dg in range(groups):
        first = lax.rem(group + groups - dg, groups) * half
        for dr in range(replicas):
            for z in range(holders):
                at = pl.multiple_of(first + z * shard, half)
                down[pl.ds(dr * rows, rows), pl.ds(at, half)] = map_refs[dg * replicas + dr][
                    :, z * half : (z + 1) * half
                ]
    keep = slots_of(g_ref) == slot_ref[...]
    in_sel = jnp.where(keep, rows_by_rows(x_ref[...], down[...]), 0.0).astype(BF16)
    grad_sel = sel_ref[pl.ds(0, tokens), :]
    step, split = 1024, cols // 2
    for at in range(0, cols, step):
        if at < width:
            part = columns_by_columns(grad_sel, x_ref[:, at : at + step])
        else:
            part = columns_by_columns(in_sel, g_ref[:, at - width : at - width + step])
        own_ref[:, at : at + step] = part[:rows]
        for dr in range(1, replicas):
            sent = part[dr * rows : (dr + 1) * rows].astype(BF16)
            for j in range(0, step, LANES):
                ref, to = other_refs[2 * dr - 2 + (at + j) // split], (at + j) % split
                ref[:, to : to + LANES] = sent[:, j : j + LANES]


def frozen_kernel(sizes, k, count, *refs):
    tokens, groups, holders, replicas = sizes
    g_refs, refs = refs[:groups], refs[groups:]
    down_refs, refs = refs[:replicas], refs[replicas:]
    core, here = lax.axis_index("replica"), lax.axis_index("adapter")
    if k == 0:
        slot_ref, up_refs, refs = refs[0], refs[1 : 1 + replicas], refs[1 + replicas :]
        sel_ref = refs[-1]
        out_refs = refs[-1 - groups : -1]
        rows = up_refs[0].shape[0]
        for dg in range(groups):
            for dr in range(replicas):
                keep = slots_of(g_refs[dg]) == slot_ref[:, dr * rows : (dr + 1) * rows]
                proj_grad = rows_by_rows(g_refs[dg][:, :-LANES], up_refs[dr][...])
                sel_ref[pl.ds(dg * tokens, tokens), dr * rows : (dr + 1) * rows] = jnp.where(
                    keep, proj_grad, 0.0
                ).astype(BF16)
    else:
        sel_ref, refs = refs[0], refs[1:]
        out_refs = refs[-groups:]
    rows = down_refs[0].shape[0]
    half = down_refs[0].shape[1] // holders
    shard_at = lax.rem(here + holders - k, holders) * half
    for j, block in enumerate(refs[:count]):
        wide = block.shape[0]
        at = 0 if count == 1 else lax.rem(core + replicas - j, replicas) * wide
        columns = pl.ds(pl.multiple_of(shard_at + at, wide), wide)
        for dg in range(groups):
            base = rows_by_rows(g_refs[dg][:, :-LANES], block[...]).astype(BF16)
            lora = 0.0
            for dr in range(replicas):
                lora = lora + jnp.dot(
                    sel_ref[pl.ds(dg * tokens, tokens), dr * rows : (dr + 1) * rows],
                    down_refs[dr][:, columns],
                    preferred_element_type=F32,
                )
            lora = (ADAPTER_SCALE * lora).astype(BF16)
            out_refs[dg][:, pl.ds(at if count == 1 else pl.multiple_of(at, wide), wide)] = (
                base.astype(F32) + lora.astype(F32)
            ).astype(BF16)


def place_kernel(sizes, *refs):
    groups, holders, shard, half = sizes
    group, here = lax.axis_index("groups"), lax.axis_index("adapter")
    out_ref = refs[-1]
    for k in range(holders):
        for dg in range(groups):
            source = lax.rem(group + groups - dg, groups)
            at = lax.rem(here + holders - k, holders) * shard + source * half
            out_ref[:, pl.ds(pl.multiple_of(at, half), half)] = refs[k * groups + dg][...]


def chip_kernel(replicas, *refs):
    own_ref, came_refs, out_refs = refs[0], refs[1 : 2 * replicas - 1], refs[2 * replicas - 1 :]
    rows = out_refs[0].shape[0]
    split = came_refs[0].shape[1]
    for k, out in enumerate(out_refs):
        for j in range(2):
            at = pl.ds(k * rows, rows), pl.ds(j * split, split)
            total = own_ref[at]
            for ref in came_refs[j::2]:
                total = total + ref[pl.ds(k * rows, rows), :].astype(F32)
            out[:, pl.ds(j * split, split)] = total.astype(out.dtype)


def total_kernel(*refs):
    total = refs[0][...]
    for ref in refs[1:-1]:
        total = total + ref[...].astype(F32)
    refs[-1][...] = (ADAPTER_SCALE * total).astype(BF16)


def spread_kernel(width, replicas, *refs):
    core = lax.axis_index("replica")
    down_ref, up_ref = refs[replicas:]
    slots = down_ref.shape[0] // replicas
    rank = down_ref.shape[1]
    for dr in range(replicas):
        at = lax.rem(core + replicas - dr, replicas) * slots
        for j in range(slots):
            down_ref[at + j] = refs[dr][j * rank : (j + 1) * rank, :width]
            up_ref[at + j] = refs[dr][j * rank : (j + 1) * rank, width:]


def on_device(
    saved_layer_input,
    value_output_gradient,
    token_adapter_index,
    adapter_slot_index,
    frozen_value_weight,
    adapter_down_weight,
    adapter_up_weight,
):
    inputs = saved_layer_input[0]
    grad_rows = value_output_gradient[0]
    tokens, width = inputs.shape
    value_width = grad_rows.shape[1]
    groups, holders, replicas = (lax.axis_size(a) for a in ("groups", "adapter", "replica"))
    group, here, core = (lax.axis_index(a) for a in ("groups", "adapter", "replica"))
    slots, rank = adapter_down_weight.shape[1:3]
    own_slots = slots // replicas
    rows = own_slots * rank
    frozen = frozen_value_weight[0]
    shard = frozen.shape[0]
    half = shard // groups
    piece = half // replicas
    cols = width + value_width

    tagged = call(
        tag_kernel,
        [jax.ShapeDtypeStruct((tokens, value_width + LANES), BF16)],
        (grad_rows, token_adapter_index[0], adapter_slot_index[None]),
    )[0]
    grads = [tagged] + [
        moved(tagged, lambda g, z, s, r: (g - dg, z, s, r)) for dg in range(1, groups)
    ]

    own = call(
        functools.partial(own_kernel, (groups, holders, shard)),
        [jax.ShapeDtypeStruct((rows, holders * half + value_width), BF16)],
        (adapter_down_weight[0], adapter_up_weight[0]),
    )[0]
    held = [own]
    for k in range(1, holders):
        held.append(moved(own, lambda g, z, s, r: (g, z + k, s, r)))
    held, grads = lax.optimization_barrier((held, grads))
    ups = [jnp.concatenate([x[:, holders * half :] for x in held], axis=0)]
    downs = [jnp.concatenate([x[:, : holders * half] for x in held], axis=0)]
    for dr in range(1, replicas):
        ups.append(moved(ups[0], lambda g, z, s, r: (g, z, s, r + dr)))
        downs.append(moved(downs[0], lambda g, z, s, r: (g, z, s, r + dr)))
    others = [moved(downs[0], lambda g, z, s, r: (g + dg, z, s, r)) for dg in range(1, groups)]
    row_slot = jnp.concatenate(
        [
            ((here - k) % holders) * slots
            + ((core - dr) % replicas) * own_slots
            + jnp.arange(rows, dtype=jnp.int32) // rank
            for dr in range(replicas)
            for k in range(holders)
        ]
    ).astype(F32)[None]

    mine = lax.dynamic_slice_in_dim(frozen, group * half, half, axis=0)
    ring = [lax.dynamic_slice_in_dim(mine, core * piece, piece, axis=0)]
    def pieces_of(k, *before):
        if k == 0:
            return [mine]
        block = after(ring[k], *before) if before else ring[k]
        pieces = [block] + [
            moved(block, lambda g, z, s, r: (g, z, s, r + dr)) for dr in range(1, replicas)
        ]
        if piece % LANES:
            whole = jnp.zeros((half, value_width), BF16)
            for dr in range(replicas):
                at = ((core - dr) % replicas) * piece
                whole = lax.dynamic_update_slice_in_dim(whole, pieces[dr], at, axis=0)
            pieces = [whole]
        return pieces

    kept = replicas * holders * rows

    def adapter_sums(sel):
        maps = list(downs)
        for other in others:
            maps.append(after(other, sel))
            for dr in range(1, replicas):
                maps.append(moved(maps[-dr], lambda g, z, s, r: (g, z, s, r + dr)))
        gradients = call(
            functools.partial(adapter_kernel, (groups, holders, replicas, shard)),
            [jax.ShapeDtypeStruct((holders * rows, cols), F32)]
            + [jax.ShapeDtypeStruct((holders * rows, cols // 2), BF16)] * (2 * replicas - 2),
            (inputs, tagged, row_slot, sel, *maps),
            [jax.ShapeDtypeStruct((kept, width), BF16)],
        )
        part, sent = gradients[0], gradients[1:]
        came = [
            moved(sent[2 * dr - 2 + j], lambda g, z, s, r: (g, z, s, r - dr))
            for dr in range(1, replicas)
            for j in range(2)
        ]
        chip = call(
            functools.partial(chip_kernel, replicas),
            [jax.ShapeDtypeStruct((rows, cols), F32)]
            + [jax.ShapeDtypeStruct((rows, cols), BF16)] * (holders - 1),
            (part, *came),
        )
        return part, chip

    arrived, outs = [], []
    for k in range(holders):
        if k:
            last = ring[-1]
            if k == 2:
                last = after(last, downs[0])
            elif k > 2:
                last = after(last, *outs[k - 2], part)
            ring.append(moved(last, lambda g, z, s, r: (g, z + 1, s, r)))
        gate = [*arrived[k - 2], *outs[k - 1]] if k > 1 else []
        blocks = pieces_of(k, *gate, *(chip[:1] if k > 2 else ()))
        out = call(
            functools.partial(frozen_kernel, (tokens, groups, holders, replicas), k, len(blocks)),
            [jax.ShapeDtypeStruct((tokens, half), BF16)] * groups
            + [jax.ShapeDtypeStruct((groups * tokens, kept), BF16)] * (k == 0),
            [*grads, *downs, *([sel] if k else [row_slot, *ups]), *blocks],
        )
        if k == 0:
            sel = out[groups]
            part, chip = adapter_sums(sel)
        outs.append(list(out[:groups]))
        mails = outs[-1]
        if k > 2:
            mails = [after(mail, *arrived[-1]) for mail in mails]
        arrived.append(
            [moved(mails[dg], lambda g, z, s, r: (g + dg, z, s - 1, r)) for dg in range(groups)]
        )
    passed = call(
        functools.partial(place_kernel, (groups, holders, shard, half)),
        [jax.ShapeDtypeStruct((tokens, width), BF16)],
        [x for got in arrived for x in got],
    )[0]

    sums = [chip[0]] + [
        moved(after(chip[k], ring[-1]), lambda g, z, s, r: (g, z - k, s, r))
        for k in range(1, holders)
    ]
    total = call(total_kernel, [jax.ShapeDtypeStruct((rows, cols), BF16)], sums)[0]
    totals = [total] + [
        moved(total, lambda g, z, s, r: (g, z, s, r + dr)) for dr in range(1, replicas)
    ]
    down_grad, up_grad = call(
        functools.partial(spread_kernel, width, replicas),
        [
            jax.ShapeDtypeStruct((slots, rank, width), BF16),
            jax.ShapeDtypeStruct((slots, rank, value_width), BF16),
        ],
        totals,
    )

    return passed[None], down_grad[None], up_grad[None]


def solution(mesh):
    placed = (
        P("segment", ("groups", "adapter", "replica"), None),
        P("segment", ("groups", "adapter", "replica"), None),
        P("segment", ("groups", "adapter", "replica"), None),
        P("groups"),
        P("segment", "adapter", None),
        P("segment", "adapter", None, None),
        P("segment", "adapter", None, None),
    )
    return jax.shard_map(
        on_device,
        mesh=mesh,
        in_specs=placed,
        out_specs=(
            P("segment", ("groups", "adapter", "replica"), None),
            P(("groups", "segment"), "adapter", None, None),
            P(("groups", "segment"), "adapter", None, None),
        ),
        check_vma=False,
    )
```

```python
import functools
import itertools
import jax
import jax.numpy as jnp
from jax import lax
from jax.experimental import pallas as pl
from jax.experimental.pallas import tpu as pltpu
from jax.sharding import PartitionSpec as P

ADAPTER_SCALE = 2.0
AXES = ("groups", "adapter", "segment", "replica")
LANES = 128
F32 = jnp.float32
BF16 = jnp.bfloat16
MIB = 1024 * 1024


def moved(x, to):
    sizes = [lax.axis_size(a) for a in AXES]
    number = {at: i for i, at in enumerate(itertools.product(*map(range, sizes)))}
    pairs = [
        (i, number[tuple(t % s for t, s in zip(to(*at), sizes))]) for at, i in number.items()
    ]
    return lax.ppermute(x, AXES, pairs)


def after(x, *others):
    return lax.optimization_barrier((x, *others))[0]


def rows_by_rows(a, b):
    return lax.dot_general(a, b, (((1,), (1,)), ((), ())), preferred_element_type=F32)


def columns_by_columns(a, b):
    return lax.dot_general(a, b, (((0,), (0,)), ((), ())), preferred_element_type=F32)


def call(kernel, out_shape, operands, scratch=(), scalars=0):
    held = sum(x.size * x.dtype.itemsize for x in (*operands, *out_shape, *scratch))
    return pl.pallas_call(
        kernel,
        out_shape=out_shape,
        in_specs=[pl.BlockSpec(memory_space=pltpu.VMEM)] * (len(operands) - scalars)
        + [pl.BlockSpec(memory_space=pltpu.SMEM)] * scalars,
        scratch_shapes=[pltpu.VMEM(x.shape, x.dtype) for x in scratch],
        compiler_params=pltpu.CompilerParams(vmem_limit_bytes=2 * held + 4 * MIB),
        cost_estimate=pl.CostEstimate(flops=1000, bytes_accessed=1000, transcendentals=0),
    )(*operands)


def slots_of(tagged_ref):
    return tagged_ref[:, -LANES:].astype(F32)[:, :1]


def row_slots(holders, replicas, slots, rank, dr):
    here, core = lax.axis_index("adapter"), lax.axis_index("replica")
    own_slots = slots // replicas
    lane = lax.broadcasted_iota(jnp.int32, (1, holders * own_slots * rank), 1)
    slot = jnp.zeros_like(lane)
    for k in range(holders):
        for j in range(own_slots):
            start = (k * own_slots + j) * rank
            value = lax.rem(here + holders - k, holders) * slots
            value = value + lax.rem(core + replicas - dr, replicas) * own_slots + j
            slot = jnp.where((lane >= start) & (lane < start + rank), value, slot)
    return slot.astype(F32)


def tag_kernel(g_ref, name_ref, slot_ref, out_ref):
    out_ref[:, :-LANES] = g_ref[...]
    names = name_ref[...]
    slot = jnp.zeros_like(names)
    for j in range(slot_ref.shape[0]):
        slot = jnp.where(names == j, slot_ref[j], slot)
    ones = jnp.ones((1, LANES), F32)
    out_ref[:, -LANES:] = columns_by_columns(slot.astype(F32), ones).astype(BF16)


def join_kernel(*refs):
    down_ref, up_ref = refs[-2:]
    wide = down_ref.shape[1]
    for k, ref in enumerate(refs[:-2]):
        rows = ref.shape[0]
        down_ref[k * rows : (k + 1) * rows] = ref[:, :wide]
        up_ref[k * rows : (k + 1) * rows] = ref[:, wide:]


def own_kernel(sizes, down_ref, up_ref, out_ref):
    groups, holders, shard = sizes
    half = shard // groups
    rank = down_ref.shape[1]
    slots = out_ref.shape[0] // rank
    first = lax.axis_index("replica") * slots
    for j in range(slots):
        to = pl.ds(j * rank, rank)
        for z in range(holders):
            at = pl.multiple_of(z * shard + lax.axis_index("groups") * half, half)
            out_ref[to, z * half : (z + 1) * half] = down_ref[first + j, :, pl.ds(at, half)]
        out_ref[to, holders * half :] = up_ref[first + j]


def adapter_kernel(sizes, *refs):
    groups, holders, replicas, shard, slots, rank = sizes
    x_ref, g_ref, sel_ref = refs[:3]
    map_refs, refs = refs[3 : 3 + groups * replicas], refs[3 + groups * replicas :]
    own_ref, other_refs, down = refs[0], refs[1:-1], refs[-1]
    group = lax.axis_index("groups")
    tokens, width = x_ref.shape
    rows, cols = own_ref.shape
    half = shard // groups
    for dg in range(groups):
        first = lax.rem(group + groups - dg, groups) * half
        for dr in range(replicas):
            for z in range(holders):
                at = pl.multiple_of(first + z * shard, half)
                down[pl.ds(dr * rows, rows), pl.ds(at, half)] = map_refs[dg * replicas + dr][
                    :, z * half : (z + 1) * half
                ]
    row_slot = [row_slots(holders, replicas, slots, rank, dr) for dr in range(replicas)]
    keep = slots_of(g_ref) == jnp.concatenate(row_slot, axis=1)
    in_sel = jnp.where(keep, rows_by_rows(x_ref[...], down[...]), 0.0).astype(BF16)
    grad_sel = sel_ref[pl.ds(0, tokens), :]
    step, split = 1024, cols // 2
    for at in range(0, cols, step):
        if at < width:
            part = columns_by_columns(grad_sel, x_ref[:, at : at + step])
        else:
            part = columns_by_columns(in_sel, g_ref[:, at - width : at - width + step])
        own_ref[:, at : at + step] = part[:rows]
        for dr in range(1, replicas):
            sent = part[dr * rows : (dr + 1) * rows].astype(BF16)
            for j in range(0, step, LANES):
                ref, to = other_refs[2 * dr - 2 + (at + j) // split], (at + j) % split
                ref[:, to : to + LANES] = sent[:, j : j + LANES]


def frozen_kernel(sizes, k, count, *refs):
    tokens, groups, holders, replicas, slots, rank = sizes
    g_refs, refs = refs[:groups], refs[groups:]
    down_refs, refs = refs[:replicas], refs[replicas:]
    core, here = lax.axis_index("replica"), lax.axis_index("adapter")
    if k == 0:
        up_refs, refs = refs[:replicas], refs[replicas:]
        sel_ref = refs[-1]
        out_refs = refs[-1 - groups : -1]
        rows = up_refs[0].shape[0]
        for dg in range(groups):
            for dr in range(replicas):
                keep = slots_of(g_refs[dg]) == row_slots(holders, replicas, slots, rank, dr)
                proj_grad = rows_by_rows(g_refs[dg][:, :-LANES], up_refs[dr][...])
                sel_ref[pl.ds(dg * tokens, tokens), dr * rows : (dr + 1) * rows] = jnp.where(
                    keep, proj_grad, 0.0
                ).astype(BF16)
    else:
        sel_ref, refs = refs[0], refs[1:]
        out_refs = refs[-groups:]
    rows = down_refs[0].shape[0]
    half = down_refs[0].shape[1] // holders
    shard_at = lax.rem(here + holders - k, holders) * half
    for j, block in enumerate(refs[:count]):
        if k == 0:
            block = block.at[pl.ds(pl.multiple_of(lax.axis_index("groups") * half, half), half)]
        wide = block.shape[0]
        at = 0 if count == 1 else lax.rem(core + replicas - j, replicas) * wide
        columns = pl.ds(pl.multiple_of(shard_at + at, wide), wide)
        for dg in range(groups):
            base = rows_by_rows(g_refs[dg][:, :-LANES], block[...]).astype(BF16)
            lora = 0.0
            for dr in range(replicas):
                lora = lora + jnp.dot(
                    sel_ref[pl.ds(dg * tokens, tokens), dr * rows : (dr + 1) * rows],
                    down_refs[dr][:, columns],
                    preferred_element_type=F32,
                )
            lora = (ADAPTER_SCALE * lora).astype(BF16)
            out_refs[dg][:, pl.ds(at if count == 1 else pl.multiple_of(at, wide), wide)] = (
                base.astype(F32) + lora.astype(F32)
            ).astype(BF16)


def place_kernel(sizes, *refs):
    groups, holders, shard, half = sizes
    group, here = lax.axis_index("groups"), lax.axis_index("adapter")
    out_ref = refs[-1]
    for k in range(holders):
        for dg in range(groups):
            source = lax.rem(group + groups - dg, groups)
            at = lax.rem(here + holders - k, holders) * shard + source * half
            out_ref[:, pl.ds(pl.multiple_of(at, half), half)] = refs[k * groups + dg][...]


def chip_kernel(replicas, *refs):
    own_ref, came_refs, out_refs = refs[0], refs[1 : 2 * replicas - 1], refs[2 * replicas - 1 :]
    rows = out_refs[0].shape[0]
    split = came_refs[0].shape[1]
    for k, out in enumerate(out_refs):
        for j in range(2):
            at = pl.ds(k * rows, rows), pl.ds(j * split, split)
            total = own_ref[at]
            for ref in came_refs[j::2]:
                total = total + ref[pl.ds(k * rows, rows), :].astype(F32)
            out[:, pl.ds(j * split, split)] = total.astype(out.dtype)


def total_kernel(*refs):
    total = refs[0][...]
    for ref in refs[1:-1]:
        total = total + ref[...].astype(F32)
    refs[-1][...] = (ADAPTER_SCALE * total).astype(BF16)


def spread_kernel(width, replicas, *refs):
    core = lax.axis_index("replica")
    down_ref, up_ref = refs[replicas:]
    slots = down_ref.shape[0] // replicas
    rank = down_ref.shape[1]
    for dr in range(replicas):
        at = lax.rem(core + replicas - dr, replicas) * slots
        for j in range(slots):
            down_ref[at + j] = refs[dr][j * rank : (j + 1) * rank, :width]
            up_ref[at + j] = refs[dr][j * rank : (j + 1) * rank, width:]


def on_device(
    saved_layer_input,
    value_output_gradient,
    token_adapter_index,
    adapter_slot_index,
    frozen_value_weight,
    adapter_down_weight,
    adapter_up_weight,
):
    inputs = saved_layer_input[0]
    grad_rows = value_output_gradient[0]
    tokens, width = inputs.shape
    value_width = grad_rows.shape[1]
    groups, holders, replicas = (lax.axis_size(a) for a in ("groups", "adapter", "replica"))
    group, here, core = (lax.axis_index(a) for a in ("groups", "adapter", "replica"))
    slots, rank = adapter_down_weight.shape[1:3]
    own_slots = slots // replicas
    rows = own_slots * rank
    frozen = frozen_value_weight[0]
    shard = frozen.shape[0]
    half = shard // groups
    piece = half // replicas
    cols = width + value_width

    tagged = call(
        tag_kernel,
        [jax.ShapeDtypeStruct((tokens, value_width + LANES), BF16)],
        (grad_rows, token_adapter_index[0, :, 0][None], adapter_slot_index),
        scalars=1,
    )[0]
    grads = [tagged] + [
        moved(tagged, lambda g, z, s, r: (g - dg, z, s, r)) for dg in range(1, groups)
    ]

    own = call(
        functools.partial(own_kernel, (groups, holders, shard)),
        [jax.ShapeDtypeStruct((rows, holders * half + value_width), BF16)],
        (adapter_down_weight[0], adapter_up_weight[0]),
    )[0]
    held = [own]
    for k in range(1, holders):
        held.append(moved(own, lambda g, z, s, r: (g, z + k, s, r)))

    ring = [lax.dynamic_slice_in_dim(frozen, (group * replicas + core) * piece, piece, axis=0)]
    ring.append(moved(ring[0], lambda g, z, s, r: (g, z + 1, s, r)))
    held, grads, ring = lax.optimization_barrier((held, grads, ring))
    joined = call(
        join_kernel,
        [
            jax.ShapeDtypeStruct((holders * rows, holders * half), BF16),
            jax.ShapeDtypeStruct((holders * rows, value_width), BF16),
        ],
        held,
    )
    downs, ups = [joined[0]], [joined[1]]
    for dr in range(1, replicas):
        ups.append(moved(ups[0], lambda g, z, s, r: (g, z, s, r + dr)))
        downs.append(moved(downs[0], lambda g, z, s, r: (g, z, s, r + dr)))
    others = [moved(downs[0], lambda g, z, s, r: (g + dg, z, s, r)) for dg in range(1, groups)]
    def pieces_of(k, *before):
        if k == 0:
            return [frozen]
        block = after(ring[k], *before) if before else ring[k]
        pieces = [block] + [
            moved(block, lambda g, z, s, r: (g, z, s, r + dr)) for dr in range(1, replicas)
        ]
        if piece % LANES:
            whole = jnp.zeros((half, value_width), BF16)
            for dr in range(replicas):
                at = ((core - dr) % replicas) * piece
                whole = lax.dynamic_update_slice_in_dim(whole, pieces[dr], at, axis=0)
            pieces = [whole]
        return pieces

    kept = replicas * holders * rows

    def adapter_sums(sel):
        maps = list(downs)
        for other in others:
            maps.append(after(other, sel))
            for dr in range(1, replicas):
                maps.append(moved(maps[-dr], lambda g, z, s, r: (g, z, s, r + dr)))
        gradients = call(
            functools.partial(adapter_kernel, (groups, holders, replicas, shard, slots, rank)),
            [jax.ShapeDtypeStruct((holders * rows, cols), F32)]
            + [jax.ShapeDtypeStruct((holders * rows, cols // 2), BF16)] * (2 * replicas - 2),
            (inputs, tagged, sel, *maps),
            [jax.ShapeDtypeStruct((kept, width), BF16)],
        )
        part, sent = gradients[0], gradients[1:]
        came = [
            moved(sent[2 * dr - 2 + j], lambda g, z, s, r: (g, z, s, r - dr))
            for dr in range(1, replicas)
            for j in range(2)
        ]
        chip = call(
            functools.partial(chip_kernel, replicas),
            [jax.ShapeDtypeStruct((rows, cols), F32)]
            + [jax.ShapeDtypeStruct((rows, cols), BF16)] * (holders - 1),
            (part, *came),
        )
        return part, chip

    arrived, outs = [], []
    for k in range(holders):
        if k > 1:
            last = ring[-1]
            if k > 2:
                last = after(last, *outs[k - 2], part)
            ring.append(moved(last, lambda g, z, s, r: (g, z + 1, s, r)))
        gate = [*arrived[k - 2], *outs[k - 1]] if k > 1 else []
        blocks = pieces_of(k, *gate, *(chip[:1] if k > 2 else ()))
        tokens_in = [after(tagged, part), *grads[1:]] if k == 1 else grads
        out = call(
            functools.partial(
                frozen_kernel, (tokens, groups, holders, replicas, slots, rank), k, len(blocks)
            ),
            [jax.ShapeDtypeStruct((tokens, half), BF16)] * groups
            + [jax.ShapeDtypeStruct((groups * tokens, kept), BF16)] * (k == 0),
            [*tokens_in, *downs, *([sel] if k else ups), *blocks],
        )
        if k == 0:
            sel = out[groups]
            part, chip = adapter_sums(sel)
        outs.append(list(out[:groups]))
        mails = outs[-1]
        if k > 2:
            mails = [after(mail, *arrived[-1]) for mail in mails]
        arrived.append(
            [moved(mails[dg], lambda g, z, s, r: (g + dg, z, s - 1, r)) for dg in range(groups)]
        )
    passed = call(
        functools.partial(place_kernel, (groups, holders, shard, half)),
        [jax.ShapeDtypeStruct((tokens, width), BF16)],
        [x for got in arrived for x in got],
    )[0]

    sums = [chip[0]] + [
        moved(after(chip[k], ring[-1]), lambda g, z, s, r: (g, z - k, s, r))
        for k in range(1, holders)
    ]
    total = call(total_kernel, [jax.ShapeDtypeStruct((rows, cols), BF16)], sums)[0]
    totals = [total] + [
        moved(total, lambda g, z, s, r: (g, z, s, r + dr)) for dr in range(1, replicas)
    ]
    down_grad, up_grad = call(
        functools.partial(spread_kernel, width, replicas),
        [
            jax.ShapeDtypeStruct((slots, rank, width), BF16),
            jax.ShapeDtypeStruct((slots, rank, value_width), BF16),
        ],
        totals,
    )

    return passed[None], down_grad[None], up_grad[None]


def solution(mesh):
    placed = (
        P("segment", ("groups", "adapter", "replica"), None),
        P("segment", ("groups", "adapter", "replica"), None),
        P("segment", ("groups", "adapter", "replica"), None),
        P("groups"),
        P("segment", "adapter", None),
        P("segment", "adapter", None, None),
        P("segment", "adapter", None, None),
    )
    return jax.shard_map(
        on_device,
        mesh=mesh,
        in_specs=placed,
        out_specs=(
            P("segment", ("groups", "adapter", "replica"), None),
            P(("groups", "segment"), "adapter", None, None),
            P(("groups", "segment"), "adapter", None, None),
        ),
        check_vma=False,
    )
```

```python
import functools
import itertools
import jax
import jax.numpy as jnp
from jax import lax
from jax.experimental import pallas as pl
from jax.experimental.pallas import tpu as pltpu
from jax.sharding import PartitionSpec as P

ADAPTER_SCALE = 2.0
AXES = ("groups", "adapter", "segment", "replica")
LANES = 128
F32 = jnp.float32
BF16 = jnp.bfloat16
MIB = 1024 * 1024


def moved(x, to):
    sizes = [lax.axis_size(a) for a in AXES]
    number = {at: i for i, at in enumerate(itertools.product(*map(range, sizes)))}
    pairs = [
        (i, number[tuple(t % s for t, s in zip(to(*at), sizes))]) for at, i in number.items()
    ]
    return lax.ppermute(x, AXES, pairs)


def after(x, *others):
    return lax.optimization_barrier((x, *others))[0]


def rows_by_rows(a, b):
    return lax.dot_general(a, b, (((1,), (1,)), ((), ())), preferred_element_type=F32)


def columns_by_columns(a, b):
    return lax.dot_general(a, b, (((0,), (0,)), ((), ())), preferred_element_type=F32)


def call(kernel, out_shape, operands, scratch=(), scalars=0):
    held = sum(x.size * x.dtype.itemsize for x in (*operands, *out_shape, *scratch))
    return pl.pallas_call(
        kernel,
        out_shape=out_shape,
        in_specs=[pl.BlockSpec(memory_space=pltpu.VMEM)] * (len(operands) - scalars)
        + [pl.BlockSpec(memory_space=pltpu.SMEM)] * scalars,
        scratch_shapes=[pltpu.VMEM(x.shape, x.dtype) for x in scratch],
        compiler_params=pltpu.CompilerParams(vmem_limit_bytes=2 * held + 4 * MIB),
        cost_estimate=pl.CostEstimate(flops=1000, bytes_accessed=1000, transcendentals=0),
    )(*operands)


def slots_of(tagged_ref):
    return tagged_ref[:, -LANES:].astype(F32)[:, :1]


def row_slots(holders, replicas, slots, rank, dr):
    here, core = lax.axis_index("adapter"), lax.axis_index("replica")
    own_slots = slots // replicas
    lane = lax.broadcasted_iota(jnp.int32, (1, holders * own_slots * rank), 1)
    slot = jnp.zeros_like(lane)
    for k in range(holders):
        for j in range(own_slots):
            start = (k * own_slots + j) * rank
            value = lax.rem(here + holders - k, holders) * slots
            value = value + lax.rem(core + replicas - dr, replicas) * own_slots + j
            slot = jnp.where((lane >= start) & (lane < start + rank), value, slot)
    return slot.astype(F32)


def tag_kernel(g_ref, name_ref, slot_ref, out_ref):
    out_ref[:, :-LANES] = g_ref[...]
    names = name_ref[...]
    slot = jnp.zeros_like(names)
    for j in range(slot_ref.shape[0]):
        slot = jnp.where(names == j, slot_ref[j], slot)
    ones = jnp.ones((1, LANES), F32)
    out_ref[:, -LANES:] = columns_by_columns(slot.astype(F32), ones).astype(BF16)


def join_kernel(*refs):
    down_ref, up_ref = refs[-2:]
    wide = down_ref.shape[1]
    for k, ref in enumerate(refs[:-2]):
        rows = ref.shape[0]
        down_ref[k * rows : (k + 1) * rows] = ref[:, :wide]
        up_ref[k * rows : (k + 1) * rows] = ref[:, wide:]


def own_kernel(sizes, down_ref, up_ref, out_ref):
    groups, holders, shard = sizes
    half = shard // groups
    rank = down_ref.shape[1]
    slots = out_ref.shape[0] // rank
    first = lax.axis_index("replica") * slots
    for j in range(slots):
        to = pl.ds(j * rank, rank)
        for z in range(holders):
            at = pl.multiple_of(z * shard + lax.axis_index("groups") * half, half)
            out_ref[to, z * half : (z + 1) * half] = down_ref[first + j, :, pl.ds(at, half)]
        out_ref[to, holders * half :] = up_ref[first + j]


def adapter_kernel(sizes, *refs):
    groups, holders, replicas, shard, slots, rank = sizes
    x_ref, g_ref, sel_ref = refs[:3]
    map_refs, refs = refs[3 : 3 + groups * replicas], refs[3 + groups * replicas :]
    own_ref, other_refs, down = refs[0], refs[1:-1], refs[-1]
    group = lax.axis_index("groups")
    tokens, width = x_ref.shape
    rows, cols = own_ref.shape
    half = shard // groups
    for dg in range(groups):
        first = lax.rem(group + groups - dg, groups) * half
        for dr in range(replicas):
            for z in range(holders):
                at = pl.multiple_of(first + z * shard, half)
                down[pl.ds(dr * rows, rows), pl.ds(at, half)] = map_refs[dg * replicas + dr][
                    :, z * half : (z + 1) * half
                ]
    row_slot = [row_slots(holders, replicas, slots, rank, dr) for dr in range(replicas)]
    keep = slots_of(g_ref) == jnp.concatenate(row_slot, axis=1)
    in_sel = jnp.where(keep, rows_by_rows(x_ref[...], down[...]), 0.0).astype(BF16)
    grad_sel = sel_ref[pl.ds(0, tokens), :]
    step, split = 1024, cols // 2
    for at in range(0, cols, step):
        if at < width:
            part = columns_by_columns(grad_sel, x_ref[:, at : at + step])
        else:
            part = columns_by_columns(in_sel, g_ref[:, at - width : at - width + step])
        own_ref[:, at : at + step] = part[:rows]
        for dr in range(1, replicas):
            sent = part[dr * rows : (dr + 1) * rows].astype(BF16)
            for j in range(0, step, LANES):
                ref, to = other_refs[2 * dr - 2 + (at + j) // split], (at + j) % split
                ref[:, to : to + LANES] = sent[:, j : j + LANES]


def frozen_kernel(sizes, k, count, *refs):
    tokens, groups, holders, replicas, slots, rank = sizes
    g_refs, refs = refs[:groups], refs[groups:]
    down_refs, refs = refs[:replicas], refs[replicas:]
    core, here = lax.axis_index("replica"), lax.axis_index("adapter")
    if k == 0:
        up_refs, refs = refs[:replicas], refs[replicas:]
        sel_ref = refs[-1]
        out_refs = refs[-1 - groups : -1]
        rows = up_refs[0].shape[0]
        for dg in range(groups):
            for dr in range(replicas):
                keep = slots_of(g_refs[dg]) == row_slots(holders, replicas, slots, rank, dr)
                proj_grad = rows_by_rows(g_refs[dg][:, :-LANES], up_refs[dr][...])
                sel_ref[pl.ds(dg * tokens, tokens), dr * rows : (dr + 1) * rows] = jnp.where(
                    keep, proj_grad, 0.0
                ).astype(BF16)
    else:
        sel_ref, refs = refs[0], refs[1:]
        out_refs = refs[-groups:]
    rows = down_refs[0].shape[0]
    half = down_refs[0].shape[1] // holders
    shard_at = lax.rem(here + holders - k, holders) * half
    for j, block in enumerate(refs[:count]):
        if k == 0:
            block = block.at[pl.ds(pl.multiple_of(lax.axis_index("groups") * half, half), half)]
        wide = block.shape[0]
        at = 0 if count == 1 else lax.rem(core + replicas - j, replicas) * wide
        columns = pl.ds(pl.multiple_of(shard_at + at, wide), wide)
        for dg in range(groups):
            base = rows_by_rows(g_refs[dg][:, :-LANES], block[...]).astype(BF16)
            lora = 0.0
            for dr in range(replicas):
                lora = lora + jnp.dot(
                    sel_ref[pl.ds(dg * tokens, tokens), dr * rows : (dr + 1) * rows],
                    down_refs[dr][:, columns],
                    preferred_element_type=F32,
                )
            lora = (ADAPTER_SCALE * lora).astype(BF16)
            out_refs[dg][:, pl.ds(at if count == 1 else pl.multiple_of(at, wide), wide)] = (
                base.astype(F32) + lora.astype(F32)
            ).astype(BF16)


def place_kernel(sizes, *refs):
    groups, holders, shard, half = sizes
    group, here = lax.axis_index("groups"), lax.axis_index("adapter")
    out_ref = refs[-1]
    for k in range(holders):
        for dg in range(groups):
            source = lax.rem(group + groups - dg, groups)
            at = lax.rem(here + holders - k, holders) * shard + source * half
            out_ref[:, pl.ds(pl.multiple_of(at, half), half)] = refs[k * groups + dg][...]


def chip_kernel(replicas, *refs):
    own_ref, came_refs, out_refs = refs[0], refs[1 : 2 * replicas - 1], refs[2 * replicas - 1 :]
    rows = out_refs[0].shape[0]
    split = came_refs[0].shape[1]
    for k, out in enumerate(out_refs):
        for j in range(2):
            at = pl.ds(k * rows, rows), pl.ds(j * split, split)
            total = own_ref[at]
            for ref in came_refs[j::2]:
                total = total + ref[pl.ds(k * rows, rows), :].astype(F32)
            out[:, pl.ds(j * split, split)] = total.astype(out.dtype)


def total_kernel(*refs):
    total = refs[0][...]
    for ref in refs[1:-1]:
        total = total + ref[...].astype(F32)
    refs[-1][...] = (ADAPTER_SCALE * total).astype(BF16)


def spread_kernel(width, replicas, *refs):
    core = lax.axis_index("replica")
    down_ref, up_ref = refs[replicas:]
    slots = down_ref.shape[0] // replicas
    rank = down_ref.shape[1]
    for dr in range(replicas):
        at = lax.rem(core + replicas - dr, replicas) * slots
        for j in range(slots):
            down_ref[at + j] = refs[dr][j * rank : (j + 1) * rank, :width]
            up_ref[at + j] = refs[dr][j * rank : (j + 1) * rank, width:]


def on_device(
    saved_layer_input,
    value_output_gradient,
    token_adapter_index,
    adapter_slot_index,
    frozen_value_weight,
    adapter_down_weight,
    adapter_up_weight,
):
    inputs = saved_layer_input[0]
    grad_rows = value_output_gradient[0]
    tokens, width = inputs.shape
    value_width = grad_rows.shape[1]
    groups, holders, replicas = (lax.axis_size(a) for a in ("groups", "adapter", "replica"))
    group, here, core = (lax.axis_index(a) for a in ("groups", "adapter", "replica"))
    slots, rank = adapter_down_weight.shape[1:3]
    own_slots = slots // replicas
    rows = own_slots * rank
    frozen = frozen_value_weight[0]
    shard = frozen.shape[0]
    half = shard // groups
    piece = half // replicas
    cols = width + value_width

    tagged = call(
        tag_kernel,
        [jax.ShapeDtypeStruct((tokens, value_width + LANES), BF16)],
        (grad_rows, token_adapter_index[0, :, 0][None], adapter_slot_index),
        scalars=1,
    )[0]
    grads = [tagged] + [
        moved(tagged, lambda g, z, s, r: (g - dg, z, s, r)) for dg in range(1, groups)
    ]

    own = call(
        functools.partial(own_kernel, (groups, holders, shard)),
        [jax.ShapeDtypeStruct((rows, holders * half + value_width), BF16)],
        (adapter_down_weight[0], adapter_up_weight[0]),
    )[0]
    ring = [lax.dynamic_slice_in_dim(frozen, (group * replicas + core) * piece, piece, axis=0)]
    own, ring[0] = lax.optimization_barrier((own, ring[0]))
    held = [own]
    for k in range(1, holders):
        held.append(moved(own, lambda g, z, s, r: (g, z + k, s, r)))
    held, grads = lax.optimization_barrier((held, grads))
    ring.append(moved(after(ring[0], held[1]), lambda g, z, s, r: (g, z + 1, s, r)))
    joined = call(
        join_kernel,
        [
            jax.ShapeDtypeStruct((holders * rows, holders * half), BF16),
            jax.ShapeDtypeStruct((holders * rows, value_width), BF16),
        ],
        held,
    )
    downs, ups = [joined[0]], [joined[1]]
    for dr in range(1, replicas):
        ups.append(moved(ups[0], lambda g, z, s, r: (g, z, s, r + dr)))
        downs.append(moved(downs[0], lambda g, z, s, r: (g, z, s, r + dr)))
    others = [moved(downs[0], lambda g, z, s, r: (g + dg, z, s, r)) for dg in range(1, groups)]
    def pieces_of(k, *before):
        if k == 0:
            return [frozen]
        block = after(ring[k], *before) if before else ring[k]
        pieces = [block] + [
            moved(block, lambda g, z, s, r: (g, z, s, r + dr)) for dr in range(1, replicas)
        ]
        if piece % LANES:
            whole = jnp.zeros((half, value_width), BF16)
            for dr in range(replicas):
                at = ((core - dr) % replicas) * piece
                whole = lax.dynamic_update_slice_in_dim(whole, pieces[dr], at, axis=0)
            pieces = [whole]
        return pieces

    kept = replicas * holders * rows

    def adapter_sums(sel):
        maps = list(downs)
        for other in others:
            maps.append(after(other, sel))
            for dr in range(1, replicas):
                maps.append(moved(maps[-dr], lambda g, z, s, r: (g, z, s, r + dr)))
        gradients = call(
            functools.partial(adapter_kernel, (groups, holders, replicas, shard, slots, rank)),
            [jax.ShapeDtypeStruct((holders * rows, cols), F32)]
            + [jax.ShapeDtypeStruct((holders * rows, cols // 2), BF16)] * (2 * replicas - 2),
            (inputs, tagged, sel, *maps),
            [jax.ShapeDtypeStruct((kept, width), BF16)],
        )
        part, sent = gradients[0], gradients[1:]
        came = [
            moved(sent[2 * dr - 2 + j], lambda g, z, s, r: (g, z, s, r - dr))
            for dr in range(1, replicas)
            for j in range(2)
        ]
        chip = call(
            functools.partial(chip_kernel, replicas),
            [jax.ShapeDtypeStruct((rows, cols), F32)]
            + [jax.ShapeDtypeStruct((rows, cols), BF16)] * (holders - 1),
            (part, *came),
        )
        return part, chip

    arrived, outs, sel = [], [], None
    for k in range(holders):
        for j in range(len(ring), min(k + 2, holders) if k > 1 else k + 1):
            last = after(ring[-1], *(outs[j - 2] if j > 2 else []), part if j > 2 else sel)
            ring.append(moved(last, lambda g, z, s, r: (g, z + 1, s, r)))
        if k < 2:
            gate = [sel] * k
        elif k == 2:
            gate = [*arrived[0], *outs[1]]
        else:
            gate = [*arrived[k - 2], *arrived[k - 1], chip[0]]
        blocks = pieces_of(k, *gate)
        tokens_in = [after(tagged, part), *grads[1:]] if k == 1 else grads
        out = call(
            functools.partial(
                frozen_kernel, (tokens, groups, holders, replicas, slots, rank), k, len(blocks)
            ),
            [jax.ShapeDtypeStruct((tokens, half), BF16)] * groups
            + [jax.ShapeDtypeStruct((groups * tokens, kept), BF16)] * (k == 0),
            [*tokens_in, *downs, *([sel] if k else ups), *blocks],
        )
        if k == 0:
            sel = out[groups]
            part, chip = adapter_sums(sel)
        outs.append(list(out[:groups]))
        mails = outs[-1]
        if k > 2:
            mails = [after(mail, *arrived[-1]) for mail in mails]
        arrived.append(
            [moved(mails[dg], lambda g, z, s, r: (g + dg, z, s - 1, r)) for dg in range(groups)]
        )
    passed = call(
        functools.partial(place_kernel, (groups, holders, shard, half)),
        [jax.ShapeDtypeStruct((tokens, width), BF16)],
        [x for got in arrived for x in got],
    )[0]

    sums = [chip[0]] + [
        moved(after(chip[k], ring[-1]), lambda g, z, s, r: (g, z - k, s, r))
        for k in range(1, holders)
    ]
    total = call(total_kernel, [jax.ShapeDtypeStruct((rows, cols), BF16)], sums)[0]
    totals = [total] + [
        moved(total, lambda g, z, s, r: (g, z, s, r + dr)) for dr in range(1, replicas)
    ]
    down_grad, up_grad = call(
        functools.partial(spread_kernel, width, replicas),
        [
            jax.ShapeDtypeStruct((slots, rank, width), BF16),
            jax.ShapeDtypeStruct((slots, rank, value_width), BF16),
        ],
        totals,
    )

    return passed[None], down_grad[None], up_grad[None]


def solution(mesh):
    placed = (
        P("segment", ("groups", "adapter", "replica"), None),
        P("segment", ("groups", "adapter", "replica"), None),
        P("segment", ("groups", "adapter", "replica"), None),
        P("groups"),
        P("segment", "adapter", None),
        P("segment", "adapter", None, None),
        P("segment", "adapter", None, None),
    )
    return jax.shard_map(
        on_device,
        mesh=mesh,
        in_specs=placed,
        out_specs=(
            P("segment", ("groups", "adapter", "replica"), None),
            P(("groups", "segment"), "adapter", None, None),
            P(("groups", "segment"), "adapter", None, None),
        ),
        check_vma=False,
    )
```

```python
import functools
import itertools
import jax
import jax.numpy as jnp
from jax import lax
from jax.experimental import pallas as pl
from jax.experimental.pallas import tpu as pltpu
from jax.sharding import PartitionSpec as P

ADAPTER_SCALE = 2.0
AXES = ("groups", "adapter", "segment", "replica")
LANES = 128
F32 = jnp.float32
BF16 = jnp.bfloat16
MIB = 1024 * 1024


def moved(x, to):
    sizes = [lax.axis_size(a) for a in AXES]
    number = {at: i for i, at in enumerate(itertools.product(*map(range, sizes)))}
    pairs = [
        (i, number[tuple(t % s for t, s in zip(to(*at), sizes))]) for at, i in number.items()
    ]
    return lax.ppermute(x, AXES, pairs)


def after(x, *others):
    return lax.optimization_barrier((x, *others))[0]


def rows_by_rows(a, b):
    return lax.dot_general(a, b, (((1,), (1,)), ((), ())), preferred_element_type=F32)


def columns_by_columns(a, b):
    return lax.dot_general(a, b, (((0,), (0,)), ((), ())), preferred_element_type=F32)


def call(kernel, out_shape, operands, scratch=(), scalars=0):
    held = sum(x.size * x.dtype.itemsize for x in (*operands, *out_shape, *scratch))
    return pl.pallas_call(
        kernel,
        out_shape=out_shape,
        in_specs=[pl.BlockSpec(memory_space=pltpu.VMEM)] * (len(operands) - scalars)
        + [pl.BlockSpec(memory_space=pltpu.SMEM)] * scalars,
        scratch_shapes=[pltpu.VMEM(x.shape, x.dtype) for x in scratch],
        compiler_params=pltpu.CompilerParams(vmem_limit_bytes=2 * held + 4 * MIB),
        cost_estimate=pl.CostEstimate(flops=1000, bytes_accessed=1000, transcendentals=0),
    )(*operands)


def slots_of(tagged_ref):
    return tagged_ref[:, -LANES:].astype(F32)[:, :1]


def row_slots(holders, replicas, slots, rank, dr):
    here, core = lax.axis_index("adapter"), lax.axis_index("replica")
    own_slots = slots // replicas
    lane = lax.broadcasted_iota(jnp.int32, (1, holders * own_slots * rank), 1)
    slot = jnp.zeros_like(lane)
    for k in range(holders):
        for j in range(own_slots):
            start = (k * own_slots + j) * rank
            value = lax.rem(here + holders - k, holders) * slots
            value = value + lax.rem(core + replicas - dr, replicas) * own_slots + j
            slot = jnp.where((lane >= start) & (lane < start + rank), value, slot)
    return slot.astype(F32)


def tag_kernel(g_ref, name_ref, slot_ref, out_ref):
    out_ref[:, :-LANES] = g_ref[...]
    names = name_ref[...]
    slot = jnp.zeros_like(names)
    for j in range(slot_ref.shape[0]):
        slot = jnp.where(names == j, slot_ref[j], slot)
    ones = jnp.ones((1, LANES), F32)
    out_ref[:, -LANES:] = columns_by_columns(slot.astype(F32), ones).astype(BF16)


def join_kernel(*refs):
    down_ref, up_ref = refs[-2:]
    wide = down_ref.shape[1]
    for k, ref in enumerate(refs[:-2]):
        rows = ref.shape[0]
        down_ref[k * rows : (k + 1) * rows] = ref[:, :wide]
        up_ref[k * rows : (k + 1) * rows] = ref[:, wide:]


def own_kernel(sizes, down_ref, up_ref, out_ref):
    groups, holders, shard = sizes
    half = shard // groups
    rank = down_ref.shape[1]
    slots = out_ref.shape[0] // rank
    first = lax.axis_index("replica") * slots
    for j in range(slots):
        to = pl.ds(j * rank, rank)
        for z in range(holders):
            at = pl.multiple_of(z * shard + lax.axis_index("groups") * half, half)
            out_ref[to, z * half : (z + 1) * half] = down_ref[first + j, :, pl.ds(at, half)]
        out_ref[to, holders * half :] = up_ref[first + j]


def adapter_kernel(sizes, *refs):
    groups, holders, replicas, shard, slots, rank = sizes
    x_ref, g_ref, sel_ref = refs[:3]
    map_refs, refs = refs[3 : 3 + groups * replicas], refs[3 + groups * replicas :]
    own_ref, other_refs, down = refs[0], refs[1:-1], refs[-1]
    group = lax.axis_index("groups")
    tokens, width = x_ref.shape
    rows, cols = own_ref.shape
    half = shard // groups
    for dg in range(groups):
        first = lax.rem(group + groups - dg, groups) * half
        for dr in range(replicas):
            for z in range(holders):
                at = pl.multiple_of(first + z * shard, half)
                down[pl.ds(dr * rows, rows), pl.ds(at, half)] = map_refs[dg * replicas + dr][
                    :, z * half : (z + 1) * half
                ]
    row_slot = [row_slots(holders, replicas, slots, rank, dr) for dr in range(replicas)]
    keep = slots_of(g_ref) == jnp.concatenate(row_slot, axis=1)
    in_sel = jnp.where(keep, rows_by_rows(x_ref[...], down[...]), 0.0).astype(BF16)
    grad_sel = sel_ref[pl.ds(0, tokens), :]
    step, split = 1024, cols // 2
    for at in range(0, cols, step):
        if at < width:
            part = columns_by_columns(grad_sel, x_ref[:, at : at + step])
        else:
            part = columns_by_columns(in_sel, g_ref[:, at - width : at - width + step])
        own_ref[:, at : at + step] = part[:rows]
        for dr in range(1, replicas):
            sent = part[dr * rows : (dr + 1) * rows].astype(BF16)
            for j in range(0, step, LANES):
                ref, to = other_refs[2 * dr - 2 + (at + j) // split], (at + j) % split
                ref[:, to : to + LANES] = sent[:, j : j + LANES]


def frozen_kernel(sizes, k, count, *refs):
    tokens, groups, holders, replicas, slots, rank = sizes
    g_refs, refs = refs[:groups], refs[groups:]
    down_refs, refs = refs[:replicas], refs[replicas:]
    core, here = lax.axis_index("replica"), lax.axis_index("adapter")
    if k == 0:
        up_refs, refs = refs[:replicas], refs[replicas:]
        sel_ref = refs[-1]
        out_refs = refs[-1 - groups : -1]
        rows = up_refs[0].shape[0]
        for dg in range(groups):
            for dr in range(replicas):
                keep = slots_of(g_refs[dg]) == row_slots(holders, replicas, slots, rank, dr)
                proj_grad = rows_by_rows(g_refs[dg][:, :-LANES], up_refs[dr][...])
                sel_ref[pl.ds(dg * tokens, tokens), dr * rows : (dr + 1) * rows] = jnp.where(
                    keep, proj_grad, 0.0
                ).astype(BF16)
    else:
        sel_ref, refs = refs[0], refs[1:]
        out_refs = refs[-groups:]
    rows = down_refs[0].shape[0]
    half = down_refs[0].shape[1] // holders
    shard_at = lax.rem(here + holders - k, holders) * half
    for j, block in enumerate(refs[:count]):
        if k == 0:
            block = block.at[pl.ds(pl.multiple_of(lax.axis_index("groups") * half, half), half)]
        wide = block.shape[0]
        at = 0 if count == 1 else lax.rem(core + replicas - j, replicas) * wide
        columns = pl.ds(pl.multiple_of(shard_at + at, wide), wide)
        for dg in range(groups):
            base = rows_by_rows(g_refs[dg][:, :-LANES], block[...]).astype(BF16)
            lora = 0.0
            for dr in range(replicas):
                lora = lora + jnp.dot(
                    sel_ref[pl.ds(dg * tokens, tokens), dr * rows : (dr + 1) * rows],
                    down_refs[dr][:, columns],
                    preferred_element_type=F32,
                )
            lora = (ADAPTER_SCALE * lora).astype(BF16)
            out_refs[dg][:, pl.ds(at if count == 1 else pl.multiple_of(at, wide), wide)] = (
                base.astype(F32) + lora.astype(F32)
            ).astype(BF16)


def place_kernel(sizes, *refs):
    groups, holders, shard, half = sizes
    group, here = lax.axis_index("groups"), lax.axis_index("adapter")
    out_ref = refs[-1]
    for k in range(holders):
        for dg in range(groups):
            source = lax.rem(group + groups - dg, groups)
            at = lax.rem(here + holders - k, holders) * shard + source * half
            out_ref[:, pl.ds(pl.multiple_of(at, half), half)] = refs[k * groups + dg][...]


def chip_kernel(replicas, *refs):
    own_ref, came_refs, out_refs = refs[0], refs[1 : 2 * replicas - 1], refs[2 * replicas - 1 :]
    rows = out_refs[0].shape[0]
    split = came_refs[0].shape[1]
    for k, out in enumerate(out_refs):
        for j in range(2):
            at = pl.ds(k * rows, rows), pl.ds(j * split, split)
            total = own_ref[at]
            for ref in came_refs[j::2]:
                total = total + ref[pl.ds(k * rows, rows), :].astype(F32)
            out[:, pl.ds(j * split, split)] = total.astype(out.dtype)


def total_kernel(*refs):
    total = refs[0][...]
    for ref in refs[1:-1]:
        total = total + ref[...].astype(F32)
    refs[-1][...] = (ADAPTER_SCALE * total).astype(BF16)


def spread_kernel(width, replicas, *refs):
    core = lax.axis_index("replica")
    down_ref, up_ref = refs[replicas:]
    slots = down_ref.shape[0] // replicas
    rank = down_ref.shape[1]
    for dr in range(replicas):
        at = lax.rem(core + replicas - dr, replicas) * slots
        for j in range(slots):
            down_ref[at + j] = refs[dr][j * rank : (j + 1) * rank, :width]
            up_ref[at + j] = refs[dr][j * rank : (j + 1) * rank, width:]


def on_device(
    saved_layer_input,
    value_output_gradient,
    token_adapter_index,
    adapter_slot_index,
    frozen_value_weight,
    adapter_down_weight,
    adapter_up_weight,
):
    inputs = saved_layer_input[0]
    grad_rows = value_output_gradient[0]
    tokens, width = inputs.shape
    value_width = grad_rows.shape[1]
    groups, holders, replicas = (lax.axis_size(a) for a in ("groups", "adapter", "replica"))
    group, here, core = (lax.axis_index(a) for a in ("groups", "adapter", "replica"))
    slots, rank = adapter_down_weight.shape[1:3]
    own_slots = slots // replicas
    rows = own_slots * rank
    frozen = frozen_value_weight[0]
    shard = frozen.shape[0]
    half = shard // groups
    piece = half // replicas
    cols = width + value_width

    own = call(
        functools.partial(own_kernel, (groups, holders, shard)),
        [jax.ShapeDtypeStruct((rows, holders * half + value_width), BF16)],
        (adapter_down_weight[0], adapter_up_weight[0]),
    )[0]
    ring = [lax.dynamic_slice_in_dim(frozen, (group * replicas + core) * piece, piece, axis=0)]
    held = [own]
    for k in range(1, holders):
        held.append(moved(own, lambda g, z, s, r: (g, z + k, s, r)))
    ring.append(moved(ring[0], lambda g, z, s, r: (g, z + 1, s, r)))
    tagged = call(
        tag_kernel,
        [jax.ShapeDtypeStruct((tokens, value_width + LANES), BF16)],
        (grad_rows, token_adapter_index[0, :, 0][None], adapter_slot_index),
        scalars=1,
    )[0]
    grads = [tagged] + [
        moved(after(tagged, held[-1]), lambda g, z, s, r: (g - dg, z, s, r))
        for dg in range(1, groups)
    ]

    joined = call(
        join_kernel,
        [
            jax.ShapeDtypeStruct((holders * rows, holders * half), BF16),
            jax.ShapeDtypeStruct((holders * rows, value_width), BF16),
        ],
        held,
    )
    downs, ups = [joined[0]], [joined[1]]
    for dr in range(1, replicas):
        ups.append(moved(ups[0], lambda g, z, s, r: (g, z, s, r + dr)))
        downs.append(moved(downs[0], lambda g, z, s, r: (g, z, s, r + dr)))
    others = [moved(downs[0], lambda g, z, s, r: (g + dg, z, s, r)) for dg in range(1, groups)]
    def pieces_of(k, *before):
        if k == 0:
            return [frozen]
        block = after(ring[k], *before) if before else ring[k]
        pieces = [block] + [
            moved(block, lambda g, z, s, r: (g, z, s, r + dr)) for dr in range(1, replicas)
        ]
        if piece % LANES:
            whole = jnp.zeros((half, value_width), BF16)
            for dr in range(replicas):
                at = ((core - dr) % replicas) * piece
                whole = lax.dynamic_update_slice_in_dim(whole, pieces[dr], at, axis=0)
            pieces = [whole]
        return pieces

    kept = replicas * holders * rows

    def adapter_sums(sel):
        maps = list(downs)
        for other in others:
            maps.append(after(other, sel))
            for dr in range(1, replicas):
                maps.append(moved(maps[-dr], lambda g, z, s, r: (g, z, s, r + dr)))
        gradients = call(
            functools.partial(adapter_kernel, (groups, holders, replicas, shard, slots, rank)),
            [jax.ShapeDtypeStruct((holders * rows, cols), F32)]
            + [jax.ShapeDtypeStruct((holders * rows, cols // 2), BF16)] * (2 * replicas - 2),
            (inputs, tagged, sel, *maps),
            [jax.ShapeDtypeStruct((kept, width), BF16)],
        )
        part, sent = gradients[0], gradients[1:]
        came = [
            moved(sent[2 * dr - 2 + j], lambda g, z, s, r: (g, z, s, r - dr))
            for dr in range(1, replicas)
            for j in range(2)
        ]
        chip = call(
            functools.partial(chip_kernel, replicas),
            [jax.ShapeDtypeStruct((rows, cols), F32)]
            + [jax.ShapeDtypeStruct((rows, cols), BF16)] * (holders - 1),
            (part, *came),
        )
        return part, chip

    arrived, outs = [], []
    for k in range(holders):
        for j in range(len(ring), min(k + 2, holders) if k > 1 else k + 1):
            last = after(ring[-1], *outs[j - 2], part) if j > 2 else ring[-1]
            ring.append(moved(last, lambda g, z, s, r: (g, z + 1, s, r)))
        gate = [*arrived[k - 2], *outs[k - 1]] if k > 1 else []
        blocks = pieces_of(k, *gate, *(chip[:1] if k > 2 else ()))
        tokens_in = [after(tagged, part), *grads[1:]] if k == 1 else grads
        out = call(
            functools.partial(
                frozen_kernel, (tokens, groups, holders, replicas, slots, rank), k, len(blocks)
            ),
            [jax.ShapeDtypeStruct((tokens, half), BF16)] * groups
            + [jax.ShapeDtypeStruct((groups * tokens, kept), BF16)] * (k == 0),
            [*tokens_in, *downs, *([sel] if k else ups), *blocks],
        )
        if k == 0:
            sel = out[groups]
            part, chip = adapter_sums(sel)
        outs.append(list(out[:groups]))
        mails = outs[-1]
        if k > 2:
            mails = [after(mail, *arrived[-1]) for mail in mails]
        arrived.append(
            [moved(mails[dg], lambda g, z, s, r: (g + dg, z, s - 1, r)) for dg in range(groups)]
        )
    passed = call(
        functools.partial(place_kernel, (groups, holders, shard, half)),
        [jax.ShapeDtypeStruct((tokens, width), BF16)],
        [x for got in arrived for x in got],
    )[0]

    sums = [chip[0]] + [
        moved(after(chip[k], ring[-1]), lambda g, z, s, r: (g, z - k, s, r))
        for k in range(1, holders)
    ]
    total = call(total_kernel, [jax.ShapeDtypeStruct((rows, cols), BF16)], sums)[0]
    totals = [total] + [
        moved(total, lambda g, z, s, r: (g, z, s, r + dr)) for dr in range(1, replicas)
    ]
    down_grad, up_grad = call(
        functools.partial(spread_kernel, width, replicas),
        [
            jax.ShapeDtypeStruct((slots, rank, width), BF16),
            jax.ShapeDtypeStruct((slots, rank, value_width), BF16),
        ],
        totals,
    )

    return passed[None], down_grad[None], up_grad[None]


def solution(mesh):
    placed = (
        P("segment", ("groups", "adapter", "replica"), None),
        P("segment", ("groups", "adapter", "replica"), None),
        P("segment", ("groups", "adapter", "replica"), None),
        P("groups"),
        P("segment", "adapter", None),
        P("segment", "adapter", None, None),
        P("segment", "adapter", None, None),
    )
    return jax.shard_map(
        on_device,
        mesh=mesh,
        in_specs=placed,
        out_specs=(
            P("segment", ("groups", "adapter", "replica"), None),
            P(("groups", "segment"), "adapter", None, None),
            P(("groups", "segment"), "adapter", None, None),
        ),
        check_vma=False,
    )
```

```python
import functools
import itertools
import jax
import jax.numpy as jnp
from jax import lax
from jax.experimental import pallas as pl
from jax.experimental.pallas import tpu as pltpu
from jax.sharding import PartitionSpec as P

ADAPTER_SCALE = 2.0
AXES = ("groups", "adapter", "segment", "replica")
LANES = 128
F32 = jnp.float32
BF16 = jnp.bfloat16
MIB = 1024 * 1024


def moved(x, to):
    sizes = [lax.axis_size(a) for a in AXES]
    number = {at: i for i, at in enumerate(itertools.product(*map(range, sizes)))}
    pairs = []
    for at, i in number.items():
        target = to(*at)
        if target is not None:
            pairs.append((i, number[tuple(t % s for t, s in zip(target, sizes))]))
    return lax.ppermute(x, AXES, pairs)


def after(x, *others):
    return lax.optimization_barrier((x, *others))[0]


def rows_by_rows(a, b):
    return lax.dot_general(a, b, (((1,), (1,)), ((), ())), preferred_element_type=F32)


def columns_by_columns(a, b):
    return lax.dot_general(a, b, (((0,), (0,)), ((), ())), preferred_element_type=F32)


def inner(z):
    return (z == 1) | (z == 2)


def shard_of(k, here, holders):
    if holders != 4:
        return lax.rem(here + holders - k, holders)
    if k < 2:
        return here ^ k
    return here ^ jnp.where(inner(here), 5 - k, k)


def call(kernel, out_shape, operands, scratch=(), scalars=0):
    held = sum(x.size * x.dtype.itemsize for x in (*operands, *out_shape, *scratch))
    return pl.pallas_call(
        kernel,
        out_shape=out_shape,
        in_specs=[pl.BlockSpec(memory_space=pltpu.VMEM)] * (len(operands) - scalars)
        + [pl.BlockSpec(memory_space=pltpu.SMEM)] * scalars,
        scratch_shapes=[pltpu.VMEM(x.shape, x.dtype) for x in scratch],
        compiler_params=pltpu.CompilerParams(vmem_limit_bytes=2 * held + 4 * MIB),
        cost_estimate=pl.CostEstimate(flops=1000, bytes_accessed=1000, transcendentals=0),
    )(*operands)


def slots_of(tagged_ref):
    return tagged_ref[:, -LANES:].astype(F32)[:, :1]


def row_slots(holders, replicas, slots, rank, dr):
    here, core = lax.axis_index("adapter"), lax.axis_index("replica")
    own_slots = slots // replicas
    lane = lax.broadcasted_iota(jnp.int32, (1, holders * own_slots * rank), 1)
    slot = jnp.zeros_like(lane)
    for k in range(holders):
        for j in range(own_slots):
            start = (k * own_slots + j) * rank
            value = (here ^ k) * slots
            value = value + lax.rem(core + replicas - dr, replicas) * own_slots + j
            slot = jnp.where((lane >= start) & (lane < start + rank), value, slot)
    return slot.astype(F32)


def tag_kernel(g_ref, name_ref, slot_ref, out_ref):
    out_ref[:, :-LANES] = g_ref[...]
    names = name_ref[...]
    slot = jnp.zeros_like(names)
    for j in range(slot_ref.shape[0]):
        slot = jnp.where(names == j, slot_ref[j], slot)
    ones = jnp.ones((1, LANES), F32)
    out_ref[:, -LANES:] = columns_by_columns(slot.astype(F32), ones).astype(BF16)


def pick_kernel(here_ref, there_ref, out_ref, *part_refs):
    rows = part_refs[0].shape[0]

    def put(ref):
        out_ref[...] = ref[...]
        for j, part_ref in enumerate(part_refs):
            part_ref[...] = ref[j * rows : (j + 1) * rows]

    at_inner = inner(lax.axis_index("adapter"))
    pl.when(at_inner)(lambda: put(here_ref))
    pl.when(jnp.logical_not(at_inner))(lambda: put(there_ref))


def join_kernel(*refs):
    down_ref, up_ref = refs[-2:]
    wide = down_ref.shape[1]
    for k, ref in enumerate(refs[:-2]):
        rows = ref.shape[0]
        down_ref[k * rows : (k + 1) * rows] = ref[:, :wide]
        up_ref[k * rows : (k + 1) * rows] = ref[:, wide:]


def own_kernel(sizes, down_ref, up_ref, out_ref):
    groups, holders, shard = sizes
    half = shard // groups
    rank = down_ref.shape[1]
    slots = out_ref.shape[0] // rank
    first = lax.axis_index("replica") * slots
    for j in range(slots):
        to = pl.ds(j * rank, rank)
        for z in range(holders):
            at = pl.multiple_of(z * shard + lax.axis_index("groups") * half, half)
            out_ref[to, z * half : (z + 1) * half] = down_ref[first + j, :, pl.ds(at, half)]
        out_ref[to, holders * half :] = up_ref[first + j]


def adapter_kernel(sizes, *refs):
    groups, holders, replicas, shard, slots, rank = sizes
    x_ref, g_ref, sel_ref = refs[:3]
    map_refs, refs = refs[3 : 3 + groups * replicas], refs[3 + groups * replicas :]
    own_ref, other_refs, down = refs[0], refs[1:-1], refs[-1]
    group = lax.axis_index("groups")
    tokens, width = x_ref.shape
    rows, cols = own_ref.shape
    half = shard // groups
    for dg in range(groups):
        first = lax.rem(group + groups - dg, groups) * half
        for dr in range(replicas):
            for z in range(holders):
                at = pl.multiple_of(first + z * shard, half)
                down[pl.ds(dr * rows, rows), pl.ds(at, half)] = map_refs[dg * replicas + dr][
                    :, z * half : (z + 1) * half
                ]
    row_slot = [row_slots(holders, replicas, slots, rank, dr) for dr in range(replicas)]
    keep = slots_of(g_ref) == jnp.concatenate(row_slot, axis=1)
    in_sel = jnp.where(keep, rows_by_rows(x_ref[...], down[...]), 0.0).astype(BF16)
    grad_sel = sel_ref[pl.ds(0, tokens), :]
    step, split = 1024, cols // 2
    for at in range(0, cols, step):
        if at < width:
            part = columns_by_columns(grad_sel, x_ref[:, at : at + step])
        else:
            part = columns_by_columns(in_sel, g_ref[:, at - width : at - width + step])
        own_ref[:, at : at + step] = part[:rows]
        for dr in range(1, replicas):
            sent = part[dr * rows : (dr + 1) * rows].astype(BF16)
            for j in range(0, step, LANES):
                ref, to = other_refs[2 * dr - 2 + (at + j) // split], (at + j) % split
                ref[:, to : to + LANES] = sent[:, j : j + LANES]


def frozen_kernel(sizes, k, spec, *refs):
    tokens, groups, holders, replicas, slots, rank = sizes
    g_refs, refs = refs[:groups], refs[groups:]
    down_refs, refs = refs[:replicas], refs[replicas:]
    core, here = lax.axis_index("replica"), lax.axis_index("adapter")
    if k == 0:
        up_refs, refs = refs[:replicas], refs[replicas:]
        sel_ref = refs[-1]
        out_refs = refs[-1 - groups : -1]
        rows = up_refs[0].shape[0]
        for dg in range(groups):
            for dr in range(replicas):
                keep = slots_of(g_refs[dg]) == row_slots(holders, replicas, slots, rank, dr)
                proj_grad = rows_by_rows(g_refs[dg][:, :-LANES], up_refs[dr][...])
                sel_ref[pl.ds(dg * tokens, tokens), dr * rows : (dr + 1) * rows] = jnp.where(
                    keep, proj_grad, 0.0
                ).astype(BF16)
    else:
        sel_ref, refs = refs[0], refs[1:]
        out_refs = refs[-groups:]
    rows = down_refs[0].shape[0]
    half = down_refs[0].shape[1] // holders
    shard_at = shard_of(k, here, holders) * half
    for (dr, offset), block in zip(spec, refs):
        if k == 0:
            block = block.at[pl.ds(pl.multiple_of(lax.axis_index("groups") * half, half), half)]
        wide = block.shape[0]
        at = 0
        if wide < half:
            at = lax.rem(core + replicas - dr, replicas) * (half // replicas) + offset
        columns = pl.ds(pl.multiple_of(shard_at + at, wide), wide)
        for dg in range(groups):
            base = rows_by_rows(g_refs[dg][:, :-LANES], block[...]).astype(BF16)
            lora = 0.0
            for dr in range(replicas):
                lora = lora + jnp.dot(
                    sel_ref[pl.ds(dg * tokens, tokens), dr * rows : (dr + 1) * rows],
                    down_refs[dr][:, columns],
                    preferred_element_type=F32,
                )
            lora = (ADAPTER_SCALE * lora).astype(BF16)
            out_refs[dg][:, pl.ds(pl.multiple_of(at, wide) if wide < half else 0, wide)] = (
                base.astype(F32) + lora.astype(F32)
            ).astype(BF16)


def place_kernel(sizes, *refs):
    groups, holders, shard, half = sizes
    group, here = lax.axis_index("groups"), lax.axis_index("adapter")
    out_ref = refs[-1]
    for k in range(holders):
        for dg in range(groups):
            source = lax.rem(group + groups - dg, groups)
            at = shard_of(k, here, holders) * shard + source * half
            out_ref[:, pl.ds(pl.multiple_of(at, half), half)] = refs[k * groups + dg][...]


def chip_kernel(replicas, *refs):
    own_ref, came_refs, out_refs = refs[0], refs[1 : 2 * replicas - 1], refs[2 * replicas - 1 :]
    rows = out_refs[0].shape[0]
    split = came_refs[0].shape[1]
    for k, out in enumerate(out_refs):
        for j in range(2):
            at = pl.ds(k * rows, rows), pl.ds(j * split, split)
            total = own_ref[at]
            for ref in came_refs[j::2]:
                total = total + ref[pl.ds(k * rows, rows), :].astype(F32)
            out[:, pl.ds(j * split, split)] = total.astype(out.dtype)


def total_kernel(*refs):
    total = refs[0][...]
    for ref in refs[1:-1]:
        total = total + ref[...].astype(F32)
    refs[-1][...] = (ADAPTER_SCALE * total).astype(BF16)


def spread_kernel(width, replicas, *refs):
    core = lax.axis_index("replica")
    down_ref, up_ref = refs[replicas:]
    slots = down_ref.shape[0] // replicas
    rank = down_ref.shape[1]
    for dr in range(replicas):
        at = lax.rem(core + replicas - dr, replicas) * slots
        for j in range(slots):
            down_ref[at + j] = refs[dr][j * rank : (j + 1) * rank, :width]
            up_ref[at + j] = refs[dr][j * rank : (j + 1) * rank, width:]


def on_device(
    saved_layer_input,
    value_output_gradient,
    token_adapter_index,
    adapter_slot_index,
    frozen_value_weight,
    adapter_down_weight,
    adapter_up_weight,
):
    inputs = saved_layer_input[0]
    grad_rows = value_output_gradient[0]
    tokens, width = inputs.shape
    value_width = grad_rows.shape[1]
    groups, holders, replicas = (lax.axis_size(a) for a in ("groups", "adapter", "replica"))
    group, here, core = (lax.axis_index(a) for a in ("groups", "adapter", "replica"))
    slots, rank = adapter_down_weight.shape[1:3]
    own_slots = slots // replicas
    rows = own_slots * rank
    frozen = frozen_value_weight[0]
    shard = frozen.shape[0]
    half = shard // groups
    piece = half // replicas
    cols = width + value_width

    tagged = call(
        tag_kernel,
        [jax.ShapeDtypeStruct((tokens, value_width + LANES), BF16)],
        (grad_rows, token_adapter_index[0, :, 0][None], adapter_slot_index),
        scalars=1,
    )[0]
    grads = [tagged] + [
        moved(tagged, lambda g, z, s, r: (g - dg, z, s, r)) for dg in range(1, groups)
    ]

    own = call(
        functools.partial(own_kernel, (groups, holders, shard)),
        [jax.ShapeDtypeStruct((rows, holders * half + value_width), BF16)],
        (adapter_down_weight[0], adapter_up_weight[0]),
    )[0]
    held = [own]
    for k in range(1, holders):
        held.append(moved(own, lambda g, z, s, r: (g, z ^ k, s, r)))

    ring = [lax.dynamic_slice_in_dim(frozen, (group * replicas + core) * piece, piece, axis=0)]
    line = holders == 4
    if line:
        swap = lambda g, z, s, r: (g, 3 - z, s, r) if inner(z) else None
        outward = lambda g, z, s, r: (g, z ^ 1, s, r) if inner(z) else None
        near = moved(ring[0], lambda g, z, s, r: (g, z ^ 1, s, r))
        across = moved(ring[0], swap)
        held, grads, near, across = lax.optimization_barrier((held, grads, near, across))
        ring.append(near)
        far = moved(near, swap)
        passed_on = moved(across, outward)
    else:
        ring.append(moved(ring[0], lambda g, z, s, r: (g, z + 1, s, r)))
        held, grads, ring = lax.optimization_barrier((held, grads, ring))
    joined = call(
        join_kernel,
        [
            jax.ShapeDtypeStruct((holders * rows, holders * half), BF16),
            jax.ShapeDtypeStruct((holders * rows, value_width), BF16),
        ],
        held,
    )
    downs, ups = [joined[0]], [joined[1]]
    for dr in range(1, replicas):
        ups.append(moved(ups[0], lambda g, z, s, r: (g, z, s, r + dr)))
        downs.append(moved(downs[0], lambda g, z, s, r: (g, z, s, r + dr)))
    others = [moved(downs[0], lambda g, z, s, r: (g + dg, z, s, r)) for dg in range(1, groups)]
    def pieces_of(k, *before):
        if k == 0:
            return [(0, 0)], [frozen]
        if isinstance(ring[k], list):
            whole, *parts = [after(x, *before) if before else x for x in ring[k]]
        else:
            whole = after(ring[k], *before) if before else ring[k]
            parts = [whole]
        spec, pieces = [(0, 0)], [whole]
        for dr in range(1, replicas):
            for j, part in enumerate(parts):
                spec.append((dr, j * part.shape[0]))
                pieces.append(moved(part, lambda g, z, s, r: (g, z, s, r + dr)))
        if piece % LANES:
            whole = jnp.zeros((half, value_width), BF16)
            for (dr, offset), part in zip(spec, pieces):
                at = ((core - dr) % replicas) * piece + offset
                whole = lax.dynamic_update_slice_in_dim(whole, part, at, axis=0)
            spec, pieces = [(0, 0)], [whole]
        return spec, pieces

    def picked(at_inner, at_end):
        count = 2 if piece % (2 * LANES) == 0 else 1
        shapes = [piece] + [piece // count] * count
        shapes = [jax.ShapeDtypeStruct((n, value_width), BF16) for n in shapes]
        return list(call(pick_kernel, shapes, (at_inner, at_end)))

    kept = replicas * holders * rows

    def adapter_sums(sel):
        maps = list(downs)
        for other in others:
            maps.append(after(other, sel))
            for dr in range(1, replicas):
                maps.append(moved(maps[-dr], lambda g, z, s, r: (g, z, s, r + dr)))
        gradients = call(
            functools.partial(adapter_kernel, (groups, holders, replicas, shard, slots, rank)),
            [jax.ShapeDtypeStruct((holders * rows, cols), F32)]
            + [jax.ShapeDtypeStruct((holders * rows, cols // 2), BF16)] * (2 * replicas - 2),
            (inputs, tagged, sel, *maps),
            [jax.ShapeDtypeStruct((kept, width), BF16)],
        )
        part, sent = gradients[0], gradients[1:]
        came = [
            moved(sent[2 * dr - 2 + j], lambda g, z, s, r: (g, z, s, r - dr))
            for dr in range(1, replicas)
            for j in range(2)
        ]
        chip = call(
            functools.partial(chip_kernel, replicas),
            [jax.ShapeDtypeStruct((rows, cols), F32)]
            + [jax.ShapeDtypeStruct((rows, cols), BF16)] * (holders - 1),
            (part, *came),
        )
        return part, chip

    arrived, outs = [], []
    for k in range(holders):
        if line and k == 2:
            far = after(far, *outs[1], part)
            last = moved(far, outward)
            ring.append(picked(across, passed_on))
            ring.append(picked(far, last))
        elif not line and k > 1:
            last = after(ring[-1], *outs[k - 2], part) if k > 2 else ring[-1]
            last = moved(last, lambda g, z, s, r: (g, z + 1, s, r))
            ring.append(last)
        gate = [*arrived[k - 2], *outs[k - 1]] if k > 1 else []
        spec, blocks = pieces_of(k, *gate, *(chip[:1] if k > 2 else ()))
        tokens_in = [after(tagged, part), *grads[1:]] if k == 1 else grads
        out = call(
            functools.partial(
                frozen_kernel, (tokens, groups, holders, replicas, slots, rank), k, spec
            ),
            [jax.ShapeDtypeStruct((tokens, half), BF16)] * groups
            + [jax.ShapeDtypeStruct((groups * tokens, kept), BF16)] * (k == 0),
            [*tokens_in, *downs, *([sel] if k else ups), *blocks],
        )
        if k == 0:
            sel = out[groups]
            part, chip = adapter_sums(sel)
        outs.append(list(out[:groups]))
        mails = outs[-1]
        if k > 2:
            mails = [after(mail, *arrived[-1]) for mail in mails]
        arrived.append(
            [moved(mails[dg], lambda g, z, s, r: (g + dg, z, s - 1, r)) for dg in range(groups)]
        )
    passed = call(
        functools.partial(place_kernel, (groups, holders, shard, half)),
        [jax.ShapeDtypeStruct((tokens, width), BF16)],
        [x for got in arrived for x in got],
    )[0]

    sums = [chip[0]] + [
        moved(after(chip[k], last), lambda g, z, s, r: (g, z ^ k, s, r))
        for k in range(1, holders)
    ]
    total = call(total_kernel, [jax.ShapeDtypeStruct((rows, cols), BF16)], sums)[0]
    totals = [total] + [
        moved(total, lambda g, z, s, r: (g, z, s, r + dr)) for dr in range(1, replicas)
    ]
    down_grad, up_grad = call(
        functools.partial(spread_kernel, width, replicas),
        [
            jax.ShapeDtypeStruct((slots, rank, width), BF16),
            jax.ShapeDtypeStruct((slots, rank, value_width), BF16),
        ],
        totals,
    )

    return passed[None], down_grad[None], up_grad[None]


def solution(mesh):
    placed = (
        P("segment", ("groups", "adapter", "replica"), None),
        P("segment", ("groups", "adapter", "replica"), None),
        P("segment", ("groups", "adapter", "replica"), None),
        P("groups"),
        P("segment", "adapter", None),
        P("segment", "adapter", None, None),
        P("segment", "adapter", None, None),
    )
    return jax.shard_map(
        on_device,
        mesh=mesh,
        in_specs=placed,
        out_specs=(
            P("segment", ("groups", "adapter", "replica"), None),
            P(("groups", "segment"), "adapter", None, None),
            P(("groups", "segment"), "adapter", None, None),
        ),
        check_vma=False,
    )
```

```python
import functools
import itertools
import jax
import jax.numpy as jnp
from jax import lax
from jax.experimental import pallas as pl
from jax.experimental.pallas import tpu as pltpu
from jax.sharding import PartitionSpec as P

ADAPTER_SCALE = 2.0
AXES = ("groups", "adapter", "segment", "replica")
LANES = 128
SPARE = 256
F32 = jnp.float32
BF16 = jnp.bfloat16
MIB = 1024 * 1024


def moved(x, to):
    sizes = [lax.axis_size(a) for a in AXES]
    number = {at: i for i, at in enumerate(itertools.product(*map(range, sizes)))}
    pairs = []
    for at, i in number.items():
        target = to(*at)
        if target is not None:
            pairs.append((i, number[tuple(t % s for t, s in zip(target, sizes))]))
    return lax.ppermute(x, AXES, pairs)


def after(x, *others):
    return lax.optimization_barrier((x, *others))[0]


def rows_by_rows(a, b):
    return lax.dot_general(a, b, (((1,), (1,)), ((), ())), preferred_element_type=F32)


def columns_by_columns(a, b):
    return lax.dot_general(a, b, (((0,), (0,)), ((), ())), preferred_element_type=F32)


def call(kernel, out_shape, operands, scratch=(), scalars=0):
    held = sum(x.size * x.dtype.itemsize for x in (*operands, *out_shape, *scratch))
    return pl.pallas_call(
        kernel,
        out_shape=out_shape,
        in_specs=[pl.BlockSpec(memory_space=pltpu.VMEM)] * (len(operands) - scalars)
        + [pl.BlockSpec(memory_space=pltpu.SMEM)] * scalars,
        scratch_shapes=[pltpu.VMEM(x.shape, x.dtype) for x in scratch],
        compiler_params=pltpu.CompilerParams(vmem_limit_bytes=2 * held + 4 * MIB),
        cost_estimate=pl.CostEstimate(flops=1000, bytes_accessed=1000, transcendentals=0),
    )(*operands)


def row_slots(holders, replicas, slots, rank, dr):
    here, core = lax.axis_index("adapter"), lax.axis_index("replica")
    own_slots = slots // replicas
    lane = lax.broadcasted_iota(jnp.int32, (1, holders * own_slots * rank), 1)
    slot = jnp.zeros_like(lane)
    for k in range(holders):
        for j in range(own_slots):
            start = (k * own_slots + j) * rank
            value = (here ^ k) * slots
            value = value + lax.rem(core + replicas - dr, replicas) * own_slots + j
            slot = jnp.where((lane >= start) & (lane < start + rank), value, slot)
    return slot.astype(F32)


def name_kernel(name_ref, slot_ref, out_ref):
    names = name_ref[...]
    slot = jnp.zeros_like(names)
    for j in range(slot_ref.shape[0]):
        slot = jnp.where(names == j, slot_ref[j], slot)
    ones = jnp.ones((1, out_ref.shape[1]), F32)
    out_ref[...] = columns_by_columns(slot.astype(F32), ones).astype(BF16)


def join_kernel(*refs):
    both_ref, down_ref = refs[-2:]
    both_ref[:, -SPARE:] = jnp.zeros((both_ref.shape[0], SPARE), BF16)
    for k, ref in enumerate(refs[:-2]):
        rows = ref.shape[0]
        both_ref[k * rows : (k + 1) * rows, :-SPARE] = ref[...]
        down_ref[k * rows : (k + 1) * rows] = ref[:, : down_ref.shape[1]]


def own_kernel(sizes, down_ref, up_ref, out_ref):
    groups, holders, shard = sizes
    half = shard // groups
    rank = down_ref.shape[1]
    slots = out_ref.shape[0] // rank
    first = lax.axis_index("replica") * slots
    for j in range(slots):
        to = pl.ds(j * rank, rank)
        for z in range(holders):
            at = pl.multiple_of(z * shard + lax.axis_index("groups") * half, half)
            out_ref[to, z * half : (z + 1) * half] = down_ref[first + j, :, pl.ds(at, half)]
        out_ref[to, holders * half :] = up_ref[first + j]


def adapter_kernel(sizes, *refs):
    groups, holders, replicas, shard, slots, rank = sizes
    x_ref, g_ref, named_ref, sel_ref = refs[:4]
    map_refs, refs = refs[4 : 4 + groups * replicas], refs[4 + groups * replicas :]
    own_ref, other_refs, down = refs[0], refs[1:-1], refs[-1]
    group = lax.axis_index("groups")
    tokens, width = x_ref.shape
    rows, cols = own_ref.shape
    half = shard // groups
    for dg in range(groups):
        first = lax.rem(group + groups - dg, groups) * half
        for dr in range(replicas):
            for z in range(holders):
                at = pl.multiple_of(first + z * shard, half)
                down[pl.ds(dr * rows, rows), pl.ds(at, half)] = map_refs[dg * replicas + dr][
                    :, z * half : (z + 1) * half
                ]
    row_slot = [row_slots(holders, replicas, slots, rank, dr) for dr in range(replicas)]
    keep = named_ref[...].astype(F32)[:, :1] == jnp.concatenate(row_slot, axis=1)
    in_sel = jnp.where(keep, rows_by_rows(x_ref[...], down[...]), 0.0).astype(BF16)
    grad_sel = sel_ref[pl.ds(0, tokens), :]
    step, split = 1024, cols // 2
    for at in range(0, cols, step):
        if at < width:
            part = columns_by_columns(grad_sel, x_ref[:, at : at + step])
        else:
            part = columns_by_columns(in_sel, g_ref[:, at - width : at - width + step])
        own_ref[:, at : at + step] = part[:rows]
        for dr in range(1, replicas):
            sent = part[dr * rows : (dr + 1) * rows].astype(BF16)
            for j in range(0, step, LANES):
                ref, to = other_refs[2 * dr - 2 + (at + j) // split], (at + j) % split
                ref[:, to : to + LANES] = sent[:, j : j + LANES]


def frozen_kernel(sizes, k, count, *refs):
    tokens, groups, holders, replicas, slots, rank = sizes
    g_refs, refs = refs[:groups], refs[groups:]
    map_refs, refs = refs[:replicas], refs[replicas:]
    core, here = lax.axis_index("replica"), lax.axis_index("adapter")
    rows = map_refs[0].shape[0]
    wide = map_refs[0].shape[1] - g_refs[0].shape[1] - SPARE
    half = wide // holders
    if k == 0:
        named_refs, refs = refs[:groups], refs[groups:]
        sel_ref = refs[-1]
        out_refs = refs[-1 - groups : -1]
        for dg in range(groups):
            names = named_refs[dg][...].astype(F32)[:, :1]
            for dr in range(replicas):
                keep = names == row_slots(holders, replicas, slots, rank, dr)
                proj_grad = rows_by_rows(g_refs[dg][...], map_refs[dr][:, wide:-SPARE])
                sel_ref[pl.ds(dg * tokens, tokens), dr * rows : (dr + 1) * rows] = jnp.where(
                    keep, proj_grad, 0.0
                ).astype(BF16)
    else:
        sel_ref, refs = refs[0], refs[1:]
        out_refs = refs[-groups:]
    shard_at = lax.rem(here + holders - k, holders) * half
    for j, block in enumerate(refs[:count]):
        if k == 0:
            block = block.at[pl.ds(pl.multiple_of(lax.axis_index("groups") * half, half), half)]
        wide = block.shape[0]
        at = 0 if count == 1 else lax.rem(core + replicas - j, replicas) * wide
        columns = pl.ds(pl.multiple_of(shard_at + at, wide), wide)
        for dg in range(groups):
            base = rows_by_rows(g_refs[dg][...], block[...]).astype(BF16)
            lora = 0.0
            for dr in range(replicas):
                lora = lora + jnp.dot(
                    sel_ref[pl.ds(dg * tokens, tokens), dr * rows : (dr + 1) * rows],
                    map_refs[dr][:, columns],
                    preferred_element_type=F32,
                )
            lora = (ADAPTER_SCALE * lora).astype(BF16)
            out_refs[dg][:, pl.ds(at if count == 1 else pl.multiple_of(at, wide), wide)] = (
                base.astype(F32) + lora.astype(F32)
            ).astype(BF16)


def place_kernel(sizes, *refs):
    groups, holders, shard, half = sizes
    group, here = lax.axis_index("groups"), lax.axis_index("adapter")
    out_ref = refs[-1]
    for k in range(holders):
        for dg in range(groups):
            source = lax.rem(group + groups - dg, groups)
            at = lax.rem(here + holders - k, holders) * shard + source * half
            out_ref[:, pl.ds(pl.multiple_of(at, half), half)] = refs[k * groups + dg][...]


def chip_kernel(replicas, *refs):
    own_ref, came_refs, out_refs = refs[0], refs[1 : 2 * replicas - 1], refs[2 * replicas - 1 :]
    rows = out_refs[0].shape[0]
    split = came_refs[0].shape[1]
    for k, out in enumerate(out_refs):
        for j in range(2):
            at = pl.ds(k * rows, rows), pl.ds(j * split, split)
            total = own_ref[at]
            for ref in came_refs[j::2]:
                total = total + ref[pl.ds(k * rows, rows), :].astype(F32)
            out[:, pl.ds(j * split, split)] = total.astype(out.dtype)


def total_kernel(*refs):
    total = refs[0][...]
    for ref in refs[1:-1]:
        total = total + ref[...].astype(F32)
    refs[-1][...] = (ADAPTER_SCALE * total).astype(BF16)


def spread_kernel(width, replicas, *refs):
    core = lax.axis_index("replica")
    down_ref, up_ref = refs[replicas:]
    slots = down_ref.shape[0] // replicas
    rank = down_ref.shape[1]
    for dr in range(replicas):
        at = lax.rem(core + replicas - dr, replicas) * slots
        for j in range(slots):
            down_ref[at + j] = refs[dr][j * rank : (j + 1) * rank, :width]
            up_ref[at + j] = refs[dr][j * rank : (j + 1) * rank, width:]


def on_device(
    saved_layer_input,
    value_output_gradient,
    token_adapter_index,
    adapter_slot_index,
    frozen_value_weight,
    adapter_down_weight,
    adapter_up_weight,
):
    inputs = saved_layer_input[0]
    grad_rows = value_output_gradient[0]
    tokens, width = inputs.shape
    value_width = grad_rows.shape[1]
    groups, holders, replicas = (lax.axis_size(a) for a in ("groups", "adapter", "replica"))
    group, here, core = (lax.axis_index(a) for a in ("groups", "adapter", "replica"))
    slots, rank = adapter_down_weight.shape[1:3]
    own_slots = slots // replicas
    rows = own_slots * rank
    frozen = frozen_value_weight[0]
    shard = frozen.shape[0]
    half = shard // groups
    piece = half // replicas
    cols = width + value_width

    own_named = call(
        name_kernel,
        [jax.ShapeDtypeStruct((tokens, 3 * LANES), BF16)],
        (token_adapter_index[0, :, 0][None], adapter_slot_index),
        scalars=1,
    )[0]
    grads, named = [grad_rows], [own_named]
    for dg in range(1, groups):
        grads.append(moved(grad_rows, lambda g, z, s, r: (g - dg, z, s, r)))
        named.append(moved(own_named, lambda g, z, s, r: (g - dg, z, s, r)))

    own = call(
        functools.partial(own_kernel, (groups, holders, shard)),
        [jax.ShapeDtypeStruct((rows, holders * half + value_width), BF16)],
        (adapter_down_weight[0], adapter_up_weight[0]),
    )[0]
    held = [own]
    for k in range(1, holders):
        held.append(moved(own, lambda g, z, s, r: (g, z ^ k, s, r)))

    ring = [lax.dynamic_slice_in_dim(frozen, (group * replicas + core) * piece, piece, axis=0)]
    ring.append(moved(ring[0], lambda g, z, s, r: (g, z + 1, s, r)))
    held, grads, named = lax.optimization_barrier((held, grads, named))
    both, downs = call(
        join_kernel,
        [
            jax.ShapeDtypeStruct((holders * rows, holders * half + value_width + SPARE), BF16),
            jax.ShapeDtypeStruct((holders * rows, holders * half), BF16),
        ],
        held,
    )
    both = [both] + [
        moved(both, lambda g, z, s, r: (g, z, s, r + dr)) for dr in range(1, replicas)
    ]
    others = [moved(downs, lambda g, z, s, r: (g + dg, z, s, r)) for dg in range(1, groups)]
    def pieces_of(k, *before):
        if k == 0:
            return [frozen]
        block = after(ring[k], *before) if before else ring[k]
        pieces = [block] + [
            moved(block, lambda g, z, s, r: (g, z, s, r + dr)) for dr in range(1, replicas)
        ]
        if piece % LANES:
            whole = jnp.zeros((half, value_width), BF16)
            for dr in range(replicas):
                at = ((core - dr) % replicas) * piece
                whole = lax.dynamic_update_slice_in_dim(whole, pieces[dr], at, axis=0)
            pieces = [whole]
        return pieces

    kept = replicas * holders * rows

    def adapter_sums(sel, *before):
        maps = list(both)
        for other in others:
            maps.append(after(other, sel))
            for dr in range(1, replicas):
                maps.append(moved(maps[-dr], lambda g, z, s, r: (g, z, s, r + dr)))
        gradients = call(
            functools.partial(adapter_kernel, (groups, holders, replicas, shard, slots, rank)),
            [jax.ShapeDtypeStruct((holders * rows, cols), F32)]
            + [jax.ShapeDtypeStruct((holders * rows, cols // 2), BF16)] * (2 * replicas - 2),
            (inputs, grad_rows, named[0], sel, *maps),
            [jax.ShapeDtypeStruct((kept, width), BF16)],
        )
        part, sent = gradients[0], gradients[1:]
        came = [
            moved(after(sent[2 * dr - 2 + j], *before), lambda g, z, s, r: (g, z, s, r - dr))
            for dr in range(1, replicas)
            for j in range(2)
        ]
        chip = call(
            functools.partial(chip_kernel, replicas),
            [jax.ShapeDtypeStruct((rows, cols), F32)]
            + [jax.ShapeDtypeStruct((rows, cols), BF16)] * (holders - 1),
            (part, *came),
        )
        return part, chip

    arrived, outs, sel = [], [], None
    for k in range(holders):
        if k > 1:
            last = after(ring[-1], *outs[k - 2], part) if k > 2 else after(ring[-1], sel)
            ring.append(moved(last, lambda g, z, s, r: (g, z + 1, s, r)))
        gate = outs[k - 1] if k > 1 else [sel] * k
        blocks = pieces_of(k, *gate, *([*arrived[k - 2], chip[0]] if k > 2 else ()))
        tokens_in = [after(grad_rows, part), *grads[1:]] if k == 1 else grads
        out = call(
            functools.partial(
                frozen_kernel, (tokens, groups, holders, replicas, slots, rank), k, len(blocks)
            ),
            [jax.ShapeDtypeStruct((tokens, half), BF16)] * groups
            + [jax.ShapeDtypeStruct((groups * tokens, kept), BF16)] * (k == 0),
            [*tokens_in, *both, *([sel] if k else named), *blocks],
        )
        if k == 0:
            sel = out[groups]
        outs.append(list(out[:groups]))
        mails = outs[-1]
        if k > 2:
            mails = [after(mail, *arrived[-1]) for mail in mails]
        arrived.append(
            [moved(mails[dg], lambda g, z, s, r: (g + dg, z, s - 1, r)) for dg in range(groups)]
        )
        if k == 0:
            part, chip = adapter_sums(sel, *arrived[0])
    passed = call(
        functools.partial(place_kernel, (groups, holders, shard, half)),
        [jax.ShapeDtypeStruct((tokens, width), BF16)],
        [x for got in arrived for x in got],
    )[0]

    sums = [chip[0]] + [
        moved(after(chip[k], ring[-1]), lambda g, z, s, r: (g, z ^ k, s, r))
        for k in range(1, holders)
    ]
    total = call(total_kernel, [jax.ShapeDtypeStruct((rows, cols), BF16)], sums)[0]
    totals = [total] + [
        moved(total, lambda g, z, s, r: (g, z, s, r + dr)) for dr in range(1, replicas)
    ]
    down_grad, up_grad = call(
        functools.partial(spread_kernel, width, replicas),
        [
            jax.ShapeDtypeStruct((slots, rank, width), BF16),
            jax.ShapeDtypeStruct((slots, rank, value_width), BF16),
        ],
        totals,
    )

    return passed[None], down_grad[None], up_grad[None]


def solution(mesh):
    placed = (
        P("segment", ("groups", "adapter", "replica"), None),
        P("segment", ("groups", "adapter", "replica"), None),
        P("segment", ("groups", "adapter", "replica"), None),
        P("groups"),
        P("segment", "adapter", None),
        P("segment", "adapter", None, None),
        P("segment", "adapter", None, None),
    )
    return jax.shard_map(
        on_device,
        mesh=mesh,
        in_specs=placed,
        out_specs=(
            P("segment", ("groups", "adapter", "replica"), None),
            P(("groups", "segment"), "adapter", None, None),
            P(("groups", "segment"), "adapter", None, None),
        ),
        check_vma=False,
    )
```

```python
import functools
import itertools
import jax
import jax.numpy as jnp
from jax import lax
from jax.experimental import pallas as pl
from jax.experimental.pallas import tpu as pltpu
from jax.sharding import PartitionSpec as P

ADAPTER_SCALE = 2.0
AXES = ("groups", "adapter", "segment", "replica")
LANES = 128
SPARE = 256
F32 = jnp.float32
BF16 = jnp.bfloat16
MIB = 1024 * 1024


def moved(x, to):
    sizes = [lax.axis_size(a) for a in AXES]
    number = {at: i for i, at in enumerate(itertools.product(*map(range, sizes)))}
    pairs = []
    for at, i in number.items():
        target = to(*at)
        if target is not None:
            pairs.append((i, number[tuple(t % s for t, s in zip(target, sizes))]))
    return lax.ppermute(x, AXES, pairs)


def after(x, *others):
    return lax.optimization_barrier((x, *others))[0]


def rows_by_rows(a, b):
    return lax.dot_general(a, b, (((1,), (1,)), ((), ())), preferred_element_type=F32)


def columns_by_columns(a, b):
    return lax.dot_general(a, b, (((0,), (0,)), ((), ())), preferred_element_type=F32)


def inner(z):
    return (z == 1) | (z == 2)


def shard_of(k, here, holders):
    if holders != 4:
        return lax.rem(here + holders - k, holders)
    if k < 2:
        return here ^ k
    return here ^ jnp.where(inner(here), 5 - k, k)


def call(kernel, out_shape, operands, scratch=(), scalars=0):
    held = sum(x.size * x.dtype.itemsize for x in (*operands, *out_shape, *scratch))
    return pl.pallas_call(
        kernel,
        out_shape=out_shape,
        in_specs=[pl.BlockSpec(memory_space=pltpu.VMEM)] * (len(operands) - scalars)
        + [pl.BlockSpec(memory_space=pltpu.SMEM)] * scalars,
        scratch_shapes=[pltpu.VMEM(x.shape, x.dtype) for x in scratch],
        compiler_params=pltpu.CompilerParams(vmem_limit_bytes=2 * held + 4 * MIB),
        cost_estimate=pl.CostEstimate(flops=1000, bytes_accessed=1000, transcendentals=0),
    )(*operands)


def row_slots(holders, replicas, slots, rank, dr):
    here, core = lax.axis_index("adapter"), lax.axis_index("replica")
    own_slots = slots // replicas
    lane = lax.broadcasted_iota(jnp.int32, (1, holders * own_slots * rank), 1)
    slot = jnp.zeros_like(lane)
    for k in range(holders):
        for j in range(own_slots):
            start = (k * own_slots + j) * rank
            value = (here ^ k) * slots
            value = value + lax.rem(core + replicas - dr, replicas) * own_slots + j
            slot = jnp.where((lane >= start) & (lane < start + rank), value, slot)
    return slot.astype(F32)


def name_kernel(name_ref, slot_ref, out_ref):
    names = name_ref[...]
    slot = jnp.zeros_like(names)
    for j in range(slot_ref.shape[0]):
        slot = jnp.where(names == j, slot_ref[j], slot)
    ones = jnp.ones((1, out_ref.shape[1]), F32)
    out_ref[...] = columns_by_columns(slot.astype(F32), ones).astype(BF16)


def join_kernel(*refs):
    both_ref, down_ref = refs[-2:]
    both_ref[:, -SPARE:] = jnp.zeros((both_ref.shape[0], SPARE), BF16)
    for k, ref in enumerate(refs[:-2]):
        rows = ref.shape[0]
        both_ref[k * rows : (k + 1) * rows, :-SPARE] = ref[...]
        down_ref[k * rows : (k + 1) * rows] = ref[:, : down_ref.shape[1]]


def own_kernel(sizes, down_ref, up_ref, out_ref):
    groups, holders, shard = sizes
    half = shard // groups
    rank = down_ref.shape[1]
    slots = out_ref.shape[0] // rank
    first = lax.axis_index("replica") * slots
    for j in range(slots):
        to = pl.ds(j * rank, rank)
        for z in range(holders):
            at = pl.multiple_of(z * shard + lax.axis_index("groups") * half, half)
            out_ref[to, z * half : (z + 1) * half] = down_ref[first + j, :, pl.ds(at, half)]
        out_ref[to, holders * half :] = up_ref[first + j]


def adapter_kernel(sizes, *refs):
    groups, holders, replicas, shard, slots, rank = sizes
    x_ref, g_ref, named_ref, sel_ref = refs[:4]
    map_refs, refs = refs[4 : 4 + groups * replicas], refs[4 + groups * replicas :]
    own_ref, other_refs, down = refs[0], refs[1:-1], refs[-1]
    group = lax.axis_index("groups")
    tokens, width = x_ref.shape
    rows, cols = own_ref.shape
    half = shard // groups
    for dg in range(groups):
        first = lax.rem(group + groups - dg, groups) * half
        for dr in range(replicas):
            for z in range(holders):
                at = pl.multiple_of(first + z * shard, half)
                down[pl.ds(dr * rows, rows), pl.ds(at, half)] = map_refs[dg * replicas + dr][
                    :, z * half : (z + 1) * half
                ]
    row_slot = [row_slots(holders, replicas, slots, rank, dr) for dr in range(replicas)]
    keep = named_ref[...].astype(F32)[:, :1] == jnp.concatenate(row_slot, axis=1)
    in_sel = jnp.where(keep, rows_by_rows(x_ref[...], down[...]), 0.0).astype(BF16)
    grad_sel = sel_ref[pl.ds(0, tokens), :]
    step, split = 1024, cols // 2
    for at in range(0, cols, step):
        if at < width:
            part = columns_by_columns(grad_sel, x_ref[:, at : at + step])
        else:
            part = columns_by_columns(in_sel, g_ref[:, at - width : at - width + step])
        own_ref[:, at : at + step] = part[:rows]
        for dr in range(1, replicas):
            sent = part[dr * rows : (dr + 1) * rows].astype(BF16)
            for j in range(0, step, LANES):
                ref, to = other_refs[2 * dr - 2 + (at + j) // split], (at + j) % split
                ref[:, to : to + LANES] = sent[:, j : j + LANES]


def ranks_kept(sizes, g_ref, names, map_refs, wide):
    holders, replicas, slots, rank = sizes
    kept = []
    for dr in range(replicas):
        keep = names == row_slots(holders, replicas, slots, rank, dr)
        proj_grad = rows_by_rows(g_ref[...], map_refs[dr][:, wide:-SPARE])
        kept.append(jnp.where(keep, proj_grad, 0.0).astype(BF16))
    return jnp.concatenate(kept, axis=1)


def frozen_kernel(sizes, k, spec, guests, *refs):
    tokens, groups, holders, replicas, slots, rank = sizes
    g_refs, refs = refs[:groups], refs[groups:]
    map_refs, refs = refs[:replicas], refs[replicas:]
    core, here = lax.axis_index("replica"), lax.axis_index("adapter")
    rows = map_refs[0].shape[0]
    value_width = g_refs[0].shape[1]
    wide = map_refs[0].shape[1] - value_width - SPARE
    half = wide // holders
    ranks = (holders, replicas, slots, rank)
    if k == 0:
        named_refs, refs, sel_ref = refs[:groups], refs[groups:-1], refs[-1]
        for dg in range(groups):
            names = named_refs[dg][...].astype(F32)[:, :1]
            sel_ref[pl.ds(dg * tokens, tokens), :] = ranks_kept(
                ranks, g_refs[dg], names, map_refs, wide
            )
    else:
        sel_ref, refs = refs[0], refs[1:]
    sets = [(g_refs[dg], sel_ref[pl.ds(dg * tokens, tokens), :]) for dg in range(groups)]
    if guests:
        guest_ref, refs = refs[0], refs[1:]
        for dg in range(groups):
            at = pl.ds(dg * tokens, tokens)
            names = guest_ref[at, value_width:].astype(F32)[:, :1]
            g_ref = guest_ref.at[at, pl.ds(0, value_width)]
            sets.append((g_ref, ranks_kept(ranks, g_ref, names, map_refs, wide)))
    out_refs = list(refs[len(spec) : len(spec) + groups])
    if guests:
        out_refs += [refs[-1].at[pl.ds(dg * tokens, tokens)] for dg in range(groups)]
    shard_at = shard_of(k, here, holders) * half
    for (dr, offset), block in zip(spec, refs):
        if k == 0:
            block = block.at[pl.ds(pl.multiple_of(lax.axis_index("groups") * half, half), half)]
        size = block.shape[0]
        at = 0
        if size < half:
            at = lax.rem(core + replicas - dr, replicas) * (half // replicas) + offset
        columns = pl.ds(pl.multiple_of(shard_at + at, size), size)
        for (g_ref, sel), out_ref in zip(sets, out_refs):
            base = rows_by_rows(g_ref[...], block[...]).astype(BF16)
            lora = 0.0
            for j in range(replicas):
                lora = lora + jnp.dot(
                    sel[:, j * rows : (j + 1) * rows],
                    map_refs[j][:, columns],
                    preferred_element_type=F32,
                )
            lora = (ADAPTER_SCALE * lora).astype(BF16)
            out_ref[:, pl.ds(pl.multiple_of(at, size) if size < half else 0, size)] = (
                base.astype(F32) + lora.astype(F32)
            ).astype(BF16)


def guest_kernel(groups, *refs):
    out_ref = refs[-1]
    tokens, value_width = refs[0].shape
    for dg in range(groups):
        at = pl.ds(dg * tokens, tokens)
        out_ref[at, :value_width] = refs[dg][...]
        out_ref[at, value_width:] = refs[groups + dg][:, :LANES]


def pick_kernel(here_ref, there_ref, out_ref):
    def put(ref):
        out_ref[...] = ref[...]

    at_inner = inner(lax.axis_index("adapter"))
    pl.when(at_inner)(lambda: put(here_ref))
    pl.when(jnp.logical_not(at_inner))(lambda: put(there_ref))


def place_kernel(sizes, *refs):
    groups, holders, shard, half = sizes
    group, here = lax.axis_index("groups"), lax.axis_index("adapter")
    out_ref = refs[-1]
    for k in range(holders):
        for dg in range(groups):
            source = lax.rem(group + groups - dg, groups)
            at = shard_of(k, here, holders) * shard + source * half
            out_ref[:, pl.ds(pl.multiple_of(at, half), half)] = refs[k * groups + dg][...]


def chip_kernel(replicas, *refs):
    own_ref, came_refs, out_refs = refs[0], refs[1 : 2 * replicas - 1], refs[2 * replicas - 1 :]
    split = came_refs[0].shape[1]
    start = 0
    for out in out_refs:
        rows = out.shape[0]
        for j in range(2):
            at = pl.ds(start, rows), pl.ds(j * split, split)
            total = own_ref[at]
            for ref in came_refs[j::2]:
                total = total + ref[pl.ds(start, rows), :].astype(F32)
            out[:, pl.ds(j * split, split)] = total.astype(out.dtype)
        start += rows


def fold_kernel(own_ref, came_ref, keep_ref, send_ref):
    rows = keep_ref.shape[0]
    keep_ref[...] = own_ref[:rows] + came_ref[:rows].astype(F32)
    send_ref[...] = (own_ref[rows:] + came_ref[rows:].astype(F32)).astype(BF16)


def total_kernel(*refs):
    total = refs[0][...]
    for ref in refs[1:-1]:
        total = total + ref[...].astype(F32)
    refs[-1][...] = (ADAPTER_SCALE * total).astype(BF16)


def spread_kernel(width, replicas, *refs):
    core = lax.axis_index("replica")
    down_ref, up_ref = refs[replicas:]
    slots = down_ref.shape[0] // replicas
    rank = down_ref.shape[1]
    for dr in range(replicas):
        at = lax.rem(core + replicas - dr, replicas) * slots
        for j in range(slots):
            down_ref[at + j] = refs[dr][j * rank : (j + 1) * rank, :width]
            up_ref[at + j] = refs[dr][j * rank : (j + 1) * rank, width:]


def on_device(
    saved_layer_input,
    value_output_gradient,
    token_adapter_index,
    adapter_slot_index,
    frozen_value_weight,
    adapter_down_weight,
    adapter_up_weight,
):
    inputs = saved_layer_input[0]
    grad_rows = value_output_gradient[0]
    tokens, width = inputs.shape
    value_width = grad_rows.shape[1]
    groups, holders, replicas = (lax.axis_size(a) for a in ("groups", "adapter", "replica"))
    group, here, core = (lax.axis_index(a) for a in ("groups", "adapter", "replica"))
    slots, rank = adapter_down_weight.shape[1:3]
    own_slots = slots // replicas
    rows = own_slots * rank
    frozen = frozen_value_weight[0]
    shard = frozen.shape[0]
    half = shard // groups
    piece = half // replicas
    cols = width + value_width

    own_named = call(
        name_kernel,
        [jax.ShapeDtypeStruct((tokens, 3 * LANES), BF16)],
        (token_adapter_index[0, :, 0][None], adapter_slot_index),
        scalars=1,
    )[0]
    grads, named = [grad_rows], [own_named]
    for dg in range(1, groups):
        grads.append(moved(grad_rows, lambda g, z, s, r: (g - dg, z, s, r)))
        named.append(moved(own_named, lambda g, z, s, r: (g - dg, z, s, r)))

    own = call(
        functools.partial(own_kernel, (groups, holders, shard)),
        [jax.ShapeDtypeStruct((rows, holders * half + value_width), BF16)],
        (adapter_down_weight[0], adapter_up_weight[0]),
    )[0]
    held = [own]
    for k in range(1, holders):
        held.append(moved(own, lambda g, z, s, r: (g, z ^ k, s, r)))

    ring = [lax.dynamic_slice_in_dim(frozen, (group * replicas + core) * piece, piece, axis=0)]
    held, grads, named = lax.optimization_barrier((held, grads, named))
    both, downs = call(
        join_kernel,
        [
            jax.ShapeDtypeStruct((holders * rows, holders * half + value_width + SPARE), BF16),
            jax.ShapeDtypeStruct((holders * rows, holders * half), BF16),
        ],
        held,
    )
    both = [both] + [
        moved(both, lambda g, z, s, r: (g, z, s, r + dr)) for dr in range(1, replicas)
    ]
    others = [moved(downs, lambda g, z, s, r: (g + dg, z, s, r)) for dg in range(1, groups)]
    line = holders == 4
    swap = lambda g, z, s, r: (g, 3 - z, s, r) if inner(z) else None
    outward = lambda g, z, s, r: (g, z ^ 1, s, r) if inner(z) else None
    inward = lambda g, z, s, r: None if inner(z) else (g, z ^ 1, s, r)
    onward = lambda g, z, s, r: (g, z + 1, s, r)
    first = after(ring[0], both[0])
    if line:
        near = moved(first, lambda g, z, s, r: (g, z ^ 1, s, r))
        across = moved(first, swap)
        ring.append(near)
    else:
        ring.append(moved(first, onward))

    def pieces_of(k, *before):
        if k == 0:
            return [(0, 0)], [frozen]
        block = after(ring[k], *before) if before else ring[k]
        pieces = [block] + [
            moved(block, lambda g, z, s, r: (g, z, s, r + dr)) for dr in range(1, replicas)
        ]
        spec = [(dr, 0) for dr in range(replicas)]
        if piece % LANES:
            whole = jnp.zeros((half, value_width), BF16)
            for (dr, offset), part in zip(spec, pieces):
                at = ((core - dr) % replicas) * piece + offset
                whole = lax.dynamic_update_slice_in_dim(whole, part, at, axis=0)
            spec, pieces = [(0, 0)], [whole]
        return spec, pieces

    kept = replicas * holders * rows

    def adapter_sums(sel, *before):
        maps = list(both)
        for other in others:
            maps.append(after(other, sel))
            for dr in range(1, replicas):
                maps.append(moved(maps[-dr], lambda g, z, s, r: (g, z, s, r + dr)))
        gradients = call(
            functools.partial(adapter_kernel, (groups, holders, replicas, shard, slots, rank)),
            [jax.ShapeDtypeStruct((holders * rows, cols), F32)]
            + [jax.ShapeDtypeStruct((holders * rows, cols // 2), BF16)] * (2 * replicas - 2),
            (inputs, grad_rows, named[0], sel, *maps),
            [jax.ShapeDtypeStruct((kept, width), BF16)],
        )
        part, sent = gradients[0], gradients[1:]
        came = [
            moved(after(sent[2 * dr - 2 + j], *before), lambda g, z, s, r: (g, z, s, r - dr))
            for dr in range(1, replicas)
            for j in range(2)
        ]
        chip = call(
            functools.partial(chip_kernel, replicas),
            [
                jax.ShapeDtypeStruct((holders // 2 * rows, cols), F32),
                jax.ShapeDtypeStruct((holders // 2 * rows, cols), BF16),
            ],
            (part, *came),
        )
        return part, chip

    arrived, outs, sel = [], [], None
    for k in range(holders):
        if line and k == 2:
            near, across = lax.optimization_barrier((near, across, part, *arrived[0]))[:2]
            last = moved(near, swap)
            guests = call(
                functools.partial(guest_kernel, groups),
                [jax.ShapeDtypeStruct((groups * tokens, value_width + LANES), BF16)],
                (*grads, *named),
            )[0]
            guests = moved(after(guests, near), inward)
            passed_on = moved(across, outward)
            last, passed_on, guests = lax.optimization_barrier(
                (last, passed_on, guests, *arrived[1], chip[0])
            )[:3]
            shape = jax.ShapeDtypeStruct(passed_on.shape, BF16)
            ring += [call(pick_kernel, [shape], (across, passed_on))[0], last]
        elif k > 1 and not line:
            last = after(ring[-1], *outs[k - 2], part) if k > 2 else after(ring[-1], sel)
            last = moved(last, onward)
            ring.append(last)
        gate = [] if k == 0 else arrived[0] if k == 1 else outs[k - 1] if k == 2 or not line else []
        spec, blocks = pieces_of(k, *gate, *([*arrived[k - 2], chip[0]] if k > 2 and not line else ()))
        hosts = line and k == 3
        out = call(
            functools.partial(
                frozen_kernel, (tokens, groups, holders, replicas, slots, rank), k, spec, hosts
            ),
            [jax.ShapeDtypeStruct((tokens, half), BF16)] * groups
            + [jax.ShapeDtypeStruct((groups * tokens, kept), BF16)] * (k == 0)
            + [jax.ShapeDtypeStruct((groups * tokens, half), BF16)] * hosts,
            [*grads, *both, *([sel] if k else named), *([guests] if hosts else []), *blocks],
        )
        if k == 0:
            sel = out[groups]
        outs.append(list(out[:groups]))
        mails = outs[-1]
        if hosts:
            back = moved(out[groups], outward).reshape(groups, tokens, half)
            mails = [jnp.where(inner(here), mails[dg], back[dg]) for dg in range(groups)]
        if k > 2:
            mails = [after(mail, *arrived[-1]) for mail in mails]
        arrived.append(
            [moved(mails[dg], lambda g, z, s, r: (g + dg, z, s - 1, r)) for dg in range(groups)]
        )
        if k == 0:
            part, chip = adapter_sums(sel, *arrived[0])
    passed = call(
        functools.partial(place_kernel, (groups, holders, shard, half)),
        [jax.ShapeDtypeStruct((tokens, width), BF16)],
        [x for got in arrived for x in got],
    )[0]

    keep, send, by = chip[0], after(chip[1], last), holders // 2
    while by > 1:
        came = moved(send, lambda g, z, s, r: (g, z ^ by, s, r))
        by //= 2
        keep, send = call(
            fold_kernel,
            [
                jax.ShapeDtypeStruct((by * rows, cols), F32),
                jax.ShapeDtypeStruct((by * rows, cols), BF16),
            ],
            (keep, came),
        )
    came = moved(after(send, *arrived[-2]), lambda g, z, s, r: (g, z ^ 1, s, r))
    total = call(total_kernel, [jax.ShapeDtypeStruct((rows, cols), BF16)], (keep, came))[0]
    totals = [total] + [
        moved(total, lambda g, z, s, r: (g, z, s, r + dr)) for dr in range(1, replicas)
    ]
    down_grad, up_grad = call(
        functools.partial(spread_kernel, width, replicas),
        [
            jax.ShapeDtypeStruct((slots, rank, width), BF16),
            jax.ShapeDtypeStruct((slots, rank, value_width), BF16),
        ],
        totals,
    )

    return passed[None], down_grad[None], up_grad[None]


def solution(mesh):
    placed = (
        P("segment", ("groups", "adapter", "replica"), None),
        P("segment", ("groups", "adapter", "replica"), None),
        P("segment", ("groups", "adapter", "replica"), None),
        P("groups"),
        P("segment", "adapter", None),
        P("segment", "adapter", None, None),
        P("segment", "adapter", None, None),
    )
    return jax.shard_map(
        on_device,
        mesh=mesh,
        in_specs=placed,
        out_specs=(
            P("segment", ("groups", "adapter", "replica"), None),
            P(("groups", "segment"), "adapter", None, None),
            P(("groups", "segment"), "adapter", None, None),
        ),
        check_vma=False,
    )
```

```python
import functools
import itertools
import jax
import jax.numpy as jnp
from jax import lax
from jax.experimental import pallas as pl
from jax.experimental.pallas import tpu as pltpu
from jax.sharding import PartitionSpec as P

ADAPTER_SCALE = 2.0
AXES = ("groups", "adapter", "segment", "replica")
LANES = 128
SPARE = 256
F32 = jnp.float32
BF16 = jnp.bfloat16
MIB = 1024 * 1024


def moved(x, to):
    sizes = [lax.axis_size(a) for a in AXES]
    number = {at: i for i, at in enumerate(itertools.product(*map(range, sizes)))}
    pairs = []
    for at, i in number.items():
        target = to(*at)
        if target is not None:
            pairs.append((i, number[tuple(t % s for t, s in zip(target, sizes))]))
    return lax.ppermute(x, AXES, pairs)


def after(x, *others):
    return lax.optimization_barrier((x, *others))[0]


def rows_by_rows(a, b):
    return lax.dot_general(a, b, (((1,), (1,)), ((), ())), preferred_element_type=F32)


def columns_by_columns(a, b):
    return lax.dot_general(a, b, (((0,), (0,)), ((), ())), preferred_element_type=F32)


def call(kernel, out_shape, operands, scratch=(), scalars=0):
    held = sum(x.size * x.dtype.itemsize for x in (*operands, *out_shape, *scratch))
    return pl.pallas_call(
        kernel,
        out_shape=out_shape,
        in_specs=[pl.BlockSpec(memory_space=pltpu.VMEM)] * (len(operands) - scalars)
        + [pl.BlockSpec(memory_space=pltpu.SMEM)] * scalars,
        scratch_shapes=[pltpu.VMEM(x.shape, x.dtype) for x in scratch],
        compiler_params=pltpu.CompilerParams(vmem_limit_bytes=2 * held + 4 * MIB),
        cost_estimate=pl.CostEstimate(flops=1000, bytes_accessed=1000, transcendentals=0),
    )(*operands)


def row_slots(holders, replicas, slots, rank, dr):
    here, core = lax.axis_index("adapter"), lax.axis_index("replica")
    own_slots = slots // replicas
    lane = lax.broadcasted_iota(jnp.int32, (1, holders * own_slots * rank), 1)
    slot = jnp.zeros_like(lane)
    for k in range(holders):
        for j in range(own_slots):
            start = (k * own_slots + j) * rank
            value = (here ^ k) * slots
            value = value + lax.rem(core + replicas - dr, replicas) * own_slots + j
            slot = jnp.where((lane >= start) & (lane < start + rank), value, slot)
    return slot.astype(F32)


def name_kernel(name_ref, slot_ref, out_ref):
    names = name_ref[...]
    slot = jnp.zeros_like(names)
    for j in range(slot_ref.shape[0]):
        slot = jnp.where(names == j, slot_ref[j], slot)
    ones = jnp.ones((1, out_ref.shape[1]), F32)
    out_ref[...] = columns_by_columns(slot.astype(F32), ones).astype(BF16)


def join_kernel(*refs):
    both_ref, down_ref = refs[-2:]
    both_ref[:, -SPARE:] = jnp.zeros((both_ref.shape[0], SPARE), BF16)
    for k, ref in enumerate(refs[:-2]):
        rows = ref.shape[0]
        both_ref[k * rows : (k + 1) * rows, :-SPARE] = ref[...]
        down_ref[k * rows : (k + 1) * rows] = ref[:, : down_ref.shape[1]]


def own_kernel(sizes, down_ref, up_ref, out_ref):
    groups, holders, shard = sizes
    half = shard // groups
    rank = down_ref.shape[1]
    slots = out_ref.shape[0] // rank
    first = lax.axis_index("replica") * slots
    for j in range(slots):
        to = pl.ds(j * rank, rank)
        for z in range(holders):
            at = pl.multiple_of(z * shard + lax.axis_index("groups") * half, half)
            out_ref[to, z * half : (z + 1) * half] = down_ref[first + j, :, pl.ds(at, half)]
        out_ref[to, holders * half :] = up_ref[first + j]


def adapter_kernel(sizes, *refs):
    groups, holders, replicas, shard, slots, rank = sizes
    x_ref, g_ref, named_ref, sel_ref = refs[:4]
    map_refs, refs = refs[4 : 4 + groups * replicas], refs[4 + groups * replicas :]
    own_ref, other_refs, down = refs[0], refs[1:-1], refs[-1]
    group = lax.axis_index("groups")
    tokens, width = x_ref.shape
    rows, cols = own_ref.shape
    half = shard // groups
    for dg in range(groups):
        first = lax.rem(group + groups - dg, groups) * half
        for dr in range(replicas):
            for z in range(holders):
                at = pl.multiple_of(first + z * shard, half)
                down[pl.ds(dr * rows, rows), pl.ds(at, half)] = map_refs[dg * replicas + dr][
                    :, z * half : (z + 1) * half
                ]
    row_slot = [row_slots(holders, replicas, slots, rank, dr) for dr in range(replicas)]
    keep = named_ref[...].astype(F32)[:, :1] == jnp.concatenate(row_slot, axis=1)
    in_sel = jnp.where(keep, rows_by_rows(x_ref[...], down[...]), 0.0).astype(BF16)
    grad_sel = sel_ref[pl.ds(0, tokens), :]
    step, split = 1024, cols // 2
    for at in range(0, cols, step):
        if at < width:
            part = columns_by_columns(grad_sel, x_ref[:, at : at + step])
        else:
            part = columns_by_columns(in_sel, g_ref[:, at - width : at - width + step])
        own_ref[:, at : at + step] = part[:rows]
        for dr in range(1, replicas):
            sent = part[dr * rows : (dr + 1) * rows].astype(BF16)
            for j in range(0, step, LANES):
                ref, to = other_refs[2 * dr - 2 + (at + j) // split], (at + j) % split
                ref[:, to : to + LANES] = sent[:, j : j + LANES]


def frozen_kernel(sizes, k, spec, *refs):
    tokens, groups, holders, replicas, slots, rank = sizes
    g_refs, refs = refs[:groups], refs[groups:]
    map_refs, refs = refs[:replicas], refs[replicas:]
    core, here = lax.axis_index("replica"), lax.axis_index("adapter")
    rows = map_refs[0].shape[0]
    wide = map_refs[0].shape[1] - g_refs[0].shape[1] - SPARE
    half = wide // holders
    if k == 0:
        named_refs, refs = refs[:groups], refs[groups:]
        sel_ref = refs[-1]
        out_refs = refs[-1 - groups : -1]
        for dg in range(groups):
            names = named_refs[dg][...].astype(F32)[:, :1]
            for dr in range(replicas):
                keep = names == row_slots(holders, replicas, slots, rank, dr)
                proj_grad = rows_by_rows(g_refs[dg][...], map_refs[dr][:, wide:-SPARE])
                sel_ref[pl.ds(dg * tokens, tokens), dr * rows : (dr + 1) * rows] = jnp.where(
                    keep, proj_grad, 0.0
                ).astype(BF16)
    else:
        sel_ref, refs = refs[0], refs[1:]
        out_refs = refs[-groups:]
    shard_at = lax.rem(here + holders - k, holders) * half
    for (dr, offset), block in zip(spec, refs):
        if k == 0:
            block = block.at[pl.ds(pl.multiple_of(lax.axis_index("groups") * half, half), half)]
        wide = half if k == 0 or len(spec) == 1 else half // len(spec)
        at = 0
        if wide < half:
            at = lax.rem(core + replicas - dr, replicas) * (half // replicas) + offset
        columns = pl.ds(pl.multiple_of(shard_at + at, wide), wide)
        for dg in range(groups):
            base = rows_by_rows(g_refs[dg][...], block[:wide]).astype(BF16)
            lora = 0.0
            for dr in range(replicas):
                lora = lora + jnp.dot(
                    sel_ref[pl.ds(dg * tokens, tokens), dr * rows : (dr + 1) * rows],
                    map_refs[dr][:, columns],
                    preferred_element_type=F32,
                )
            lora = (ADAPTER_SCALE * lora).astype(BF16)
            out_refs[dg][:, pl.ds(pl.multiple_of(at, wide) if wide < half else 0, wide)] = (
                base.astype(F32) + lora.astype(F32)
            ).astype(BF16)


def place_kernel(sizes, *refs):
    groups, holders, shard, half = sizes
    group, here = lax.axis_index("groups"), lax.axis_index("adapter")
    out_ref = refs[-1]
    for k in range(holders):
        for dg in range(groups):
            source = lax.rem(group + groups - dg, groups)
            at = lax.rem(here + holders - k, holders) * shard + source * half
            out_ref[:, pl.ds(pl.multiple_of(at, half), half)] = refs[k * groups + dg][...]


def chip_kernel(replicas, *refs):
    own_ref, came_refs, out_refs = refs[0], refs[1 : 2 * replicas - 1], refs[2 * replicas - 1 :]
    rows = out_refs[0].shape[0]
    split = came_refs[0].shape[1]
    for k, out in enumerate(out_refs):
        for j in range(2):
            at = pl.ds(k * rows, rows), pl.ds(j * split, split)
            total = own_ref[at]
            for ref in came_refs[j::2]:
                total = total + ref[pl.ds(k * rows, rows), :].astype(F32)
            out[:, pl.ds(j * split, split)] = total.astype(out.dtype)


def total_kernel(*refs):
    total = refs[0][...]
    for ref in refs[1:-1]:
        total = total + ref[...].astype(F32)
    refs[-1][...] = (ADAPTER_SCALE * total).astype(BF16)


def spread_kernel(width, replicas, *refs):
    core = lax.axis_index("replica")
    down_ref, up_ref = refs[replicas:]
    slots = down_ref.shape[0] // replicas
    rank = down_ref.shape[1]
    for dr in range(replicas):
        at = lax.rem(core + replicas - dr, replicas) * slots
        for j in range(slots):
            down_ref[at + j] = refs[dr][j * rank : (j + 1) * rank, :width]
            up_ref[at + j] = refs[dr][j * rank : (j + 1) * rank, width:]


def on_device(
    saved_layer_input,
    value_output_gradient,
    token_adapter_index,
    adapter_slot_index,
    frozen_value_weight,
    adapter_down_weight,
    adapter_up_weight,
):
    inputs = saved_layer_input[0]
    grad_rows = value_output_gradient[0]
    tokens, width = inputs.shape
    value_width = grad_rows.shape[1]
    groups, holders, replicas = (lax.axis_size(a) for a in ("groups", "adapter", "replica"))
    group, here, core = (lax.axis_index(a) for a in ("groups", "adapter", "replica"))
    slots, rank = adapter_down_weight.shape[1:3]
    own_slots = slots // replicas
    rows = own_slots * rank
    frozen = frozen_value_weight[0]
    shard = frozen.shape[0]
    half = shard // groups
    piece = half // replicas
    cols = width + value_width

    own_named = call(
        name_kernel,
        [jax.ShapeDtypeStruct((tokens, 3 * LANES), BF16)],
        (token_adapter_index[0, :, 0][None], adapter_slot_index),
        scalars=1,
    )[0]
    own = call(
        functools.partial(own_kernel, (groups, holders, shard)),
        [jax.ShapeDtypeStruct((rows, holders * half + value_width), BF16)],
        (adapter_down_weight[0], adapter_up_weight[0]),
    )[0]
    grads, named = [grad_rows], [own_named]
    for dg in range(1, groups):
        grads.append(moved(grad_rows, lambda g, z, s, r: (g - dg, z, s, r)))
        named.append(moved(own_named, lambda g, z, s, r: (g - dg, z, s, r)))

    held = [own]
    for k in range(1, holders):
        held.append(moved(own, lambda g, z, s, r: (g, z ^ k, s, r)))

    part_rows = piece // 2
    quarter = (group * replicas + core) * piece
    parts = [
        lax.dynamic_slice_in_dim(frozen, quarter + j * part_rows, part_rows + spare, axis=0)
        for j, spare in enumerate((16, 0))
    ]
    own_named, parts = lax.optimization_barrier((own_named, parts))
    held = [own]
    for k in range(1, holders):
        held.append(moved(own, lambda g, z, s, r: (g, z ^ k, s, r)))

    ring = [lax.dynamic_slice_in_dim(frozen, (group * replicas + core) * piece, piece, axis=0)]
    held, grads, named = lax.optimization_barrier((held, grads, named))
    both, downs = call(
        join_kernel,
        [
            jax.ShapeDtypeStruct((holders * rows, holders * half + value_width + SPARE), BF16),
            jax.ShapeDtypeStruct((holders * rows, holders * half), BF16),
        ],
        held,
    )
    both = [both] + [
        moved(both, lambda g, z, s, r: (g, z, s, r + dr)) for dr in range(1, replicas)
    ]
    others = [moved(downs, lambda g, z, s, r: (g + dg, z, s, r)) for dg in range(1, groups)]
    onward = lambda g, z, s, r: (g, z + 1, s, r)
    ring = [parts, [moved(after(x, both[0]), onward) for x in parts]]

    def pieces_of(k, *before):
        if k == 0:
            return [(0, 0)], [frozen]
        spec, pieces = [], []
        for dr in range(replicas):
            for j, part in enumerate(ring[k]):
                spec.append((dr, j * part_rows))
                mail = after(part, *before) if before else part
                pieces.append(moved(mail, lambda g, z, s, r: (g, z, s, r + dr)) if dr else part)
        if part_rows % LANES:
            whole = jnp.zeros((half, value_width), BF16)
            for (dr, offset), part in zip(spec, pieces):
                at = ((core - dr) % replicas) * piece + offset
                whole = lax.dynamic_update_slice_in_dim(whole, part[:part_rows], at, axis=0)
            spec, pieces = [(0, 0)], [whole]
        return spec, pieces

    kept = replicas * holders * rows

    def adapter_sums(sel, *before):
        maps = list(both)
        for other in others:
            maps.append(after(other, sel))
            for dr in range(1, replicas):
                maps.append(moved(maps[-dr], lambda g, z, s, r: (g, z, s, r + dr)))
        gradients = call(
            functools.partial(adapter_kernel, (groups, holders, replicas, shard, slots, rank)),
            [jax.ShapeDtypeStruct((holders * rows, cols), F32)]
            + [jax.ShapeDtypeStruct((holders * rows, cols // 2), BF16)] * (2 * replicas - 2),
            (inputs, grad_rows, named[0], sel, *maps),
            [jax.ShapeDtypeStruct((kept, width), BF16)],
        )
        part, sent = gradients[0], gradients[1:]
        came = [
            moved(after(sent[2 * dr - 2 + j], *before), lambda g, z, s, r: (g, z, s, r - dr))
            for dr in range(1, replicas)
            for j in range(2)
        ]
        chip = call(
            functools.partial(chip_kernel, replicas),
            [jax.ShapeDtypeStruct((rows, cols), F32)]
            + [jax.ShapeDtypeStruct((rows, cols), BF16)] * (holders - 1),
            (part, *came),
        )
        return part, chip

    arrived, outs, sel = [], [], None
    for k in range(holders):
        if k > 1:
            gate = [part] if k > 2 else [sel]
            ring.append([moved(after(x, *gate), onward) for x in ring[-1]])
        gate = outs[k - 1] if k > 1 else arrived[0] if k else []
        spec, blocks = pieces_of(k, *gate, *([*arrived[k - 2], chip[0]] if k > 2 else ()))
        tokens_in = [after(grad_rows, part), *grads[1:]] if k == 1 else grads
        out = call(
            functools.partial(
                frozen_kernel, (tokens, groups, holders, replicas, slots, rank), k, spec
            ),
            [jax.ShapeDtypeStruct((tokens, half), BF16)] * groups
            + [jax.ShapeDtypeStruct((groups * tokens, kept), BF16)] * (k == 0),
            [*tokens_in, *both, *([sel] if k else named), *blocks],
        )
        if k == 0:
            sel = out[groups]
        outs.append(list(out[:groups]))
        mails = outs[-1]
        if k > 2:
            mails = [after(mail, *arrived[-1]) for mail in mails]
        arrived.append(
            [moved(mails[dg], lambda g, z, s, r: (g + dg, z, s - 1, r)) for dg in range(groups)]
        )
        if k == 0:
            part, chip = adapter_sums(sel, *arrived[0])
    passed = call(
        functools.partial(place_kernel, (groups, holders, shard, half)),
        [jax.ShapeDtypeStruct((tokens, width), BF16)],
        [x for got in arrived for x in got],
    )[0]

    sums = [chip[0]] + [
        moved(after(chip[k], *ring[-1]), lambda g, z, s, r: (g, z ^ k, s, r))
        for k in range(1, holders)
    ]
    total = call(total_kernel, [jax.ShapeDtypeStruct((rows, cols), BF16)], sums)[0]
    totals = [total] + [
        moved(total, lambda g, z, s, r: (g, z, s, r + dr)) for dr in range(1, replicas)
    ]
    down_grad, up_grad = call(
        functools.partial(spread_kernel, width, replicas),
        [
            jax.ShapeDtypeStruct((slots, rank, width), BF16),
            jax.ShapeDtypeStruct((slots, rank, value_width), BF16),
        ],
        totals,
    )

    return passed[None], down_grad[None], up_grad[None]


def solution(mesh):
    placed = (
        P("segment", ("groups", "adapter", "replica"), None),
        P("segment", ("groups", "adapter", "replica"), None),
        P("segment", ("groups", "adapter", "replica"), None),
        P("groups"),
        P("segment", "adapter", None),
        P("segment", "adapter", None, None),
        P("segment", "adapter", None, None),
    )
    return jax.shard_map(
        on_device,
        mesh=mesh,
        in_specs=placed,
        out_specs=(
            P("segment", ("groups", "adapter", "replica"), None),
            P(("groups", "segment"), "adapter", None, None),
            P(("groups", "segment"), "adapter", None, None),
        ),
        check_vma=False,
    )
```

```python
import functools
import itertools
import jax
import jax.numpy as jnp
from jax import lax
from jax.experimental import pallas as pl
from jax.experimental.pallas import tpu as pltpu
from jax.sharding import PartitionSpec as P

ADAPTER_SCALE = 2.0
AXES = ("groups", "adapter", "segment", "replica")
LANES = 128
F32 = jnp.float32
BF16 = jnp.bfloat16
MIB = 1024 * 1024


def moved(x, to):
    sizes = [lax.axis_size(a) for a in AXES]
    number = {at: i for i, at in enumerate(itertools.product(*map(range, sizes)))}
    pairs = [
        (i, number[tuple(t % s for t, s in zip(to(*at), sizes))]) for at, i in number.items()
    ]
    return lax.ppermute(x, AXES, pairs)


def after(x, *others):
    return lax.optimization_barrier((x, *others))[0]


def rows_by_rows(a, b):
    return lax.dot_general(a, b, (((1,), (1,)), ((), ())), preferred_element_type=F32)


def columns_by_columns(a, b):
    return lax.dot_general(a, b, (((0,), (0,)), ((), ())), preferred_element_type=F32)


def call(kernel, out_shape, operands, scratch=(), scalars=0):
    held = sum(x.size * x.dtype.itemsize for x in (*operands, *out_shape, *scratch))
    return pl.pallas_call(
        kernel,
        out_shape=out_shape,
        in_specs=[pl.BlockSpec(memory_space=pltpu.VMEM)] * (len(operands) - scalars)
        + [pl.BlockSpec(memory_space=pltpu.SMEM)] * scalars,
        scratch_shapes=[pltpu.VMEM(x.shape, x.dtype) for x in scratch],
        compiler_params=pltpu.CompilerParams(vmem_limit_bytes=2 * held + 4 * MIB),
        cost_estimate=pl.CostEstimate(flops=1000, bytes_accessed=1000, transcendentals=0),
    )(*operands)


def slots_of(tagged_ref):
    return tagged_ref[:, -LANES:].astype(F32)[:, :1]


def row_slots(holders, replicas, slots, rank, dr):
    here, core = lax.axis_index("adapter"), lax.axis_index("replica")
    own_slots = slots // replicas
    lane = lax.broadcasted_iota(jnp.int32, (1, holders * own_slots * rank), 1)
    slot = jnp.zeros_like(lane)
    for k in range(holders):
        for j in range(own_slots):
            start = (k * own_slots + j) * rank
            value = lax.rem(here + holders - k, holders) * slots
            value = value + lax.rem(core + replicas - dr, replicas) * own_slots + j
            slot = jnp.where((lane >= start) & (lane < start + rank), value, slot)
    return slot.astype(F32)


def tag_kernel(g_ref, name_ref, slot_ref, out_ref):
    out_ref[:, :-LANES] = g_ref[...]
    names = name_ref[...]
    slot = jnp.zeros_like(names)
    for j in range(slot_ref.shape[0]):
        slot = jnp.where(names == j, slot_ref[j], slot)
    ones = jnp.ones((1, LANES), F32)
    out_ref[:, -LANES:] = columns_by_columns(slot.astype(F32), ones).astype(BF16)


def join_kernel(*refs):
    down_ref, up_ref = refs[-2:]
    wide = down_ref.shape[1]
    for k, ref in enumerate(refs[:-2]):
        rows = ref.shape[0]
        down_ref[k * rows : (k + 1) * rows] = ref[:, :wide]
        up_ref[k * rows : (k + 1) * rows] = ref[:, wide:]


def own_kernel(sizes, down_ref, up_ref, out_ref):
    groups, holders, shard = sizes
    half = shard // groups
    rank = down_ref.shape[1]
    slots = out_ref.shape[0] // rank
    first = lax.axis_index("replica") * slots
    for j in range(slots):
        to = pl.ds(j * rank, rank)
        for z in range(holders):
            at = pl.multiple_of(z * shard + lax.axis_index("groups") * half, half)
            out_ref[to, z * half : (z + 1) * half] = down_ref[first + j, :, pl.ds(at, half)]
        out_ref[to, holders * half :] = up_ref[first + j]


def adapter_kernel(sizes, *refs):
    groups, holders, replicas, shard, slots, rank = sizes
    x_ref, g_ref, sel_ref = refs[:3]
    map_refs, refs = refs[3 : 3 + groups * replicas], refs[3 + groups * replicas :]
    own_ref, other_refs, down = refs[0], refs[1:-1], refs[-1]
    group = lax.axis_index("groups")
    tokens, width = x_ref.shape
    rows, cols = own_ref.shape
    half = shard // groups
    for dg in range(groups):
        first = lax.rem(group + groups - dg, groups) * half
        for dr in range(replicas):
            for z in range(holders):
                at = pl.multiple_of(first + z * shard, half)
                down[pl.ds(dr * rows, rows), pl.ds(at, half)] = map_refs[dg * replicas + dr][
                    :, z * half : (z + 1) * half
                ]
    row_slot = [row_slots(holders, replicas, slots, rank, dr) for dr in range(replicas)]
    keep = slots_of(g_ref) == jnp.concatenate(row_slot, axis=1)
    in_sel = jnp.where(keep, rows_by_rows(x_ref[...], down[...]), 0.0).astype(BF16)
    grad_sel = sel_ref[pl.ds(0, tokens), :]
    step, split = 1024, cols // 2
    for at in range(0, cols, step):
        if at < width:
            part = columns_by_columns(grad_sel, x_ref[:, at : at + step])
        else:
            part = columns_by_columns(in_sel, g_ref[:, at - width : at - width + step])
        own_ref[:, at : at + step] = part[:rows]
        for dr in range(1, replicas):
            sent = part[dr * rows : (dr + 1) * rows].astype(BF16)
            for j in range(0, step, LANES):
                ref, to = other_refs[2 * dr - 2 + (at + j) // split], (at + j) % split
                ref[:, to : to + LANES] = sent[:, j : j + LANES]


def frozen_kernel(sizes, batch, *refs):
    tokens, groups, holders, replicas, slots, rank = sizes
    g_refs, refs = refs[:groups], refs[groups:]
    down_refs, refs = refs[:replicas], refs[replicas:]
    core, here = lax.axis_index("replica"), lax.axis_index("adapter")
    rows = down_refs[0].shape[0]
    half = down_refs[0].shape[1] // holders
    if batch[0][0] == 0:
        up_refs, refs = refs[:replicas], refs[replicas:]
        sel_ref = refs[-1]
        out_refs = refs[-1 - groups : -1]
        for dg in range(groups):
            for dr in range(replicas):
                keep = slots_of(g_refs[dg]) == row_slots(holders, replicas, slots, rank, dr)
                proj_grad = rows_by_rows(g_refs[dg][:, :-LANES], up_refs[dr][...])
                sel_ref[pl.ds(dg * tokens, tokens), dr * rows : (dr + 1) * rows] = jnp.where(
                    keep, proj_grad, 0.0
                ).astype(BF16)
    else:
        sel_ref, refs = refs[0], refs[1:]
        out_refs = refs[-groups:]
    for i, (k, spec) in enumerate(batch):
        shard_at = lax.rem(here + holders - k, holders) * half
        for (dr, offset), block in zip(spec, refs):
            if k == 0:
                first = pl.multiple_of(lax.axis_index("groups") * half, half)
                block = block.at[pl.ds(first, half)]
            wide = block.shape[0]
            at = 0
            if wide < half:
                at = lax.rem(core + replicas - dr, replicas) * (half // replicas) + offset
            columns = pl.ds(pl.multiple_of(shard_at + at, wide), wide)
            for dg in range(groups):
                base = rows_by_rows(g_refs[dg][:, :-LANES], block[...]).astype(BF16)
                lora = 0.0
                for j in range(replicas):
                    lora = lora + jnp.dot(
                        sel_ref[pl.ds(dg * tokens, tokens), j * rows : (j + 1) * rows],
                        down_refs[j][:, columns],
                        preferred_element_type=F32,
                    )
                lora = (ADAPTER_SCALE * lora).astype(BF16)
                out_refs[dg][:, pl.ds(pl.multiple_of(i * half + at, wide), wide)] = (
                    base.astype(F32) + lora.astype(F32)
                ).astype(BF16)
        refs = refs[len(spec) :]


def place_kernel(sizes, batches, *refs):
    groups, holders, shard, half = sizes
    group, here = lax.axis_index("groups"), lax.axis_index("adapter")
    out_ref = refs[-1]
    for i, batch in enumerate(batches):
        for dg in range(groups):
            source = lax.rem(group + groups - dg, groups)
            for j, k in enumerate(batch):
                at = lax.rem(here + holders - k, holders) * shard + source * half
                out_ref[:, pl.ds(pl.multiple_of(at, half), half)] = refs[i * groups + dg][
                    :, j * half : (j + 1) * half
                ]


def chip_kernel(replicas, *refs):
    own_ref, came_refs, out_refs = refs[0], refs[1 : 2 * replicas - 1], refs[2 * replicas - 1 :]
    rows = out_refs[0].shape[0]
    split = came_refs[0].shape[1]
    for k, out in enumerate(out_refs):
        for j in range(2):
            at = pl.ds(k * rows, rows), pl.ds(j * split, split)
            total = own_ref[at]
            for ref in came_refs[j::2]:
                total = total + ref[pl.ds(k * rows, rows), :].astype(F32)
            out[:, pl.ds(j * split, split)] = total.astype(out.dtype)


def total_kernel(*refs):
    total = refs[0][...]
    for ref in refs[1:-1]:
        total = total + ref[...].astype(F32)
    refs[-1][...] = (ADAPTER_SCALE * total).astype(BF16)


def spread_kernel(width, replicas, *refs):
    core = lax.axis_index("replica")
    down_ref, up_ref = refs[replicas:]
    slots = down_ref.shape[0] // replicas
    rank = down_ref.shape[1]
    for dr in range(replicas):
        at = lax.rem(core + replicas - dr, replicas) * slots
        for j in range(slots):
            down_ref[at + j] = refs[dr][j * rank : (j + 1) * rank, :width]
            up_ref[at + j] = refs[dr][j * rank : (j + 1) * rank, width:]


def on_device(
    saved_layer_input,
    value_output_gradient,
    token_adapter_index,
    adapter_slot_index,
    frozen_value_weight,
    adapter_down_weight,
    adapter_up_weight,
):
    inputs = saved_layer_input[0]
    grad_rows = value_output_gradient[0]
    tokens, width = inputs.shape
    value_width = grad_rows.shape[1]
    groups, holders, replicas = (lax.axis_size(a) for a in ("groups", "adapter", "replica"))
    group, here, core = (lax.axis_index(a) for a in ("groups", "adapter", "replica"))
    slots, rank = adapter_down_weight.shape[1:3]
    own_slots = slots // replicas
    rows = own_slots * rank
    frozen = frozen_value_weight[0]
    shard = frozen.shape[0]
    half = shard // groups
    piece = half // replicas
    cols = width + value_width

    tagged = call(
        tag_kernel,
        [jax.ShapeDtypeStruct((tokens, value_width + LANES), BF16)],
        (grad_rows, token_adapter_index[0, :, 0][None], adapter_slot_index),
        scalars=1,
    )[0]
    grads = [tagged] + [
        moved(tagged, lambda g, z, s, r: (g - dg, z, s, r)) for dg in range(1, groups)
    ]

    own = call(
        functools.partial(own_kernel, (groups, holders, shard)),
        [jax.ShapeDtypeStruct((rows, holders * half + value_width), BF16)],
        (adapter_down_weight[0], adapter_up_weight[0]),
    )[0]
    held = [own]
    for k in range(1, holders):
        held.append(moved(own, lambda g, z, s, r: (g, z + k, s, r)))

    ring = [lax.dynamic_slice_in_dim(frozen, (group * replicas + core) * piece, piece, axis=0)]
    ring.append(moved(ring[0], lambda g, z, s, r: (g, z + 1, s, r)))
    held, grads, ring = lax.optimization_barrier((held, grads, ring))
    joined = call(
        join_kernel,
        [
            jax.ShapeDtypeStruct((holders * rows, holders * half), BF16),
            jax.ShapeDtypeStruct((holders * rows, value_width), BF16),
        ],
        held,
    )
    downs, ups = [joined[0]], [joined[1]]
    for dr in range(1, replicas):
        ups.append(moved(ups[0], lambda g, z, s, r: (g, z, s, r + dr)))
        downs.append(moved(downs[0], lambda g, z, s, r: (g, z, s, r + dr)))
    def pieces_of(k, *before):
        if k == 0:
            return [(0, 0)], [frozen]
        block = after(ring[k], *before) if before else ring[k]
        spec = [(dr, 0) for dr in range(replicas)]
        pieces = [block] + [
            moved(block, lambda g, z, s, r: (g, z, s, r + dr)) for dr in range(1, replicas)
        ]
        if piece % LANES:
            whole = jnp.zeros((half, value_width), BF16)
            for (dr, offset), part in zip(spec, pieces):
                at = ((core - dr) % replicas) * piece + offset
                whole = lax.dynamic_update_slice_in_dim(whole, part, at, axis=0)
            spec, pieces = [(0, 0)], [whole]
        return spec, pieces

    kept = replicas * holders * rows

    def adapter_sums(sel, *before):
        maps = list(downs)
        for dg in range(1, groups):
            maps.append(moved(downs[0], lambda g, z, s, r: (g + dg, z, s, r)))
            for dr in range(1, replicas):
                maps.append(moved(maps[-dr], lambda g, z, s, r: (g, z, s, r + dr)))
        gradients = call(
            functools.partial(adapter_kernel, (groups, holders, replicas, shard, slots, rank)),
            [jax.ShapeDtypeStruct((holders * rows, cols), F32)]
            + [jax.ShapeDtypeStruct((holders * rows, cols // 2), BF16)] * (2 * replicas - 2),
            (inputs, tagged, sel, *maps),
            [jax.ShapeDtypeStruct((kept, width), BF16)],
        )
        part, sent = gradients[0], gradients[1:]
        came = [
            moved(after(sent[2 * dr - 2 + j], *before), lambda g, z, s, r: (g, z, s, r - dr))
            for dr in range(1, replicas)
            for j in range(2)
        ]
        chip = call(
            functools.partial(chip_kernel, replicas),
            [jax.ShapeDtypeStruct((rows, cols), F32)]
            + [jax.ShapeDtypeStruct((rows, cols), BF16)] * (holders - 1),
            (part, *came),
        )
        return part, chip

    batches = [list(range(min(2, holders)))] + [[k] for k in range(2, holders)]
    arrived = []
    for i, batch in enumerate(batches):
        operands, specs = [], []
        for k in batch:
            if k > 1:
                last = after(ring[-1], sel) if k > 2 else ring[-1]
                ring.append(moved(last, lambda g, z, s, r: (g, z + 1, s, r)))
            gate = arrived[0] if k == 2 else [*arrived[i - 2], chip[0]] if k > 2 else []
            spec, blocks = pieces_of(k, *gate)
            specs.append((k, spec))
            operands += blocks
        out = call(
            functools.partial(
                frozen_kernel, (tokens, groups, holders, replicas, slots, rank), specs
            ),
            [jax.ShapeDtypeStruct((tokens, half * len(batch)), BF16)] * groups
            + [jax.ShapeDtypeStruct((groups * tokens, kept), BF16)] * (i == 0),
            [*grads, *downs, *([sel] if i else ups), *operands],
        )
        if i == 0:
            sel = out[groups]
        mails = list(out[:groups])
        if i > 1:
            mails = [after(mail, *arrived[-1]) for mail in mails]
        arrived.append(
            [moved(mails[dg], lambda g, z, s, r: (g + dg, z, s - 1, r)) for dg in range(groups)]
        )
        if i == 0:
            part, chip = adapter_sums(sel, *arrived[0])
    passed = call(
        functools.partial(place_kernel, (groups, holders, shard, half), batches),
        [jax.ShapeDtypeStruct((tokens, width), BF16)],
        [x for got in arrived for x in got],
    )[0]

    sums = [chip[0]] + [
        moved(after(chip[k], ring[-1]), lambda g, z, s, r: (g, z - k, s, r))
        for k in range(1, holders)
    ]
    total = call(total_kernel, [jax.ShapeDtypeStruct((rows, cols), BF16)], sums)[0]
    totals = [total] + [
        moved(total, lambda g, z, s, r: (g, z, s, r + dr)) for dr in range(1, replicas)
    ]
    down_grad, up_grad = call(
        functools.partial(spread_kernel, width, replicas),
        [
            jax.ShapeDtypeStruct((slots, rank, width), BF16),
            jax.ShapeDtypeStruct((slots, rank, value_width), BF16),
        ],
        totals,
    )

    return passed[None], down_grad[None], up_grad[None]


def solution(mesh):
    placed = (
        P("segment", ("groups", "adapter", "replica"), None),
        P("segment", ("groups", "adapter", "replica"), None),
        P("segment", ("groups", "adapter", "replica"), None),
        P("groups"),
        P("segment", "adapter", None),
        P("segment", "adapter", None, None),
        P("segment", "adapter", None, None),
    )
    return jax.shard_map(
        on_device,
        mesh=mesh,
        in_specs=placed,
        out_specs=(
            P("segment", ("groups", "adapter", "replica"), None),
            P(("groups", "segment"), "adapter", None, None),
            P(("groups", "segment"), "adapter", None, None),
        ),
        check_vma=False,
    )
```

```python
import functools
import itertools
import jax
import jax.numpy as jnp
from jax import lax
from jax.experimental import pallas as pl
from jax.experimental.pallas import tpu as pltpu
from jax.sharding import PartitionSpec as P

ADAPTER_SCALE = 2.0
AXES = ("groups", "adapter", "segment", "replica")
LANES = 128
F32 = jnp.float32
BF16 = jnp.bfloat16
MIB = 1024 * 1024


def moved(x, to):
    sizes = [lax.axis_size(a) for a in AXES]
    number = {at: i for i, at in enumerate(itertools.product(*map(range, sizes)))}
    pairs = [
        (i, number[tuple(t % s for t, s in zip(to(*at), sizes))]) for at, i in number.items()
    ]
    return lax.ppermute(x, AXES, pairs)


def after(x, *others):
    return lax.optimization_barrier((x, *others))[0]


def rows_by_rows(a, b):
    return lax.dot_general(a, b, (((1,), (1,)), ((), ())), preferred_element_type=F32)


def columns_by_columns(a, b):
    return lax.dot_general(a, b, (((0,), (0,)), ((), ())), preferred_element_type=F32)


def call(kernel, out_shape, operands, scratch=(), scalars=0):
    held = sum(x.size * x.dtype.itemsize for x in (*operands, *out_shape, *scratch))
    return pl.pallas_call(
        kernel,
        out_shape=out_shape,
        in_specs=[pl.BlockSpec(memory_space=pltpu.VMEM)] * (len(operands) - scalars)
        + [pl.BlockSpec(memory_space=pltpu.SMEM)] * scalars,
        scratch_shapes=[pltpu.VMEM(x.shape, x.dtype) for x in scratch],
        compiler_params=pltpu.CompilerParams(vmem_limit_bytes=2 * held + 4 * MIB),
        cost_estimate=pl.CostEstimate(flops=1000, bytes_accessed=1000, transcendentals=0),
    )(*operands)


def slots_of(tagged_ref):
    return tagged_ref[:, -LANES:].astype(F32)[:, :1]


def row_slots(holders, replicas, slots, rank, dr):
    here, core = lax.axis_index("adapter"), lax.axis_index("replica")
    own_slots = slots // replicas
    lane = lax.broadcasted_iota(jnp.int32, (1, holders * own_slots * rank), 1)
    slot = jnp.zeros_like(lane)
    for k in range(holders):
        for j in range(own_slots):
            start = (k * own_slots + j) * rank
            value = lax.rem(here + holders - k, holders) * slots
            value = value + lax.rem(core + replicas - dr, replicas) * own_slots + j
            slot = jnp.where((lane >= start) & (lane < start + rank), value, slot)
    return slot.astype(F32)


def tag_kernel(g_ref, name_ref, slot_ref, out_ref):
    out_ref[:, :-LANES] = g_ref[...]
    names = name_ref[...]
    slot = jnp.zeros_like(names)
    for j in range(slot_ref.shape[0]):
        slot = jnp.where(names == j, slot_ref[j], slot)
    ones = jnp.ones((1, LANES), F32)
    out_ref[:, -LANES:] = columns_by_columns(slot.astype(F32), ones).astype(BF16)


def join_kernel(*refs):
    down_ref, up_ref = refs[-2:]
    wide = down_ref.shape[1]
    for k, ref in enumerate(refs[:-2]):
        rows = ref.shape[0]
        down_ref[k * rows : (k + 1) * rows] = ref[:, :wide]
        up_ref[k * rows : (k + 1) * rows] = ref[:, wide:]


def own_kernel(sizes, down_ref, up_ref, out_ref):
    groups, holders, shard = sizes
    half = shard // groups
    rank = down_ref.shape[1]
    slots = out_ref.shape[0] // rank
    first = lax.axis_index("replica") * slots
    for j in range(slots):
        to = pl.ds(j * rank, rank)
        for z in range(holders):
            at = pl.multiple_of(z * shard + lax.axis_index("groups") * half, half)
            out_ref[to, z * half : (z + 1) * half] = down_ref[first + j, :, pl.ds(at, half)]
        out_ref[to, holders * half :] = up_ref[first + j]


def adapter_kernel(sizes, *refs):
    groups, holders, replicas, shard, slots, rank = sizes
    x_ref, g_ref, sel_ref = refs[:3]
    map_refs, refs = refs[3 : 3 + groups * replicas], refs[3 + groups * replicas :]
    own_ref, other_refs, down = refs[0], refs[1:-1], refs[-1]
    group = lax.axis_index("groups")
    tokens, width = x_ref.shape
    rows, cols = own_ref.shape
    half = shard // groups
    for dg in range(groups):
        first = lax.rem(group + groups - dg, groups) * half
        for dr in range(replicas):
            for z in range(holders):
                at = pl.multiple_of(first + z * shard, half)
                down[pl.ds(dr * rows, rows), pl.ds(at, half)] = map_refs[dg * replicas + dr][
                    :, z * half : (z + 1) * half
                ]
    row_slot = [row_slots(holders, replicas, slots, rank, dr) for dr in range(replicas)]
    keep = slots_of(g_ref) == jnp.concatenate(row_slot, axis=1)
    in_sel = jnp.where(keep, rows_by_rows(x_ref[...], down[...]), 0.0).astype(BF16)
    grad_sel = sel_ref[pl.ds(0, tokens), :]
    step, split = 1024, cols // 2
    for at in range(0, cols, step):
        if at < width:
            part = columns_by_columns(grad_sel, x_ref[:, at : at + step])
        else:
            part = columns_by_columns(in_sel, g_ref[:, at - width : at - width + step])
        own_ref[:, at : at + step] = part[:rows]
        for dr in range(1, replicas):
            sent = part[dr * rows : (dr + 1) * rows].astype(BF16)
            for j in range(0, step, LANES):
                ref, to = other_refs[2 * dr - 2 + (at + j) // split], (at + j) % split
                ref[:, to : to + LANES] = sent[:, j : j + LANES]


def frozen_kernel(sizes, batch, *refs):
    tokens, groups, holders, replicas, slots, rank = sizes
    g_refs, refs = refs[:groups], refs[groups:]
    down_refs, refs = refs[:replicas], refs[replicas:]
    core, here = lax.axis_index("replica"), lax.axis_index("adapter")
    rows = down_refs[0].shape[0]
    half = down_refs[0].shape[1] // holders
    if batch[0][0] == 0:
        up_refs, refs = refs[:replicas], refs[replicas:]
        sel_ref = refs[-1]
        out_refs = refs[-1 - groups : -1]
        for dg in range(groups):
            for dr in range(replicas):
                keep = slots_of(g_refs[dg]) == row_slots(holders, replicas, slots, rank, dr)
                proj_grad = rows_by_rows(g_refs[dg][:, :-LANES], up_refs[dr][...])
                sel_ref[pl.ds(dg * tokens, tokens), dr * rows : (dr + 1) * rows] = jnp.where(
                    keep, proj_grad, 0.0
                ).astype(BF16)
    else:
        sel_ref, refs = refs[0], refs[1:]
        out_refs = refs[-groups:]
        if refs[-1].shape[0] > tokens:
            out_refs = [refs[-1].at[pl.ds(dg * tokens, tokens)] for dg in range(groups)]
    for i, (k, spec) in enumerate(batch):
        shard_at = lax.rem(here + holders - k, holders) * half
        for (dr, offset), block in zip(spec, refs):
            if k == 0:
                first = pl.multiple_of(lax.axis_index("groups") * half, half)
                block = block.at[pl.ds(first, half)]
            wide = block.shape[0]
            at = 0
            if wide < half:
                at = lax.rem(core + replicas - dr, replicas) * (half // replicas) + offset
            columns = pl.ds(pl.multiple_of(shard_at + at, wide), wide)
            for dg in range(groups):
                base = rows_by_rows(g_refs[dg][:, :-LANES], block[...]).astype(BF16)
                lora = 0.0
                for j in range(replicas):
                    lora = lora + jnp.dot(
                        sel_ref[pl.ds(dg * tokens, tokens), j * rows : (j + 1) * rows],
                        down_refs[j][:, columns],
                        preferred_element_type=F32,
                    )
                lora = (ADAPTER_SCALE * lora).astype(BF16)
                out_refs[dg][:, pl.ds(pl.multiple_of(i * half + at, wide), wide)] = (
                    base.astype(F32) + lora.astype(F32)
                ).astype(BF16)
        refs = refs[len(spec) :]


def split_kernel(block_ref, *part_refs):
    rows = part_refs[0].shape[0]
    for j, ref in enumerate(part_refs):
        ref[...] = block_ref[j * rows : (j + 1) * rows]


def place_kernel(sizes, batches, *refs):
    groups, holders, shard, half = sizes
    group, here = lax.axis_index("groups"), lax.axis_index("adapter")
    out_ref = refs[-1]
    for i, batch in enumerate(batches):
        for dg in range(groups):
            source = lax.rem(group + groups - dg, groups)
            for j, k in enumerate(batch):
                at = lax.rem(here + holders - k, holders) * shard + source * half
                out_ref[:, pl.ds(pl.multiple_of(at, half), half)] = refs[i * groups + dg][
                    :, j * half : (j + 1) * half
                ]


def chip_kernel(replicas, *refs):
    own_ref, came_refs, out_refs = refs[0], refs[1 : 2 * replicas - 1], refs[2 * replicas - 1 :]
    rows = out_refs[0].shape[0]
    split = came_refs[0].shape[1]
    for k, out in enumerate(out_refs):
        for j in range(2):
            at = pl.ds(k * rows, rows), pl.ds(j * split, split)
            total = own_ref[at]
            for ref in came_refs[j::2]:
                total = total + ref[pl.ds(k * rows, rows), :].astype(F32)
            out[:, pl.ds(j * split, split)] = total.astype(out.dtype)


def total_kernel(*refs):
    half_refs, refs = refs[-2:], refs[:-2]
    wide = half_refs[0].shape[1]
    for j, out_ref in enumerate(half_refs):
        at = pl.ds(j * wide, wide)
        total = refs[0][:, at]
        for ref in refs[1:]:
            total = total + ref[:, at].astype(F32)
        out_ref[...] = (ADAPTER_SCALE * total).astype(BF16)


def spread_kernel(width, replicas, *refs):
    core = lax.axis_index("replica")
    down_ref, up_ref = refs[2 * replicas :]
    slots = down_ref.shape[0] // replicas
    rank = down_ref.shape[1]
    wide = refs[0].shape[1]
    for dr in range(replicas):
        at = lax.rem(core + replicas - dr, replicas) * slots
        for j in range(slots):
            rows = slice(j * rank, (j + 1) * rank)
            down_ref[at + j, :, :wide] = refs[2 * dr][rows]
            down_ref[at + j, :, wide:] = refs[2 * dr + 1][rows, : width - wide]
            up_ref[at + j] = refs[2 * dr + 1][rows, width - wide :]


def on_device(
    saved_layer_input,
    value_output_gradient,
    token_adapter_index,
    adapter_slot_index,
    frozen_value_weight,
    adapter_down_weight,
    adapter_up_weight,
):
    inputs = saved_layer_input[0]
    grad_rows = value_output_gradient[0]
    tokens, width = inputs.shape
    value_width = grad_rows.shape[1]
    groups, holders, replicas = (lax.axis_size(a) for a in ("groups", "adapter", "replica"))
    group, here, core = (lax.axis_index(a) for a in ("groups", "adapter", "replica"))
    slots, rank = adapter_down_weight.shape[1:3]
    own_slots = slots // replicas
    rows = own_slots * rank
    frozen = frozen_value_weight[0]
    shard = frozen.shape[0]
    half = shard // groups
    piece = half // replicas
    cols = width + value_width

    tagged = call(
        tag_kernel,
        [jax.ShapeDtypeStruct((tokens, value_width + LANES), BF16)],
        (grad_rows, token_adapter_index[0, :, 0][None], adapter_slot_index),
        scalars=1,
    )[0]
    grads = [tagged] + [
        moved(tagged, lambda g, z, s, r: (g - dg, z, s, r)) for dg in range(1, groups)
    ]

    own = call(
        functools.partial(own_kernel, (groups, holders, shard)),
        [jax.ShapeDtypeStruct((rows, holders * half + value_width), BF16)],
        (adapter_down_weight[0], adapter_up_weight[0]),
    )[0]
    held = [own]
    for k in range(1, holders):
        held.append(moved(own, lambda g, z, s, r: (g, z + k, s, r)))

    ring = [lax.dynamic_slice_in_dim(frozen, (group * replicas + core) * piece, piece, axis=0)]
    ring.append(moved(ring[0], lambda g, z, s, r: (g, z + 1, s, r)))
    held, grads, ring = lax.optimization_barrier((held, grads, ring))
    joined = call(
        join_kernel,
        [
            jax.ShapeDtypeStruct((holders * rows, holders * half), BF16),
            jax.ShapeDtypeStruct((holders * rows, value_width), BF16),
        ],
        held,
    )
    downs, ups = [joined[0]], [joined[1]]
    for dr in range(1, replicas):
        ups.append(moved(ups[0], lambda g, z, s, r: (g, z, s, r + dr)))
        downs.append(moved(downs[0], lambda g, z, s, r: (g, z, s, r + dr)))
    def pieces_of(k, *before):
        if k == 0:
            return [(0, 0)], [frozen]
        mails = [ring[k]]
        if k > 1 and piece % (2 * LANES) == 0:
            shape = jax.ShapeDtypeStruct((piece // 2, value_width), BF16)
            mails = call(split_kernel, [shape] * 2, (ring[k],))
        mails = [after(mail, *before) if before else mail for mail in mails]
        spec, pieces = [(0, 0)], [ring[k]]
        for dr in range(1, replicas):
            for j, mail in enumerate(mails):
                spec.append((dr, j * mail.shape[0]))
                pieces.append(moved(mail, lambda g, z, s, r: (g, z, s, r + dr)))
        if piece % LANES:
            whole = jnp.zeros((half, value_width), BF16)
            for (dr, offset), part in zip(spec, pieces):
                at = ((core - dr) % replicas) * piece + offset
                whole = lax.dynamic_update_slice_in_dim(whole, part, at, axis=0)
            spec, pieces = [(0, 0)], [whole]
        return spec, pieces

    kept = replicas * holders * rows

    def adapter_sums(sel, *before):
        maps = list(downs)
        for dg in range(1, groups):
            maps.append(moved(downs[0], lambda g, z, s, r: (g + dg, z, s, r)))
            for dr in range(1, replicas):
                maps.append(moved(maps[-dr], lambda g, z, s, r: (g, z, s, r + dr)))
        gradients = call(
            functools.partial(adapter_kernel, (groups, holders, replicas, shard, slots, rank)),
            [jax.ShapeDtypeStruct((holders * rows, cols), F32)]
            + [jax.ShapeDtypeStruct((holders * rows, cols // 2), BF16)] * (2 * replicas - 2),
            (inputs, tagged, sel, *maps),
            [jax.ShapeDtypeStruct((kept, width), BF16)],
        )
        part, sent = gradients[0], gradients[1:]
        came = [
            moved(after(sent[2 * dr - 2 + j], *before), lambda g, z, s, r: (g, z, s, r - dr))
            for dr in range(1, replicas)
            for j in range(2)
        ]
        chip = call(
            functools.partial(chip_kernel, replicas),
            [jax.ShapeDtypeStruct((rows, cols), F32)]
            + [jax.ShapeDtypeStruct((rows, cols), BF16)] * (holders - 1),
            (part, *came),
        )
        return part, chip

    batches = [list(range(min(2, holders)))] + [[k] for k in range(2, holders)]
    arrived, crossed = [], []
    for i, batch in enumerate(batches):
        operands, specs = [], []
        for k in batch:
            if k > 1:
                last = after(ring[-1], sel) if k > 2 else ring[-1]
                ring.append(moved(last, lambda g, z, s, r: (g, z + 1, s, r)))
            gate = arrived[0] if k == 2 else [*arrived[i - 2], chip[0]] if k > 2 else []
            spec, blocks = pieces_of(k, *gate)
            specs.append((k, spec))
            operands += blocks
        out = call(
            functools.partial(
                frozen_kernel, (tokens, groups, holders, replicas, slots, rank), specs
            ),
            (
                [jax.ShapeDtypeStruct((groups * tokens, half), BF16)]
                if i == 1 and len(batches) > 2
                else [jax.ShapeDtypeStruct((tokens, half * len(batch)), BF16)] * groups
            )
            + [jax.ShapeDtypeStruct((groups * tokens, kept), BF16)] * (i == 0),
            [*grads, *downs, *([sel] if i else ups), *operands],
        )
        if i == 0:
            sel = out[groups]
        mails = list(out[:groups])
        if i == 1 and len(batches) > 2:
            got = moved(out[0], lambda g, z, s, r: (g, z, s - 1, r))
            got = [got[dg * tokens : (dg + 1) * tokens] for dg in range(groups)]
            crossed.append(got[:1])
            for dg in range(1, groups):
                crossed[0].append(moved(got[dg], lambda g, z, s, r: (g + dg, z, s, r)))
            arrived.append(crossed[0])
            continue
        if i > 2:
            mails = [after(mail, *arrived[-1]) for mail in mails]
        arrived.append(
            [moved(mails[dg], lambda g, z, s, r: (g + dg, z, s - 1, r)) for dg in range(groups)]
        )
        if i == 0:
            part, chip = adapter_sums(sel, *arrived[0])
    passed = call(
        functools.partial(place_kernel, (groups, holders, shard, half), batches),
        [jax.ShapeDtypeStruct((tokens, width), BF16)],
        [x for got in arrived for x in got],
    )[0]

    sums = [chip[0]] + [
        moved(after(chip[k], ring[-1]), lambda g, z, s, r: (g, z - k, s, r))
        for k in range(1, holders)
    ]
    total = call(total_kernel, [jax.ShapeDtypeStruct((rows, cols // 2), BF16)] * 2, sums)
    totals = list(total)
    for dr in range(1, replicas):
        totals += [moved(x, lambda g, z, s, r: (g, z, s, r + dr)) for x in total]
    down_grad, up_grad = call(
        functools.partial(spread_kernel, width, replicas),
        [
            jax.ShapeDtypeStruct((slots, rank, width), BF16),
            jax.ShapeDtypeStruct((slots, rank, value_width), BF16),
        ],
        totals,
    )

    return passed[None], down_grad[None], up_grad[None]


def solution(mesh):
    placed = (
        P("segment", ("groups", "adapter", "replica"), None),
        P("segment", ("groups", "adapter", "replica"), None),
        P("segment", ("groups", "adapter", "replica"), None),
        P("groups"),
        P("segment", "adapter", None),
        P("segment", "adapter", None, None),
        P("segment", "adapter", None, None),
    )
    return jax.shard_map(
        on_device,
        mesh=mesh,
        in_specs=placed,
        out_specs=(
            P("segment", ("groups", "adapter", "replica"), None),
            P(("groups", "segment"), "adapter", None, None),
            P(("groups", "segment"), "adapter", None, None),
        ),
        check_vma=False,
    )
```

```python
import functools
import itertools
import jax
import jax.numpy as jnp
from jax import lax
from jax.experimental import pallas as pl
from jax.experimental.pallas import tpu as pltpu
from jax.sharding import PartitionSpec as P

ADAPTER_SCALE = 2.0
AXES = ("groups", "adapter", "segment", "replica")
LANES = 128
F32 = jnp.float32
BF16 = jnp.bfloat16
MIB = 1024 * 1024


def moved(x, to):
    sizes = [lax.axis_size(a) for a in AXES]
    number = {at: i for i, at in enumerate(itertools.product(*map(range, sizes)))}
    pairs = [
        (i, number[tuple(t % s for t, s in zip(to(*at), sizes))]) for at, i in number.items()
    ]
    return lax.ppermute(x, AXES, pairs)


def after(x, *others):
    return lax.optimization_barrier((x, *others))[0]


def rows_by_rows(a, b):
    return lax.dot_general(a, b, (((1,), (1,)), ((), ())), preferred_element_type=F32)


def columns_by_columns(a, b):
    return lax.dot_general(a, b, (((0,), (0,)), ((), ())), preferred_element_type=F32)


def call(kernel, out_shape, operands, scratch=(), scalars=0):
    held = sum(x.size * x.dtype.itemsize for x in (*operands, *out_shape, *scratch))
    return pl.pallas_call(
        kernel,
        out_shape=out_shape,
        in_specs=[pl.BlockSpec(memory_space=pltpu.VMEM)] * (len(operands) - scalars)
        + [pl.BlockSpec(memory_space=pltpu.SMEM)] * scalars,
        scratch_shapes=[pltpu.VMEM(x.shape, x.dtype) for x in scratch],
        compiler_params=pltpu.CompilerParams(vmem_limit_bytes=2 * held + 4 * MIB),
        cost_estimate=pl.CostEstimate(flops=1000, bytes_accessed=1000, transcendentals=0),
    )(*operands)


def slots_of(tagged_ref):
    return tagged_ref[:, -LANES:].astype(F32)[:, :1]


def row_slots(holders, replicas, slots, rank, dr):
    here, core = lax.axis_index("adapter"), lax.axis_index("replica")
    own_slots = slots // replicas
    lane = lax.broadcasted_iota(jnp.int32, (1, holders * own_slots * rank), 1)
    slot = jnp.zeros_like(lane)
    for k in range(holders):
        for j in range(own_slots):
            start = (k * own_slots + j) * rank
            value = lax.rem(here + holders - k, holders) * slots
            value = value + lax.rem(core + replicas - dr, replicas) * own_slots + j
            slot = jnp.where((lane >= start) & (lane < start + rank), value, slot)
    return slot.astype(F32)


def tag_kernel(g_ref, name_ref, slot_ref, out_ref):
    out_ref[:, :-LANES] = g_ref[...]
    names = name_ref[...]
    slot = jnp.zeros_like(names)
    for j in range(slot_ref.shape[0]):
        slot = jnp.where(names == j, slot_ref[j], slot)
    ones = jnp.ones((1, LANES), F32)
    out_ref[:, -LANES:] = columns_by_columns(slot.astype(F32), ones).astype(BF16)


def join_kernel(*refs):
    down_ref, up_ref = refs[-2:]
    wide = down_ref.shape[1]
    for k, ref in enumerate(refs[:-2]):
        rows = ref.shape[0]
        down_ref[k * rows : (k + 1) * rows] = ref[:, :wide]
        up_ref[k * rows : (k + 1) * rows] = ref[:, wide:]


def piece_kernel(replicas, frozen_ref, out_ref, sem):
    rows = out_ref.shape[0]
    at = (lax.axis_index("groups") * replicas + lax.axis_index("replica")) * rows
    copy = pltpu.make_async_copy(
        frozen_ref.at[pl.ds(pl.multiple_of(at, rows), rows)], out_ref, sem
    )
    copy.start()
    copy.wait()


def own_kernel(sizes, down_ref, up_ref, out_ref):
    groups, holders, shard = sizes
    half = shard // groups
    rank = down_ref.shape[1]
    slots = out_ref.shape[0] // rank
    first = lax.axis_index("replica") * slots
    for j in range(slots):
        to = pl.ds(j * rank, rank)
        for z in range(holders):
            at = pl.multiple_of(z * shard + lax.axis_index("groups") * half, half)
            out_ref[to, z * half : (z + 1) * half] = down_ref[first + j, :, pl.ds(at, half)]
        out_ref[to, holders * half :] = up_ref[first + j]


def adapter_kernel(sizes, *refs):
    groups, holders, replicas, shard, slots, rank = sizes
    x_ref, g_ref, sel_ref = refs[:3]
    map_refs, refs = refs[3 : 3 + groups * replicas], refs[3 + groups * replicas :]
    own_ref, other_refs, down = refs[0], refs[1:-1], refs[-1]
    group = lax.axis_index("groups")
    tokens, width = x_ref.shape
    rows, cols = own_ref.shape
    half = shard // groups
    for dg in range(groups):
        first = lax.rem(group + groups - dg, groups) * half
        for dr in range(replicas):
            for z in range(holders):
                at = pl.multiple_of(first + z * shard, half)
                down[pl.ds(dr * rows, rows), pl.ds(at, half)] = map_refs[dg * replicas + dr][
                    :, z * half : (z + 1) * half
                ]
    row_slot = [row_slots(holders, replicas, slots, rank, dr) for dr in range(replicas)]
    keep = slots_of(g_ref) == jnp.concatenate(row_slot, axis=1)
    in_sel = jnp.where(keep, rows_by_rows(x_ref[...], down[...]), 0.0).astype(BF16)
    grad_sel = sel_ref[pl.ds(0, tokens), :]
    step, split = 1024, cols // 2
    for at in range(0, cols, step):
        if at < width:
            part = columns_by_columns(grad_sel, x_ref[:, at : at + step])
        else:
            part = columns_by_columns(in_sel, g_ref[:, at - width : at - width + step])
        own_ref[:, at : at + step] = part[:rows]
        for dr in range(1, replicas):
            sent = part[dr * rows : (dr + 1) * rows].astype(BF16)
            for j in range(0, step, LANES):
                ref, to = other_refs[2 * dr - 2 + (at + j) // split], (at + j) % split
                ref[:, to : to + LANES] = sent[:, j : j + LANES]


def frozen_kernel(sizes, batch, *refs):
    tokens, groups, holders, replicas, slots, rank = sizes
    g_refs, refs = refs[:groups], refs[groups:]
    down_refs, refs = refs[:replicas], refs[replicas:]
    core, here = lax.axis_index("replica"), lax.axis_index("adapter")
    rows = down_refs[0].shape[0]
    half = down_refs[0].shape[1] // holders
    if batch[0][0] == 0:
        up_refs, refs = refs[:replicas], refs[replicas:]
        sel_ref = refs[-1]
        out_refs = refs[-1 - groups : -1]
        for dg in range(groups):
            for dr in range(replicas):
                keep = slots_of(g_refs[dg]) == row_slots(holders, replicas, slots, rank, dr)
                proj_grad = rows_by_rows(g_refs[dg][:, :-LANES], up_refs[dr][...])
                sel_ref[pl.ds(dg * tokens, tokens), dr * rows : (dr + 1) * rows] = jnp.where(
                    keep, proj_grad, 0.0
                ).astype(BF16)
    else:
        sel_ref, refs = refs[0], refs[1:]
        out_refs = refs[-groups:]
        if refs[-1].shape[0] > tokens:
            out_refs = [refs[-1].at[pl.ds(dg * tokens, tokens)] for dg in range(groups)]
    for i, (k, spec) in enumerate(batch):
        shard_at = lax.rem(here + holders - k, holders) * half
        for (dr, offset), block in zip(spec, refs):
            if k == 0:
                first = pl.multiple_of(lax.axis_index("groups") * half, half)
                block = block.at[pl.ds(first, half)]
            wide = block.shape[0]
            at = 0
            if wide < half:
                at = lax.rem(core + replicas - dr, replicas) * (half // replicas) + offset
            columns = pl.ds(pl.multiple_of(shard_at + at, wide), wide)
            for dg in range(groups):
                base = rows_by_rows(g_refs[dg][:, :-LANES], block[...]).astype(BF16)
                lora = 0.0
                for j in range(replicas):
                    lora = lora + jnp.dot(
                        sel_ref[pl.ds(dg * tokens, tokens), j * rows : (j + 1) * rows],
                        down_refs[j][:, columns],
                        preferred_element_type=F32,
                    )
                lora = (ADAPTER_SCALE * lora).astype(BF16)
                out_refs[dg][:, pl.ds(pl.multiple_of(i * half + at, wide), wide)] = (
                    base.astype(F32) + lora.astype(F32)
                ).astype(BF16)
        refs = refs[len(spec) :]


def split_kernel(block_ref, *part_refs):
    rows = part_refs[0].shape[0]
    for j, ref in enumerate(part_refs):
        ref[...] = block_ref[j * rows : (j + 1) * rows]


def place_kernel(sizes, places, *refs):
    groups, holders, shard, half = sizes
    group, here = lax.axis_index("groups"), lax.axis_index("adapter")
    out_ref = refs[-1]
    for ref, (batch, dg) in zip(refs, places):
        source = lax.rem(group + groups - dg, groups)
        for j, k in enumerate(batch):
            at = lax.rem(here + holders - k, holders) * shard + source * half
            out_ref[:, pl.ds(pl.multiple_of(at, half), half)] = ref[:, j * half : (j + 1) * half]


def chip_kernel(replicas, *refs):
    own_ref, came_refs, out_refs = refs[0], refs[1 : 2 * replicas - 1], refs[2 * replicas - 1 :]
    rows = out_refs[0].shape[0]
    split = came_refs[0].shape[1]
    for k, out in enumerate(out_refs):
        for j in range(2):
            at = pl.ds(k * rows, rows), pl.ds(j * split, split)
            total = own_ref[at]
            for ref in came_refs[j::2]:
                total = total + ref[pl.ds(k * rows, rows), :].astype(F32)
            out[:, pl.ds(j * split, split)] = total.astype(out.dtype)


def total_kernel(*refs):
    half_refs, refs = refs[-2:], refs[:-2]
    wide = half_refs[0].shape[1]
    for j, out_ref in enumerate(half_refs):
        at = pl.ds(j * wide, wide)
        total = refs[0][:, at]
        for ref in refs[1:]:
            total = total + ref[:, at].astype(F32)
        out_ref[...] = (ADAPTER_SCALE * total).astype(BF16)


def spread_kernel(width, replicas, *refs):
    core = lax.axis_index("replica")
    down_ref, up_ref = refs[2 * replicas :]
    slots = down_ref.shape[0] // replicas
    rank = down_ref.shape[1]
    wide = refs[0].shape[1]
    for dr in range(replicas):
        at = lax.rem(core + replicas - dr, replicas) * slots
        for j in range(slots):
            rows = slice(j * rank, (j + 1) * rank)
            down_ref[at + j, :, :wide] = refs[2 * dr][rows]
            down_ref[at + j, :, wide:] = refs[2 * dr + 1][rows, : width - wide]
            up_ref[at + j] = refs[2 * dr + 1][rows, width - wide :]


def on_device(
    saved_layer_input,
    value_output_gradient,
    token_adapter_index,
    adapter_slot_index,
    frozen_value_weight,
    adapter_down_weight,
    adapter_up_weight,
):
    inputs = saved_layer_input[0]
    grad_rows = value_output_gradient[0]
    tokens, width = inputs.shape
    value_width = grad_rows.shape[1]
    groups, holders, replicas = (lax.axis_size(a) for a in ("groups", "adapter", "replica"))
    group, here, core = (lax.axis_index(a) for a in ("groups", "adapter", "replica"))
    slots, rank = adapter_down_weight.shape[1:3]
    own_slots = slots // replicas
    rows = own_slots * rank
    frozen = frozen_value_weight[0]
    shard = frozen.shape[0]
    half = shard // groups
    piece = half // replicas
    cols = width + value_width

    tagged = call(
        tag_kernel,
        [jax.ShapeDtypeStruct((tokens, value_width + LANES), BF16)],
        (grad_rows, token_adapter_index[0, :, 0][None], adapter_slot_index),
        scalars=1,
    )[0]
    grads = [tagged] + [
        moved(tagged, lambda g, z, s, r: (g - dg, z, s, r)) for dg in range(1, groups)
    ]

    own = call(
        functools.partial(own_kernel, (groups, holders, shard)),
        [jax.ShapeDtypeStruct((rows, holders * half + value_width), BF16)],
        (adapter_down_weight[0], adapter_up_weight[0]),
    )[0]
    held = [own]
    for k in range(1, holders):
        held.append(moved(own, lambda g, z, s, r: (g, z + k, s, r)))

    ring = [
        pl.pallas_call(
            functools.partial(piece_kernel, replicas),
            out_shape=jax.ShapeDtypeStruct((piece, value_width), BF16),
            in_specs=[pl.BlockSpec(memory_space=pltpu.HBM)],
            out_specs=pl.BlockSpec(memory_space=pltpu.VMEM),
            scratch_shapes=[pltpu.SemaphoreType.DMA],
            compiler_params=pltpu.CompilerParams(vmem_limit_bytes=4 * MIB),
            cost_estimate=pl.CostEstimate(flops=1000, bytes_accessed=1000, transcendentals=0),
        )(frozen)
    ]
    ring.append(moved(ring[0], lambda g, z, s, r: (g, z + 1, s, r)))
    held, grads, ring = lax.optimization_barrier((held, grads, ring))
    joined = call(
        join_kernel,
        [
            jax.ShapeDtypeStruct((holders * rows, holders * half), BF16),
            jax.ShapeDtypeStruct((holders * rows, value_width), BF16),
        ],
        held,
    )
    downs, ups = [joined[0]], [joined[1]]
    for dr in range(1, replicas):
        ups.append(moved(ups[0], lambda g, z, s, r: (g, z, s, r + dr)))
        downs.append(moved(downs[0], lambda g, z, s, r: (g, z, s, r + dr)))
    def pieces_of(k, *before):
        if k == 0:
            return [(0, 0)], [frozen]
        mails = [ring[k]]
        if k > 1 and piece % (2 * LANES) == 0:
            shape = jax.ShapeDtypeStruct((piece // 2, value_width), BF16)
            mails = call(split_kernel, [shape] * 2, (ring[k],))
        mails = [after(mail, *before) if before else mail for mail in mails]
        spec, pieces = [(0, 0)], [ring[k]]
        for dr in range(1, replicas):
            for j, mail in enumerate(mails):
                spec.append((dr, j * mail.shape[0]))
                pieces.append(moved(mail, lambda g, z, s, r: (g, z, s, r + dr)))
        if piece % LANES:
            whole = jnp.zeros((half, value_width), BF16)
            for (dr, offset), part in zip(spec, pieces):
                at = ((core - dr) % replicas) * piece + offset
                whole = lax.dynamic_update_slice_in_dim(whole, part, at, axis=0)
            spec, pieces = [(0, 0)], [whole]
        return spec, pieces

    kept = replicas * holders * rows

    def adapter_sums(sel, *before):
        maps = list(downs)
        for dg in range(1, groups):
            maps.append(moved(downs[0], lambda g, z, s, r: (g + dg, z, s, r)))
            for dr in range(1, replicas):
                maps.append(moved(maps[-dr], lambda g, z, s, r: (g, z, s, r + dr)))
        gradients = call(
            functools.partial(adapter_kernel, (groups, holders, replicas, shard, slots, rank)),
            [jax.ShapeDtypeStruct((holders * rows, cols), F32)]
            + [jax.ShapeDtypeStruct((holders * rows, cols // 2), BF16)] * (2 * replicas - 2),
            (inputs, tagged, sel, *maps),
            [jax.ShapeDtypeStruct((kept, width), BF16)],
        )
        part, sent = gradients[0], gradients[1:]
        came = [
            moved(after(sent[2 * dr - 2 + j], *before), lambda g, z, s, r: (g, z, s, r - dr))
            for dr in range(1, replicas)
            for j in range(2)
        ]
        chip = call(
            functools.partial(chip_kernel, replicas),
            [jax.ShapeDtypeStruct((rows, cols), F32)]
            + [jax.ShapeDtypeStruct((rows, cols), BF16)] * (holders - 1),
            (part, *came),
        )
        return part, chip

    batches = [list(range(min(2, holders)))] + [[k] for k in range(2, holders)]
    arrived, crossed = [], []
    for i, batch in enumerate(batches):
        operands, specs = [], []
        for k in batch:
            if k > 1:
                last = after(ring[-1], sel) if k > 2 else ring[-1]
                ring.append(moved(last, lambda g, z, s, r: (g, z + 1, s, r)))
            gate = arrived[0] if k == 2 else [*arrived[i - 2], chip[0]] if k > 2 else []
            spec, blocks = pieces_of(k, *gate)
            specs.append((k, spec))
            operands += blocks
        out = call(
            functools.partial(
                frozen_kernel, (tokens, groups, holders, replicas, slots, rank), specs
            ),
            (
                [jax.ShapeDtypeStruct((groups * tokens, half), BF16)]
                if i == 1 and len(batches) > 2
                else [jax.ShapeDtypeStruct((tokens, half * len(batch)), BF16)] * groups
            )
            + [jax.ShapeDtypeStruct((groups * tokens, kept), BF16)] * (i == 0),
            [*grads, *downs, *([sel] if i else ups), *operands],
        )
        if i == 0:
            sel = out[groups]
        mails = list(out[:groups])
        if i == 1 and len(batches) > 2:
            got = moved(out[0], lambda g, z, s, r: (g, z, s - 1, r))
            got = [got[dg * tokens : (dg + 1) * tokens] for dg in range(groups)]
            crossed.append(got[:1])
            for dg in range(1, groups):
                crossed[0].append(moved(got[dg], lambda g, z, s, r: (g + dg, z, s, r)))
            arrived.append(crossed[0])
            continue
        if i > 2:
            mails = [after(mail, *arrived[-1]) for mail in mails]
        arrived.append(
            [moved(mails[dg], lambda g, z, s, r: (g + dg, z, s - 1, r)) for dg in range(groups)]
        )
        if i == 0:
            part, chip = adapter_sums(sel, *arrived[0])
    places = [(batch, dg) for batch in batches for dg in range(groups)]
    parts = dict(zip([(b[0], dg) for b, dg in places], [x for got in arrived for x in got]))
    places[-groups:] = places[-groups:][::-1]
    passed = call(
        functools.partial(place_kernel, (groups, holders, shard, half), places),
        [jax.ShapeDtypeStruct((tokens, width), BF16)],
        [parts[batch[0], dg] for batch, dg in places],
    )[0]

    sums = [chip[0]] + [
        moved(after(chip[k], ring[-1]), lambda g, z, s, r: (g, z - k, s, r))
        for k in range(1, holders)
    ]
    total = call(total_kernel, [jax.ShapeDtypeStruct((rows, cols // 2), BF16)] * 2, sums)
    totals = list(total)
    for dr in range(1, replicas):
        totals += [moved(x, lambda g, z, s, r: (g, z, s, r + dr)) for x in total]
    down_grad, up_grad = call(
        functools.partial(spread_kernel, width, replicas),
        [
            jax.ShapeDtypeStruct((slots, rank, width), BF16),
            jax.ShapeDtypeStruct((slots, rank, value_width), BF16),
        ],
        totals,
    )

    return passed[None], down_grad[None], up_grad[None]


def solution(mesh):
    placed = (
        P("segment", ("groups", "adapter", "replica"), None),
        P("segment", ("groups", "adapter", "replica"), None),
        P("segment", ("groups", "adapter", "replica"), None),
        P("groups"),
        P("segment", "adapter", None),
        P("segment", "adapter", None, None),
        P("segment", "adapter", None, None),
    )
    return jax.shard_map(
        on_device,
        mesh=mesh,
        in_specs=placed,
        out_specs=(
            P("segment", ("groups", "adapter", "replica"), None),
            P(("groups", "segment"), "adapter", None, None),
            P(("groups", "segment"), "adapter", None, None),
        ),
        check_vma=False,
    )
```

```python
import functools
import itertools
import jax
import jax.numpy as jnp
from jax import lax
from jax.experimental import pallas as pl
from jax.experimental.pallas import tpu as pltpu
from jax.sharding import PartitionSpec as P

ADAPTER_SCALE = 2.0
AXES = ("groups", "adapter", "segment", "replica")
LANES = 128
F32 = jnp.float32
BF16 = jnp.bfloat16
MIB = 1024 * 1024


def moved(x, to):
    sizes = [lax.axis_size(a) for a in AXES]
    number = {at: i for i, at in enumerate(itertools.product(*map(range, sizes)))}
    pairs = [
        (i, number[tuple(t % s for t, s in zip(to(*at), sizes))]) for at, i in number.items()
    ]
    return lax.ppermute(x, AXES, pairs)


def after(x, *others):
    return lax.optimization_barrier((x, *others))[0]


def rows_by_rows(a, b):
    return lax.dot_general(a, b, (((1,), (1,)), ((), ())), preferred_element_type=F32)


def columns_by_columns(a, b):
    return lax.dot_general(a, b, (((0,), (0,)), ((), ())), preferred_element_type=F32)


def call(kernel, out_shape, operands, scratch=(), scalars=0):
    held = sum(x.size * x.dtype.itemsize for x in (*operands, *out_shape, *scratch))
    return pl.pallas_call(
        kernel,
        out_shape=out_shape,
        in_specs=[pl.BlockSpec(memory_space=pltpu.VMEM)] * (len(operands) - scalars)
        + [pl.BlockSpec(memory_space=pltpu.SMEM)] * scalars,
        scratch_shapes=[pltpu.VMEM(x.shape, x.dtype) for x in scratch],
        compiler_params=pltpu.CompilerParams(vmem_limit_bytes=2 * held + 4 * MIB),
        cost_estimate=pl.CostEstimate(flops=1000, bytes_accessed=1000, transcendentals=0),
    )(*operands)


def slots_of(tagged_ref):
    return tagged_ref[:, -LANES:].astype(F32)[:, :1]


def row_slots(holders, replicas, slots, rank, dr):
    here, core = lax.axis_index("adapter"), lax.axis_index("replica")
    own_slots = slots // replicas
    lane = lax.broadcasted_iota(jnp.int32, (1, holders * own_slots * rank), 1)
    slot = jnp.zeros_like(lane)
    for k in range(holders):
        for j in range(own_slots):
            start = (k * own_slots + j) * rank
            value = lax.rem(here + holders - k, holders) * slots
            value = value + lax.rem(core + replicas - dr, replicas) * own_slots + j
            slot = jnp.where((lane >= start) & (lane < start + rank), value, slot)
    return slot.astype(F32)


def tag_kernel(g_ref, name_ref, slot_ref, out_ref):
    out_ref[:, :-LANES] = g_ref[...]
    names = name_ref[...]
    slot = jnp.zeros_like(names)
    for j in range(slot_ref.shape[0]):
        slot = jnp.where(names == j, slot_ref[j], slot)
    ones = jnp.ones((1, LANES), F32)
    out_ref[:, -LANES:] = columns_by_columns(slot.astype(F32), ones).astype(BF16)


def join_kernel(*refs):
    down_ref, up_ref = refs[-2:]
    wide = down_ref.shape[1]
    for k, ref in enumerate(refs[:-2]):
        rows = ref.shape[0]
        down_ref[k * rows : (k + 1) * rows] = ref[:, :wide]
        up_ref[k * rows : (k + 1) * rows] = ref[:, wide:]


def own_kernel(sizes, down_ref, up_ref, out_ref):
    groups, holders, shard = sizes
    half = shard // groups
    rank = down_ref.shape[1]
    slots = out_ref.shape[0] // rank
    first = lax.axis_index("replica") * slots
    for j in range(slots):
        to = pl.ds(j * rank, rank)
        for z in range(holders):
            at = pl.multiple_of(z * shard + lax.axis_index("groups") * half, half)
            out_ref[to, z * half : (z + 1) * half] = down_ref[first + j, :, pl.ds(at, half)]
        out_ref[to, holders * half :] = up_ref[first + j]


def adapter_kernel(sizes, *refs):
    groups, holders, replicas, shard, slots, rank = sizes
    x_ref, g_ref, sel_ref = refs[:3]
    map_refs, refs = refs[3 : 3 + groups * replicas], refs[3 + groups * replicas :]
    own_ref, other_refs, down = refs[0], refs[1:-1], refs[-1]
    group = lax.axis_index("groups")
    tokens, width = x_ref.shape
    rows, cols = own_ref.shape
    half = shard // groups
    for dg in range(groups):
        first = lax.rem(group + groups - dg, groups) * half
        for dr in range(replicas):
            for z in range(holders):
                at = pl.multiple_of(first + z * shard, half)
                down[pl.ds(dr * rows, rows), pl.ds(at, half)] = map_refs[dg * replicas + dr][
                    :, z * half : (z + 1) * half
                ]
    row_slot = [row_slots(holders, replicas, slots, rank, dr) for dr in range(replicas)]
    keep = slots_of(g_ref) == jnp.concatenate(row_slot, axis=1)
    in_sel = jnp.where(keep, rows_by_rows(x_ref[...], down[...]), 0.0).astype(BF16)
    grad_sel = sel_ref[pl.ds(0, tokens), :]
    step, split = 1024, cols // 2
    for at in range(0, cols, step):
        if at < width:
            part = columns_by_columns(grad_sel, x_ref[:, at : at + step])
        else:
            part = columns_by_columns(in_sel, g_ref[:, at - width : at - width + step])
        own_ref[:, at : at + step] = part[:rows]
        for dr in range(1, replicas):
            sent = part[dr * rows : (dr + 1) * rows].astype(BF16)
            for j in range(0, step, LANES):
                ref, to = other_refs[2 * dr - 2 + (at + j) // split], (at + j) % split
                ref[:, to : to + LANES] = sent[:, j : j + LANES]


def frozen_kernel(sizes, batch, *refs):
    tokens, groups, holders, replicas, slots, rank = sizes
    g_refs, refs = refs[:groups], refs[groups:]
    down_refs, refs = refs[:replicas], refs[replicas:]
    core, here = lax.axis_index("replica"), lax.axis_index("adapter")
    rows = down_refs[0].shape[0]
    half = down_refs[0].shape[1] // holders
    if batch[0][0] == 0:
        up_refs, refs = refs[:replicas], refs[replicas:]
        sel_ref = refs[-1]
        out_refs = refs[-1 - groups : -1]
        for dg in range(groups):
            for dr in range(replicas):
                keep = slots_of(g_refs[dg]) == row_slots(holders, replicas, slots, rank, dr)
                proj_grad = rows_by_rows(g_refs[dg][:, :-LANES], up_refs[dr][...])
                sel_ref[pl.ds(dg * tokens, tokens), dr * rows : (dr + 1) * rows] = jnp.where(
                    keep, proj_grad, 0.0
                ).astype(BF16)
    else:
        sel_ref, refs = refs[0], refs[1:]
        out_refs = refs[-groups:]
        if refs[-1].shape[0] > tokens:
            out_refs = [refs[-1].at[pl.ds(dg * tokens, tokens)] for dg in range(groups)]
    for i, (k, spec) in enumerate(batch):
        shard_at = lax.rem(here + holders - k, holders) * half
        for (dr, offset), block in zip(spec, refs):
            if k == 0:
                first = pl.multiple_of(lax.axis_index("groups") * half, half)
                block = block.at[pl.ds(first, half)]
            wide = block.shape[0]
            at = 0
            if wide < half:
                at = lax.rem(core + replicas - dr, replicas) * (half // replicas) + offset
            columns = pl.ds(pl.multiple_of(shard_at + at, wide), wide)
            for dg in range(groups):
                base = rows_by_rows(g_refs[dg][:, :-LANES], block[...]).astype(BF16)
                lora = 0.0
                for j in range(replicas):
                    lora = lora + jnp.dot(
                        sel_ref[pl.ds(dg * tokens, tokens), j * rows : (j + 1) * rows],
                        down_refs[j][:, columns],
                        preferred_element_type=F32,
                    )
                lora = (ADAPTER_SCALE * lora).astype(BF16)
                out_refs[dg][:, pl.ds(pl.multiple_of(i * half + at, wide), wide)] = (
                    base.astype(F32) + lora.astype(F32)
                ).astype(BF16)
        refs = refs[len(spec) :]


def split_kernel(block_ref, *part_refs):
    rows = part_refs[0].shape[0]
    for j, ref in enumerate(part_refs):
        ref[...] = block_ref[j * rows : (j + 1) * rows]


def column_of(sizes, k, dg):
    groups, holders, shard, half = sizes
    group, here = lax.axis_index("groups"), lax.axis_index("adapter")
    source = lax.rem(group + groups - dg, groups)
    at = lax.rem(here + holders - k, holders) * shard + source * half
    return pl.ds(pl.multiple_of(at, half), half)


def place_kernel(sizes, places, *refs):
    half = sizes[-1]
    for ref, (batch, dg) in zip(refs, places):
        for j, k in enumerate(batch):
            refs[-1][:, column_of(sizes, k, dg)] = ref[:, j * half : (j + 1) * half]


def late_kernel(sizes, places, *refs):
    out_ref, sems = refs[-2:]
    copies = [
        pltpu.make_async_copy(ref, out_ref.at[:, column_of(sizes, batch[0], dg)], sems.at[i])
        for i, (ref, (batch, dg)) in enumerate(zip(refs, places))
    ]
    for copy in copies:
        copy.start()
    for copy in copies:
        copy.wait()


def chip_kernel(replicas, *refs):
    own_ref, came_refs, out_refs = refs[0], refs[1 : 2 * replicas - 1], refs[2 * replicas - 1 :]
    rows = out_refs[0].shape[0]
    split = came_refs[0].shape[1]
    for k, out in enumerate(out_refs):
        for j in range(2):
            at = pl.ds(k * rows, rows), pl.ds(j * split, split)
            total = own_ref[at]
            for ref in came_refs[j::2]:
                total = total + ref[pl.ds(k * rows, rows), :].astype(F32)
            out[:, pl.ds(j * split, split)] = total.astype(out.dtype)


def total_kernel(*refs):
    half_refs, refs = refs[-2:], refs[:-2]
    wide = half_refs[0].shape[1]
    for j, out_ref in enumerate(half_refs):
        at = pl.ds(j * wide, wide)
        total = refs[0][:, at]
        for ref in refs[1:]:
            total = total + ref[:, at].astype(F32)
        out_ref[...] = (ADAPTER_SCALE * total).astype(BF16)


def spread_kernel(width, replicas, *refs):
    core = lax.axis_index("replica")
    down_ref, up_ref = refs[2 * replicas :]
    slots = down_ref.shape[0] // replicas
    rank = down_ref.shape[1]
    wide = refs[0].shape[1]
    for dr in range(replicas):
        at = lax.rem(core + replicas - dr, replicas) * slots
        for j in range(slots):
            rows = slice(j * rank, (j + 1) * rank)
            down_ref[at + j, :, :wide] = refs[2 * dr][rows]
            down_ref[at + j, :, wide:] = refs[2 * dr + 1][rows, : width - wide]
            up_ref[at + j] = refs[2 * dr + 1][rows, width - wide :]


def on_device(
    saved_layer_input,
    value_output_gradient,
    token_adapter_index,
    adapter_slot_index,
    frozen_value_weight,
    adapter_down_weight,
    adapter_up_weight,
):
    inputs = saved_layer_input[0]
    grad_rows = value_output_gradient[0]
    tokens, width = inputs.shape
    value_width = grad_rows.shape[1]
    groups, holders, replicas = (lax.axis_size(a) for a in ("groups", "adapter", "replica"))
    group, here, core = (lax.axis_index(a) for a in ("groups", "adapter", "replica"))
    slots, rank = adapter_down_weight.shape[1:3]
    own_slots = slots // replicas
    rows = own_slots * rank
    frozen = frozen_value_weight[0]
    shard = frozen.shape[0]
    half = shard // groups
    piece = half // replicas
    cols = width + value_width

    tagged = call(
        tag_kernel,
        [jax.ShapeDtypeStruct((tokens, value_width + LANES), BF16)],
        (grad_rows, token_adapter_index[0, :, 0][None], adapter_slot_index),
        scalars=1,
    )[0]
    grads = [tagged] + [
        moved(tagged, lambda g, z, s, r: (g - dg, z, s, r)) for dg in range(1, groups)
    ]

    own = call(
        functools.partial(own_kernel, (groups, holders, shard)),
        [jax.ShapeDtypeStruct((rows, holders * half + value_width), BF16)],
        (adapter_down_weight[0], adapter_up_weight[0]),
    )[0]
    held = [own]
    for k in range(1, holders):
        held.append(moved(own, lambda g, z, s, r: (g, z + k, s, r)))

    ring = [lax.dynamic_slice_in_dim(frozen, (group * replicas + core) * piece, piece, axis=0)]
    ring.append(moved(ring[0], lambda g, z, s, r: (g, z + 1, s, r)))
    held, grads, ring = lax.optimization_barrier((held, grads, ring))
    joined = call(
        join_kernel,
        [
            jax.ShapeDtypeStruct((holders * rows, holders * half), BF16),
            jax.ShapeDtypeStruct((holders * rows, value_width), BF16),
        ],
        held,
    )
    downs, ups = [joined[0]], [joined[1]]
    for dr in range(1, replicas):
        ups.append(moved(ups[0], lambda g, z, s, r: (g, z, s, r + dr)))
        downs.append(moved(downs[0], lambda g, z, s, r: (g, z, s, r + dr)))
    def pieces_of(k, *before):
        if k == 0:
            return [(0, 0)], [frozen]
        mails = [ring[k]]
        if k > 1 and piece % (2 * LANES) == 0:
            shape = jax.ShapeDtypeStruct((piece // 2, value_width), BF16)
            mails = call(split_kernel, [shape] * 2, (ring[k],))
        mails = [after(mail, *before) if before else mail for mail in mails]
        spec, pieces = [(0, 0)], [ring[k]]
        for dr in range(1, replicas):
            for j, mail in enumerate(mails):
                spec.append((dr, j * mail.shape[0]))
                pieces.append(moved(mail, lambda g, z, s, r: (g, z, s, r + dr)))
        if piece % LANES:
            whole = jnp.zeros((half, value_width), BF16)
            for (dr, offset), part in zip(spec, pieces):
                at = ((core - dr) % replicas) * piece + offset
                whole = lax.dynamic_update_slice_in_dim(whole, part, at, axis=0)
            spec, pieces = [(0, 0)], [whole]
        return spec, pieces

    kept = replicas * holders * rows

    def adapter_sums(sel, *before):
        maps = list(downs)
        for dg in range(1, groups):
            maps.append(moved(downs[0], lambda g, z, s, r: (g + dg, z, s, r)))
            for dr in range(1, replicas):
                maps.append(moved(maps[-dr], lambda g, z, s, r: (g, z, s, r + dr)))
        gradients = call(
            functools.partial(adapter_kernel, (groups, holders, replicas, shard, slots, rank)),
            [jax.ShapeDtypeStruct((holders * rows, cols), F32)]
            + [jax.ShapeDtypeStruct((holders * rows, cols // 2), BF16)] * (2 * replicas - 2),
            (inputs, tagged, sel, *maps),
            [jax.ShapeDtypeStruct((kept, width), BF16)],
        )
        part, sent = gradients[0], gradients[1:]
        came = [
            moved(after(sent[2 * dr - 2 + j], *before), lambda g, z, s, r: (g, z, s, r - dr))
            for dr in range(1, replicas)
            for j in range(2)
        ]
        chip = call(
            functools.partial(chip_kernel, replicas),
            [jax.ShapeDtypeStruct((rows, cols), F32)]
            + [jax.ShapeDtypeStruct((rows, cols), BF16)] * (holders - 1),
            (part, *came),
        )
        return part, chip

    batches = [list(range(min(2, holders)))] + [[k] for k in range(2, holders)]
    arrived, crossed = [], []
    for i, batch in enumerate(batches):
        operands, specs = [], []
        for k in batch:
            if k > 1:
                last = after(ring[-1], sel) if k > 2 else ring[-1]
                ring.append(moved(last, lambda g, z, s, r: (g, z + 1, s, r)))
            gate = arrived[0] if k == 2 else [*arrived[i - 2], chip[0]] if k > 2 else []
            spec, blocks = pieces_of(k, *gate)
            specs.append((k, spec))
            operands += blocks
        out = call(
            functools.partial(
                frozen_kernel, (tokens, groups, holders, replicas, slots, rank), specs
            ),
            (
                [jax.ShapeDtypeStruct((groups * tokens, half), BF16)]
                if i == 1 and len(batches) > 2
                else [jax.ShapeDtypeStruct((tokens, half * len(batch)), BF16)] * groups
            )
            + [jax.ShapeDtypeStruct((groups * tokens, kept), BF16)] * (i == 0),
            [*grads, *downs, *([sel] if i else ups), *operands],
        )
        if i == 0:
            sel = out[groups]
        mails = list(out[:groups])
        if i == 1 and len(batches) > 2:
            got = moved(out[0], lambda g, z, s, r: (g, z, s - 1, r))
            got = [got[dg * tokens : (dg + 1) * tokens] for dg in range(groups)]
            early = [(batches[0], dg) for dg in range(groups)] + [(batch, 0)]
            passed = call(
                functools.partial(place_kernel, (groups, holders, shard, half), early),
                [jax.ShapeDtypeStruct((tokens, width), BF16)],
                [*arrived[0], got[0]],
            )[0]
            got, passed = lax.optimization_barrier((got, passed))
            late = [
                ((batch, dg), moved(got[dg], lambda g, z, s, r: (g + dg, z, s, r)))
                for dg in range(1, groups)
            ]
            arrived.append([])
            continue
        if i > 2:
            mails = [after(mail, *arrived[-1]) for mail in mails]
        arrived.append(
            [moved(mails[dg], lambda g, z, s, r: (g + dg, z, s - 1, r)) for dg in range(groups)]
        )
        if i > 1:
            late += [((batch, dg), arrived[-1][dg]) for dg in reversed(range(groups))]
        if i == 0:
            part, chip = adapter_sums(sel, *arrived[0])
    sizes = (groups, holders, shard, half)
    if len(batches) > 2:
        passed = pl.pallas_call(
            functools.partial(late_kernel, sizes, [place for place, _ in late]),
            out_shape=jax.ShapeDtypeStruct((tokens, width), BF16),
            in_specs=[pl.BlockSpec(memory_space=pltpu.VMEM)] * len(late)
            + [pl.BlockSpec(memory_space=pl.ANY)],
            out_specs=pl.BlockSpec(memory_space=pl.ANY),
            input_output_aliases={len(late): 0},
            scratch_shapes=[pltpu.SemaphoreType.DMA((len(late),))],
            compiler_params=pltpu.CompilerParams(vmem_limit_bytes=8 * MIB),
            cost_estimate=pl.CostEstimate(flops=1000, bytes_accessed=1000, transcendentals=0),
        )(*[part for _, part in late], passed)
    else:
        passed = call(
            functools.partial(
                place_kernel, sizes, [(batch, dg) for batch in batches for dg in range(groups)]
            ),
            [jax.ShapeDtypeStruct((tokens, width), BF16)],
            [x for got in arrived for x in got],
        )[0]

    sums = [chip[0]] + [
        moved(after(chip[k], ring[-1]), lambda g, z, s, r: (g, z - k, s, r))
        for k in [*range(1, holders, 2), *range(2, holders, 2)]
    ]
    total = call(total_kernel, [jax.ShapeDtypeStruct((rows, cols // 2), BF16)] * 2, sums)
    totals = list(total)
    for dr in range(1, replicas):
        totals += [moved(x, lambda g, z, s, r: (g, z, s, r + dr)) for x in total]
    down_grad, up_grad = call(
        functools.partial(spread_kernel, width, replicas),
        [
            jax.ShapeDtypeStruct((slots, rank, width), BF16),
            jax.ShapeDtypeStruct((slots, rank, value_width), BF16),
        ],
        totals,
    )

    return passed[None], down_grad[None], up_grad[None]


def solution(mesh):
    placed = (
        P("segment", ("groups", "adapter", "replica"), None),
        P("segment", ("groups", "adapter", "replica"), None),
        P("segment", ("groups", "adapter", "replica"), None),
        P("groups"),
        P("segment", "adapter", None),
        P("segment", "adapter", None, None),
        P("segment", "adapter", None, None),
    )
    return jax.shard_map(
        on_device,
        mesh=mesh,
        in_specs=placed,
        out_specs=(
            P("segment", ("groups", "adapter", "replica"), None),
            P(("groups", "segment"), "adapter", None, None),
            P(("groups", "segment"), "adapter", None, None),
        ),
        check_vma=False,
    )
```

```python
import functools
import itertools
import jax
import jax.numpy as jnp
from jax import lax
from jax.experimental import pallas as pl
from jax.experimental.pallas import tpu as pltpu
from jax.sharding import PartitionSpec as P

ADAPTER_SCALE = 2.0
AXES = ("groups", "adapter", "segment", "replica")
LANES = 128
F32 = jnp.float32
BF16 = jnp.bfloat16
MIB = 1024 * 1024


def moved(x, to):
    sizes = [lax.axis_size(a) for a in AXES]
    number = {at: i for i, at in enumerate(itertools.product(*map(range, sizes)))}
    pairs = [
        (i, number[tuple(t % s for t, s in zip(to(*at), sizes))]) for at, i in number.items()
    ]
    return lax.ppermute(x, AXES, pairs)


def after(x, *others):
    return lax.optimization_barrier((x, *others))[0]


def rows_by_rows(a, b):
    return lax.dot_general(a, b, (((1,), (1,)), ((), ())), preferred_element_type=F32)


def columns_by_columns(a, b):
    return lax.dot_general(a, b, (((0,), (0,)), ((), ())), preferred_element_type=F32)


def call(kernel, out_shape, operands, scratch=(), scalars=0):
    held = sum(x.size * x.dtype.itemsize for x in (*operands, *out_shape, *scratch))
    return pl.pallas_call(
        kernel,
        out_shape=out_shape,
        in_specs=[pl.BlockSpec(memory_space=pltpu.VMEM)] * (len(operands) - scalars)
        + [pl.BlockSpec(memory_space=pltpu.SMEM)] * scalars,
        scratch_shapes=[pltpu.VMEM(x.shape, x.dtype) for x in scratch],
        compiler_params=pltpu.CompilerParams(vmem_limit_bytes=2 * held + 4 * MIB),
        cost_estimate=pl.CostEstimate(flops=1000, bytes_accessed=1000, transcendentals=0),
    )(*operands)


def slots_of(tagged_ref):
    return tagged_ref[:, -LANES:].astype(F32)[:, :1]


def row_slots(holders, replicas, slots, rank, dr):
    here, core = lax.axis_index("adapter"), lax.axis_index("replica")
    own_slots = slots // replicas
    lane = lax.broadcasted_iota(jnp.int32, (1, holders * own_slots * rank), 1)
    slot = jnp.zeros_like(lane)
    for k in range(holders):
        for j in range(own_slots):
            start = (k * own_slots + j) * rank
            value = lax.rem(here + holders - k, holders) * slots
            value = value + lax.rem(core + replicas - dr, replicas) * own_slots + j
            slot = jnp.where((lane >= start) & (lane < start + rank), value, slot)
    return slot.astype(F32)


def tag_kernel(g_ref, name_ref, slot_ref, out_ref):
    out_ref[:, :-LANES] = g_ref[...]
    names = name_ref[...]
    slot = jnp.zeros_like(names)
    for j in range(slot_ref.shape[0]):
        slot = jnp.where(names == j, slot_ref[j], slot)
    ones = jnp.ones((1, LANES), F32)
    out_ref[:, -LANES:] = columns_by_columns(slot.astype(F32), ones).astype(BF16)


def join_kernel(*refs):
    down_ref, up_ref = refs[-2:]
    wide = down_ref.shape[1]
    for k, ref in enumerate(refs[:-2]):
        rows = ref.shape[0]
        down_ref[k * rows : (k + 1) * rows] = ref[:, :wide]
        up_ref[k * rows : (k + 1) * rows] = ref[:, wide:]


def own_kernel(sizes, down_ref, up_ref, out_ref):
    groups, holders, shard = sizes
    half = shard // groups
    rank = down_ref.shape[1]
    slots = out_ref.shape[0] // rank
    first = lax.axis_index("replica") * slots
    for j in range(slots):
        to = pl.ds(j * rank, rank)
        for z in range(holders):
            at = pl.multiple_of(z * shard + lax.axis_index("groups") * half, half)
            out_ref[to, z * half : (z + 1) * half] = down_ref[first + j, :, pl.ds(at, half)]
        out_ref[to, holders * half :] = up_ref[first + j]


def adapter_kernel(sizes, *refs):
    groups, holders, replicas, shard, slots, rank = sizes
    x_ref, g_ref, sel_ref = refs[:3]
    map_refs, refs = refs[3 : 3 + groups * replicas], refs[3 + groups * replicas :]
    own_ref, other_refs, down = refs[0], refs[1:-1], refs[-1]
    group = lax.axis_index("groups")
    tokens, width = x_ref.shape
    rows, cols = own_ref.shape
    half = shard // groups
    for dg in range(groups):
        first = lax.rem(group + groups - dg, groups) * half
        for dr in range(replicas):
            for z in range(holders):
                at = pl.multiple_of(first + z * shard, half)
                down[pl.ds(dr * rows, rows), pl.ds(at, half)] = map_refs[dg * replicas + dr][
                    :, z * half : (z + 1) * half
                ]
    row_slot = [row_slots(holders, replicas, slots, rank, dr) for dr in range(replicas)]
    keep = slots_of(g_ref) == jnp.concatenate(row_slot, axis=1)
    in_sel = jnp.where(keep, rows_by_rows(x_ref[...], down[...]), 0.0).astype(BF16)
    grad_sel = sel_ref[pl.ds(0, tokens), :]
    step, split = 1024, cols // 2
    for at in range(0, cols, step):
        if at < width:
            part = columns_by_columns(grad_sel, x_ref[:, at : at + step])
        else:
            part = columns_by_columns(in_sel, g_ref[:, at - width : at - width + step])
        own_ref[:, at : at + step] = part[:rows]
        for dr in range(1, replicas):
            sent = part[dr * rows : (dr + 1) * rows].astype(BF16)
            for j in range(0, step, LANES):
                ref, to = other_refs[2 * dr - 2 + (at + j) // split], (at + j) % split
                ref[:, to : to + LANES] = sent[:, j : j + LANES]


def frozen_kernel(sizes, batch, *refs):
    tokens, groups, holders, replicas, slots, rank = sizes
    g_refs, refs = refs[:groups], refs[groups:]
    down_refs, refs = refs[:replicas], refs[replicas:]
    core, here = lax.axis_index("replica"), lax.axis_index("adapter")
    rows = down_refs[0].shape[0]
    half = down_refs[0].shape[1] // holders
    if batch[0][0] == 0:
        up_refs, refs = refs[:replicas], refs[replicas:]
        sel_ref = refs[-1]
        out_refs = refs[-1 - groups : -1]
        for dg in range(groups):
            for dr in range(replicas):
                keep = slots_of(g_refs[dg]) == row_slots(holders, replicas, slots, rank, dr)
                proj_grad = rows_by_rows(g_refs[dg][:, :-LANES], up_refs[dr][...])
                sel_ref[pl.ds(dg * tokens, tokens), dr * rows : (dr + 1) * rows] = jnp.where(
                    keep, proj_grad, 0.0
                ).astype(BF16)
    else:
        sel_ref, refs = refs[0], refs[1:]
        out_refs = refs[-groups:]
        if refs[-1].shape[0] > tokens:
            out_refs = [refs[-1].at[pl.ds(dg * tokens, tokens)] for dg in range(groups)]
    for i, (k, spec) in enumerate(batch):
        shard_at = lax.rem(here + holders - k, holders) * half
        for (dr, offset), block in zip(spec, refs):
            if k == 0:
                first = pl.multiple_of(lax.axis_index("groups") * half, half)
                block = block.at[pl.ds(first, half)]
            wide = block.shape[0]
            at = 0
            if wide < half:
                at = lax.rem(core + replicas - dr, replicas) * (half // replicas) + offset
            columns = pl.ds(pl.multiple_of(shard_at + at, wide), wide)
            for dg in range(groups):
                base = rows_by_rows(g_refs[dg][:, :-LANES], block[...]).astype(BF16)
                lora = 0.0
                for j in range(replicas):
                    lora = lora + jnp.dot(
                        sel_ref[pl.ds(dg * tokens, tokens), j * rows : (j + 1) * rows],
                        down_refs[j][:, columns],
                        preferred_element_type=F32,
                    )
                lora = (ADAPTER_SCALE * lora).astype(BF16)
                out_refs[dg][:, pl.ds(pl.multiple_of(i * half + at, wide), wide)] = (
                    base.astype(F32) + lora.astype(F32)
                ).astype(BF16)
        refs = refs[len(spec) :]


def split_kernel(block_ref, *part_refs):
    rows = part_refs[0].shape[0]
    for j, ref in enumerate(part_refs):
        ref[...] = block_ref[j * rows : (j + 1) * rows]


def column_of(sizes, k, dg):
    groups, holders, shard, half = sizes
    group, here = lax.axis_index("groups"), lax.axis_index("adapter")
    source = lax.rem(group + groups - dg, groups)
    at = lax.rem(here + holders - k, holders) * shard + source * half
    return pl.ds(pl.multiple_of(at, half), half)


def place_kernel(sizes, places, *refs):
    half = sizes[-1]
    for ref, (batch, dg) in zip(refs, places):
        for j, k in enumerate(batch):
            refs[-1][:, column_of(sizes, k, dg)] = ref[:, j * half : (j + 1) * half]


def late_kernel(sizes, places, *refs):
    out_ref, sems = refs[-2:]
    copies = [
        pltpu.make_async_copy(ref, out_ref.at[:, column_of(sizes, batch[0], dg)], sems.at[i])
        for i, (ref, (batch, dg)) in enumerate(zip(refs, places))
    ]
    for copy in copies:
        copy.start()
    for copy in copies:
        copy.wait()


def chip_kernel(replicas, *refs):
    own_ref, came_refs, out_refs = refs[0], refs[1 : 2 * replicas - 1], refs[2 * replicas - 1 :]
    rows = out_refs[0].shape[0]
    split = came_refs[0].shape[1]
    for k, out in enumerate(out_refs):
        for j in range(2):
            at = pl.ds(k * rows, rows), pl.ds(j * split, split)
            total = own_ref[at]
            for ref in came_refs[j::2]:
                total = total + ref[pl.ds(k * rows, rows), :].astype(F32)
            out[:, pl.ds(j * split, split)] = total.astype(out.dtype)


def total_kernel(*refs):
    half_refs, refs = refs[-2:], refs[:-2]
    wide = half_refs[0].shape[1]
    for j, out_ref in enumerate(half_refs):
        at = pl.ds(j * wide, wide)
        total = refs[0][:, at]
        for ref in refs[1:]:
            total = total + ref[:, at].astype(F32)
        out_ref[...] = (ADAPTER_SCALE * total).astype(BF16)


def spread_kernel(width, replicas, *refs):
    core = lax.axis_index("replica")
    down_ref, up_ref = refs[2 * replicas :]
    slots = down_ref.shape[0] // replicas
    rank = down_ref.shape[1]
    wide = refs[0].shape[1]
    for dr in range(replicas):
        at = lax.rem(core + replicas - dr, replicas) * slots
        for j in range(slots):
            rows = slice(j * rank, (j + 1) * rank)
            down_ref[at + j, :, :wide] = refs[2 * dr][rows]
            down_ref[at + j, :, wide:] = refs[2 * dr + 1][rows, : width - wide]
            up_ref[at + j] = refs[2 * dr + 1][rows, width - wide :]


def on_device(
    saved_layer_input,
    value_output_gradient,
    token_adapter_index,
    adapter_slot_index,
    frozen_value_weight,
    adapter_down_weight,
    adapter_up_weight,
):
    inputs = saved_layer_input[0]
    grad_rows = value_output_gradient[0]
    tokens, width = inputs.shape
    value_width = grad_rows.shape[1]
    groups, holders, replicas = (lax.axis_size(a) for a in ("groups", "adapter", "replica"))
    group, here, core = (lax.axis_index(a) for a in ("groups", "adapter", "replica"))
    slots, rank = adapter_down_weight.shape[1:3]
    own_slots = slots // replicas
    rows = own_slots * rank
    frozen = frozen_value_weight[0]
    shard = frozen.shape[0]
    half = shard // groups
    piece = half // replicas
    cols = width + value_width

    tagged = call(
        tag_kernel,
        [jax.ShapeDtypeStruct((tokens, value_width + LANES), BF16)],
        (grad_rows, token_adapter_index[0, :, 0][None], adapter_slot_index),
        scalars=1,
    )[0]
    grads = [tagged] + [
        moved(tagged, lambda g, z, s, r: (g - dg, z, s, r)) for dg in range(1, groups)
    ]

    own = call(
        functools.partial(own_kernel, (groups, holders, shard)),
        [jax.ShapeDtypeStruct((rows, holders * half + value_width), BF16)],
        (adapter_down_weight[0], adapter_up_weight[0]),
    )[0]
    held = [own]
    for k in range(1, holders):
        held.append(moved(own, lambda g, z, s, r: (g, z + k, s, r)))

    ring = [lax.dynamic_slice_in_dim(frozen, (group * replicas + core) * piece, piece, axis=0)]
    ring.append(moved(ring[0], lambda g, z, s, r: (g, z + 1, s, r)))
    held, grads, ring = lax.optimization_barrier((held, grads, ring))
    joined = call(
        join_kernel,
        [
            jax.ShapeDtypeStruct((holders * rows, holders * half), BF16),
            jax.ShapeDtypeStruct((holders * rows, value_width), BF16),
        ],
        held,
    )
    downs, ups = [joined[0]], [joined[1]]
    for dr in range(1, replicas):
        ups.append(moved(ups[0], lambda g, z, s, r: (g, z, s, r + dr)))
        downs.append(moved(downs[0], lambda g, z, s, r: (g, z, s, r + dr)))
    def pieces_of(k, *before):
        if k == 0:
            return [(0, 0)], [frozen]
        mails = [ring[k]]
        if k > 1 and piece % (2 * LANES) == 0:
            shape = jax.ShapeDtypeStruct((piece // 2, value_width), BF16)
            mails = call(split_kernel, [shape] * 2, (ring[k],))
        mails = [after(mail, *before) if before else mail for mail in mails]
        spec, pieces = [(0, 0)], [ring[k]]
        for dr in range(1, replicas):
            for j, mail in enumerate(mails):
                spec.append((dr, j * mail.shape[0]))
                pieces.append(moved(mail, lambda g, z, s, r: (g, z, s, r + dr)))
        if piece % LANES:
            whole = jnp.zeros((half, value_width), BF16)
            for (dr, offset), part in zip(spec, pieces):
                at = ((core - dr) % replicas) * piece + offset
                whole = lax.dynamic_update_slice_in_dim(whole, part, at, axis=0)
            spec, pieces = [(0, 0)], [whole]
        return spec, pieces

    kept = replicas * holders * rows

    def adapter_sums(sel, *before):
        maps = list(downs)
        for dg in range(1, groups):
            maps.append(moved(downs[0], lambda g, z, s, r: (g + dg, z, s, r)))
            for dr in range(1, replicas):
                maps.append(moved(maps[-dr], lambda g, z, s, r: (g, z, s, r + dr)))
        gradients = call(
            functools.partial(adapter_kernel, (groups, holders, replicas, shard, slots, rank)),
            [jax.ShapeDtypeStruct((holders * rows, cols), F32)]
            + [jax.ShapeDtypeStruct((holders * rows, cols // 2), BF16)] * (2 * replicas - 2),
            (inputs, tagged, sel, *maps),
            [jax.ShapeDtypeStruct((kept, width), BF16)],
        )
        part, sent = gradients[0], gradients[1:]
        came = [
            moved(after(sent[2 * dr - 2 + j], *before), lambda g, z, s, r: (g, z, s, r - dr))
            for dr in range(1, replicas)
            for j in range(2)
        ]
        chip = call(
            functools.partial(chip_kernel, replicas),
            [jax.ShapeDtypeStruct((rows, cols), F32)]
            + [jax.ShapeDtypeStruct((rows, cols), BF16)] * (holders - 1),
            (part, *came),
        )
        return part, chip

    batches = [list(range(min(2, holders)))] + [[k] for k in range(2, holders)]
    arrived, crossed = [], []
    for i, batch in enumerate(batches):
        operands, specs = [], []
        for k in batch:
            if k > 1:
                last = after(ring[-1], sel) if k > 2 else ring[-1]
                ring.append(moved(last, lambda g, z, s, r: (g, z + 1, s, r)))
            gate = arrived[0][::-1] if k == 2 else [*arrived[i - 2], chip[0]] if k > 2 else []
            spec, blocks = pieces_of(k, *gate)
            specs.append((k, spec))
            operands += blocks
        out = call(
            functools.partial(
                frozen_kernel, (tokens, groups, holders, replicas, slots, rank), specs
            ),
            (
                [jax.ShapeDtypeStruct((groups * tokens, half), BF16)]
                if i == 1 and len(batches) > 2
                else [jax.ShapeDtypeStruct((tokens, half * len(batch)), BF16)] * groups
            )
            + [jax.ShapeDtypeStruct((groups * tokens, kept), BF16)] * (i == 0),
            [*grads, *downs, *([sel] if i else ups), *operands],
        )
        if i == 0:
            sel = out[groups]
        mails = list(out[:groups])
        if i == 1 and len(batches) > 2:
            got = moved(out[0], lambda g, z, s, r: (g, z, s - 1, r))
            got = [got[dg * tokens : (dg + 1) * tokens] for dg in range(groups)]
            early = [(batches[0], dg) for dg in range(groups)] + [(batch, 0)]
            passed = call(
                functools.partial(place_kernel, (groups, holders, shard, half), early),
                [jax.ShapeDtypeStruct((tokens, width), BF16)],
                [*arrived[0], got[0]],
            )[0]
            got, passed = lax.optimization_barrier((got, passed))
            late = [
                ((batch, dg), moved(got[dg], lambda g, z, s, r: (g + dg, z, s, r)))
                for dg in range(1, groups)
            ]
            arrived.append([])
            continue
        if i > 2:
            mails = [after(mail, *arrived[-1]) for mail in mails]
        arrived.append(
            [moved(mails[dg], lambda g, z, s, r: (g + dg, z, s - 1, r)) for dg in range(groups)]
        )
        if i > 1:
            late += [((batch, dg), arrived[-1][dg]) for dg in reversed(range(groups))]
        if i == 0:
            part, chip = adapter_sums(sel, *arrived[0][::-1])
    sizes = (groups, holders, shard, half)
    if len(batches) > 2:
        passed = pl.pallas_call(
            functools.partial(late_kernel, sizes, [place for place, _ in late]),
            out_shape=jax.ShapeDtypeStruct((tokens, width), BF16),
            in_specs=[pl.BlockSpec(memory_space=pltpu.VMEM)] * len(late)
            + [pl.BlockSpec(memory_space=pl.ANY)],
            out_specs=pl.BlockSpec(memory_space=pl.ANY),
            input_output_aliases={len(late): 0},
            scratch_shapes=[pltpu.SemaphoreType.DMA((len(late),))],
            compiler_params=pltpu.CompilerParams(vmem_limit_bytes=8 * MIB),
            cost_estimate=pl.CostEstimate(flops=1000, bytes_accessed=1000, transcendentals=0),
        )(*[part for _, part in late], passed)
    else:
        passed = call(
            functools.partial(
                place_kernel, sizes, [(batch, dg) for batch in batches for dg in range(groups)]
            ),
            [jax.ShapeDtypeStruct((tokens, width), BF16)],
            [x for got in arrived for x in got],
        )[0]

    sums = [chip[0]] + [
        moved(after(chip[k], ring[-1]), lambda g, z, s, r: (g, z - k, s, r))
        for k in range(1, holders)
    ]
    total = call(total_kernel, [jax.ShapeDtypeStruct((rows, cols // 2), BF16)] * 2, sums)
    totals = list(total)
    for dr in range(1, replicas):
        totals += [moved(x, lambda g, z, s, r: (g, z, s, r + dr)) for x in total]
    down_grad, up_grad = call(
        functools.partial(spread_kernel, width, replicas),
        [
            jax.ShapeDtypeStruct((slots, rank, width), BF16),
            jax.ShapeDtypeStruct((slots, rank, value_width), BF16),
        ],
        totals,
    )

    return passed[None], down_grad[None], up_grad[None]


def solution(mesh):
    placed = (
        P("segment", ("groups", "adapter", "replica"), None),
        P("segment", ("groups", "adapter", "replica"), None),
        P("segment", ("groups", "adapter", "replica"), None),
        P("groups"),
        P("segment", "adapter", None),
        P("segment", "adapter", None, None),
        P("segment", "adapter", None, None),
    )
    return jax.shard_map(
        on_device,
        mesh=mesh,
        in_specs=placed,
        out_specs=(
            P("segment", ("groups", "adapter", "replica"), None),
            P(("groups", "segment"), "adapter", None, None),
            P(("groups", "segment"), "adapter", None, None),
        ),
        check_vma=False,
    )
```

```python
import functools
import itertools
import jax
import jax.numpy as jnp
from jax import lax
from jax.experimental import pallas as pl
from jax.experimental.pallas import tpu as pltpu
from jax.sharding import PartitionSpec as P

ADAPTER_SCALE = 2.0
AXES = ("groups", "adapter", "segment", "replica")
LANES = 128
F32 = jnp.float32
BF16 = jnp.bfloat16
MIB = 1024 * 1024
GRANT = 62 * MIB


def moved(x, to):
    sizes = [lax.axis_size(a) for a in AXES]
    number = {at: i for i, at in enumerate(itertools.product(*map(range, sizes)))}
    pairs = [
        (i, number[tuple(t % s for t, s in zip(to(*at), sizes))]) for at, i in number.items()
    ]
    return lax.ppermute(x, AXES, pairs)


def after(x, *others):
    return lax.optimization_barrier((x, *others))[0]


def rows_by_rows(a, b):
    return lax.dot_general(a, b, (((1,), (1,)), ((), ())), preferred_element_type=F32)


def columns_by_columns(a, b):
    return lax.dot_general(a, b, (((0,), (0,)), ((), ())), preferred_element_type=F32)


def call(kernel, out_shape, operands, scratch=(), scalars=0):
    held = sum(x.size * x.dtype.itemsize for x in (*operands, *out_shape, *scratch))
    return pl.pallas_call(
        kernel,
        out_shape=out_shape,
        in_specs=[pl.BlockSpec(memory_space=pltpu.VMEM)] * (len(operands) - scalars)
        + [pl.BlockSpec(memory_space=pltpu.SMEM)] * scalars,
        scratch_shapes=[pltpu.VMEM(x.shape, x.dtype) for x in scratch],
        compiler_params=pltpu.CompilerParams(vmem_limit_bytes=2 * held + 4 * MIB),
        cost_estimate=pl.CostEstimate(flops=1000, bytes_accessed=1000, transcendentals=0),
    )(*operands)


def slots_of(tagged_ref):
    return tagged_ref[:, -LANES:].astype(F32)[:, :1]


def row_slots(holders, replicas, slots, rank, dr):
    here, core = lax.axis_index("adapter"), lax.axis_index("replica")
    own_slots = slots // replicas
    lane = lax.broadcasted_iota(jnp.int32, (1, holders * own_slots * rank), 1)
    slot = jnp.zeros_like(lane)
    for k in range(holders):
        for j in range(own_slots):
            start = (k * own_slots + j) * rank
            value = lax.rem(here + holders - k, holders) * slots
            value = value + lax.rem(core + replicas - dr, replicas) * own_slots + j
            slot = jnp.where((lane >= start) & (lane < start + rank), value, slot)
    return slot.astype(F32)


def tag_kernel(g_ref, name_ref, slot_ref, out_ref):
    out_ref[:, :-LANES] = g_ref[...]
    names = name_ref[...]
    slot = jnp.zeros_like(names)
    for j in range(slot_ref.shape[0]):
        slot = jnp.where(names == j, slot_ref[j], slot)
    ones = jnp.ones((1, LANES), F32)
    out_ref[:, -LANES:] = columns_by_columns(slot.astype(F32), ones).astype(BF16)


def join_kernel(*refs):
    down_ref, up_ref = refs[-2:]
    wide = down_ref.shape[1]
    for k, ref in enumerate(refs[:-2]):
        rows = ref.shape[0]
        down_ref[k * rows : (k + 1) * rows] = ref[:, :wide]
        up_ref[k * rows : (k + 1) * rows] = ref[:, wide:]


def piece_kernel(replicas, frozen_ref, out_ref, sem):
    rows = out_ref.shape[0]
    at = (lax.axis_index("groups") * replicas + lax.axis_index("replica")) * rows
    copy = pltpu.make_async_copy(
        frozen_ref.at[pl.ds(pl.multiple_of(at, rows), rows)], out_ref, sem
    )
    copy.start()
    copy.wait()


def own_kernel(sizes, down_ref, up_ref, out_ref):
    groups, holders, shard = sizes
    half = shard // groups
    rank = down_ref.shape[1]
    slots = out_ref.shape[0] // rank
    first = lax.axis_index("replica") * slots
    for j in range(slots):
        to = pl.ds(j * rank, rank)
        for z in range(holders):
            at = pl.multiple_of(z * shard + lax.axis_index("groups") * half, half)
            out_ref[to, z * half : (z + 1) * half] = down_ref[first + j, :, pl.ds(at, half)]
        out_ref[to, holders * half :] = up_ref[first + j]


def adapter_kernel(sizes, *refs):
    groups, holders, replicas, shard, slots, rank = sizes
    x_ref, g_ref, sel_ref = refs[:3]
    map_refs, refs = refs[3 : 3 + groups * replicas], refs[3 + groups * replicas :]
    own_ref, other_refs, down = refs[0], refs[1:-1], refs[-1]
    group = lax.axis_index("groups")
    tokens, width = x_ref.shape
    rows, cols = own_ref.shape
    half = shard // groups
    for dg in range(groups):
        first = lax.rem(group + groups - dg, groups) * half
        for dr in range(replicas):
            for z in range(holders):
                at = pl.multiple_of(first + z * shard, half)
                down[pl.ds(dr * rows, rows), pl.ds(at, half)] = map_refs[dg * replicas + dr][
                    :, z * half : (z + 1) * half
                ]
    row_slot = [row_slots(holders, replicas, slots, rank, dr) for dr in range(replicas)]
    keep = slots_of(g_ref) == jnp.concatenate(row_slot, axis=1)
    in_sel = jnp.where(keep, rows_by_rows(x_ref[...], down[...]), 0.0).astype(BF16)
    grad_sel = sel_ref[pl.ds(0, tokens), :]
    step, split = 1024, cols // 2
    for at in range(0, cols, step):
        if at < width:
            part = columns_by_columns(grad_sel, x_ref[:, at : at + step])
        else:
            part = columns_by_columns(in_sel, g_ref[:, at - width : at - width + step])
        own_ref[:, at : at + step] = part[:rows]
        for dr in range(1, replicas):
            sent = part[dr * rows : (dr + 1) * rows].astype(BF16)
            for j in range(0, step, LANES):
                ref, to = other_refs[2 * dr - 2 + (at + j) // split], (at + j) % split
                ref[:, to : to + LANES] = sent[:, j : j + LANES]


def frozen_kernel(sizes, batch, *refs):
    tokens, groups, holders, replicas, slots, rank = sizes
    g_refs, refs = refs[:groups], refs[groups:]
    down_refs, refs = refs[:replicas], refs[replicas:]
    core, here = lax.axis_index("replica"), lax.axis_index("adapter")
    rows = down_refs[0].shape[0]
    half = down_refs[0].shape[1] // holders
    if batch[0][0] == 0:
        up_refs, refs = refs[:replicas], refs[replicas:]
        sel_ref = refs[-1]
        out_refs = refs[-1 - groups : -1]
        for dg in range(groups):
            for dr in range(replicas):
                keep = slots_of(g_refs[dg]) == row_slots(holders, replicas, slots, rank, dr)
                proj_grad = rows_by_rows(g_refs[dg][:, :-LANES], up_refs[dr][...])
                sel_ref[pl.ds(dg * tokens, tokens), dr * rows : (dr + 1) * rows] = jnp.where(
                    keep, proj_grad, 0.0
                ).astype(BF16)
    else:
        sel_ref, refs = refs[0], refs[1:]
        out_refs = refs[-groups:]
        if refs[-1].shape[0] > tokens:
            out_refs = [refs[-1].at[pl.ds(dg * tokens, tokens)] for dg in range(groups)]
    for i, (k, spec) in enumerate(batch):
        shard_at = lax.rem(here + holders - k, holders) * half
        for (dr, offset), block in zip(spec, refs):
            if k == 0:
                first = pl.multiple_of(lax.axis_index("groups") * half, half)
                block = block.at[pl.ds(first, half)]
            wide = block.shape[0]
            at = 0
            if wide < half:
                at = lax.rem(core + replicas - dr, replicas) * (half // replicas) + offset
            columns = pl.ds(pl.multiple_of(shard_at + at, wide), wide)
            for dg in range(groups):
                base = rows_by_rows(g_refs[dg][:, :-LANES], block[...]).astype(BF16)
                lora = 0.0
                for j in range(replicas):
                    lora = lora + jnp.dot(
                        sel_ref[pl.ds(dg * tokens, tokens), j * rows : (j + 1) * rows],
                        down_refs[j][:, columns],
                        preferred_element_type=F32,
                    )
                lora = (ADAPTER_SCALE * lora).astype(BF16)
                out_refs[dg][:, pl.ds(pl.multiple_of(i * half + at, wide), wide)] = (
                    base.astype(F32) + lora.astype(F32)
                ).astype(BF16)
        refs = refs[len(spec) :]


def split_kernel(block_ref, *part_refs):
    rows = part_refs[0].shape[0]
    for j, ref in enumerate(part_refs):
        ref[...] = block_ref[j * rows : (j + 1) * rows]


def column_of(sizes, k, dg):
    groups, holders, shard, half = sizes
    group, here = lax.axis_index("groups"), lax.axis_index("adapter")
    source = lax.rem(group + groups - dg, groups)
    at = lax.rem(here + holders - k, holders) * shard + source * half
    return pl.ds(pl.multiple_of(at, half), half)


def place_kernel(sizes, places, *refs):
    half = sizes[-1]
    for ref, (batch, dg) in zip(refs, places):
        for j, k in enumerate(batch):
            refs[-1][:, column_of(sizes, k, dg)] = ref[:, j * half : (j + 1) * half]


def late_kernel(sizes, places, *refs):
    out_ref, sems = refs[-2:]
    copies = [
        pltpu.make_async_copy(ref, out_ref.at[:, column_of(sizes, batch[0], dg)], sems.at[i])
        for i, (ref, (batch, dg)) in enumerate(zip(refs, places))
    ]
    for copy in copies:
        copy.start()
    for copy in copies:
        copy.wait()


def chip_kernel(replicas, *refs):
    own_ref, came_refs, out_refs = refs[0], refs[1 : 2 * replicas - 1], refs[2 * replicas - 1 :]
    rows = out_refs[0].shape[0]
    split = came_refs[0].shape[1]
    for k, out in enumerate(out_refs):
        for j in range(2):
            at = pl.ds(k * rows, rows), pl.ds(j * split, split)
            total = own_ref[at]
            for ref in came_refs[j::2]:
                total = total + ref[pl.ds(k * rows, rows), :].astype(F32)
            out[:, pl.ds(j * split, split)] = total.astype(out.dtype)


def total_kernel(*refs):
    half_refs, refs = refs[-2:], refs[:-2]
    wide = half_refs[0].shape[1]
    for j, out_ref in enumerate(half_refs):
        at = pl.ds(j * wide, wide)
        total = refs[0][:, at]
        for ref in refs[1:]:
            total = total + ref[:, at].astype(F32)
        out_ref[...] = (ADAPTER_SCALE * total).astype(BF16)


def spread_kernel(width, replicas, *refs):
    core = lax.axis_index("replica")
    down_ref, up_ref = refs[2 * replicas :]
    slots = down_ref.shape[0] // replicas
    rank = down_ref.shape[1]
    wide = refs[0].shape[1]
    for dr in range(replicas):
        at = lax.rem(core + replicas - dr, replicas) * slots
        for j in range(slots):
            rows = slice(j * rank, (j + 1) * rank)
            down_ref[at + j, :, :wide] = refs[2 * dr][rows]
            down_ref[at + j, :, wide:] = refs[2 * dr + 1][rows, : width - wide]
            up_ref[at + j] = refs[2 * dr + 1][rows, width - wide :]


def on_device(
    saved_layer_input,
    value_output_gradient,
    token_adapter_index,
    adapter_slot_index,
    frozen_value_weight,
    adapter_down_weight,
    adapter_up_weight,
):
    inputs = saved_layer_input[0]
    grad_rows = value_output_gradient[0]
    tokens, width = inputs.shape
    value_width = grad_rows.shape[1]
    groups, holders, replicas = (lax.axis_size(a) for a in ("groups", "adapter", "replica"))
    group, here, core = (lax.axis_index(a) for a in ("groups", "adapter", "replica"))
    slots, rank = adapter_down_weight.shape[1:3]
    own_slots = slots // replicas
    rows = own_slots * rank
    frozen = frozen_value_weight[0]
    shard = frozen.shape[0]
    half = shard // groups
    piece = half // replicas
    cols = width + value_width

    tagged = call(
        tag_kernel,
        [jax.ShapeDtypeStruct((tokens, value_width + LANES), BF16)],
        (grad_rows, token_adapter_index[0, :, 0][None], adapter_slot_index),
        scalars=1,
    )[0]
    grads = [tagged] + [
        moved(tagged, lambda g, z, s, r: (g - dg, z, s, r)) for dg in range(1, groups)
    ]

    own = call(
        functools.partial(own_kernel, (groups, holders, shard)),
        [jax.ShapeDtypeStruct((rows, holders * half + value_width), BF16)],
        (adapter_down_weight[0], adapter_up_weight[0]),
    )[0]
    held = [own]
    for k in range(1, holders):
        held.append(moved(own, lambda g, z, s, r: (g, z + k, s, r)))

    ring = [
        pl.pallas_call(
            functools.partial(piece_kernel, replicas),
            out_shape=jax.ShapeDtypeStruct((piece, value_width), BF16),
            in_specs=[pl.BlockSpec(memory_space=pl.ANY)],
            out_specs=pl.BlockSpec(memory_space=pltpu.VMEM),
            scratch_shapes=[pltpu.SemaphoreType.DMA],
            compiler_params=pltpu.CompilerParams(vmem_limit_bytes=GRANT),
            cost_estimate=pl.CostEstimate(flops=1000, bytes_accessed=1000, transcendentals=0),
        )(frozen)
    ]
    ring.append(moved(ring[0], lambda g, z, s, r: (g, z + 1, s, r)))
    held, grads, ring = lax.optimization_barrier((held, grads, ring))
    joined = call(
        join_kernel,
        [
            jax.ShapeDtypeStruct((holders * rows, holders * half), BF16),
            jax.ShapeDtypeStruct((holders * rows, value_width), BF16),
        ],
        held,
    )
    downs, ups = [joined[0]], [joined[1]]
    for dr in range(1, replicas):
        ups.append(moved(ups[0], lambda g, z, s, r: (g, z, s, r + dr)))
        downs.append(moved(downs[0], lambda g, z, s, r: (g, z, s, r + dr)))
    def pieces_of(k, *before):
        if k == 0:
            return [(0, 0)], [frozen]
        mails = [ring[k]]
        if k > 1 and piece % (2 * LANES) == 0:
            shape = jax.ShapeDtypeStruct((piece // 2, value_width), BF16)
            mails = call(split_kernel, [shape] * 2, (ring[k],))
        mails = [after(mail, *before) if before else mail for mail in mails]
        spec, pieces = [(0, 0)], [ring[k]]
        for dr in range(1, replicas):
            for j, mail in enumerate(mails):
                spec.append((dr, j * mail.shape[0]))
                pieces.append(moved(mail, lambda g, z, s, r: (g, z, s, r + dr)))
        if piece % LANES:
            whole = jnp.zeros((half, value_width), BF16)
            for (dr, offset), part in zip(spec, pieces):
                at = ((core - dr) % replicas) * piece + offset
                whole = lax.dynamic_update_slice_in_dim(whole, part, at, axis=0)
            spec, pieces = [(0, 0)], [whole]
        return spec, pieces

    kept = replicas * holders * rows

    def adapter_sums(sel, *before):
        maps = list(downs)
        for dg in range(1, groups):
            maps.append(moved(downs[0], lambda g, z, s, r: (g + dg, z, s, r)))
            for dr in range(1, replicas):
                maps.append(moved(maps[-dr], lambda g, z, s, r: (g, z, s, r + dr)))
        gradients = call(
            functools.partial(adapter_kernel, (groups, holders, replicas, shard, slots, rank)),
            [jax.ShapeDtypeStruct((holders * rows, cols), F32)]
            + [jax.ShapeDtypeStruct((holders * rows, cols // 2), BF16)] * (2 * replicas - 2),
            (inputs, tagged, sel, *maps),
            [jax.ShapeDtypeStruct((kept, width), BF16)],
        )
        part, sent = gradients[0], gradients[1:]
        came = [
            moved(after(sent[2 * dr - 2 + j], *before), lambda g, z, s, r: (g, z, s, r - dr))
            for dr in range(1, replicas)
            for j in range(2)
        ]
        chip = call(
            functools.partial(chip_kernel, replicas),
            [jax.ShapeDtypeStruct((rows, cols), F32)]
            + [jax.ShapeDtypeStruct((rows, cols), BF16)] * (holders - 1),
            (part, *came),
        )
        return part, chip

    batches = [list(range(min(2, holders)))] + [[k] for k in range(2, holders)]
    arrived, crossed = [], []
    for i, batch in enumerate(batches):
        operands, specs = [], []
        for k in batch:
            if k > 1:
                last = after(ring[-1], sel) if k > 2 else ring[-1]
                ring.append(moved(last, lambda g, z, s, r: (g, z + 1, s, r)))
            gate = arrived[0][::-1] if k == 2 else [*arrived[i - 2], chip[0]] if k > 2 else []
            spec, blocks = pieces_of(k, *gate)
            specs.append((k, spec))
            operands += blocks
        out = call(
            functools.partial(
                frozen_kernel, (tokens, groups, holders, replicas, slots, rank), specs
            ),
            (
                [jax.ShapeDtypeStruct((groups * tokens, half), BF16)]
                if i == 1 and len(batches) > 2
                else [jax.ShapeDtypeStruct((tokens, half * len(batch)), BF16)] * groups
            )
            + [jax.ShapeDtypeStruct((groups * tokens, kept), BF16)] * (i == 0),
            [*grads, *downs, *([sel] if i else ups), *operands],
        )
        if i == 0:
            sel = out[groups]
        mails = list(out[:groups])
        if i == 1 and len(batches) > 2:
            got = moved(out[0], lambda g, z, s, r: (g, z, s - 1, r))
            got = [got[dg * tokens : (dg + 1) * tokens] for dg in range(groups)]
            early = [(batches[0], dg) for dg in range(groups)] + [(batch, 0)]
            passed = call(
                functools.partial(place_kernel, (groups, holders, shard, half), early),
                [jax.ShapeDtypeStruct((tokens, width), BF16)],
                [*arrived[0], got[0]],
            )[0]
            got, passed = lax.optimization_barrier((got, passed))
            late = [
                ((batch, dg), moved(got[dg], lambda g, z, s, r: (g + dg, z, s, r)))
                for dg in range(1, groups)
            ]
            arrived.append([])
            continue
        if i > 2:
            mails = [after(mail, *arrived[-1]) for mail in mails]
        arrived.append(
            [moved(mails[dg], lambda g, z, s, r: (g + dg, z, s - 1, r)) for dg in range(groups)]
        )
        if i > 1:
            late += [((batch, dg), arrived[-1][dg]) for dg in reversed(range(groups))]
        if i == 0:
            part, chip = adapter_sums(sel, *arrived[0][::-1])
    sizes = (groups, holders, shard, half)
    if len(batches) > 2:
        passed = pl.pallas_call(
            functools.partial(late_kernel, sizes, [place for place, _ in late]),
            out_shape=jax.ShapeDtypeStruct((tokens, width), BF16),
            in_specs=[pl.BlockSpec(memory_space=pltpu.VMEM)] * len(late)
            + [pl.BlockSpec(memory_space=pl.ANY)],
            out_specs=pl.BlockSpec(memory_space=pl.ANY),
            input_output_aliases={len(late): 0},
            scratch_shapes=[pltpu.SemaphoreType.DMA((len(late),))],
            compiler_params=pltpu.CompilerParams(vmem_limit_bytes=8 * MIB),
            cost_estimate=pl.CostEstimate(flops=1000, bytes_accessed=1000, transcendentals=0),
        )(*[part for _, part in late], passed)
    else:
        passed = call(
            functools.partial(
                place_kernel, sizes, [(batch, dg) for batch in batches for dg in range(groups)]
            ),
            [jax.ShapeDtypeStruct((tokens, width), BF16)],
            [x for got in arrived for x in got],
        )[0]

    sums = [chip[0]] + [
        moved(after(chip[k], ring[-1]), lambda g, z, s, r: (g, z - k, s, r))
        for k in range(1, holders)
    ]
    total = call(total_kernel, [jax.ShapeDtypeStruct((rows, cols // 2), BF16)] * 2, sums)
    totals = list(total)
    for dr in range(1, replicas):
        totals += [moved(x, lambda g, z, s, r: (g, z, s, r + dr)) for x in total]
    totals[0], passed = lax.optimization_barrier((totals[0], passed))
    down_grad, up_grad = call(
        functools.partial(spread_kernel, width, replicas),
        [
            jax.ShapeDtypeStruct((slots, rank, width), BF16),
            jax.ShapeDtypeStruct((slots, rank, value_width), BF16),
        ],
        totals,
    )

    return passed[None], down_grad[None], up_grad[None]


def solution(mesh):
    placed = (
        P("segment", ("groups", "adapter", "replica"), None),
        P("segment", ("groups", "adapter", "replica"), None),
        P("segment", ("groups", "adapter", "replica"), None),
        P("groups"),
        P("segment", "adapter", None),
        P("segment", "adapter", None, None),
        P("segment", "adapter", None, None),
    )
    return jax.shard_map(
        on_device,
        mesh=mesh,
        in_specs=placed,
        out_specs=(
            P("segment", ("groups", "adapter", "replica"), None),
            P(("groups", "segment"), "adapter", None, None),
            P(("groups", "segment"), "adapter", None, None),
        ),
        check_vma=False,
    )
```

```python
import functools
import itertools
import jax
import jax.numpy as jnp
from jax import lax
from jax.experimental import pallas as pl
from jax.experimental.pallas import tpu as pltpu
from jax.sharding import PartitionSpec as P

ADAPTER_SCALE = 2.0
AXES = ("groups", "adapter", "segment", "replica")
LANES = 128
F32 = jnp.float32
BF16 = jnp.bfloat16
MIB = 1024 * 1024


def moved(x, to):
    sizes = [lax.axis_size(a) for a in AXES]
    number = {at: i for i, at in enumerate(itertools.product(*map(range, sizes)))}
    pairs = [
        (i, number[tuple(t % s for t, s in zip(to(*at), sizes))]) for at, i in number.items()
    ]
    return lax.ppermute(x, AXES, pairs)


def after(x, *others):
    return lax.optimization_barrier((x, *others))[0]


def rows_by_rows(a, b):
    return lax.dot_general(a, b, (((1,), (1,)), ((), ())), preferred_element_type=F32)


def columns_by_columns(a, b):
    return lax.dot_general(a, b, (((0,), (0,)), ((), ())), preferred_element_type=F32)


def call(kernel, out_shape, operands, scratch=(), scalars=0):
    held = sum(x.size * x.dtype.itemsize for x in (*operands, *out_shape, *scratch))
    return pl.pallas_call(
        kernel,
        out_shape=out_shape,
        in_specs=[pl.BlockSpec(memory_space=pltpu.VMEM)] * (len(operands) - scalars)
        + [pl.BlockSpec(memory_space=pltpu.SMEM)] * scalars,
        scratch_shapes=[pltpu.VMEM(x.shape, x.dtype) for x in scratch],
        compiler_params=pltpu.CompilerParams(vmem_limit_bytes=2 * held + 4 * MIB),
        cost_estimate=pl.CostEstimate(flops=1000, bytes_accessed=1000, transcendentals=0),
    )(*operands)


def slots_of(tagged_ref):
    return tagged_ref[:, -LANES:].astype(F32)[:, :1]


def row_slots(holders, replicas, slots, rank, dr):
    here, core = lax.axis_index("adapter"), lax.axis_index("replica")
    own_slots = slots // replicas
    lane = lax.broadcasted_iota(jnp.int32, (1, holders * own_slots * rank), 1)
    slot = jnp.zeros_like(lane)
    for k in range(holders):
        for j in range(own_slots):
            start = (k * own_slots + j) * rank
            value = lax.rem(here + holders - k, holders) * slots
            value = value + lax.rem(core + replicas - dr, replicas) * own_slots + j
            slot = jnp.where((lane >= start) & (lane < start + rank), value, slot)
    return slot.astype(F32)


def tag_kernel(g_ref, name_ref, slot_ref, out_ref):
    out_ref[:, :-LANES] = g_ref[...]
    names = name_ref[...]
    slot = jnp.zeros_like(names)
    for j in range(slot_ref.shape[0]):
        slot = jnp.where(names == j, slot_ref[j], slot)
    ones = jnp.ones((1, LANES), F32)
    out_ref[:, -LANES:] = columns_by_columns(slot.astype(F32), ones).astype(BF16)


def join_kernel(*refs):
    down_ref, up_ref = refs[-2:]
    wide = down_ref.shape[1]
    for k, ref in enumerate(refs[:-2]):
        rows = ref.shape[0]
        down_ref[k * rows : (k + 1) * rows] = ref[:, :wide]
        up_ref[k * rows : (k + 1) * rows] = ref[:, wide:]


def own_kernel(sizes, down_ref, up_ref, out_ref):
    groups, holders, shard = sizes
    half = shard // groups
    rank = down_ref.shape[1]
    slots = out_ref.shape[0] // rank
    first = lax.axis_index("replica") * slots
    for j in range(slots):
        to = pl.ds(j * rank, rank)
        for z in range(holders):
            at = pl.multiple_of(z * shard + lax.axis_index("groups") * half, half)
            out_ref[to, z * half : (z + 1) * half] = down_ref[first + j, :, pl.ds(at, half)]
        out_ref[to, holders * half :] = up_ref[first + j]


def adapter_kernel(sizes, *refs):
    groups, holders, replicas, shard, slots, rank = sizes
    x_ref, g_ref, sel_ref = refs[:3]
    map_refs, refs = refs[3 : 3 + groups * replicas], refs[3 + groups * replicas :]
    own_ref, other_refs, down = refs[0], refs[1:-1], refs[-1]
    group = lax.axis_index("groups")
    tokens, width = x_ref.shape
    rows, cols = own_ref.shape
    half = shard // groups
    for dg in range(groups):
        first = lax.rem(group + groups - dg, groups) * half
        for dr in range(replicas):
            for z in range(holders):
                at = pl.multiple_of(first + z * shard, half)
                down[pl.ds(dr * rows, rows), pl.ds(at, half)] = map_refs[dg * replicas + dr][
                    :, z * half : (z + 1) * half
                ]
    row_slot = [row_slots(holders, replicas, slots, rank, dr) for dr in range(replicas)]
    keep = slots_of(g_ref) == jnp.concatenate(row_slot, axis=1)
    in_sel = jnp.where(keep, rows_by_rows(x_ref[...], down[...]), 0.0).astype(BF16)
    grad_sel = sel_ref[pl.ds(0, tokens), :]
    step, split = 1024, cols // 2
    for at in range(0, cols, step):
        if at < width:
            part = columns_by_columns(grad_sel, x_ref[:, at : at + step])
        else:
            part = columns_by_columns(in_sel, g_ref[:, at - width : at - width + step])
        own_ref[:, at : at + step] = part[:rows]
        for dr in range(1, replicas):
            sent = part[dr * rows : (dr + 1) * rows].astype(BF16)
            for j in range(0, step, LANES):
                ref, to = other_refs[2 * dr - 2 + (at + j) // split], (at + j) % split
                ref[:, to : to + LANES] = sent[:, j : j + LANES]


def frozen_kernel(sizes, batch, *refs):
    tokens, groups, holders, replicas, slots, rank = sizes
    g_refs, refs = refs[:groups], refs[groups:]
    down_refs, refs = refs[:replicas], refs[replicas:]
    core, here = lax.axis_index("replica"), lax.axis_index("adapter")
    rows = down_refs[0].shape[0]
    half = down_refs[0].shape[1] // holders
    if batch[0][0] == 0:
        up_refs, refs = refs[:replicas], refs[replicas:]
        sel_ref = refs[-1]
        out_refs = refs[-1 - groups : -1]
        for dg in range(groups):
            for dr in range(replicas):
                keep = slots_of(g_refs[dg]) == row_slots(holders, replicas, slots, rank, dr)
                proj_grad = rows_by_rows(g_refs[dg][:, :-LANES], up_refs[dr][...])
                sel_ref[pl.ds(dg * tokens, tokens), dr * rows : (dr + 1) * rows] = jnp.where(
                    keep, proj_grad, 0.0
                ).astype(BF16)
    else:
        sel_ref, refs = refs[0], refs[1:]
        out_refs = refs[-groups:]
        if refs[-1].shape[0] > tokens:
            out_refs = [refs[-1].at[pl.ds(dg * tokens, tokens)] for dg in range(groups)]
    for i, (k, spec) in enumerate(batch):
        shard_at = lax.rem(here + holders - k, holders) * half
        for (dr, offset), block in zip(spec, refs):
            if k == 0:
                first = pl.multiple_of(lax.axis_index("groups") * half, half)
                block = block.at[pl.ds(first, half)]
            wide = block.shape[0]
            at = 0
            if wide < half:
                at = lax.rem(core + replicas - dr, replicas) * (half // replicas) + offset
            columns = pl.ds(pl.multiple_of(shard_at + at, wide), wide)
            for dg in range(groups):
                base = rows_by_rows(g_refs[dg][:, :-LANES], block[...]).astype(BF16)
                lora = 0.0
                for j in range(replicas):
                    lora = lora + jnp.dot(
                        sel_ref[pl.ds(dg * tokens, tokens), j * rows : (j + 1) * rows],
                        down_refs[j][:, columns],
                        preferred_element_type=F32,
                    )
                lora = (ADAPTER_SCALE * lora).astype(BF16)
                out_refs[dg][:, pl.ds(pl.multiple_of(i * half + at, wide), wide)] = (
                    base.astype(F32) + lora.astype(F32)
                ).astype(BF16)
        refs = refs[len(spec) :]


def split_kernel(block_ref, *part_refs):
    rows = part_refs[0].shape[0]
    for j, ref in enumerate(part_refs):
        ref[...] = block_ref[j * rows : (j + 1) * rows]


def column_of(sizes, k, dg):
    groups, holders, shard, half = sizes
    group, here = lax.axis_index("groups"), lax.axis_index("adapter")
    source = lax.rem(group + groups - dg, groups)
    at = lax.rem(here + holders - k, holders) * shard + source * half
    return pl.ds(pl.multiple_of(at, half), half)


def place_kernel(sizes, places, *refs):
    half = sizes[-1]
    for ref, (batch, dg) in zip(refs, places):
        for j, k in enumerate(batch):
            refs[-1][:, column_of(sizes, k, dg)] = ref[:, j * half : (j + 1) * half]


def late_kernel(sizes, places, *refs):
    out_ref, sems = refs[-2:]
    copies = [
        pltpu.make_async_copy(ref, out_ref.at[:, column_of(sizes, batch[0], dg)], sems.at[i])
        for i, (ref, (batch, dg)) in enumerate(zip(refs, places))
    ]
    for copy in copies:
        copy.start()
    for copy in copies:
        copy.wait()


def chip_kernel(replicas, *refs):
    own_ref, came_refs, out_refs = refs[0], refs[1 : 2 * replicas - 1], refs[2 * replicas - 1 :]
    rows = out_refs[0].shape[0]
    split = came_refs[0].shape[1]
    for k, out in enumerate(out_refs):
        for j in range(2):
            at = pl.ds(k * rows, rows), pl.ds(j * split, split)
            total = own_ref[at]
            for ref in came_refs[j::2]:
                total = total + ref[pl.ds(k * rows, rows), :].astype(F32)
            out[:, pl.ds(j * split, split)] = total.astype(out.dtype)


def total_kernel(*refs):
    half_refs, refs = refs[-2:], refs[:-2]
    wide = half_refs[0].shape[1]
    for j, out_ref in enumerate(half_refs):
        at = pl.ds(j * wide, wide)
        total = refs[0][:, at]
        for ref in refs[1:]:
            total = total + ref[:, at].astype(F32)
        out_ref[...] = (ADAPTER_SCALE * total).astype(BF16)


def spread_kernel(width, replicas, *refs):
    core = lax.axis_index("replica")
    down_ref, up_ref = refs[2 * replicas :]
    slots = down_ref.shape[0] // replicas
    rank = down_ref.shape[1]
    wide = refs[0].shape[1]
    for dr in range(replicas):
        at = lax.rem(core + replicas - dr, replicas) * slots
        for j in range(slots):
            rows = slice(j * rank, (j + 1) * rank)
            down_ref[at + j, :, :wide] = refs[2 * dr][rows]
            down_ref[at + j, :, wide:] = refs[2 * dr + 1][rows, : width - wide]
            up_ref[at + j] = refs[2 * dr + 1][rows, width - wide :]


def on_device(
    saved_layer_input,
    value_output_gradient,
    token_adapter_index,
    adapter_slot_index,
    frozen_value_weight,
    adapter_down_weight,
    adapter_up_weight,
):
    inputs = saved_layer_input[0]
    grad_rows = value_output_gradient[0]
    tokens, width = inputs.shape
    value_width = grad_rows.shape[1]
    groups, holders, replicas = (lax.axis_size(a) for a in ("groups", "adapter", "replica"))
    group, here, core = (lax.axis_index(a) for a in ("groups", "adapter", "replica"))
    slots, rank = adapter_down_weight.shape[1:3]
    own_slots = slots // replicas
    rows = own_slots * rank
    frozen = frozen_value_weight[0]
    shard = frozen.shape[0]
    half = shard // groups
    piece = half // replicas
    cols = width + value_width

    tagged = call(
        tag_kernel,
        [jax.ShapeDtypeStruct((tokens, value_width + LANES), BF16)],
        (grad_rows, token_adapter_index[0, :, 0][None], adapter_slot_index),
        scalars=1,
    )[0]
    grads = [tagged] + [
        moved(tagged, lambda g, z, s, r: (g - dg, z, s, r)) for dg in range(1, groups)
    ]

    own = call(
        functools.partial(own_kernel, (groups, holders, shard)),
        [jax.ShapeDtypeStruct((rows, holders * half + value_width), BF16)],
        (adapter_down_weight[0], adapter_up_weight[0]),
    )[0]
    held = [own]
    for k in range(1, holders):
        held.append(moved(held[-1], lambda g, z, s, r: (g, z + 1, s, r)))

    ring = [lax.dynamic_slice_in_dim(frozen, (group * replicas + core) * piece, piece, axis=0)]
    ring.append(moved(ring[0], lambda g, z, s, r: (g, z + 1, s, r)))
    held, grads, ring = lax.optimization_barrier((held, grads, ring))
    joined = call(
        join_kernel,
        [
            jax.ShapeDtypeStruct((holders * rows, holders * half), BF16),
            jax.ShapeDtypeStruct((holders * rows, value_width), BF16),
        ],
        held,
    )
    downs, ups = [joined[0]], [joined[1]]
    for dr in range(1, replicas):
        ups.append(moved(ups[0], lambda g, z, s, r: (g, z, s, r + dr)))
        downs.append(moved(downs[0], lambda g, z, s, r: (g, z, s, r + dr)))
    def pieces_of(k, *before):
        if k == 0:
            return [(0, 0)], [frozen]
        mails = [ring[k]]
        if k > 1 and piece % (2 * LANES) == 0:
            shape = jax.ShapeDtypeStruct((piece // 2, value_width), BF16)
            mails = call(split_kernel, [shape] * 2, (ring[k],))
        mails = [after(mail, *before) if before else mail for mail in mails]
        spec, pieces = [(0, 0)], [ring[k]]
        for dr in range(1, replicas):
            for j, mail in enumerate(mails):
                spec.append((dr, j * mail.shape[0]))
                pieces.append(moved(mail, lambda g, z, s, r: (g, z, s, r + dr)))
        if piece % LANES:
            whole = jnp.zeros((half, value_width), BF16)
            for (dr, offset), part in zip(spec, pieces):
                at = ((core - dr) % replicas) * piece + offset
                whole = lax.dynamic_update_slice_in_dim(whole, part, at, axis=0)
            spec, pieces = [(0, 0)], [whole]
        return spec, pieces

    kept = replicas * holders * rows

    def adapter_sums(sel, *before):
        maps = list(downs)
        for dg in range(1, groups):
            maps.append(moved(downs[0], lambda g, z, s, r: (g + dg, z, s, r)))
            for dr in range(1, replicas):
                maps.append(moved(maps[-dr], lambda g, z, s, r: (g, z, s, r + dr)))
        gradients = call(
            functools.partial(adapter_kernel, (groups, holders, replicas, shard, slots, rank)),
            [jax.ShapeDtypeStruct((holders * rows, cols), F32)]
            + [jax.ShapeDtypeStruct((holders * rows, cols // 2), BF16)] * (2 * replicas - 2),
            (inputs, tagged, sel, *maps),
            [jax.ShapeDtypeStruct((kept, width), BF16)],
        )
        part, sent = gradients[0], gradients[1:]
        came = [
            moved(after(sent[2 * dr - 2 + j], *before), lambda g, z, s, r: (g, z, s, r - dr))
            for dr in range(1, replicas)
            for j in range(2)
        ]
        chip = call(
            functools.partial(chip_kernel, replicas),
            [jax.ShapeDtypeStruct((rows, cols), F32)]
            + [jax.ShapeDtypeStruct((rows, cols), BF16)] * (holders - 1),
            (part, *came),
        )
        return part, chip

    batches = [list(range(min(2, holders)))] + [[k] for k in range(2, holders)]
    arrived, crossed = [], []
    for i, batch in enumerate(batches):
        operands, specs = [], []
        for k in batch:
            if k > 1:
                last = after(ring[-1], sel) if k > 2 else ring[-1]
                ring.append(moved(last, lambda g, z, s, r: (g, z + 1, s, r)))
            gate = arrived[0][::-1] if k == 2 else [*arrived[i - 2], chip[0]] if k > 2 else []
            spec, blocks = pieces_of(k, *gate)
            specs.append((k, spec))
            operands += blocks
        out = call(
            functools.partial(
                frozen_kernel, (tokens, groups, holders, replicas, slots, rank), specs
            ),
            (
                [jax.ShapeDtypeStruct((groups * tokens, half), BF16)]
                if i == 1 and len(batches) > 2
                else [jax.ShapeDtypeStruct((tokens, half * len(batch)), BF16)] * groups
            )
            + [jax.ShapeDtypeStruct((groups * tokens, kept), BF16)] * (i == 0),
            [*grads, *downs, *([sel] if i else ups), *operands],
        )
        if i == 0:
            sel = out[groups]
        mails = list(out[:groups])
        if i == 1 and len(batches) > 2:
            got = moved(out[0], lambda g, z, s, r: (g, z, s - 1, r))
            got = [got[dg * tokens : (dg + 1) * tokens] for dg in range(groups)]
            early = [(batches[0], dg) for dg in range(groups)] + [(batch, 0)]
            passed = call(
                functools.partial(place_kernel, (groups, holders, shard, half), early),
                [jax.ShapeDtypeStruct((tokens, width), BF16)],
                [*arrived[0], got[0]],
            )[0]
            got, passed = lax.optimization_barrier((got, passed))
            late = [
                ((batch, dg), moved(got[dg], lambda g, z, s, r: (g + dg, z, s, r)))
                for dg in range(1, groups)
            ]
            arrived.append([])
            continue
        if i > 2:
            mails = [after(mail, *arrived[-1]) for mail in mails]
        arrived.append(
            [moved(mails[dg], lambda g, z, s, r: (g + dg, z, s - 1, r)) for dg in range(groups)]
        )
        if i > 1:
            late += [((batch, dg), arrived[-1][dg]) for dg in reversed(range(groups))]
        if i == 0:
            part, chip = adapter_sums(sel, *arrived[0][::-1])
    sizes = (groups, holders, shard, half)
    if len(batches) > 2:
        passed = pl.pallas_call(
            functools.partial(late_kernel, sizes, [place for place, _ in late]),
            out_shape=jax.ShapeDtypeStruct((tokens, width), BF16),
            in_specs=[pl.BlockSpec(memory_space=pltpu.VMEM)] * len(late)
            + [pl.BlockSpec(memory_space=pl.ANY)],
            out_specs=pl.BlockSpec(memory_space=pl.ANY),
            input_output_aliases={len(late): 0},
            scratch_shapes=[pltpu.SemaphoreType.DMA((len(late),))],
            compiler_params=pltpu.CompilerParams(vmem_limit_bytes=8 * MIB),
            cost_estimate=pl.CostEstimate(flops=1000, bytes_accessed=1000, transcendentals=0),
        )(*[part for _, part in late], passed)
    else:
        passed = call(
            functools.partial(
                place_kernel, sizes, [(batch, dg) for batch in batches for dg in range(groups)]
            ),
            [jax.ShapeDtypeStruct((tokens, width), BF16)],
            [x for got in arrived for x in got],
        )[0]

    sums = [chip[0]] + [
        moved(after(chip[k], ring[-1]), lambda g, z, s, r: (g, z - k, s, r))
        for k in range(1, holders)
    ]
    total = call(total_kernel, [jax.ShapeDtypeStruct((rows, cols // 2), BF16)] * 2, sums)
    totals = list(total)
    for dr in range(1, replicas):
        totals += [moved(x, lambda g, z, s, r: (g, z, s, r + dr)) for x in total]
    down_grad, up_grad = call(
        functools.partial(spread_kernel, width, replicas),
        [
            jax.ShapeDtypeStruct((slots, rank, width), BF16),
            jax.ShapeDtypeStruct((slots, rank, value_width), BF16),
        ],
        totals,
    )

    return passed[None], down_grad[None], up_grad[None]


def solution(mesh):
    placed = (
        P("segment", ("groups", "adapter", "replica"), None),
        P("segment", ("groups", "adapter", "replica"), None),
        P("segment", ("groups", "adapter", "replica"), None),
        P("groups"),
        P("segment", "adapter", None),
        P("segment", "adapter", None, None),
        P("segment", "adapter", None, None),
    )
    return jax.shard_map(
        on_device,
        mesh=mesh,
        in_specs=placed,
        out_specs=(
            P("segment", ("groups", "adapter", "replica"), None),
            P(("groups", "segment"), "adapter", None, None),
            P(("groups", "segment"), "adapter", None, None),
        ),
        check_vma=False,
    )
```

```python
import functools
import itertools
import jax
import jax.numpy as jnp
from jax import lax
from jax.experimental import pallas as pl
from jax.experimental.pallas import tpu as pltpu
from jax.sharding import PartitionSpec as P

ADAPTER_SCALE = 2.0
AXES = ("groups", "adapter", "segment", "replica")
LANES = 128
F32 = jnp.float32
BF16 = jnp.bfloat16
MIB = 1024 * 1024


def moved(x, to):
    sizes = [lax.axis_size(a) for a in AXES]
    number = {at: i for i, at in enumerate(itertools.product(*map(range, sizes)))}
    pairs = [
        (i, number[tuple(t % s for t, s in zip(to(*at), sizes))]) for at, i in number.items()
    ]
    return lax.ppermute(x, AXES, pairs)


def after(x, *others):
    return lax.optimization_barrier((x, *others))[0]


def rows_by_rows(a, b):
    return lax.dot_general(a, b, (((1,), (1,)), ((), ())), preferred_element_type=F32)


def columns_by_columns(a, b):
    return lax.dot_general(a, b, (((0,), (0,)), ((), ())), preferred_element_type=F32)


def call(kernel, out_shape, operands, scratch=(), scalars=0):
    held = sum(x.size * x.dtype.itemsize for x in (*operands, *out_shape, *scratch))
    return pl.pallas_call(
        kernel,
        out_shape=out_shape,
        in_specs=[pl.BlockSpec(memory_space=pltpu.VMEM)] * (len(operands) - scalars)
        + [pl.BlockSpec(memory_space=pltpu.SMEM)] * scalars,
        scratch_shapes=[pltpu.VMEM(x.shape, x.dtype) for x in scratch],
        compiler_params=pltpu.CompilerParams(vmem_limit_bytes=2 * held + 4 * MIB),
        cost_estimate=pl.CostEstimate(flops=1000, bytes_accessed=1000, transcendentals=0),
    )(*operands)


def slots_of(tagged_ref):
    return tagged_ref[:, -LANES:].astype(F32)[:, :1]


def row_slots(holders, replicas, slots, rank, dr):
    here, core = lax.axis_index("adapter"), lax.axis_index("replica")
    own_slots = slots // replicas
    lane = lax.broadcasted_iota(jnp.int32, (1, holders * own_slots * rank), 1)
    slot = jnp.zeros_like(lane)
    for k in range(holders):
        for j in range(own_slots):
            start = (k * own_slots + j) * rank
            value = lax.rem(here + holders - k, holders) * slots
            value = value + lax.rem(core + replicas - dr, replicas) * own_slots + j
            slot = jnp.where((lane >= start) & (lane < start + rank), value, slot)
    return slot.astype(F32)


def tag_kernel(g_ref, name_ref, slot_ref, out_ref):
    out_ref[:, :-LANES] = g_ref[...]
    names = name_ref[...]
    slot = jnp.zeros_like(names)
    for j in range(slot_ref.shape[0]):
        slot = jnp.where(names == j, slot_ref[j], slot)
    ones = jnp.ones((1, LANES), F32)
    out_ref[:, -LANES:] = columns_by_columns(slot.astype(F32), ones).astype(BF16)


def join_kernel(*refs):
    down_ref, up_ref = refs[-2:]
    wide = down_ref.shape[1]
    for k, ref in enumerate(refs[:-2]):
        rows = ref.shape[0]
        down_ref[k * rows : (k + 1) * rows] = ref[:, :wide]
        up_ref[k * rows : (k + 1) * rows] = ref[:, wide:]


def own_kernel(sizes, down_ref, up_ref, out_ref):
    groups, holders, shard = sizes
    half = shard // groups
    rank = down_ref.shape[1]
    slots = out_ref.shape[0] // rank
    first = lax.axis_index("replica") * slots
    for j in range(slots):
        to = pl.ds(j * rank, rank)
        for z in range(holders):
            at = pl.multiple_of(z * shard + lax.axis_index("groups") * half, half)
            out_ref[to, z * half : (z + 1) * half] = down_ref[first + j, :, pl.ds(at, half)]
        out_ref[to, holders * half :] = up_ref[first + j]


def adapter_kernel(sizes, *refs):
    groups, holders, replicas, shard, slots, rank = sizes
    x_ref, g_ref, sel_ref = refs[:3]
    map_refs, refs = refs[3 : 3 + groups * replicas], refs[3 + groups * replicas :]
    own_ref, other_refs, down = refs[0], refs[1:-1], refs[-1]
    group = lax.axis_index("groups")
    tokens, width = x_ref.shape
    rows, cols = own_ref.shape
    half = shard // groups
    for dg in range(groups):
        first = lax.rem(group + groups - dg, groups) * half
        for dr in range(replicas):
            for z in range(holders):
                at = pl.multiple_of(first + z * shard, half)
                down[pl.ds(dr * rows, rows), pl.ds(at, half)] = map_refs[dg * replicas + dr][
                    :, z * half : (z + 1) * half
                ]
    row_slot = [row_slots(holders, replicas, slots, rank, dr) for dr in range(replicas)]
    keep = slots_of(g_ref) == jnp.concatenate(row_slot, axis=1)
    in_sel = jnp.where(keep, rows_by_rows(x_ref[...], down[...]), 0.0).astype(BF16)
    grad_sel = sel_ref[pl.ds(0, tokens), :]
    step, split = 1024, cols // 2
    for at in range(0, cols, step):
        if at < width:
            part = columns_by_columns(grad_sel, x_ref[:, at : at + step])
        else:
            part = columns_by_columns(in_sel, g_ref[:, at - width : at - width + step])
        own_ref[:, at : at + step] = part[:rows]
        for dr in range(1, replicas):
            sent = part[dr * rows : (dr + 1) * rows].astype(BF16)
            for j in range(0, step, LANES):
                ref, to = other_refs[2 * dr - 2 + (at + j) // split], (at + j) % split
                ref[:, to : to + LANES] = sent[:, j : j + LANES]


def frozen_kernel(sizes, batch, *refs):
    tokens, groups, holders, replicas, slots, rank = sizes
    g_refs, refs = refs[:groups], refs[groups:]
    down_refs, refs = refs[:replicas], refs[replicas:]
    core, here = lax.axis_index("replica"), lax.axis_index("adapter")
    rows = down_refs[0].shape[0]
    half = down_refs[0].shape[1] // holders
    if batch[0][0] == 0:
        up_refs, refs = refs[:replicas], refs[replicas:]
        sel_ref = refs[-1]
        out_refs = refs[-1 - groups : -1]
        for dg in range(groups):
            for dr in range(replicas):
                keep = slots_of(g_refs[dg]) == row_slots(holders, replicas, slots, rank, dr)
                proj_grad = rows_by_rows(g_refs[dg][:, :-LANES], up_refs[dr][...])
                sel_ref[pl.ds(dg * tokens, tokens), dr * rows : (dr + 1) * rows] = jnp.where(
                    keep, proj_grad, 0.0
                ).astype(BF16)
    else:
        sel_ref, refs = refs[0], refs[1:]
        out_refs = refs[-groups:]
        if refs[-1].shape[0] > tokens:
            out_refs = [refs[-1].at[pl.ds(dg * tokens, tokens)] for dg in range(groups)]
    for i, (k, spec) in enumerate(batch):
        shard_at = lax.rem(here + holders - k, holders) * half
        for (dr, offset), block in zip(spec, refs):
            if k == 0:
                first = pl.multiple_of(lax.axis_index("groups") * half, half)
                block = block.at[pl.ds(first, half)]
            wide = block.shape[0]
            at = 0
            if wide < half:
                at = lax.rem(core + replicas - dr, replicas) * (half // replicas) + offset
            columns = pl.ds(pl.multiple_of(shard_at + at, wide), wide)
            for dg in range(groups):
                base = rows_by_rows(g_refs[dg][:, :-LANES], block[...]).astype(BF16)
                lora = 0.0
                for j in range(replicas):
                    lora = lora + jnp.dot(
                        sel_ref[pl.ds(dg * tokens, tokens), j * rows : (j + 1) * rows],
                        down_refs[j][:, columns],
                        preferred_element_type=F32,
                    )
                lora = (ADAPTER_SCALE * lora).astype(BF16)
                out_refs[dg][:, pl.ds(pl.multiple_of(i * half + at, wide), wide)] = (
                    base.astype(F32) + lora.astype(F32)
                ).astype(BF16)
        refs = refs[len(spec) :]


def split_kernel(block_ref, *part_refs):
    rows = part_refs[0].shape[0]
    for j, ref in enumerate(part_refs):
        ref[...] = block_ref[j * rows : (j + 1) * rows]


def column_of(sizes, k, dg):
    groups, holders, shard, half = sizes
    group, here = lax.axis_index("groups"), lax.axis_index("adapter")
    source = lax.rem(group + groups - dg, groups)
    at = lax.rem(here + holders - k, holders) * shard + source * half
    return pl.ds(pl.multiple_of(at, half), half)


def place_kernel(sizes, places, *refs):
    half = sizes[-1]
    for ref, (batch, dg) in zip(refs, places):
        for j, k in enumerate(batch):
            refs[-1][:, column_of(sizes, k, dg)] = ref[:, j * half : (j + 1) * half]


def late_kernel(sizes, places, *refs):
    out_ref, sems = refs[-2:]
    copies = [
        pltpu.make_async_copy(ref, out_ref.at[:, column_of(sizes, batch[0], dg)], sems.at[i])
        for i, (ref, (batch, dg)) in enumerate(zip(refs, places))
    ]
    for copy in copies:
        copy.start()
    for copy in copies:
        copy.wait()


def chip_kernel(replicas, *refs):
    own_ref, came_refs, out_refs = refs[0], refs[1 : 2 * replicas - 1], refs[2 * replicas - 1 :]
    rows = out_refs[0].shape[0]
    split = came_refs[0].shape[1]
    for k, out in enumerate(out_refs):
        for j in range(2):
            at = pl.ds(k * rows, rows), pl.ds(j * split, split)
            total = own_ref[at]
            for ref in came_refs[j::2]:
                total = total + ref[pl.ds(k * rows, rows), :].astype(F32)
            out[:, pl.ds(j * split, split)] = total.astype(out.dtype)


def total_kernel(*refs):
    half_refs, refs = refs[-2:], refs[:-2]
    wide = half_refs[0].shape[1]
    for j, out_ref in enumerate(half_refs):
        at = pl.ds(j * wide, wide)
        total = refs[0][:, at]
        for ref in refs[1:]:
            total = total + ref[:, at].astype(F32)
        out_ref[...] = (ADAPTER_SCALE * total).astype(BF16)


def spread_kernel(width, replicas, *refs):
    core = lax.axis_index("replica")
    down_ref, up_ref = refs[2 * replicas :]
    slots = down_ref.shape[0] // replicas
    rank = down_ref.shape[1]
    wide = refs[0].shape[1]
    for dr in range(replicas):
        at = lax.rem(core + replicas - dr, replicas) * slots
        for j in range(slots):
            rows = slice(j * rank, (j + 1) * rank)
            down_ref[at + j, :, :wide] = refs[2 * dr][rows]
            down_ref[at + j, :, wide:] = refs[2 * dr + 1][rows, : width - wide]
            up_ref[at + j] = refs[2 * dr + 1][rows, width - wide :]


def on_device(
    saved_layer_input,
    value_output_gradient,
    token_adapter_index,
    adapter_slot_index,
    frozen_value_weight,
    adapter_down_weight,
    adapter_up_weight,
):
    inputs = saved_layer_input[0]
    grad_rows = value_output_gradient[0]
    tokens, width = inputs.shape
    value_width = grad_rows.shape[1]
    groups, holders, replicas = (lax.axis_size(a) for a in ("groups", "adapter", "replica"))
    group, here, core = (lax.axis_index(a) for a in ("groups", "adapter", "replica"))
    slots, rank = adapter_down_weight.shape[1:3]
    own_slots = slots // replicas
    rows = own_slots * rank
    frozen = frozen_value_weight[0]
    shard = frozen.shape[0]
    half = shard // groups
    piece = half // replicas
    cols = width + value_width

    tagged = call(
        tag_kernel,
        [jax.ShapeDtypeStruct((tokens, value_width + LANES), BF16)],
        (grad_rows, token_adapter_index[0, :, 0][None], adapter_slot_index),
        scalars=1,
    )[0]
    grads = [tagged] + [
        moved(tagged, lambda g, z, s, r: (g - dg, z, s, r)) for dg in range(1, groups)
    ]

    own = call(
        functools.partial(own_kernel, (groups, holders, shard)),
        [jax.ShapeDtypeStruct((rows, holders * half + value_width), BF16)],
        (adapter_down_weight[0], adapter_up_weight[0]),
    )[0]
    held = [own]
    for k in range(1, holders):
        held.append(moved(own, lambda g, z, s, r: (g, z + k, s, r)))

    ring = [lax.dynamic_slice_in_dim(frozen, (group * replicas + core) * piece, piece, axis=0)]
    ring.append(moved(ring[0], lambda g, z, s, r: (g, z + 1, s, r)))
    held, grads, ring = lax.optimization_barrier((held, grads, ring))
    joined = call(
        join_kernel,
        [
            jax.ShapeDtypeStruct((holders * rows, holders * half), BF16),
            jax.ShapeDtypeStruct((holders * rows, value_width), BF16),
        ],
        held,
    )
    downs, ups = [joined[0]], [joined[1]]
    for dr in range(1, replicas):
        ups.append(moved(ups[0], lambda g, z, s, r: (g, z, s, r + dr)))
        downs.append(moved(downs[0], lambda g, z, s, r: (g, z, s, r + dr)))
    def pieces_of(k, *before):
        if k == 0:
            return [(0, 0)], [frozen]
        mails = [ring[k]]
        if k > 1 and piece % (2 * LANES) == 0:
            shape = jax.ShapeDtypeStruct((piece // 2, value_width), BF16)
            mails = call(split_kernel, [shape] * 2, (ring[k],))
        mails = [after(mail, *before) if before else mail for mail in mails]
        spec, pieces = [(0, 0)], [ring[k]]
        for dr in range(1, replicas):
            for j, mail in enumerate(mails):
                spec.append((dr, j * mail.shape[0]))
                pieces.append(moved(mail, lambda g, z, s, r: (g, z, s, r + dr)))
        if piece % LANES:
            whole = jnp.zeros((half, value_width), BF16)
            for (dr, offset), part in zip(spec, pieces):
                at = ((core - dr) % replicas) * piece + offset
                whole = lax.dynamic_update_slice_in_dim(whole, part, at, axis=0)
            spec, pieces = [(0, 0)], [whole]
        return spec, pieces

    kept = replicas * holders * rows

    def adapter_sums(sel, *before):
        maps = list(downs)
        for dg in range(1, groups):
            maps.append(moved(downs[0], lambda g, z, s, r: (g + dg, z, s, r)))
            for dr in range(1, replicas):
                maps.append(moved(maps[-dr], lambda g, z, s, r: (g, z, s, r + dr)))
        gradients = call(
            functools.partial(adapter_kernel, (groups, holders, replicas, shard, slots, rank)),
            [jax.ShapeDtypeStruct((holders * rows, cols), F32)]
            + [jax.ShapeDtypeStruct((holders * rows, cols // 2), BF16)] * (2 * replicas - 2),
            (inputs, tagged, sel, *maps),
            [jax.ShapeDtypeStruct((kept, width), BF16)],
        )
        part, sent = gradients[0], gradients[1:]
        came = [
            moved(after(sent[2 * dr - 2 + j], *before), lambda g, z, s, r: (g, z, s, r - dr))
            for dr in range(1, replicas)
            for j in range(2)
        ]
        chip = call(
            functools.partial(chip_kernel, replicas),
            [jax.ShapeDtypeStruct((rows, cols), F32)]
            + [jax.ShapeDtypeStruct((rows, cols), BF16)] * (holders - 1),
            (part, *came),
        )
        return part, chip

    batches = [list(range(min(2, holders)))] + [[k] for k in range(2, holders)]
    arrived, crossed = [], []
    for i, batch in enumerate(batches):
        operands, specs = [], []
        for k in batch:
            if k > 1:
                if 2 < k == holders - 1:
                    last = moved(after(ring[0], sel), lambda g, z, s, r: (g, z - 1, s, r))
                else:
                    last = after(ring[-1], sel) if k > 2 else ring[-1]
                    last = moved(last, lambda g, z, s, r: (g, z + 1, s, r))
                ring.append(last)
            gate = arrived[0][::-1] if k == 2 else [*arrived[i - 2], chip[0]] if k > 2 else []
            spec, blocks = pieces_of(k, *gate)
            specs.append((k, spec))
            operands += blocks
        out = call(
            functools.partial(
                frozen_kernel, (tokens, groups, holders, replicas, slots, rank), specs
            ),
            (
                [jax.ShapeDtypeStruct((groups * tokens, half), BF16)]
                if i == 1 and len(batches) > 2
                else [jax.ShapeDtypeStruct((tokens, half * len(batch)), BF16)] * groups
            )
            + [jax.ShapeDtypeStruct((groups * tokens, kept), BF16)] * (i == 0),
            [*grads, *downs, *([sel] if i else ups), *operands],
        )
        if i == 0:
            sel = out[groups]
        mails = list(out[:groups])
        if i == 1 and len(batches) > 2:
            got = moved(out[0], lambda g, z, s, r: (g, z, s - 1, r))
            got = [got[dg * tokens : (dg + 1) * tokens] for dg in range(groups)]
            early = [(batches[0], dg) for dg in range(groups)] + [(batch, 0)]
            passed = call(
                functools.partial(place_kernel, (groups, holders, shard, half), early),
                [jax.ShapeDtypeStruct((tokens, width), BF16)],
                [*arrived[0], got[0]],
            )[0]
            got, passed = lax.optimization_barrier((got, passed))
            late = [
                ((batch, dg), moved(got[dg], lambda g, z, s, r: (g + dg, z, s, r)))
                for dg in range(1, groups)
            ]
            arrived.append([])
            continue
        if i > 2:
            mails = [after(mail, *arrived[-1]) for mail in mails]
        arrived.append(
            [moved(mails[dg], lambda g, z, s, r: (g + dg, z, s - 1, r)) for dg in range(groups)]
        )
        if i > 1:
            late += [((batch, dg), arrived[-1][dg]) for dg in reversed(range(groups))]
        if i == 0:
            part, chip = adapter_sums(sel, *arrived[0][::-1])
    sizes = (groups, holders, shard, half)
    if len(batches) > 2:
        passed = pl.pallas_call(
            functools.partial(late_kernel, sizes, [place for place, _ in late]),
            out_shape=jax.ShapeDtypeStruct((tokens, width), BF16),
            in_specs=[pl.BlockSpec(memory_space=pltpu.VMEM)] * len(late)
            + [pl.BlockSpec(memory_space=pl.ANY)],
            out_specs=pl.BlockSpec(memory_space=pl.ANY),
            input_output_aliases={len(late): 0},
            scratch_shapes=[pltpu.SemaphoreType.DMA((len(late),))],
            compiler_params=pltpu.CompilerParams(vmem_limit_bytes=8 * MIB),
            cost_estimate=pl.CostEstimate(flops=1000, bytes_accessed=1000, transcendentals=0),
        )(*[part for _, part in late], passed)
    else:
        passed = call(
            functools.partial(
                place_kernel, sizes, [(batch, dg) for batch in batches for dg in range(groups)]
            ),
            [jax.ShapeDtypeStruct((tokens, width), BF16)],
            [x for got in arrived for x in got],
        )[0]

    sums = [chip[0]] + [
        moved(after(chip[k], ring[-1]), lambda g, z, s, r: (g, z - k, s, r))
        for k in range(1, holders)
    ]
    total = call(total_kernel, [jax.ShapeDtypeStruct((rows, cols // 2), BF16)] * 2, sums)
    totals = list(total)
    for dr in range(1, replicas):
        totals += [moved(x, lambda g, z, s, r: (g, z, s, r + dr)) for x in total]
    down_grad, up_grad = call(
        functools.partial(spread_kernel, width, replicas),
        [
            jax.ShapeDtypeStruct((slots, rank, width), BF16),
            jax.ShapeDtypeStruct((slots, rank, value_width), BF16),
        ],
        totals,
    )

    return passed[None], down_grad[None], up_grad[None]


def solution(mesh):
    placed = (
        P("segment", ("groups", "adapter", "replica"), None),
        P("segment", ("groups", "adapter", "replica"), None),
        P("segment", ("groups", "adapter", "replica"), None),
        P("groups"),
        P("segment", "adapter", None),
        P("segment", "adapter", None, None),
        P("segment", "adapter", None, None),
    )
    return jax.shard_map(
        on_device,
        mesh=mesh,
        in_specs=placed,
        out_specs=(
            P("segment", ("groups", "adapter", "replica"), None),
            P(("groups", "segment"), "adapter", None, None),
            P(("groups", "segment"), "adapter", None, None),
        ),
        check_vma=False,
    )
```

```python
import functools
import itertools
import jax
import jax.numpy as jnp
from jax import lax
from jax.experimental import pallas as pl
from jax.experimental.pallas import tpu as pltpu
from jax.sharding import PartitionSpec as P

ADAPTER_SCALE = 2.0
AXES = ("groups", "adapter", "segment", "replica")
LANES = 128
F32 = jnp.float32
BF16 = jnp.bfloat16
MIB = 1024 * 1024


def moved(x, to):
    sizes = [lax.axis_size(a) for a in AXES]
    number = {at: i for i, at in enumerate(itertools.product(*map(range, sizes)))}
    pairs = [
        (i, number[tuple(t % s for t, s in zip(to(*at), sizes))]) for at, i in number.items()
    ]
    return lax.ppermute(x, AXES, pairs)


def after(x, *others):
    return lax.optimization_barrier((x, *others))[0]


def rows_by_rows(a, b):
    return lax.dot_general(a, b, (((1,), (1,)), ((), ())), preferred_element_type=F32)


def columns_by_columns(a, b):
    return lax.dot_general(a, b, (((0,), (0,)), ((), ())), preferred_element_type=F32)


def call(kernel, out_shape, operands, scratch=(), scalars=0):
    held = sum(x.size * x.dtype.itemsize for x in (*operands, *out_shape, *scratch))
    return pl.pallas_call(
        kernel,
        out_shape=out_shape,
        in_specs=[pl.BlockSpec(memory_space=pltpu.VMEM)] * (len(operands) - scalars)
        + [pl.BlockSpec(memory_space=pltpu.SMEM)] * scalars,
        scratch_shapes=[pltpu.VMEM(x.shape, x.dtype) for x in scratch],
        compiler_params=pltpu.CompilerParams(vmem_limit_bytes=2 * held + 4 * MIB),
        cost_estimate=pl.CostEstimate(flops=1000, bytes_accessed=1000, transcendentals=0),
    )(*operands)


def slots_of(tagged_ref):
    return tagged_ref[:, -LANES:].astype(F32)[:, :1]


def row_slots(holders, replicas, slots, rank, dr):
    here, core = lax.axis_index("adapter"), lax.axis_index("replica")
    own_slots = slots // replicas
    lane = lax.broadcasted_iota(jnp.int32, (1, holders * own_slots * rank), 1)
    slot = jnp.zeros_like(lane)
    for k in range(holders):
        for j in range(own_slots):
            start = (k * own_slots + j) * rank
            value = lax.rem(here + holders - k, holders) * slots
            value = value + lax.rem(core + replicas - dr, replicas) * own_slots + j
            slot = jnp.where((lane >= start) & (lane < start + rank), value, slot)
    return slot.astype(F32)


def tag_kernel(g_ref, name_ref, slot_ref, out_ref):
    out_ref[:, :-LANES] = g_ref[...]
    names = name_ref[...]
    slot = jnp.zeros_like(names)
    for j in range(slot_ref.shape[0]):
        slot = jnp.where(names == j, slot_ref[j], slot)
    ones = jnp.ones((1, LANES), F32)
    out_ref[:, -LANES:] = columns_by_columns(slot.astype(F32), ones).astype(BF16)


def join_kernel(*refs):
    both_ref, down_ref = refs[-2:]
    for k, ref in enumerate(refs[:-2]):
        rows = ref.shape[0]
        both_ref[k * rows : (k + 1) * rows] = ref[...]
        down_ref[k * rows : (k + 1) * rows] = ref[:, : down_ref.shape[1]]


def own_kernel(sizes, down_ref, up_ref, out_ref):
    groups, holders, shard = sizes
    half = shard // groups
    rank = down_ref.shape[1]
    slots = out_ref.shape[0] // rank
    first = lax.axis_index("replica") * slots
    for j in range(slots):
        to = pl.ds(j * rank, rank)
        for z in range(holders):
            at = pl.multiple_of(z * shard + lax.axis_index("groups") * half, half)
            out_ref[to, z * half : (z + 1) * half] = down_ref[first + j, :, pl.ds(at, half)]
        out_ref[to, holders * half :] = up_ref[first + j]


def adapter_kernel(sizes, *refs):
    groups, holders, replicas, shard, slots, rank = sizes
    x_ref, g_ref, sel_ref = refs[:3]
    map_refs, refs = refs[3 : 3 + groups * replicas], refs[3 + groups * replicas :]
    own_ref, other_refs, down = refs[0], refs[1:-1], refs[-1]
    group = lax.axis_index("groups")
    tokens, width = x_ref.shape
    rows, cols = own_ref.shape
    half = shard // groups
    for dg in range(groups):
        first = lax.rem(group + groups - dg, groups) * half
        for dr in range(replicas):
            for z in range(holders):
                at = pl.multiple_of(first + z * shard, half)
                down[pl.ds(dr * rows, rows), pl.ds(at, half)] = map_refs[dg * replicas + dr][
                    :, z * half : (z + 1) * half
                ]
    row_slot = [row_slots(holders, replicas, slots, rank, dr) for dr in range(replicas)]
    keep = slots_of(g_ref) == jnp.concatenate(row_slot, axis=1)
    in_sel = jnp.where(keep, rows_by_rows(x_ref[...], down[...]), 0.0).astype(BF16)
    grad_sel = sel_ref[pl.ds(0, tokens), :]
    step, split = 1024, cols // 2
    for at in range(0, cols, step):
        if at < width:
            part = columns_by_columns(grad_sel, x_ref[:, at : at + step])
        else:
            part = columns_by_columns(in_sel, g_ref[:, at - width : at - width + step])
        own_ref[:, at : at + step] = part[:rows]
        for dr in range(1, replicas):
            sent = part[dr * rows : (dr + 1) * rows].astype(BF16)
            for j in range(0, step, LANES):
                ref, to = other_refs[2 * dr - 2 + (at + j) // split], (at + j) % split
                ref[:, to : to + LANES] = sent[:, j : j + LANES]


def frozen_kernel(sizes, batch, *refs):
    tokens, groups, holders, replicas, slots, rank = sizes
    g_refs, refs = refs[:groups], refs[groups:]
    map_refs, refs = refs[:replicas], refs[replicas:]
    core, here = lax.axis_index("replica"), lax.axis_index("adapter")
    rows = map_refs[0].shape[0]
    width = map_refs[0].shape[1] - (g_refs[0].shape[1] - LANES)
    half = width // holders
    if batch[0][0] == 0:
        sel_ref = refs[-1]
        out_refs = refs[-1 - groups : -1]
        for dg in range(groups):
            for dr in range(replicas):
                keep = slots_of(g_refs[dg]) == row_slots(holders, replicas, slots, rank, dr)
                proj_grad = rows_by_rows(g_refs[dg][:, :-LANES], map_refs[dr][:, width:])
                sel_ref[pl.ds(dg * tokens, tokens), dr * rows : (dr + 1) * rows] = jnp.where(
                    keep, proj_grad, 0.0
                ).astype(BF16)
    else:
        sel_ref, refs = refs[0], refs[1:]
        out_refs = refs[-groups:]
        if refs[-1].shape[0] > tokens:
            out_refs = [refs[-1].at[pl.ds(dg * tokens, tokens)] for dg in range(groups)]
    for i, (k, spec) in enumerate(batch):
        shard_at = lax.rem(here + holders - k, holders) * half
        for (dr, offset), block in zip(spec, refs):
            if k == 0:
                first = pl.multiple_of(lax.axis_index("groups") * half, half)
                block = block.at[pl.ds(first, half)]
            wide = block.shape[0]
            at = 0
            if wide < half:
                at = lax.rem(core + replicas - dr, replicas) * (half // replicas) + offset
            columns = pl.ds(pl.multiple_of(shard_at + at, wide), wide)
            for dg in range(groups):
                base = rows_by_rows(g_refs[dg][:, :-LANES], block[...]).astype(BF16)
                lora = 0.0
                for j in range(replicas):
                    lora = lora + jnp.dot(
                        sel_ref[pl.ds(dg * tokens, tokens), j * rows : (j + 1) * rows],
                        map_refs[j][:, columns],
                        preferred_element_type=F32,
                    )
                lora = (ADAPTER_SCALE * lora).astype(BF16)
                out_refs[dg][:, pl.ds(pl.multiple_of(i * half + at, wide), wide)] = (
                    base.astype(F32) + lora.astype(F32)
                ).astype(BF16)
        refs = refs[len(spec) :]


def split_kernel(block_ref, *part_refs):
    rows = part_refs[0].shape[0]
    for j, ref in enumerate(part_refs):
        ref[...] = block_ref[j * rows : (j + 1) * rows]


def column_of(sizes, k, dg):
    groups, holders, shard, half = sizes
    group, here = lax.axis_index("groups"), lax.axis_index("adapter")
    source = lax.rem(group + groups - dg, groups)
    at = lax.rem(here + holders - k, holders) * shard + source * half
    return pl.ds(pl.multiple_of(at, half), half)


def place_kernel(sizes, places, *refs):
    half = sizes[-1]
    for ref, (batch, dg) in zip(refs, places):
        for j, k in enumerate(batch):
            refs[-1][:, column_of(sizes, k, dg)] = ref[:, j * half : (j + 1) * half]


def late_kernel(sizes, places, *refs):
    out_ref, sems = refs[-2:]
    copies = [
        pltpu.make_async_copy(ref, out_ref.at[:, column_of(sizes, batch[0], dg)], sems.at[i])
        for i, (ref, (batch, dg)) in enumerate(zip(refs, places))
    ]
    for copy in copies:
        copy.start()
    for copy in copies:
        copy.wait()


def chip_kernel(replicas, *refs):
    own_ref, came_refs, out_refs = refs[0], refs[1 : 2 * replicas - 1], refs[2 * replicas - 1 :]
    rows = out_refs[0].shape[0]
    split = came_refs[0].shape[1]
    for k, out in enumerate(out_refs):
        for j in range(2):
            at = pl.ds(k * rows, rows), pl.ds(j * split, split)
            total = own_ref[at]
            for ref in came_refs[j::2]:
                total = total + ref[pl.ds(k * rows, rows), :].astype(F32)
            out[:, pl.ds(j * split, split)] = total.astype(out.dtype)


def total_kernel(*refs):
    half_refs, refs = refs[-2:], refs[:-2]
    wide = half_refs[0].shape[1]
    for j, out_ref in enumerate(half_refs):
        at = pl.ds(j * wide, wide)
        total = refs[0][:, at]
        for ref in refs[1:]:
            total = total + ref[:, at].astype(F32)
        out_ref[...] = (ADAPTER_SCALE * total).astype(BF16)


def spread_kernel(width, replicas, *refs):
    core = lax.axis_index("replica")
    down_ref, up_ref = refs[2 * replicas :]
    slots = down_ref.shape[0] // replicas
    rank = down_ref.shape[1]
    wide = refs[0].shape[1]
    for dr in range(replicas):
        at = lax.rem(core + replicas - dr, replicas) * slots
        for j in range(slots):
            rows = slice(j * rank, (j + 1) * rank)
            down_ref[at + j, :, :wide] = refs[2 * dr][rows]
            down_ref[at + j, :, wide:] = refs[2 * dr + 1][rows, : width - wide]
            up_ref[at + j] = refs[2 * dr + 1][rows, width - wide :]


def on_device(
    saved_layer_input,
    value_output_gradient,
    token_adapter_index,
    adapter_slot_index,
    frozen_value_weight,
    adapter_down_weight,
    adapter_up_weight,
):
    inputs = saved_layer_input[0]
    grad_rows = value_output_gradient[0]
    tokens, width = inputs.shape
    value_width = grad_rows.shape[1]
    groups, holders, replicas = (lax.axis_size(a) for a in ("groups", "adapter", "replica"))
    group, here, core = (lax.axis_index(a) for a in ("groups", "adapter", "replica"))
    slots, rank = adapter_down_weight.shape[1:3]
    own_slots = slots // replicas
    rows = own_slots * rank
    frozen = frozen_value_weight[0]
    shard = frozen.shape[0]
    half = shard // groups
    piece = half // replicas
    cols = width + value_width

    tagged = call(
        tag_kernel,
        [jax.ShapeDtypeStruct((tokens, value_width + LANES), BF16)],
        (grad_rows, token_adapter_index[0, :, 0][None], adapter_slot_index),
        scalars=1,
    )[0]
    grads = [tagged] + [
        moved(tagged, lambda g, z, s, r: (g - dg, z, s, r)) for dg in range(1, groups)
    ]

    own = call(
        functools.partial(own_kernel, (groups, holders, shard)),
        [jax.ShapeDtypeStruct((rows, holders * half + value_width), BF16)],
        (adapter_down_weight[0], adapter_up_weight[0]),
    )[0]
    held = [own]
    for k in range(1, holders):
        held.append(moved(own, lambda g, z, s, r: (g, z + k, s, r)))

    ring = [lax.dynamic_slice_in_dim(frozen, (group * replicas + core) * piece, piece, axis=0)]
    ring.append(moved(ring[0], lambda g, z, s, r: (g, z + 1, s, r)))
    held, grads, ring = lax.optimization_barrier((held, grads, ring))
    both, downs = call(
        join_kernel,
        [
            jax.ShapeDtypeStruct((holders * rows, holders * half + value_width), BF16),
            jax.ShapeDtypeStruct((holders * rows, holders * half), BF16),
        ],
        held,
    )
    both = [both] + [
        moved(both, lambda g, z, s, r: (g, z, s, r + dr)) for dr in range(1, replicas)
    ]

    def pieces_of(k, *before):
        if k == 0:
            return [(0, 0)], [frozen]
        mails = [ring[k]]
        if k > 1 and piece % (2 * LANES) == 0:
            shape = jax.ShapeDtypeStruct((piece // 2, value_width), BF16)
            mails = call(split_kernel, [shape] * 2, (ring[k],))
        mails = [after(mail, *before) if before else mail for mail in mails]
        spec, pieces = [(0, 0)], [ring[k]]
        for dr in range(1, replicas):
            for j, mail in enumerate(mails):
                spec.append((dr, j * mail.shape[0]))
                pieces.append(moved(mail, lambda g, z, s, r: (g, z, s, r + dr)))
        if piece % LANES:
            whole = jnp.zeros((half, value_width), BF16)
            for (dr, offset), part in zip(spec, pieces):
                at = ((core - dr) % replicas) * piece + offset
                whole = lax.dynamic_update_slice_in_dim(whole, part, at, axis=0)
            spec, pieces = [(0, 0)], [whole]
        return spec, pieces

    kept = replicas * holders * rows

    def adapter_sums(sel, *before):
        maps = list(both)
        for dg in range(1, groups):
            maps.append(moved(downs, lambda g, z, s, r: (g + dg, z, s, r)))
            for dr in range(1, replicas):
                maps.append(moved(maps[-dr], lambda g, z, s, r: (g, z, s, r + dr)))
        gradients = call(
            functools.partial(adapter_kernel, (groups, holders, replicas, shard, slots, rank)),
            [jax.ShapeDtypeStruct((holders * rows, cols), F32)]
            + [jax.ShapeDtypeStruct((holders * rows, cols // 2), BF16)] * (2 * replicas - 2),
            (inputs, tagged, sel, *maps),
            [jax.ShapeDtypeStruct((kept, width), BF16)],
        )
        part, sent = gradients[0], gradients[1:]
        came = [
            moved(after(sent[2 * dr - 2 + j], *before), lambda g, z, s, r: (g, z, s, r - dr))
            for dr in range(1, replicas)
            for j in range(2)
        ]
        chip = call(
            functools.partial(chip_kernel, replicas),
            [jax.ShapeDtypeStruct((rows, cols), F32)]
            + [jax.ShapeDtypeStruct((rows, cols), BF16)] * (holders - 1),
            (part, *came),
        )
        return part, chip

    batches = [list(range(min(2, holders)))] + [[k] for k in range(2, holders)]
    arrived, crossed = [], []
    for i, batch in enumerate(batches):
        operands, specs = [], []
        for k in batch:
            if k > 1:
                if 2 < k == holders - 1:
                    last = moved(after(ring[0], sel), lambda g, z, s, r: (g, z - 1, s, r))
                else:
                    last = after(ring[-1], sel) if k > 2 else ring[-1]
                    last = moved(last, lambda g, z, s, r: (g, z + 1, s, r))
                ring.append(last)
            gate = arrived[0] if k == 2 else [*arrived[i - 2]] if k > 2 else []
            spec, blocks = pieces_of(k, *gate)
            specs.append((k, spec))
            operands += blocks
        tokens_in = [after(grads[0], part), *grads[1:]] if i == 1 else grads
        out = call(
            functools.partial(
                frozen_kernel, (tokens, groups, holders, replicas, slots, rank), specs
            ),
            (
                [jax.ShapeDtypeStruct((groups * tokens, half), BF16)]
                if i == 1 and len(batches) > 2
                else [jax.ShapeDtypeStruct((tokens, half * len(batch)), BF16)] * groups
            )
            + [jax.ShapeDtypeStruct((groups * tokens, kept), BF16)] * (i == 0),
            [*tokens_in, *both, *([sel] if i else []), *operands],
        )
        if i == 0:
            sel = out[groups]
        mails = list(out[:groups])
        if i == 1 and len(batches) > 2:
            got = moved(out[0], lambda g, z, s, r: (g, z, s - 1, r))
            got = [got[dg * tokens : (dg + 1) * tokens] for dg in range(groups)]
            early = [(batches[0], dg) for dg in range(groups)] + [(batch, 0)]
            passed = call(
                functools.partial(place_kernel, (groups, holders, shard, half), early),
                [jax.ShapeDtypeStruct((tokens, width), BF16)],
                [*arrived[0], got[0]],
            )[0]
            got, passed = lax.optimization_barrier((got, passed))
            late = [
                ((batch, dg), moved(got[dg], lambda g, z, s, r: (g + dg, z, s, r)))
                for dg in range(1, groups)
            ]
            arrived.append([])
            continue
        if i > 2:
            mails = [after(mail, *arrived[-1]) for mail in mails]
        arrived.append(
            [moved(mails[dg], lambda g, z, s, r: (g + dg, z, s - 1, r)) for dg in range(groups)]
        )
        if i > 1:
            late += [((batch, dg), arrived[-1][dg]) for dg in reversed(range(groups))]
        if i == 0:
            part, chip = adapter_sums(sel, *arrived[0])
    sizes = (groups, holders, shard, half)
    if len(batches) > 2:
        passed = pl.pallas_call(
            functools.partial(late_kernel, sizes, [place for place, _ in late]),
            out_shape=jax.ShapeDtypeStruct((tokens, width), BF16),
            in_specs=[pl.BlockSpec(memory_space=pltpu.VMEM)] * len(late)
            + [pl.BlockSpec(memory_space=pl.ANY)],
            out_specs=pl.BlockSpec(memory_space=pl.ANY),
            input_output_aliases={len(late): 0},
            scratch_shapes=[pltpu.SemaphoreType.DMA((len(late),))],
            compiler_params=pltpu.CompilerParams(vmem_limit_bytes=8 * MIB),
            cost_estimate=pl.CostEstimate(flops=1000, bytes_accessed=1000, transcendentals=0),
        )(*[part for _, part in late], passed)
    else:
        passed = call(
            functools.partial(
                place_kernel, sizes, [(batch, dg) for batch in batches for dg in range(groups)]
            ),
            [jax.ShapeDtypeStruct((tokens, width), BF16)],
            [x for got in arrived for x in got],
        )[0]

    sums = [chip[0]] + [
        moved(after(chip[k], ring[-1]), lambda g, z, s, r: (g, z - k, s, r))
        for k in range(1, holders)
    ]
    total = call(total_kernel, [jax.ShapeDtypeStruct((rows, cols // 2), BF16)] * 2, sums)
    totals = list(total)
    for dr in range(1, replicas):
        totals += [moved(x, lambda g, z, s, r: (g, z, s, r + dr)) for x in total]
    down_grad, up_grad = call(
        functools.partial(spread_kernel, width, replicas),
        [
            jax.ShapeDtypeStruct((slots, rank, width), BF16),
            jax.ShapeDtypeStruct((slots, rank, value_width), BF16),
        ],
        totals,
    )

    return passed[None], down_grad[None], up_grad[None]


def solution(mesh):
    placed = (
        P("segment", ("groups", "adapter", "replica"), None),
        P("segment", ("groups", "adapter", "replica"), None),
        P("segment", ("groups", "adapter", "replica"), None),
        P("groups"),
        P("segment", "adapter", None),
        P("segment", "adapter", None, None),
        P("segment", "adapter", None, None),
    )
    return jax.shard_map(
        on_device,
        mesh=mesh,
        in_specs=placed,
        out_specs=(
            P("segment", ("groups", "adapter", "replica"), None),
            P(("groups", "segment"), "adapter", None, None),
            P(("groups", "segment"), "adapter", None, None),
        ),
        check_vma=False,
    )
```

```python
import functools
import itertools
import jax
import jax.numpy as jnp
from jax import lax
from jax.experimental import pallas as pl
from jax.experimental.pallas import tpu as pltpu
from jax.sharding import PartitionSpec as P

ADAPTER_SCALE = 2.0
AXES = ("groups", "adapter", "segment", "replica")
LANES = 128
F32 = jnp.float32
BF16 = jnp.bfloat16
MIB = 1024 * 1024


def moved(x, to):
    sizes = [lax.axis_size(a) for a in AXES]
    number = {at: i for i, at in enumerate(itertools.product(*map(range, sizes)))}
    pairs = [
        (i, number[tuple(t % s for t, s in zip(to(*at), sizes))]) for at, i in number.items()
    ]
    return lax.ppermute(x, AXES, pairs)


def after(x, *others):
    return lax.optimization_barrier((x, *others))[0]


def rows_by_rows(a, b):
    return lax.dot_general(a, b, (((1,), (1,)), ((), ())), preferred_element_type=F32)


def columns_by_columns(a, b):
    return lax.dot_general(a, b, (((0,), (0,)), ((), ())), preferred_element_type=F32)


def call(kernel, out_shape, operands, scratch=(), scalars=0):
    held = sum(x.size * x.dtype.itemsize for x in (*operands, *out_shape, *scratch))
    return pl.pallas_call(
        kernel,
        out_shape=out_shape,
        in_specs=[pl.BlockSpec(memory_space=pltpu.VMEM)] * (len(operands) - scalars)
        + [pl.BlockSpec(memory_space=pltpu.SMEM)] * scalars,
        scratch_shapes=[pltpu.VMEM(x.shape, x.dtype) for x in scratch],
        compiler_params=pltpu.CompilerParams(vmem_limit_bytes=2 * held + 4 * MIB),
        cost_estimate=pl.CostEstimate(flops=1000, bytes_accessed=1000, transcendentals=0),
    )(*operands)


def slots_of(tagged_ref):
    return tagged_ref[:, -LANES:].astype(F32)[:, :1]


def row_slots(holders, replicas, slots, rank, dr):
    here, core = lax.axis_index("adapter"), lax.axis_index("replica")
    own_slots = slots // replicas
    lane = lax.broadcasted_iota(jnp.int32, (1, holders * own_slots * rank), 1)
    slot = jnp.zeros_like(lane)
    for k in range(holders):
        for j in range(own_slots):
            start = (k * own_slots + j) * rank
            value = lax.rem(here + holders - k, holders) * slots
            value = value + lax.rem(core + replicas - dr, replicas) * own_slots + j
            slot = jnp.where((lane >= start) & (lane < start + rank), value, slot)
    return slot.astype(F32)


def tag_kernel(g_ref, name_ref, slot_ref, out_ref):
    out_ref[:, :-LANES] = g_ref[...]
    names = name_ref[...]
    slot = jnp.zeros_like(names)
    for j in range(slot_ref.shape[0]):
        slot = jnp.where(names == j, slot_ref[j], slot)
    ones = jnp.ones((1, LANES), F32)
    out_ref[:, -LANES:] = columns_by_columns(slot.astype(F32), ones).astype(BF16)


def join_kernel(*refs):
    both_ref, down_ref = refs[-2:]
    for k, ref in enumerate(refs[:-2]):
        rows = ref.shape[0]
        both_ref[k * rows : (k + 1) * rows] = ref[...]
        down_ref[k * rows : (k + 1) * rows] = ref[:, : down_ref.shape[1]]


def own_kernel(sizes, down_ref, up_ref, out_ref):
    groups, holders, shard = sizes
    half = shard // groups
    rank = down_ref.shape[1]
    slots = out_ref.shape[0] // rank
    first = lax.axis_index("replica") * slots
    for j in range(slots):
        to = pl.ds(j * rank, rank)
        for z in range(holders):
            at = pl.multiple_of(z * shard + lax.axis_index("groups") * half, half)
            out_ref[to, z * half : (z + 1) * half] = down_ref[first + j, :, pl.ds(at, half)]
        out_ref[to, holders * half :] = up_ref[first + j]


def adapter_kernel(sizes, *refs):
    groups, holders, replicas, shard, slots, rank = sizes
    x_ref, g_ref, sel_ref = refs[:3]
    map_refs, refs = refs[3 : 3 + groups * replicas], refs[3 + groups * replicas :]
    own_ref, other_refs, down = refs[0], refs[1:-1], refs[-1]
    group = lax.axis_index("groups")
    tokens, width = x_ref.shape
    rows, cols = own_ref.shape
    half = shard // groups
    for dg in range(groups):
        first = lax.rem(group + groups - dg, groups) * half
        for dr in range(replicas):
            for z in range(holders):
                at = pl.multiple_of(first + z * shard, half)
                down[pl.ds(dr * rows, rows), pl.ds(at, half)] = map_refs[dg * replicas + dr][
                    :, z * half : (z + 1) * half
                ]
    row_slot = [row_slots(holders, replicas, slots, rank, dr) for dr in range(replicas)]
    keep = slots_of(g_ref) == jnp.concatenate(row_slot, axis=1)
    in_sel = jnp.where(keep, rows_by_rows(x_ref[...], down[...]), 0.0).astype(BF16)
    grad_sel = sel_ref[pl.ds(0, tokens), :]
    step, split = 1024, cols // 2
    for at in range(0, cols, step):
        if at < width:
            part = columns_by_columns(grad_sel, x_ref[:, at : at + step])
        else:
            part = columns_by_columns(in_sel, g_ref[:, at - width : at - width + step])
        own_ref[:, at : at + step] = part[:rows]
        for dr in range(1, replicas):
            sent = part[dr * rows : (dr + 1) * rows].astype(BF16)
            for j in range(0, step, LANES):
                ref, to = other_refs[2 * dr - 2 + (at + j) // split], (at + j) % split
                ref[:, to : to + LANES] = sent[:, j : j + LANES]


def frozen_kernel(sizes, batch, *refs):
    tokens, groups, holders, replicas, slots, rank = sizes
    g_refs, refs = refs[:groups], refs[groups:]
    map_refs, refs = refs[:replicas], refs[replicas:]
    core, here = lax.axis_index("replica"), lax.axis_index("adapter")
    rows = map_refs[0].shape[0]
    width = map_refs[0].shape[1] - (g_refs[0].shape[1] - LANES)
    half = width // holders
    if batch[0][0] == 0:
        sel_ref = refs[-1]
        out_refs = refs[-1 - groups : -1]
        for dg in range(groups):
            for dr in range(replicas):
                keep = slots_of(g_refs[dg]) == row_slots(holders, replicas, slots, rank, dr)
                proj_grad = rows_by_rows(g_refs[dg][:, :-LANES], map_refs[dr][:, width:])
                sel_ref[pl.ds(dg * tokens, tokens), dr * rows : (dr + 1) * rows] = jnp.where(
                    keep, proj_grad, 0.0
                ).astype(BF16)
    else:
        sel_ref, refs = refs[0], refs[1:]
        out_refs = refs[-groups:]
        if refs[-1].shape[0] > tokens:
            out_refs = [refs[-1].at[pl.ds(dg * tokens, tokens)] for dg in range(groups)]
    for i, (k, spec) in enumerate(batch):
        shard_at = lax.rem(here + holders - k, holders) * half
        for (dr, offset), block in zip(spec, refs):
            if k == 0:
                first = pl.multiple_of(lax.axis_index("groups") * half, half)
                block = block.at[pl.ds(first, half)]
            wide = block.shape[0]
            at = 0
            if wide < half:
                at = lax.rem(core + replicas - dr, replicas) * (half // replicas) + offset
            columns = pl.ds(pl.multiple_of(shard_at + at, wide), wide)
            for dg in range(groups):
                base = rows_by_rows(g_refs[dg][:, :-LANES], block[...]).astype(BF16)
                lora = 0.0
                for j in range(replicas):
                    lora = lora + jnp.dot(
                        sel_ref[pl.ds(dg * tokens, tokens), j * rows : (j + 1) * rows],
                        map_refs[j][:, columns],
                        preferred_element_type=F32,
                    )
                lora = (ADAPTER_SCALE * lora).astype(BF16)
                out_refs[dg][:, pl.ds(pl.multiple_of(i * half + at, wide), wide)] = (
                    base.astype(F32) + lora.astype(F32)
                ).astype(BF16)
        refs = refs[len(spec) :]


def split_kernel(block_ref, *part_refs):
    rows = part_refs[0].shape[0]
    for j, ref in enumerate(part_refs):
        ref[...] = block_ref[j * rows : (j + 1) * rows]


def column_of(sizes, k, dg):
    groups, holders, shard, half = sizes
    group, here = lax.axis_index("groups"), lax.axis_index("adapter")
    source = lax.rem(group + groups - dg, groups)
    at = lax.rem(here + holders - k, holders) * shard + source * half
    return pl.ds(pl.multiple_of(at, half), half)


def place_kernel(sizes, places, *refs):
    half = sizes[-1]
    for ref, (batch, dg) in zip(refs, places):
        for j, k in enumerate(batch):
            refs[-1][:, column_of(sizes, k, dg)] = ref[:, j * half : (j + 1) * half]


def late_kernel(sizes, places, *refs):
    out_ref, sems = refs[-2:]
    copies = [
        pltpu.make_async_copy(ref, out_ref.at[:, column_of(sizes, batch[0], dg)], sems.at[i])
        for i, (ref, (batch, dg)) in enumerate(zip(refs, places))
    ]
    for copy in copies:
        copy.start()
    for copy in copies:
        copy.wait()


def chip_kernel(replicas, *refs):
    own_ref, came_refs, out_refs = refs[0], refs[1 : 2 * replicas - 1], refs[2 * replicas - 1 :]
    rows = out_refs[0].shape[0]
    split = came_refs[0].shape[1]
    for k, out in enumerate(out_refs):
        for j in range(2):
            at = pl.ds(k * rows, rows), pl.ds(j * split, split)
            total = own_ref[at]
            for ref in came_refs[j::2]:
                total = total + ref[pl.ds(k * rows, rows), :].astype(F32)
            out[:, pl.ds(j * split, split)] = total.astype(out.dtype)


def total_kernel(*refs):
    half_refs, refs = refs[-2:], refs[:-2]
    wide = half_refs[0].shape[1]
    for j, out_ref in enumerate(half_refs):
        at = pl.ds(j * wide, wide)
        total = refs[0][:, at]
        for ref in refs[1:]:
            total = total + ref[:, at].astype(F32)
        out_ref[...] = (ADAPTER_SCALE * total).astype(BF16)


def spread_kernel(width, replicas, *refs):
    core = lax.axis_index("replica")
    down_ref, up_ref = refs[2 * replicas :]
    slots = down_ref.shape[0] // replicas
    rank = down_ref.shape[1]
    wide = refs[0].shape[1]
    for dr in range(replicas):
        at = lax.rem(core + replicas - dr, replicas) * slots
        for j in range(slots):
            rows = slice(j * rank, (j + 1) * rank)
            down_ref[at + j, :, :wide] = refs[2 * dr][rows]
            down_ref[at + j, :, wide:] = refs[2 * dr + 1][rows, : width - wide]
            up_ref[at + j] = refs[2 * dr + 1][rows, width - wide :]


def on_device(
    saved_layer_input,
    value_output_gradient,
    token_adapter_index,
    adapter_slot_index,
    frozen_value_weight,
    adapter_down_weight,
    adapter_up_weight,
):
    inputs = saved_layer_input[0]
    grad_rows = value_output_gradient[0]
    tokens, width = inputs.shape
    value_width = grad_rows.shape[1]
    groups, holders, replicas = (lax.axis_size(a) for a in ("groups", "adapter", "replica"))
    group, here, core = (lax.axis_index(a) for a in ("groups", "adapter", "replica"))
    slots, rank = adapter_down_weight.shape[1:3]
    own_slots = slots // replicas
    rows = own_slots * rank
    frozen = frozen_value_weight[0]
    shard = frozen.shape[0]
    half = shard // groups
    piece = half // replicas
    cols = width + value_width

    tagged = call(
        tag_kernel,
        [jax.ShapeDtypeStruct((tokens, value_width + LANES), BF16)],
        (grad_rows, token_adapter_index[0, :, 0][None], adapter_slot_index),
        scalars=1,
    )[0]
    grads = [tagged] + [
        moved(tagged, lambda g, z, s, r: (g - dg, z, s, r)) for dg in range(1, groups)
    ]

    own = call(
        functools.partial(own_kernel, (groups, holders, shard)),
        [jax.ShapeDtypeStruct((rows, holders * half + value_width), BF16)],
        (adapter_down_weight[0], adapter_up_weight[0]),
    )[0]
    held = [own]
    for k in range(1, holders):
        held.append(moved(own, lambda g, z, s, r: (g, z + k, s, r)))

    ring = [lax.dynamic_slice_in_dim(frozen, (group * replicas + core) * piece, piece, axis=0)]
    ring.append(moved(ring[0], lambda g, z, s, r: (g, z + 1, s, r)))
    held, grads, ring = lax.optimization_barrier((held, grads, ring))
    both, downs = call(
        join_kernel,
        [
            jax.ShapeDtypeStruct((holders * rows, holders * half + value_width), BF16),
            jax.ShapeDtypeStruct((holders * rows, holders * half), BF16),
        ],
        held,
    )
    both = [both] + [
        moved(both, lambda g, z, s, r: (g, z, s, r + dr)) for dr in range(1, replicas)
    ]

    def pieces_of(k, *before):
        if k == 0:
            return [(0, 0)], [frozen]
        mails = [ring[k]]
        if k > 1 and piece % (2 * LANES) == 0:
            shape = jax.ShapeDtypeStruct((piece // 2, value_width), BF16)
            mails = call(split_kernel, [shape] * 2, (ring[k],))
        mails = [after(mail, *before) if before else mail for mail in mails]
        spec, pieces = [(0, 0)], [ring[k]]
        for dr in range(1, replicas):
            for j, mail in enumerate(mails):
                spec.append((dr, j * mail.shape[0]))
                pieces.append(moved(mail, lambda g, z, s, r: (g, z, s, r + dr)))
        if piece % LANES:
            whole = jnp.zeros((half, value_width), BF16)
            for (dr, offset), part in zip(spec, pieces):
                at = ((core - dr) % replicas) * piece + offset
                whole = lax.dynamic_update_slice_in_dim(whole, part, at, axis=0)
            spec, pieces = [(0, 0)], [whole]
        return spec, pieces

    kept = replicas * holders * rows

    def adapter_sums(sel, *before):
        maps = list(both)
        for dg in range(1, groups):
            maps.append(moved(downs, lambda g, z, s, r: (g + dg, z, s, r)))
            for dr in range(1, replicas):
                maps.append(moved(maps[-dr], lambda g, z, s, r: (g, z, s, r + dr)))
        gradients = call(
            functools.partial(adapter_kernel, (groups, holders, replicas, shard, slots, rank)),
            [jax.ShapeDtypeStruct((holders * rows, cols), F32)]
            + [jax.ShapeDtypeStruct((holders * rows, cols // 2), BF16)] * (2 * replicas - 2),
            (inputs, tagged, sel, *maps),
            [jax.ShapeDtypeStruct((kept, width), BF16)],
        )
        part, sent = gradients[0], gradients[1:]
        came = [
            moved(after(sent[2 * dr - 2 + j], *before), lambda g, z, s, r: (g, z, s, r - dr))
            for dr in range(1, replicas)
            for j in range(2)
        ]
        chip = call(
            functools.partial(chip_kernel, replicas),
            [jax.ShapeDtypeStruct((rows, cols), F32)]
            + [jax.ShapeDtypeStruct((rows, cols), BF16)] * (holders - 1),
            (part, *came),
        )
        return part, chip

    batches = [list(range(min(2, holders)))] + [[k] for k in range(2, holders)]
    arrived, crossed = [], []
    for i, batch in enumerate(batches):
        operands, specs = [], []
        for k in batch:
            if k > 1:
                if 2 < k == holders - 1:
                    last = moved(after(ring[0], sel), lambda g, z, s, r: (g, z - 1, s, r))
                else:
                    last = after(ring[-1], sel) if k > 2 else ring[-1]
                    last = moved(last, lambda g, z, s, r: (g, z + 1, s, r))
                ring.append(last)
            gate = arrived[0] if k == 2 else [*arrived[i - 2]] if k > 2 else []
            spec, blocks = pieces_of(k, *gate)
            specs.append((k, spec))
            operands += blocks
        tokens_in = [after(grads[0], part), *grads[1:]] if i == 1 else grads
        out = call(
            functools.partial(
                frozen_kernel, (tokens, groups, holders, replicas, slots, rank), specs
            ),
            (
                [jax.ShapeDtypeStruct((groups * tokens, half), BF16)]
                if i == 1 and len(batches) > 2
                else [jax.ShapeDtypeStruct((tokens, half * len(batch)), BF16)] * groups
            )
            + [jax.ShapeDtypeStruct((groups * tokens, kept), BF16)] * (i == 0),
            [*tokens_in, *both, *([sel] if i else []), *operands],
        )
        if i == 0:
            sel = out[groups]
        mails = list(out[:groups])
        if i == 1 and len(batches) > 2:
            got = moved(out[0], lambda g, z, s, r: (g, z, s - 1, r))
            got = [got[dg * tokens : (dg + 1) * tokens] for dg in range(groups)]
            early = [(batches[0], dg) for dg in range(groups)] + [(batch, 0)]
            passed = call(
                functools.partial(place_kernel, (groups, holders, shard, half), early),
                [jax.ShapeDtypeStruct((tokens, width), BF16)],
                [*arrived[0], got[0]],
            )[0]
            got, passed = lax.optimization_barrier((got, passed))
            late = [
                ((batch, dg), moved(got[dg], lambda g, z, s, r: (g + dg, z, s, r)))
                for dg in range(1, groups)
            ]
            arrived.append([])
            continue
        if i > 2:
            mails = [after(mail, *arrived[-1]) for mail in mails]
        arrived.append(
            [moved(mails[dg], lambda g, z, s, r: (g + dg, z, s - 1, r)) for dg in range(groups)]
        )
        if i > 1:
            late += [((batch, dg), arrived[-1][dg]) for dg in reversed(range(groups))]
        if i == 0:
            part, chip = adapter_sums(sel, *arrived[0])
    sizes = (groups, holders, shard, half)
    if len(batches) > 2:
        passed = pl.pallas_call(
            functools.partial(late_kernel, sizes, [place for place, _ in late]),
            out_shape=jax.ShapeDtypeStruct((tokens, width), BF16),
            in_specs=[pl.BlockSpec(memory_space=pltpu.VMEM)] * len(late)
            + [pl.BlockSpec(memory_space=pl.ANY)],
            out_specs=pl.BlockSpec(memory_space=pl.ANY),
            input_output_aliases={len(late): 0},
            scratch_shapes=[pltpu.SemaphoreType.DMA((len(late),))],
            compiler_params=pltpu.CompilerParams(vmem_limit_bytes=8 * MIB),
            cost_estimate=pl.CostEstimate(flops=1000, bytes_accessed=1000, transcendentals=0),
        )(*[part for _, part in late], passed)
    else:
        passed = call(
            functools.partial(
                place_kernel, sizes, [(batch, dg) for batch in batches for dg in range(groups)]
            ),
            [jax.ShapeDtypeStruct((tokens, width), BF16)],
            [x for got in arrived for x in got],
        )[0]

    sums = [chip[0]] + [
        moved(after(chip[k], ring[-1]), lambda g, z, s, r: (g, z - k, s, r))
        for k in reversed(range(1, holders))
    ]
    total = call(total_kernel, [jax.ShapeDtypeStruct((rows, cols // 2), BF16)] * 2, sums)
    totals = list(total)
    for dr in range(1, replicas):
        totals += [moved(x, lambda g, z, s, r: (g, z, s, r + dr)) for x in total]
    totals[0], passed = lax.optimization_barrier((totals[0], passed))
    down_grad, up_grad = call(
        functools.partial(spread_kernel, width, replicas),
        [
            jax.ShapeDtypeStruct((slots, rank, width), BF16),
            jax.ShapeDtypeStruct((slots, rank, value_width), BF16),
        ],
        totals,
    )

    return passed[None], down_grad[None], up_grad[None]


def solution(mesh):
    placed = (
        P("segment", ("groups", "adapter", "replica"), None),
        P("segment", ("groups", "adapter", "replica"), None),
        P("segment", ("groups", "adapter", "replica"), None),
        P("groups"),
        P("segment", "adapter", None),
        P("segment", "adapter", None, None),
        P("segment", "adapter", None, None),
    )
    return jax.shard_map(
        on_device,
        mesh=mesh,
        in_specs=placed,
        out_specs=(
            P("segment", ("groups", "adapter", "replica"), None),
            P(("groups", "segment"), "adapter", None, None),
            P(("groups", "segment"), "adapter", None, None),
        ),
        check_vma=False,
    )
```

```python
import functools
import itertools
import jax
import jax.numpy as jnp
from jax import lax
from jax.experimental import pallas as pl
from jax.experimental.pallas import tpu as pltpu
from jax.sharding import PartitionSpec as P

ADAPTER_SCALE = 2.0
AXES = ("groups", "adapter", "segment", "replica")
LANES = 128
F32 = jnp.float32
BF16 = jnp.bfloat16
MIB = 1024 * 1024


def moved(x, to):
    sizes = [lax.axis_size(a) for a in AXES]
    number = {at: i for i, at in enumerate(itertools.product(*map(range, sizes)))}
    pairs = [
        (i, number[tuple(t % s for t, s in zip(to(*at), sizes))]) for at, i in number.items()
    ]
    return lax.ppermute(x, AXES, pairs)


def after(x, *others):
    return lax.optimization_barrier((x, *others))[0]


def rows_by_rows(a, b):
    return lax.dot_general(a, b, (((1,), (1,)), ((), ())), preferred_element_type=F32)


def columns_by_columns(a, b):
    return lax.dot_general(a, b, (((0,), (0,)), ((), ())), preferred_element_type=F32)


def call(kernel, out_shape, operands, scratch=(), scalars=0):
    held = sum(x.size * x.dtype.itemsize for x in (*operands, *out_shape, *scratch))
    return pl.pallas_call(
        kernel,
        out_shape=out_shape,
        in_specs=[pl.BlockSpec(memory_space=pltpu.VMEM)] * (len(operands) - scalars)
        + [pl.BlockSpec(memory_space=pltpu.SMEM)] * scalars,
        scratch_shapes=[pltpu.VMEM(x.shape, x.dtype) for x in scratch],
        compiler_params=pltpu.CompilerParams(vmem_limit_bytes=2 * held + 4 * MIB),
        cost_estimate=pl.CostEstimate(flops=1000, bytes_accessed=1000, transcendentals=0),
    )(*operands)


def slots_of(tagged_ref):
    return tagged_ref[:, -LANES:].astype(F32)[:, :1]


def row_slots(holders, replicas, slots, rank, dr):
    here, core = lax.axis_index("adapter"), lax.axis_index("replica")
    own_slots = slots // replicas
    lane = lax.broadcasted_iota(jnp.int32, (1, holders * own_slots * rank), 1)
    slot = jnp.zeros_like(lane)
    for k in range(holders):
        for j in range(own_slots):
            start = (k * own_slots + j) * rank
            value = lax.rem(here + holders - k, holders) * slots
            value = value + lax.rem(core + replicas - dr, replicas) * own_slots + j
            slot = jnp.where((lane >= start) & (lane < start + rank), value, slot)
    return slot.astype(F32)


def tag_kernel(g_ref, name_ref, slot_ref, out_ref):
    out_ref[:, :-LANES] = g_ref[...]
    names = name_ref[...]
    slot = jnp.zeros_like(names)
    for j in range(slot_ref.shape[0]):
        slot = jnp.where(names == j, slot_ref[j], slot)
    ones = jnp.ones((1, LANES), F32)
    out_ref[:, -LANES:] = columns_by_columns(slot.astype(F32), ones).astype(BF16)


def join_kernel(*refs):
    both_ref, down_ref = refs[-2:]
    for k, ref in enumerate(refs[:-2]):
        rows = ref.shape[0]
        both_ref[k * rows : (k + 1) * rows] = ref[...]
        down_ref[k * rows : (k + 1) * rows] = ref[:, : down_ref.shape[1]]


def own_kernel(sizes, down_ref, up_ref, out_ref):
    groups, holders, shard = sizes
    half = shard // groups
    rank = down_ref.shape[1]
    slots = out_ref.shape[0] // rank
    first = lax.axis_index("replica") * slots
    for j in range(slots):
        to = pl.ds(j * rank, rank)
        for z in range(holders):
            at = pl.multiple_of(z * shard + lax.axis_index("groups") * half, half)
            out_ref[to, z * half : (z + 1) * half] = down_ref[first + j, :, pl.ds(at, half)]
        out_ref[to, holders * half :] = up_ref[first + j]


def adapter_kernel(sizes, *refs):
    groups, holders, replicas, shard, slots, rank = sizes
    x_ref, g_ref, sel_ref = refs[:3]
    map_refs, refs = refs[3 : 3 + groups * replicas], refs[3 + groups * replicas :]
    own_ref, other_refs, down = refs[0], refs[1:-1], refs[-1]
    group = lax.axis_index("groups")
    tokens, width = x_ref.shape
    rows, cols = own_ref.shape
    half = shard // groups
    for dg in range(groups):
        first = lax.rem(group + groups - dg, groups) * half
        for dr in range(replicas):
            for z in range(holders):
                at = pl.multiple_of(first + z * shard, half)
                down[pl.ds(dr * rows, rows), pl.ds(at, half)] = map_refs[dg * replicas + dr][
                    :, z * half : (z + 1) * half
                ]
    row_slot = [row_slots(holders, replicas, slots, rank, dr) for dr in range(replicas)]
    keep = slots_of(g_ref) == jnp.concatenate(row_slot, axis=1)
    in_sel = jnp.where(keep, rows_by_rows(x_ref[...], down[...]), 0.0).astype(BF16)
    grad_sel = sel_ref[pl.ds(0, tokens), :]
    step, split = 1024, cols // 2
    for at in range(0, cols, step):
        if at < width:
            part = columns_by_columns(grad_sel, x_ref[:, at : at + step])
        else:
            part = columns_by_columns(in_sel, g_ref[:, at - width : at - width + step])
        own_ref[:, at : at + step] = part[:rows]
        for dr in range(1, replicas):
            sent = part[dr * rows : (dr + 1) * rows].astype(BF16)
            for j in range(0, step, LANES):
                ref, to = other_refs[2 * dr - 2 + (at + j) // split], (at + j) % split
                ref[:, to : to + LANES] = sent[:, j : j + LANES]


def frozen_kernel(sizes, batch, *refs):
    tokens, groups, holders, replicas, slots, rank = sizes
    g_refs, refs = refs[:groups], refs[groups:]
    map_refs, refs = refs[:replicas], refs[replicas:]
    core, here = lax.axis_index("replica"), lax.axis_index("adapter")
    rows = map_refs[0].shape[0]
    width = map_refs[0].shape[1] - (g_refs[0].shape[1] - LANES)
    half = width // holders
    if batch[0][0] == 0:
        sel_ref = refs[-1]
        out_refs = refs[-1 - groups : -1]
        for dg in range(groups):
            for dr in range(replicas):
                keep = slots_of(g_refs[dg]) == row_slots(holders, replicas, slots, rank, dr)
                proj_grad = rows_by_rows(g_refs[dg][:, :-LANES], map_refs[dr][:, width:])
                sel_ref[pl.ds(dg * tokens, tokens), dr * rows : (dr + 1) * rows] = jnp.where(
                    keep, proj_grad, 0.0
                ).astype(BF16)
    else:
        sel_ref, refs = refs[0], refs[1:]
        out_refs = refs[-groups:]
        if refs[-1].shape[0] > tokens:
            out_refs = [refs[-1].at[pl.ds(dg * tokens, tokens)] for dg in range(groups)]
    for i, (k, spec) in enumerate(batch):
        shard_at = lax.rem(here + holders - k, holders) * half
        for (dr, offset), block in zip(spec, refs):
            if k == 0:
                first = pl.multiple_of(lax.axis_index("groups") * half, half)
                block = block.at[pl.ds(first, half)]
            wide = block.shape[0]
            at = 0
            if wide < half:
                at = lax.rem(core + replicas - dr, replicas) * (half // replicas) + offset
            columns = pl.ds(pl.multiple_of(shard_at + at, wide), wide)
            for dg in range(groups):
                base = rows_by_rows(g_refs[dg][:, :-LANES], block[...]).astype(BF16)
                lora = 0.0
                for j in range(replicas):
                    lora = lora + jnp.dot(
                        sel_ref[pl.ds(dg * tokens, tokens), j * rows : (j + 1) * rows],
                        map_refs[j][:, columns],
                        preferred_element_type=F32,
                    )
                lora = (ADAPTER_SCALE * lora).astype(BF16)
                out_refs[dg][:, pl.ds(pl.multiple_of(i * half + at, wide), wide)] = (
                    base.astype(F32) + lora.astype(F32)
                ).astype(BF16)
        refs = refs[len(spec) :]


def split_kernel(block_ref, *part_refs):
    rows = part_refs[0].shape[0]
    for j, ref in enumerate(part_refs):
        ref[...] = block_ref[j * rows : (j + 1) * rows]


def column_of(sizes, k, dg):
    groups, holders, shard, half = sizes
    group, here = lax.axis_index("groups"), lax.axis_index("adapter")
    source = lax.rem(group + groups - dg, groups)
    at = lax.rem(here + holders - k, holders) * shard + source * half
    return pl.ds(pl.multiple_of(at, half), half)


def place_kernel(sizes, places, *refs):
    half = sizes[-1]
    for ref, (batch, dg) in zip(refs, places):
        for j, k in enumerate(batch):
            refs[-1][:, column_of(sizes, k, dg)] = ref[:, j * half : (j + 1) * half]


def late_kernel(sizes, places, *refs):
    out_ref, sems = refs[-2:]
    copies = [
        pltpu.make_async_copy(ref, out_ref.at[:, column_of(sizes, batch[0], dg)], sems.at[i])
        for i, (ref, (batch, dg)) in enumerate(zip(refs, places))
    ]
    for copy in copies:
        copy.start()
    for copy in copies:
        copy.wait()


def chip_kernel(replicas, *refs):
    own_ref, came_refs, out_refs = refs[0], refs[1 : 2 * replicas - 1], refs[2 * replicas - 1 :]
    rows = out_refs[0].shape[0]
    split = came_refs[0].shape[1]
    for k, out in enumerate(out_refs):
        for j in range(2):
            at = pl.ds(k * rows, rows), pl.ds(j * split, split)
            total = own_ref[at]
            for ref in came_refs[j::2]:
                total = total + ref[pl.ds(k * rows, rows), :].astype(F32)
            out[:, pl.ds(j * split, split)] = total.astype(out.dtype)


def total_kernel(*refs):
    half_refs, refs = refs[-2:], refs[:-2]
    wide = half_refs[0].shape[1]
    for j, out_ref in enumerate(half_refs):
        at = pl.ds(j * wide, wide)
        total = refs[0][:, at]
        for ref in refs[1:]:
            total = total + ref[:, at].astype(F32)
        out_ref[...] = (ADAPTER_SCALE * total).astype(BF16)


def spread_kernel(width, replicas, *refs):
    core = lax.axis_index("replica")
    down_ref, up_ref = refs[2 * replicas :]
    slots = down_ref.shape[0] // replicas
    rank = down_ref.shape[1]
    wide = refs[0].shape[1]
    for dr in range(replicas):
        at = lax.rem(core + replicas - dr, replicas) * slots
        for j in range(slots):
            rows = slice(j * rank, (j + 1) * rank)
            down_ref[at + j, :, :wide] = refs[2 * dr][rows]
            down_ref[at + j, :, wide:] = refs[2 * dr + 1][rows, : width - wide]
            up_ref[at + j] = refs[2 * dr + 1][rows, width - wide :]


def on_device(
    saved_layer_input,
    value_output_gradient,
    token_adapter_index,
    adapter_slot_index,
    frozen_value_weight,
    adapter_down_weight,
    adapter_up_weight,
):
    inputs = saved_layer_input[0]
    grad_rows = value_output_gradient[0]
    tokens, width = inputs.shape
    value_width = grad_rows.shape[1]
    groups, holders, replicas = (lax.axis_size(a) for a in ("groups", "adapter", "replica"))
    group, here, core = (lax.axis_index(a) for a in ("groups", "adapter", "replica"))
    slots, rank = adapter_down_weight.shape[1:3]
    own_slots = slots // replicas
    rows = own_slots * rank
    frozen = frozen_value_weight[0]
    shard = frozen.shape[0]
    half = shard // groups
    piece = half // replicas
    cols = width + value_width

    tagged = call(
        tag_kernel,
        [jax.ShapeDtypeStruct((tokens, value_width + LANES), BF16)],
        (grad_rows, token_adapter_index[0, :, 0][None], adapter_slot_index),
        scalars=1,
    )[0]
    grads = [tagged] + [
        moved(tagged, lambda g, z, s, r: (g - dg, z, s, r)) for dg in range(1, groups)
    ]

    own = call(
        functools.partial(own_kernel, (groups, holders, shard)),
        [jax.ShapeDtypeStruct((rows, holders * half + value_width), BF16)],
        (adapter_down_weight[0], adapter_up_weight[0]),
    )[0]
    held = [own]
    for k in range(1, holders):
        held.append(moved(own, lambda g, z, s, r: (g, z + k, s, r)))

    ring = [lax.dynamic_slice_in_dim(frozen, (group * replicas + core) * piece, piece, axis=0)]
    ring.append(moved(ring[0], lambda g, z, s, r: (g, z + 1, s, r)))
    held, grads, ring = lax.optimization_barrier((held, grads, ring))
    both, downs = call(
        join_kernel,
        [
            jax.ShapeDtypeStruct((holders * rows, holders * half + value_width), BF16),
            jax.ShapeDtypeStruct((holders * rows, holders * half), BF16),
        ],
        held,
    )
    both = [both] + [
        moved(both, lambda g, z, s, r: (g, z, s, r + dr)) for dr in range(1, replicas)
    ]

    def pieces_of(k, *before):
        if k == 0:
            return [(0, 0)], [frozen]
        mails = [ring[k]]
        if k > 1 and piece % (2 * LANES) == 0:
            shape = jax.ShapeDtypeStruct((piece // 2, value_width), BF16)
            mails = call(split_kernel, [shape] * 2, (ring[k],))
        mails = [after(mail, *before) if before else mail for mail in mails]
        spec, pieces = [(0, 0)], [ring[k]]
        for dr in range(1, replicas):
            for j, mail in enumerate(mails):
                spec.append((dr, j * mail.shape[0]))
                pieces.append(moved(mail, lambda g, z, s, r: (g, z, s, r + dr)))
        if piece % LANES:
            whole = jnp.zeros((half, value_width), BF16)
            for (dr, offset), part in zip(spec, pieces):
                at = ((core - dr) % replicas) * piece + offset
                whole = lax.dynamic_update_slice_in_dim(whole, part, at, axis=0)
            spec, pieces = [(0, 0)], [whole]
        return spec, pieces

    kept = replicas * holders * rows

    def adapter_sums(sel, *before):
        maps = list(both)
        for dg in range(1, groups):
            maps.append(moved(downs, lambda g, z, s, r: (g + dg, z, s, r)))
            for dr in range(1, replicas):
                maps.append(moved(maps[-dr], lambda g, z, s, r: (g, z, s, r + dr)))
        gradients = call(
            functools.partial(adapter_kernel, (groups, holders, replicas, shard, slots, rank)),
            [jax.ShapeDtypeStruct((holders * rows, cols), F32)]
            + [jax.ShapeDtypeStruct((holders * rows, cols // 2), BF16)] * (2 * replicas - 2),
            (inputs, tagged, sel, *maps),
            [jax.ShapeDtypeStruct((kept, width), BF16)],
        )
        part, sent = gradients[0], gradients[1:]
        came = [
            moved(after(sent[2 * dr - 2 + j], *before), lambda g, z, s, r: (g, z, s, r - dr))
            for dr in range(1, replicas)
            for j in range(2)
        ]
        chip = call(
            functools.partial(chip_kernel, replicas),
            [jax.ShapeDtypeStruct((rows, cols), F32)]
            + [jax.ShapeDtypeStruct((rows, cols), BF16)] * (holders - 1),
            (part, *came),
        )
        return part, chip

    batches = [list(range(min(2, holders)))] + [[k] for k in range(2, holders)]
    arrived, crossed = [], []
    for i, batch in enumerate(batches):
        operands, specs = [], []
        for k in batch:
            if k > 1:
                if 2 < k == holders - 1:
                    last = moved(after(ring[0], sel), lambda g, z, s, r: (g, z - 1, s, r))
                else:
                    last = after(ring[-1], sel) if k > 2 else ring[-1]
                    last = moved(last, lambda g, z, s, r: (g, z + 1, s, r))
                ring.append(last)
            gate = arrived[0] if k == 2 else [*arrived[i - 2]] if k > 2 else []
            spec, blocks = pieces_of(k, *gate)
            specs.append((k, spec))
            operands += blocks
        tokens_in = [after(grads[0], part), *grads[1:]] if i == 1 else grads
        out = call(
            functools.partial(
                frozen_kernel, (tokens, groups, holders, replicas, slots, rank), specs
            ),
            (
                [jax.ShapeDtypeStruct((groups * tokens, half), BF16)]
                if i == 1 and len(batches) > 2
                else [jax.ShapeDtypeStruct((tokens, half * len(batch)), BF16)] * groups
            )
            + [jax.ShapeDtypeStruct((groups * tokens, kept), BF16)] * (i == 0),
            [*tokens_in, *both, *([sel] if i else []), *operands],
        )
        if i == 0:
            sel = out[groups]
        mails = list(out[:groups])
        if i == 1 and len(batches) > 2:
            got = moved(after(out[0], chip[0]), lambda g, z, s, r: (g, z, s - 1, r))
            got = [got[dg * tokens : (dg + 1) * tokens] for dg in range(groups)]
            early = [(batches[0], dg) for dg in range(groups)] + [(batch, 0)]
            passed = call(
                functools.partial(place_kernel, (groups, holders, shard, half), early),
                [jax.ShapeDtypeStruct((tokens, width), BF16)],
                [*arrived[0], got[0]],
            )[0]
            got, passed = lax.optimization_barrier((got, passed))
            late = [
                ((batch, dg), moved(got[dg], lambda g, z, s, r: (g + dg, z, s, r)))
                for dg in range(1, groups)
            ]
            arrived.append([])
            continue
        if i > 2:
            mails = [after(mail, *arrived[-1]) for mail in mails]
        arrived.append(
            [moved(mails[dg], lambda g, z, s, r: (g + dg, z, s - 1, r)) for dg in range(groups)]
        )
        if i > 1:
            late += [((batch, dg), arrived[-1][dg]) for dg in reversed(range(groups))]
        if i == 0:
            part, chip = adapter_sums(sel, *arrived[0])
    sizes = (groups, holders, shard, half)
    if len(batches) > 2:
        passed = pl.pallas_call(
            functools.partial(late_kernel, sizes, [place for place, _ in late]),
            out_shape=jax.ShapeDtypeStruct((tokens, width), BF16),
            in_specs=[pl.BlockSpec(memory_space=pltpu.VMEM)] * len(late)
            + [pl.BlockSpec(memory_space=pl.ANY)],
            out_specs=pl.BlockSpec(memory_space=pl.ANY),
            input_output_aliases={len(late): 0},
            scratch_shapes=[pltpu.SemaphoreType.DMA((len(late),))],
            compiler_params=pltpu.CompilerParams(vmem_limit_bytes=8 * MIB),
            cost_estimate=pl.CostEstimate(flops=1000, bytes_accessed=1000, transcendentals=0),
        )(*[part for _, part in late], passed)
    else:
        passed = call(
            functools.partial(
                place_kernel, sizes, [(batch, dg) for batch in batches for dg in range(groups)]
            ),
            [jax.ShapeDtypeStruct((tokens, width), BF16)],
            [x for got in arrived for x in got],
        )[0]

    sums = [chip[0]] + [
        moved(after(chip[k], ring[-1]), lambda g, z, s, r: (g, z - k, s, r))
        for k in reversed(range(1, holders))
    ]
    total = call(total_kernel, [jax.ShapeDtypeStruct((rows, cols // 2), BF16)] * 2, sums)
    totals = list(total)
    for dr in range(1, replicas):
        totals += [moved(x, lambda g, z, s, r: (g, z, s, r + dr)) for x in total]
    totals[0], passed = lax.optimization_barrier((totals[0], passed))
    down_grad, up_grad = call(
        functools.partial(spread_kernel, width, replicas),
        [
            jax.ShapeDtypeStruct((slots, rank, width), BF16),
            jax.ShapeDtypeStruct((slots, rank, value_width), BF16),
        ],
        totals,
    )

    return passed[None], down_grad[None], up_grad[None]


def solution(mesh):
    placed = (
        P("segment", ("groups", "adapter", "replica"), None),
        P("segment", ("groups", "adapter", "replica"), None),
        P("segment", ("groups", "adapter", "replica"), None),
        P("groups"),
        P("segment", "adapter", None),
        P("segment", "adapter", None, None),
        P("segment", "adapter", None, None),
    )
    return jax.shard_map(
        on_device,
        mesh=mesh,
        in_specs=placed,
        out_specs=(
            P("segment", ("groups", "adapter", "replica"), None),
            P(("groups", "segment"), "adapter", None, None),
            P(("groups", "segment"), "adapter", None, None),
        ),
        check_vma=False,
    )
```

```python
import functools
import itertools
import jax
import jax.numpy as jnp
from jax import lax
from jax.experimental import pallas as pl
from jax.experimental.pallas import tpu as pltpu
from jax.sharding import PartitionSpec as P

ADAPTER_SCALE = 2.0
AXES = ("groups", "adapter", "segment", "replica")
LANES = 128
F32 = jnp.float32
BF16 = jnp.bfloat16
MIB = 1024 * 1024


def moved(x, to):
    sizes = [lax.axis_size(a) for a in AXES]
    number = {at: i for i, at in enumerate(itertools.product(*map(range, sizes)))}
    pairs = [
        (i, number[tuple(t % s for t, s in zip(to(*at), sizes))]) for at, i in number.items()
    ]
    return lax.ppermute(x, AXES, pairs)


def after(x, *others):
    return lax.optimization_barrier((x, *others))[0]


def rows_by_rows(a, b):
    return lax.dot_general(a, b, (((1,), (1,)), ((), ())), preferred_element_type=F32)


def columns_by_columns(a, b):
    return lax.dot_general(a, b, (((0,), (0,)), ((), ())), preferred_element_type=F32)


def call(kernel, out_shape, operands, scratch=(), scalars=0):
    held = sum(x.size * x.dtype.itemsize for x in (*operands, *out_shape, *scratch))
    return pl.pallas_call(
        kernel,
        out_shape=out_shape,
        in_specs=[pl.BlockSpec(memory_space=pltpu.VMEM)] * (len(operands) - scalars)
        + [pl.BlockSpec(memory_space=pltpu.SMEM)] * scalars,
        scratch_shapes=[pltpu.VMEM(x.shape, x.dtype) for x in scratch],
        compiler_params=pltpu.CompilerParams(vmem_limit_bytes=2 * held + 4 * MIB),
        cost_estimate=pl.CostEstimate(flops=1000, bytes_accessed=1000, transcendentals=0),
    )(*operands)


def slots_of(tagged_ref):
    return tagged_ref[:, -LANES:].astype(F32)[:, :1]


def row_slots(holders, replicas, slots, rank, dr):
    here, core = lax.axis_index("adapter"), lax.axis_index("replica")
    own_slots = slots // replicas
    lane = lax.broadcasted_iota(jnp.int32, (1, holders * own_slots * rank), 1)
    slot = jnp.zeros_like(lane)
    for k in range(holders):
        for j in range(own_slots):
            start = (k * own_slots + j) * rank
            value = lax.rem(here + holders - k, holders) * slots
            value = value + lax.rem(core + replicas - dr, replicas) * own_slots + j
            slot = jnp.where((lane >= start) & (lane < start + rank), value, slot)
    return slot.astype(F32)


def tag_kernel(g_ref, name_ref, slot_ref, out_ref):
    out_ref[:, :-LANES] = g_ref[...]
    names = name_ref[...]
    slot = jnp.zeros_like(names)
    for j in range(slot_ref.shape[0]):
        slot = jnp.where(names == j, slot_ref[j], slot)
    ones = jnp.ones((1, LANES), F32)
    out_ref[:, -LANES:] = columns_by_columns(slot.astype(F32), ones).astype(BF16)


def join_kernel(*refs):
    both_ref, down_ref = refs[-2:]
    for k, ref in enumerate(refs[:-2]):
        rows = ref.shape[0]
        both_ref[k * rows : (k + 1) * rows] = ref[...]
        down_ref[k * rows : (k + 1) * rows] = ref[:, : down_ref.shape[1]]


def own_kernel(sizes, down_ref, up_ref, out_ref):
    groups, holders, shard = sizes
    half = shard // groups
    rank = down_ref.shape[1]
    slots = out_ref.shape[0] // rank
    first = lax.axis_index("replica") * slots
    for j in range(slots):
        to = pl.ds(j * rank, rank)
        for z in range(holders):
            at = pl.multiple_of(z * shard + lax.axis_index("groups") * half, half)
            out_ref[to, z * half : (z + 1) * half] = down_ref[first + j, :, pl.ds(at, half)]
        out_ref[to, holders * half :] = up_ref[first + j]


def adapter_kernel(sizes, *refs):
    groups, holders, replicas, shard, slots, rank = sizes
    x_ref, g_ref, sel_ref = refs[:3]
    map_refs, refs = refs[3 : 3 + groups * replicas], refs[3 + groups * replicas :]
    own_ref, other_refs, down = refs[0], refs[1:-1], refs[-1]
    group = lax.axis_index("groups")
    tokens, width = x_ref.shape
    rows, cols = own_ref.shape
    half = shard // groups
    for dg in range(groups):
        first = lax.rem(group + groups - dg, groups) * half
        for dr in range(replicas):
            for z in range(holders):
                at = pl.multiple_of(first + z * shard, half)
                down[pl.ds(dr * rows, rows), pl.ds(at, half)] = map_refs[dg * replicas + dr][
                    :, z * half : (z + 1) * half
                ]
    row_slot = [row_slots(holders, replicas, slots, rank, dr) for dr in range(replicas)]
    keep = slots_of(g_ref) == jnp.concatenate(row_slot, axis=1)
    in_sel = jnp.where(keep, rows_by_rows(x_ref[...], down[...]), 0.0).astype(BF16)
    grad_sel = sel_ref[pl.ds(0, tokens), :]
    step, split = 1024, cols // 2
    for at in range(0, cols, step):
        if at < width:
            part = columns_by_columns(grad_sel, x_ref[:, at : at + step])
        else:
            part = columns_by_columns(in_sel, g_ref[:, at - width : at - width + step])
        own_ref[:, at : at + step] = part[:rows]
        for dr in range(1, replicas):
            sent = part[dr * rows : (dr + 1) * rows].astype(BF16)
            for j in range(0, step, LANES):
                ref, to = other_refs[2 * dr - 2 + (at + j) // split], (at + j) % split
                ref[:, to : to + LANES] = sent[:, j : j + LANES]


def frozen_kernel(sizes, batch, *refs):
    tokens, groups, holders, replicas, slots, rank = sizes
    g_refs, refs = refs[:groups], refs[groups:]
    map_refs, refs = refs[:replicas], refs[replicas:]
    core, here = lax.axis_index("replica"), lax.axis_index("adapter")
    rows = map_refs[0].shape[0]
    width = map_refs[0].shape[1] - (g_refs[0].shape[1] - LANES)
    half = width // holders
    if batch[0][0] == 0:
        sel_ref = refs[-1]
        out_refs = refs[-1 - groups : -1]
        for dg in range(groups):
            for dr in range(replicas):
                keep = slots_of(g_refs[dg]) == row_slots(holders, replicas, slots, rank, dr)
                proj_grad = rows_by_rows(g_refs[dg][:, :-LANES], map_refs[dr][:, width:])
                sel_ref[pl.ds(dg * tokens, tokens), dr * rows : (dr + 1) * rows] = jnp.where(
                    keep, proj_grad, 0.0
                ).astype(BF16)
    else:
        sel_ref, refs = refs[0], refs[1:]
        out_refs = refs[-groups:]
        if refs[-1].shape[0] > tokens:
            out_refs = [refs[-1].at[pl.ds(dg * tokens, tokens)] for dg in range(groups)]
    for i, (k, spec) in enumerate(batch):
        shard_at = lax.rem(here + holders - k, holders) * half
        for (dr, offset), block in zip(spec, refs):
            if k == 0:
                first = pl.multiple_of(lax.axis_index("groups") * half, half)
                block = block.at[pl.ds(first, half)]
            wide = block.shape[0]
            at = 0
            if wide < half:
                at = lax.rem(core + replicas - dr, replicas) * (half // replicas) + offset
            columns = pl.ds(pl.multiple_of(shard_at + at, wide), wide)
            for dg in range(groups):
                base = rows_by_rows(g_refs[dg][:, :-LANES], block[...]).astype(BF16)
                lora = 0.0
                for j in range(replicas):
                    lora = lora + jnp.dot(
                        sel_ref[pl.ds(dg * tokens, tokens), j * rows : (j + 1) * rows],
                        map_refs[j][:, columns],
                        preferred_element_type=F32,
                    )
                lora = (ADAPTER_SCALE * lora).astype(BF16)
                out_refs[dg][:, pl.ds(pl.multiple_of(i * half + at, wide), wide)] = (
                    base.astype(F32) + lora.astype(F32)
                ).astype(BF16)
        refs = refs[len(spec) :]


def split_kernel(block_ref, *part_refs):
    rows = part_refs[0].shape[0]
    for j, ref in enumerate(part_refs):
        ref[...] = block_ref[j * rows : (j + 1) * rows]


def column_of(sizes, k, dg):
    groups, holders, shard, half = sizes
    group, here = lax.axis_index("groups"), lax.axis_index("adapter")
    source = lax.rem(group + groups - dg, groups)
    at = lax.rem(here + holders - k, holders) * shard + source * half
    return pl.ds(pl.multiple_of(at, half), half)


def place_kernel(sizes, places, *refs):
    half = sizes[-1]
    for ref, (batch, dg) in zip(refs, places):
        for j, k in enumerate(batch):
            refs[-1][:, column_of(sizes, k, dg)] = ref[:, j * half : (j + 1) * half]


def late_kernel(sizes, places, *refs):
    out_ref, sems = refs[-2:]
    copies = [
        pltpu.make_async_copy(ref, out_ref.at[:, column_of(sizes, batch[0], dg)], sems.at[i])
        for i, (ref, (batch, dg)) in enumerate(zip(refs, places))
    ]
    for copy in copies:
        copy.start()
    for copy in copies:
        copy.wait()


def chip_kernel(replicas, *refs):
    own_ref, came_refs, out_refs = refs[0], refs[1 : 2 * replicas - 1], refs[2 * replicas - 1 :]
    rows = out_refs[0].shape[0]
    split = came_refs[0].shape[1]
    for k, out in enumerate(out_refs):
        for j in range(2):
            at = pl.ds(k * rows, rows), pl.ds(j * split, split)
            total = own_ref[at]
            for ref in came_refs[j::2]:
                total = total + ref[pl.ds(k * rows, rows), :].astype(F32)
            out[:, pl.ds(j * split, split)] = total.astype(out.dtype)


def total_kernel(*refs):
    half_refs, refs = refs[-2:], refs[:-2]
    wide = half_refs[0].shape[1]
    for j, out_ref in enumerate(half_refs):
        at = pl.ds(j * wide, wide)
        total = refs[0][:, at]
        for ref in refs[1:]:
            total = total + ref[:, at].astype(F32)
        out_ref[...] = (ADAPTER_SCALE * total).astype(BF16)


def spread_kernel(width, replicas, *refs):
    core = lax.axis_index("replica")
    down_ref, up_ref = refs[2 * replicas :]
    slots = down_ref.shape[0] // replicas
    rank = down_ref.shape[1]
    wide = refs[0].shape[1]
    for dr in range(replicas):
        at = lax.rem(core + replicas - dr, replicas) * slots
        for j in range(slots):
            rows = slice(j * rank, (j + 1) * rank)
            down_ref[at + j, :, :wide] = refs[2 * dr][rows]
            down_ref[at + j, :, wide:] = refs[2 * dr + 1][rows, : width - wide]
            up_ref[at + j] = refs[2 * dr + 1][rows, width - wide :]


def on_device(
    saved_layer_input,
    value_output_gradient,
    token_adapter_index,
    adapter_slot_index,
    frozen_value_weight,
    adapter_down_weight,
    adapter_up_weight,
):
    inputs = saved_layer_input[0]
    grad_rows = value_output_gradient[0]
    tokens, width = inputs.shape
    value_width = grad_rows.shape[1]
    groups, holders, replicas = (lax.axis_size(a) for a in ("groups", "adapter", "replica"))
    group, here, core = (lax.axis_index(a) for a in ("groups", "adapter", "replica"))
    slots, rank = adapter_down_weight.shape[1:3]
    own_slots = slots // replicas
    rows = own_slots * rank
    frozen = frozen_value_weight[0]
    shard = frozen.shape[0]
    half = shard // groups
    piece = half // replicas
    cols = width + value_width

    tagged = call(
        tag_kernel,
        [jax.ShapeDtypeStruct((tokens, value_width + LANES), BF16)],
        (grad_rows, token_adapter_index[0, :, 0][None], adapter_slot_index),
        scalars=1,
    )[0]
    grads = [tagged] + [
        moved(tagged, lambda g, z, s, r: (g - dg, z, s, r)) for dg in range(1, groups)
    ]

    own = call(
        functools.partial(own_kernel, (groups, holders, shard)),
        [jax.ShapeDtypeStruct((rows, holders * half + value_width), BF16)],
        (adapter_down_weight[0], adapter_up_weight[0]),
    )[0]
    held = [own]
    for k in range(1, holders):
        held.append(moved(own, lambda g, z, s, r: (g, z + k, s, r)))

    ring = [lax.dynamic_slice_in_dim(frozen, (group * replicas + core) * piece, piece, axis=0)]
    ring.append(moved(ring[0], lambda g, z, s, r: (g, z + 1, s, r)))
    held, grads, ring = lax.optimization_barrier((held, grads, ring))
    both, downs = call(
        join_kernel,
        [
            jax.ShapeDtypeStruct((holders * rows, holders * half + value_width), BF16),
            jax.ShapeDtypeStruct((holders * rows, holders * half), BF16),
        ],
        held,
    )
    both = [both] + [
        moved(both, lambda g, z, s, r: (g, z, s, r + dr)) for dr in range(1, replicas)
    ]

    def pieces_of(k, *before):
        if k == 0:
            return [(0, 0)], [frozen]
        mails = [ring[k]]
        if k > 1 and piece % (2 * LANES) == 0:
            shape = jax.ShapeDtypeStruct((piece // 2, value_width), BF16)
            mails = call(split_kernel, [shape] * 2, (ring[k],))
        mails = [after(mail, *before) if before else mail for mail in mails]
        spec, pieces = [(0, 0)], [ring[k]]
        for dr in range(1, replicas):
            for j, mail in enumerate(mails):
                spec.append((dr, j * mail.shape[0]))
                pieces.append(moved(mail, lambda g, z, s, r: (g, z, s, r + dr)))
        if piece % LANES:
            whole = jnp.zeros((half, value_width), BF16)
            for (dr, offset), part in zip(spec, pieces):
                at = ((core - dr) % replicas) * piece + offset
                whole = lax.dynamic_update_slice_in_dim(whole, part, at, axis=0)
            spec, pieces = [(0, 0)], [whole]
        return spec, pieces

    kept = replicas * holders * rows

    def adapter_sums(sel, *before):
        maps = list(both)
        for dg in range(1, groups):
            maps.append(moved(downs, lambda g, z, s, r: (g + dg, z, s, r)))
            for dr in range(1, replicas):
                maps.append(moved(maps[-dr], lambda g, z, s, r: (g, z, s, r + dr)))
        gradients = call(
            functools.partial(adapter_kernel, (groups, holders, replicas, shard, slots, rank)),
            [jax.ShapeDtypeStruct((holders * rows, cols), F32)]
            + [jax.ShapeDtypeStruct((holders * rows, cols // 2), BF16)] * (2 * replicas - 2),
            (inputs, tagged, sel, *maps),
            [jax.ShapeDtypeStruct((kept, width), BF16)],
        )
        part, sent = gradients[0], gradients[1:]
        came = [
            moved(after(sent[2 * dr - 2 + j], *before), lambda g, z, s, r: (g, z, s, r - dr))
            for dr in range(1, replicas)
            for j in range(2)
        ]
        chip = call(
            functools.partial(chip_kernel, replicas),
            [jax.ShapeDtypeStruct((rows, cols), F32)]
            + [jax.ShapeDtypeStruct((rows, cols), BF16)] * (holders - 1),
            (part, *came),
        )
        return part, chip

    batches = [list(range(min(2, holders)))] + [[k] for k in range(2, holders)]
    arrived, crossed = [], []
    for i, batch in enumerate(batches):
        operands, specs = [], []
        for k in batch:
            if k > 1:
                if 2 < k == holders - 1:
                    last = moved(after(ring[0], sel), lambda g, z, s, r: (g, z - 1, s, r))
                else:
                    last = after(ring[-1], sel) if k > 2 else ring[-1]
                    last = moved(last, lambda g, z, s, r: (g, z + 1, s, r))
                ring.append(last)
            gate = arrived[0] if k == 2 else [*arrived[i - 2]] if k > 2 else []
            spec, blocks = pieces_of(k, *gate)
            specs.append((k, spec))
            operands += blocks
        tokens_in = [after(grads[0], part), *grads[1:]] if i == 1 else grads
        out = call(
            functools.partial(
                frozen_kernel, (tokens, groups, holders, replicas, slots, rank), specs
            ),
            (
                [jax.ShapeDtypeStruct((groups * tokens, half), BF16)]
                if i == 1 and len(batches) > 2
                else [jax.ShapeDtypeStruct((tokens, half * len(batch)), BF16)] * groups
            )
            + [jax.ShapeDtypeStruct((groups * tokens, kept), BF16)] * (i == 0),
            [*tokens_in, *both, *([sel] if i else []), *operands],
        )
        if i == 0:
            sel = out[groups]
        mails = list(out[:groups])
        if i == 1 and len(batches) > 2:
            got = moved(out[0], lambda g, z, s, r: (g, z, s - 1, r))
            got = [got[dg * tokens : (dg + 1) * tokens] for dg in range(groups)]
            early = [(batches[0], dg) for dg in range(groups)] + [(batch, 0)]
            passed = call(
                functools.partial(place_kernel, (groups, holders, shard, half), early),
                [jax.ShapeDtypeStruct((tokens, width), BF16)],
                [*arrived[0], got[0]],
            )[0]
            got, passed = lax.optimization_barrier((got, passed))
            late = [
                ((batch, dg), moved(got[dg], lambda g, z, s, r: (g + dg, z, s, r)))
                for dg in range(1, groups)
            ]
            arrived.append([])
            continue
        if i > 2:
            mails = [after(mail, *arrived[-1]) for mail in mails]
        arrived.append(
            [moved(mails[dg], lambda g, z, s, r: (g + dg, z, s - 1, r)) for dg in range(groups)]
        )
        if i > 1:
            late += [((batch, dg), arrived[-1][dg]) for dg in reversed(range(groups))]
        if i == 0:
            part, chip = adapter_sums(sel, *arrived[0])
    sizes = (groups, holders, shard, half)
    if len(batches) > 2:
        passed = pl.pallas_call(
            functools.partial(late_kernel, sizes, [place for place, _ in late]),
            out_shape=jax.ShapeDtypeStruct((tokens, width), BF16),
            in_specs=[pl.BlockSpec(memory_space=pltpu.VMEM)] * len(late)
            + [pl.BlockSpec(memory_space=pl.ANY)],
            out_specs=pl.BlockSpec(memory_space=pl.ANY),
            input_output_aliases={len(late): 0},
            scratch_shapes=[pltpu.SemaphoreType.DMA((len(late),))],
            compiler_params=pltpu.CompilerParams(vmem_limit_bytes=8 * MIB),
            cost_estimate=pl.CostEstimate(flops=1000, bytes_accessed=1000, transcendentals=0),
        )(*[part for _, part in late], passed)
    else:
        passed = call(
            functools.partial(
                place_kernel, sizes, [(batch, dg) for batch in batches for dg in range(groups)]
            ),
            [jax.ShapeDtypeStruct((tokens, width), BF16)],
            [x for got in arrived for x in got],
        )[0]

    sums = [chip[0]] + [
        moved(after(chip[k], ring[-1]), lambda g, z, s, r: (g, z - k, s, r))
        for k in range(1, holders)
    ]
    total = call(total_kernel, [jax.ShapeDtypeStruct((rows, cols // 2), BF16)] * 2, sums)
    totals = list(total)
    for dr in range(1, replicas):
        totals += [moved(x, lambda g, z, s, r: (g, z, s, r + dr)) for x in total]
    totals[0], passed = lax.optimization_barrier((totals[0], passed))
    down_grad, up_grad = call(
        functools.partial(spread_kernel, width, replicas),
        [
            jax.ShapeDtypeStruct((slots, rank, width), BF16),
            jax.ShapeDtypeStruct((slots, rank, value_width), BF16),
        ],
        totals,
    )

    return passed[None], down_grad[None], up_grad[None]


def solution(mesh):
    placed = (
        P("segment", ("groups", "adapter", "replica"), None),
        P("segment", ("groups", "adapter", "replica"), None),
        P("segment", ("groups", "adapter", "replica"), None),
        P("groups"),
        P("segment", "adapter", None),
        P("segment", "adapter", None, None),
        P("segment", "adapter", None, None),
    )
    return jax.shard_map(
        on_device,
        mesh=mesh,
        in_specs=placed,
        out_specs=(
            P("segment", ("groups", "adapter", "replica"), None),
            P(("groups", "segment"), "adapter", None, None),
            P(("groups", "segment"), "adapter", None, None),
        ),
        check_vma=False,
    )
```

```python
import functools
import itertools
import jax
import jax.numpy as jnp
from jax import lax
from jax.experimental import pallas as pl
from jax.experimental.pallas import tpu as pltpu
from jax.sharding import PartitionSpec as P

ADAPTER_SCALE = 2.0
AXES = ("groups", "adapter", "segment", "replica")
LANES = 128
F32 = jnp.float32
BF16 = jnp.bfloat16
MIB = 1024 * 1024


def moved(x, to):
    sizes = [lax.axis_size(a) for a in AXES]
    number = {at: i for i, at in enumerate(itertools.product(*map(range, sizes)))}
    pairs = [
        (i, number[tuple(t % s for t, s in zip(to(*at), sizes))]) for at, i in number.items()
    ]
    return lax.ppermute(x, AXES, pairs)


def after(x, *others):
    return lax.optimization_barrier((x, *others))[0]


def rows_by_rows(a, b):
    return lax.dot_general(a, b, (((1,), (1,)), ((), ())), preferred_element_type=F32)


def columns_by_columns(a, b):
    return lax.dot_general(a, b, (((0,), (0,)), ((), ())), preferred_element_type=F32)


def call(kernel, out_shape, operands, scratch=(), scalars=0):
    held = sum(x.size * x.dtype.itemsize for x in (*operands, *out_shape, *scratch))
    return pl.pallas_call(
        kernel,
        out_shape=out_shape,
        in_specs=[pl.BlockSpec(memory_space=pltpu.VMEM)] * (len(operands) - scalars)
        + [pl.BlockSpec(memory_space=pltpu.SMEM)] * scalars,
        scratch_shapes=[pltpu.VMEM(x.shape, x.dtype) for x in scratch],
        compiler_params=pltpu.CompilerParams(vmem_limit_bytes=2 * held + 4 * MIB),
        cost_estimate=pl.CostEstimate(flops=1000, bytes_accessed=1000, transcendentals=0),
    )(*operands)


def slots_of(tagged_ref):
    return tagged_ref[:, -LANES:].astype(F32)[:, :1]


def row_slots(holders, replicas, slots, rank, dr):
    here, core = lax.axis_index("adapter"), lax.axis_index("replica")
    own_slots = slots // replicas
    lane = lax.broadcasted_iota(jnp.int32, (1, holders * own_slots * rank), 1)
    slot = jnp.zeros_like(lane)
    for k in range(holders):
        for j in range(own_slots):
            start = (k * own_slots + j) * rank
            value = lax.rem(here + holders - k, holders) * slots
            value = value + lax.rem(core + replicas - dr, replicas) * own_slots + j
            slot = jnp.where((lane >= start) & (lane < start + rank), value, slot)
    return slot.astype(F32)


def tag_kernel(g_ref, name_ref, slot_ref, out_ref):
    out_ref[:, :-LANES] = g_ref[...]
    names = name_ref[...]
    slot = jnp.zeros_like(names)
    for j in range(slot_ref.shape[0]):
        slot = jnp.where(names == j, slot_ref[j], slot)
    ones = jnp.ones((1, LANES), F32)
    out_ref[:, -LANES:] = columns_by_columns(slot.astype(F32), ones).astype(BF16)


def join_kernel(*refs):
    both_ref, down_ref = refs[-2:]
    for k, ref in enumerate(refs[:-2]):
        rows = ref.shape[0]
        both_ref[k * rows : (k + 1) * rows] = ref[...]
        down_ref[k * rows : (k + 1) * rows] = ref[:, : down_ref.shape[1]]


def own_kernel(sizes, down_ref, up_ref, out_ref):
    groups, holders, shard = sizes
    half = shard // groups
    rank = down_ref.shape[1]
    slots = out_ref.shape[0] // rank
    first = lax.axis_index("replica") * slots
    for j in range(slots):
        to = pl.ds(j * rank, rank)
        for z in range(holders):
            at = pl.multiple_of(z * shard + lax.axis_index("groups") * half, half)
            out_ref[to, z * half : (z + 1) * half] = down_ref[first + j, :, pl.ds(at, half)]
        out_ref[to, holders * half :] = up_ref[first + j]


def adapter_kernel(sizes, *refs):
    groups, holders, replicas, shard, slots, rank = sizes
    x_ref, g_ref, sel_ref = refs[:3]
    map_refs, refs = refs[3 : 3 + groups * replicas], refs[3 + groups * replicas :]
    own_ref, other_refs, down = refs[0], refs[1:-1], refs[-1]
    group = lax.axis_index("groups")
    tokens, width = x_ref.shape
    rows, cols = own_ref.shape
    half = shard // groups
    for dg in range(groups):
        first = lax.rem(group + groups - dg, groups) * half
        for dr in range(replicas):
            for z in range(holders):
                at = pl.multiple_of(first + z * shard, half)
                down[pl.ds(dr * rows, rows), pl.ds(at, half)] = map_refs[dg * replicas + dr][
                    :, z * half : (z + 1) * half
                ]
    row_slot = [row_slots(holders, replicas, slots, rank, dr) for dr in range(replicas)]
    keep = slots_of(g_ref) == jnp.concatenate(row_slot, axis=1)
    in_sel = jnp.where(keep, rows_by_rows(x_ref[...], down[...]), 0.0).astype(BF16)
    grad_sel = sel_ref[pl.ds(0, tokens), :]
    step, split = 1024, cols // 2
    for at in range(0, cols, step):
        if at < width:
            part = columns_by_columns(grad_sel, x_ref[:, at : at + step])
        else:
            part = columns_by_columns(in_sel, g_ref[:, at - width : at - width + step])
        own_ref[:, at : at + step] = part[:rows]
        for dr in range(1, replicas):
            sent = part[dr * rows : (dr + 1) * rows].astype(BF16)
            for j in range(0, step, LANES):
                ref, to = other_refs[2 * dr - 2 + (at + j) // split], (at + j) % split
                ref[:, to : to + LANES] = sent[:, j : j + LANES]


def frozen_kernel(sizes, batch, *refs):
    tokens, groups, holders, replicas, slots, rank = sizes
    g_refs, refs = refs[:groups], refs[groups:]
    map_refs, refs = refs[:replicas], refs[replicas:]
    core, here = lax.axis_index("replica"), lax.axis_index("adapter")
    rows = map_refs[0].shape[0]
    width = map_refs[0].shape[1] - (g_refs[0].shape[1] - LANES)
    half = width // holders
    if batch[0][0] == 0:
        sel_ref = refs[-1]
        out_refs = refs[-1 - groups : -1]
        for dg in range(groups):
            for dr in range(replicas):
                keep = slots_of(g_refs[dg]) == row_slots(holders, replicas, slots, rank, dr)
                proj_grad = rows_by_rows(g_refs[dg][:, :-LANES], map_refs[dr][:, width:])
                sel_ref[pl.ds(dg * tokens, tokens), dr * rows : (dr + 1) * rows] = jnp.where(
                    keep, proj_grad, 0.0
                ).astype(BF16)
    else:
        sel_ref, refs = refs[0], refs[1:]
        out_refs = refs[-groups:]
        if refs[-1].shape[0] > tokens:
            out_refs = [refs[-1].at[pl.ds(dg * tokens, tokens)] for dg in range(groups)]
    for i, (k, spec) in enumerate(batch):
        shard_at = lax.rem(here + holders - k, holders) * half
        for (dr, offset), block in zip(spec, refs):
            if k == 0:
                first = pl.multiple_of(lax.axis_index("groups") * half, half)
                block = block.at[pl.ds(first, half)]
            wide = block.shape[0]
            at = 0
            if wide < half:
                at = lax.rem(core + replicas - dr, replicas) * (half // replicas) + offset
            columns = pl.ds(pl.multiple_of(shard_at + at, wide), wide)
            for dg in range(groups):
                base = rows_by_rows(g_refs[dg][:, :-LANES], block[...]).astype(BF16)
                lora = 0.0
                for j in range(replicas):
                    lora = lora + jnp.dot(
                        sel_ref[pl.ds(dg * tokens, tokens), j * rows : (j + 1) * rows],
                        map_refs[j][:, columns],
                        preferred_element_type=F32,
                    )
                lora = (ADAPTER_SCALE * lora).astype(BF16)
                out_refs[dg][:, pl.ds(pl.multiple_of(i * half + at, wide), wide)] = (
                    base.astype(F32) + lora.astype(F32)
                ).astype(BF16)
        refs = refs[len(spec) :]


def split_kernel(block_ref, *part_refs):
    rows = part_refs[0].shape[0]
    for j, ref in enumerate(part_refs):
        ref[...] = block_ref[j * rows : (j + 1) * rows]


def column_of(sizes, k, dg):
    groups, holders, shard, half = sizes
    group, here = lax.axis_index("groups"), lax.axis_index("adapter")
    source = lax.rem(group + groups - dg, groups)
    at = lax.rem(here + holders - k, holders) * shard + source * half
    return pl.ds(pl.multiple_of(at, half), half)


def place_kernel(sizes, places, *refs):
    half = sizes[-1]
    for ref, (batch, dg) in zip(refs, places):
        for j, k in enumerate(batch):
            refs[-1][:, column_of(sizes, k, dg)] = ref[:, j * half : (j + 1) * half]


def late_kernel(sizes, places, *refs):
    out_ref, sems = refs[-2:]
    copies = [
        pltpu.make_async_copy(ref, out_ref.at[:, column_of(sizes, batch[0], dg)], sems.at[i])
        for i, (ref, (batch, dg)) in enumerate(zip(refs, places))
    ]
    for copy in copies:
        copy.start()
    for copy in copies:
        copy.wait()


def chip_kernel(replicas, *refs):
    own_ref, came_refs, out_refs = refs[0], refs[1 : 2 * replicas - 1], refs[2 * replicas - 1 :]
    rows = out_refs[0].shape[0]
    split = came_refs[0].shape[1]
    for k, out in enumerate(out_refs):
        for j in range(2):
            at = pl.ds(k * rows, rows), pl.ds(j * split, split)
            total = own_ref[at]
            for ref in came_refs[j::2]:
                total = total + ref[pl.ds(k * rows, rows), :].astype(F32)
            out[:, pl.ds(j * split, split)] = total.astype(out.dtype)


def total_kernel(*refs):
    half_refs, refs = refs[-2:], refs[:-2]
    wide = half_refs[0].shape[1]
    for j, out_ref in enumerate(half_refs):
        at = pl.ds(j * wide, wide)
        total = refs[0][:, at]
        for ref in refs[1:]:
            total = total + ref[:, at].astype(F32)
        out_ref[...] = (ADAPTER_SCALE * total).astype(BF16)


def spread_kernel(width, replicas, *refs):
    core = lax.axis_index("replica")
    down_ref, up_ref = refs[2 * replicas :]
    slots = down_ref.shape[0] // replicas
    rank = down_ref.shape[1]
    wide = refs[0].shape[1]
    for dr in range(replicas):
        at = lax.rem(core + replicas - dr, replicas) * slots
        for j in range(slots):
            rows = slice(j * rank, (j + 1) * rank)
            down_ref[at + j, :, :wide] = refs[2 * dr][rows]
            down_ref[at + j, :, wide:] = refs[2 * dr + 1][rows, : width - wide]
            up_ref[at + j] = refs[2 * dr + 1][rows, width - wide :]


def on_device(
    saved_layer_input,
    value_output_gradient,
    token_adapter_index,
    adapter_slot_index,
    frozen_value_weight,
    adapter_down_weight,
    adapter_up_weight,
):
    inputs = saved_layer_input[0]
    grad_rows = value_output_gradient[0]
    tokens, width = inputs.shape
    value_width = grad_rows.shape[1]
    groups, holders, replicas = (lax.axis_size(a) for a in ("groups", "adapter", "replica"))
    group, here, core = (lax.axis_index(a) for a in ("groups", "adapter", "replica"))
    slots, rank = adapter_down_weight.shape[1:3]
    own_slots = slots // replicas
    rows = own_slots * rank
    frozen = frozen_value_weight[0]
    shard = frozen.shape[0]
    half = shard // groups
    piece = half // replicas
    cols = width + value_width

    tagged = call(
        tag_kernel,
        [jax.ShapeDtypeStruct((tokens, value_width + LANES), BF16)],
        (grad_rows, token_adapter_index[0, :, 0][None], adapter_slot_index),
        scalars=1,
    )[0]
    grads = [tagged] + [
        moved(tagged, lambda g, z, s, r: (g - dg, z, s, r)) for dg in range(1, groups)
    ]

    own = call(
        functools.partial(own_kernel, (groups, holders, shard)),
        [jax.ShapeDtypeStruct((rows, holders * half + value_width), BF16)],
        (adapter_down_weight[0], adapter_up_weight[0]),
    )[0]
    held = [own]
    for k in range(1, holders):
        held.append(moved(own, lambda g, z, s, r: (g, z + k, s, r)))

    ring = [lax.dynamic_slice_in_dim(frozen, (group * replicas + core) * piece, piece, axis=0)]
    ring.append(moved(ring[0], lambda g, z, s, r: (g, z + 1, s, r)))
    held, grads, ring = lax.optimization_barrier((held, grads, ring))
    both, downs = call(
        join_kernel,
        [
            jax.ShapeDtypeStruct((holders * rows, holders * half + value_width), BF16),
            jax.ShapeDtypeStruct((holders * rows, holders * half), BF16),
        ],
        held,
    )
    both = [both] + [
        moved(both, lambda g, z, s, r: (g, z, s, r + dr)) for dr in range(1, replicas)
    ]

    def pieces_of(k, *before):
        if k == 0:
            return [(0, 0)], [frozen]
        mails = [ring[k]]
        if k > 1 and piece % (2 * LANES) == 0:
            shape = jax.ShapeDtypeStruct((piece // 2, value_width), BF16)
            mails = call(split_kernel, [shape] * 2, (ring[k],))
        mails = [after(mail, *before) if before else mail for mail in mails]
        spec, pieces = [(0, 0)], [ring[k]]
        for dr in range(1, replicas):
            for j, mail in enumerate(mails):
                spec.append((dr, j * mail.shape[0]))
                pieces.append(moved(mail, lambda g, z, s, r: (g, z, s, r + dr)))
        if piece % LANES:
            whole = jnp.zeros((half, value_width), BF16)
            for (dr, offset), part in zip(spec, pieces):
                at = ((core - dr) % replicas) * piece + offset
                whole = lax.dynamic_update_slice_in_dim(whole, part, at, axis=0)
            spec, pieces = [(0, 0)], [whole]
        return spec, pieces

    kept = replicas * holders * rows

    def adapter_sums(sel, *before):
        maps = list(both)
        for dg in range(1, groups):
            maps.append(moved(downs, lambda g, z, s, r: (g + dg, z, s, r)))
            for dr in range(1, replicas):
                maps.append(moved(maps[-dr], lambda g, z, s, r: (g, z, s, r + dr)))
        gradients = call(
            functools.partial(adapter_kernel, (groups, holders, replicas, shard, slots, rank)),
            [jax.ShapeDtypeStruct((holders * rows, cols), F32)]
            + [jax.ShapeDtypeStruct((holders * rows, cols // 2), BF16)] * (2 * replicas - 2),
            (inputs, tagged, sel, *maps),
            [jax.ShapeDtypeStruct((kept, width), BF16)],
        )
        part, sent = gradients[0], gradients[1:]
        came = [
            moved(after(sent[2 * dr - 2 + j], *before), lambda g, z, s, r: (g, z, s, r - dr))
            for dr in range(1, replicas)
            for j in range(2)
        ]
        chip = call(
            functools.partial(chip_kernel, replicas),
            [jax.ShapeDtypeStruct((rows, cols), F32)]
            + [jax.ShapeDtypeStruct((rows, cols), BF16)] * (holders - 1),
            (part, *came),
        )
        return part, chip

    batches = [list(range(min(2, holders)))] + [[k] for k in range(2, holders)]
    arrived, crossed = [], []
    for i, batch in enumerate(batches):
        operands, specs = [], []
        for k in batch:
            if k > 1:
                if 2 < k == holders - 1:
                    last = moved(after(ring[0], sel), lambda g, z, s, r: (g, z - 1, s, r))
                else:
                    last = after(ring[-1], sel) if k > 2 else ring[-1]
                    last = moved(last, lambda g, z, s, r: (g, z + 1, s, r))
                ring.append(last)
            gate = arrived[0] if k == 2 else [*arrived[i - 2]] if k > 2 else []
            spec, blocks = pieces_of(k, *gate)
            specs.append((k, spec))
            operands += blocks
        tokens_in = [after(grads[0], part), *grads[1:]] if i == 1 else grads
        out = call(
            functools.partial(
                frozen_kernel, (tokens, groups, holders, replicas, slots, rank), specs
            ),
            (
                [jax.ShapeDtypeStruct((groups * tokens, half), BF16)]
                if i == 1 and len(batches) > 2
                else [jax.ShapeDtypeStruct((tokens, half * len(batch)), BF16)] * groups
            )
            + [jax.ShapeDtypeStruct((groups * tokens, kept), BF16)] * (i == 0),
            [*tokens_in, *both, *([sel] if i else []), *operands],
        )
        if i == 0:
            sel = out[groups]
        mails = list(out[:groups])
        if i == 1 and len(batches) > 2:
            got = moved(out[0], lambda g, z, s, r: (g, z, s - 1, r))
            got = [got[dg * tokens : (dg + 1) * tokens] for dg in range(groups)]
            early = [(batches[0], dg) for dg in range(groups)] + [(batch, 0)]
            passed = call(
                functools.partial(place_kernel, (groups, holders, shard, half), early),
                [jax.ShapeDtypeStruct((tokens, width), BF16)],
                [*arrived[0], got[0]],
            )[0]
            got, passed = lax.optimization_barrier((got, passed))
            late = [
                ((batch, dg), moved(got[dg], lambda g, z, s, r: (g + dg, z, s, r)))
                for dg in range(1, groups)
            ]
            arrived.append([])
            continue
        if i > 2:
            mails = [after(mail, *arrived[-1]) for mail in mails]
        arrived.append(
            [moved(mails[dg], lambda g, z, s, r: (g + dg, z, s - 1, r)) for dg in range(groups)]
        )
        if i > 1:
            late += [((batch, dg), arrived[-1][dg]) for dg in reversed(range(groups))]
        if i == 0:
            part, chip = adapter_sums(sel, *arrived[0])
    sizes = (groups, holders, shard, half)
    if len(batches) > 2:
        passed = pl.pallas_call(
            functools.partial(late_kernel, sizes, [place for place, _ in late]),
            out_shape=jax.ShapeDtypeStruct((tokens, width), BF16),
            in_specs=[pl.BlockSpec(memory_space=pltpu.VMEM)] * len(late)
            + [pl.BlockSpec(memory_space=pl.ANY)],
            out_specs=pl.BlockSpec(memory_space=pl.ANY),
            input_output_aliases={len(late): 0},
            scratch_shapes=[pltpu.SemaphoreType.DMA((len(late),))],
            compiler_params=pltpu.CompilerParams(vmem_limit_bytes=8 * MIB),
            cost_estimate=pl.CostEstimate(flops=1000, bytes_accessed=1000, transcendentals=0),
        )(*[part for _, part in late], passed)
    else:
        passed = call(
            functools.partial(
                place_kernel, sizes, [(batch, dg) for batch in batches for dg in range(groups)]
            ),
            [jax.ShapeDtypeStruct((tokens, width), BF16)],
            [x for got in arrived for x in got],
        )[0]

    sums = [chip[0]] + [
        moved(after(chip[k], ring[-1]), lambda g, z, s, r: (g, z - k, s, r))
        for k in [holders - 1, *range(1, holders - 1)]
    ]
    total = call(total_kernel, [jax.ShapeDtypeStruct((rows, cols // 2), BF16)] * 2, sums)
    totals = list(total)
    for dr in range(1, replicas):
        totals += [moved(x, lambda g, z, s, r: (g, z, s, r + dr)) for x in total]
    totals[0], passed = lax.optimization_barrier((totals[0], passed))
    down_grad, up_grad = call(
        functools.partial(spread_kernel, width, replicas),
        [
            jax.ShapeDtypeStruct((slots, rank, width), BF16),
            jax.ShapeDtypeStruct((slots, rank, value_width), BF16),
        ],
        totals,
    )

    return passed[None], down_grad[None], up_grad[None]


def solution(mesh):
    placed = (
        P("segment", ("groups", "adapter", "replica"), None),
        P("segment", ("groups", "adapter", "replica"), None),
        P("segment", ("groups", "adapter", "replica"), None),
        P("groups"),
        P("segment", "adapter", None),
        P("segment", "adapter", None, None),
        P("segment", "adapter", None, None),
    )
    return jax.shard_map(
        on_device,
        mesh=mesh,
        in_specs=placed,
        out_specs=(
            P("segment", ("groups", "adapter", "replica"), None),
            P(("groups", "segment"), "adapter", None, None),
            P(("groups", "segment"), "adapter", None, None),
        ),
        check_vma=False,
    )
```
